32 devices in a mesh: member: 2 (over x), tx: 8 (over z, y), ty: 2 (over core).
Axes of the slice: x: 2, y: 2, z: 4, core: 2. Of those that a mesh axis runs over, the one named last changes fastest.
Arguments:
- state: float32 [12, 3, 4, 48, 48], P('member', None, None, 'tx', 'ty'), parts along dimension 0, may hold values from -6 to 6
- coriolis: float32 [6, 48, 48], P(None, 'tx', 'ty'), may hold values from -0.3 to 0.3
- wave_speed: float32 [4], replicated, may hold values from 0.1 to 0.4
- edges: int32 [6, 4, 3], replicated, may hold values from 0 to 5, as said below
Outputs:
- state_out: float32 [12, 3, 4, 48, 48], P('member', None, None, 'tx', 'ty'), parts along dimension 0
The draws below stay inside these ranges and needn't reach their ends.
There are 2 independent parts, one for each index of `member`. The reference program is written for one: setup_inputs(seed, part) draws one part's arguments, and reference() takes and returns one part's arrays. A program takes and returns all parts, laid end to end along the dimension named above; an argument that names none is the same for every part. Nothing has to cross between parts.
Inputs may be any that keep to these rules, and one draw needn't show every extreme that they name: edges[f, s] = (g, t, r): side s of face f meets side t of face g, r = 1 where the along-edge directions are opposite. The table is the connectivity of a cube whose faces carry arbitrary labels and frame rotations; the relation is symmetric.
All inputs are finite; a program needn't handle non-finite values.
Results may differ from the reference program's by a relative error of at most 0.00002.
Values sent between devices are 32-bit elements; how exact they have to be, the bound alone decides.
No kernel may reach another device: no remote copies, remote signals or barrier semaphores. Data moves between devices by JAX's collectives and lax.ppermute only.
A program may use at most 128 MiB of HBM per device.

```python
import math
import jax
import jax.numpy as jnp
from jax import lax

FACES = 6
NF = 48
LEV = 4
SUBSTEPS = 2


def cross_ints(left, right):
    return jnp.stack([left[..., 1] * right[..., 2] - left[..., 2] * right[..., 1], left[..., 2] * right[..., 0] - left[..., 0] * right[..., 2], left[..., 0] * right[..., 1] - left[..., 1] * right[..., 0]], -1)


def draw_edges(key, part):
    key = jax.random.fold_in(key, 11)
    key_perm, key_turn = jax.random.split(key)
    ordering = jax.random.permutation(key_perm, FACES).astype(jnp.int32)
    rotations = jax.random.randint(key_turn, (FACES,), 0, 4).astype(jnp.int32)
    axis_index = ordering // 2
    sign_normal = 1 - 2 * (ordering % 2)
    unit_vectors = jnp.eye(3, dtype=jnp.int32)
    normals = unit_vectors[axis_index] * sign_normal[:, None]
    first_axis = unit_vectors[(axis_index + 1) % 3]
    second = cross_ints(normals, first_axis)
    turned = rotations[:, None]
    along_a = jnp.where(turned == 0, first_axis, jnp.where(turned == 1, second, jnp.where(turned == 2, -first_axis, -second)))
    along_b = jnp.where(turned == 0, second, jnp.where(turned == 1, -first_axis, jnp.where(turned == 2, -second, first_axis)))
    outward = jnp.stack([-along_a, along_a, -along_b, along_b], 1)
    matches = jnp.all(outward[:, :, None, :] == normals[None, None, :, :], -1)
    neighbour = jnp.argmax(matches.astype(jnp.int32), -1).astype(jnp.int32)
    returning = outward[neighbour]
    meeting = jnp.all(returning == normals[:, None, None, :], -1)
    far_side = jnp.argmax(meeting.astype(jnp.int32), -1).astype(jnp.int32)
    along_dirs = jnp.stack([along_b, along_b, along_a, along_a], 1)
    far_along = along_dirs[neighbour, far_side]
    flipped = (jnp.sum(along_dirs * far_along, -1) < 0).astype(jnp.int32)
    return jnp.stack([neighbour, far_side, flipped], -1).astype(jnp.int32)


def block_scale(stream_key, shape, cuts, least, top_value):
    def one(axis_at, shards_of):
        heights = jax.random.uniform(jax.random.fold_in(jax.random.fold_in(stream_key, 6), axis_at), (shards_of,), jnp.float32, least / len(cuts), top_value / len(cuts))
        return jnp.repeat(jnp.exp(heights), shape[axis_at] // shards_of).reshape((-1,) + (1,) * (len(shape) - axis_at - 1))

    factor_of = one(*cuts[0])
    for cut in cuts[1:]:
        factor_of = factor_of * one(*cut)
    return factor_of


def normal_values(rng, dims, width, bound, cuts=(), held_as=jnp.bfloat16):
    values = jax.random.normal(rng, dims, jnp.float32) * width
    if len(cuts) > 0:
        values = block_scale(rng, dims, cuts, -0.22, 0.18) * values
    return jnp.clip(values, min=-bound, max=bound).astype(held_as)


def setup_inputs(seed: int = 0, part: int = 0) -> dict:
    arg_keys = jax.random.split(jax.random.key(seed), 5)
    part_splits = jax.random.split(jax.random.fold_in(arg_keys[4], part), 5)
    state = normal_values(part_splits[0], (FACES, 3, LEV, NF, NF), 1.0, 6.0, ((3, 8), (4, 2)), jnp.float32)
    coriolis = jnp.clip(jax.random.uniform(arg_keys[1], (FACES, NF, NF), jnp.float32, -0.3, 0.3) * block_scale(arg_keys[1], (FACES, NF, NF), ((1, 8), (2, 2)), -0.4, 0.0), -0.3, 0.3)
    wave_speed = jnp.clip(jnp.exp(jax.random.uniform(arg_keys[2], (LEV,), jnp.float32, math.log(0.1), math.log(0.4))), 0.1, 0.4)
    edges = draw_edges(jax.random.fold_in(arg_keys[4], 71), part)
    return {"state": state, "coriolis": coriolis, "wave_speed": wave_speed, "edges": edges}


def face_strips(state):
    west_rim = state[:, :, :, 0:3, :]
    east_rim = jnp.flip(state[:, :, :, -3:, :], 3)
    south_rim = jnp.swapaxes(state[:, :, :, :, 0:3], 3, 4)
    north_rim = jnp.swapaxes(jnp.flip(state[:, :, :, :, -3:], 4), 3, 4)
    return jnp.stack([west_rim, east_rim, south_rim, north_rim])


def side_halo(edge_store, edges, face_index, side_index):
    neighbour = edges[face_index, side_index, 0]
    far_side = edges[face_index, side_index, 1]
    flipped = edges[face_index, side_index, 2]
    by_side = lax.dynamic_index_in_dim(edge_store, far_side, 0, False)
    strip_data = lax.dynamic_index_in_dim(by_side, neighbour, 0, False)
    strip_data = jnp.where(flipped == 1, jnp.flip(strip_data, 3), strip_data)
    normal_part = jnp.where(far_side < 2, strip_data[1], strip_data[2])
    along_part = jnp.where(far_side < 2, strip_data[2], strip_data[1])
    sign_here = 2.0 * (side_index % 2) - 1.0
    sign_there = (2 * (far_side % 2) - 1).astype(jnp.float32)
    normal_part = (-sign_here) * sign_there * normal_part
    along_part = (1 - 2 * flipped).astype(jnp.float32) * along_part
    if side_index < 2:
        return jnp.stack([strip_data[0], normal_part, along_part])
    return jnp.stack([strip_data[0], along_part, normal_part])


def advance(padded, wave_speed, coriolis_part, cells_x, cells_y):
    height = padded[..., 0, :, :, :]
    wind_east = padded[..., 1, :, :, :]
    wind_north = padded[..., 2, :, :, :]
    speed = wave_speed[:, None, None]
    east_pred = wind_east[..., 1:cells_x + 5, 3:cells_y + 3] - speed * (0.5 * (height[..., 2:cells_x + 6, 3:cells_y + 3] - height[..., 0:cells_x + 4, 3:cells_y + 3]))
    north_pred = wind_north[..., 3:cells_x + 3, 1:cells_y + 5] - speed * (0.5 * (height[..., 3:cells_x + 3, 2:cells_y + 6] - height[..., 3:cells_x + 3, 0:cells_y + 4]))
    flux_east = (8.0 * (east_pred[..., 3:cells_x + 3, :] - east_pred[..., 1:cells_x + 1, :]) - (east_pred[..., 4:cells_x + 4, :] - east_pred[..., 0:cells_x, :])) / 12.0
    flux_north = (8.0 * (north_pred[..., 3:cells_y + 3] - north_pred[..., 1:cells_y + 1]) - (north_pred[..., 4:cells_y + 4] - north_pred[..., 0:cells_y])) / 12.0
    height_new = height[..., 3:cells_x + 3, 3:cells_y + 3] - speed * (flux_east + flux_north)
    east_inner = east_pred[..., 2:cells_x + 2, :]
    north_inner = north_pred[..., 2:cells_y + 2]
    turning = coriolis_part[..., None, :, :]
    return jnp.stack([height_new, east_inner + turning * north_inner, north_inner - turning * east_inner], axis=-4)


def one_substep(state, coriolis, wave_speed, edges):
    edge_store = face_strips(state)
    results = []
    for face_index in range(FACES):
        padded = jnp.pad(state[face_index], ((0, 0), (0, 0), (3, 3), (3, 3)))
        west_halo = side_halo(edge_store, edges, face_index, 0)
        east_halo = side_halo(edge_store, edges, face_index, 1)
        south_halo = side_halo(edge_store, edges, face_index, 2)
        north_halo = side_halo(edge_store, edges, face_index, 3)
        padded = padded.at[:, :, 0:3, 3:NF + 3].set(jnp.flip(west_halo, 2))
        padded = padded.at[:, :, NF + 3:NF + 6, 3:NF + 3].set(east_halo)
        padded = padded.at[:, :, 3:NF + 3, 0:3].set(jnp.swapaxes(jnp.flip(south_halo, 2), 2, 3))
        padded = padded.at[:, :, 3:NF + 3, NF + 3:NF + 6].set(jnp.swapaxes(north_halo, 2, 3))
        results.append(advance(padded, wave_speed, coriolis[face_index], NF, NF))
    return jnp.stack(results)


def reference(state, coriolis, wave_speed, edges):
    for substep_index in range(SUBSTEPS):
        state = one_substep(state, coriolis, wave_speed, edges)
    return state
```

```python
import functools

import jax
import jax.numpy as jnp
from jax import lax
from jax.experimental import pallas as pl
from jax.experimental.pallas import tpu as pltpu
from jax.sharding import PartitionSpec as P

SUBSTEPS = 2
LANES = 128
WINDOW = 64
MARGIN = 8
VMEM_LIMIT = 32 * 1024 * 1024


def pack_kernel(cx, cy, state_ref, coriolis_ref, out_ref):
    faces, fields = state_ref.shape[:2]
    levels = state_ref.shape[3]
    pairs = faces // 2
    group = pairs * levels
    half = cx // 2
    base = fields * half * group
    out_ref[0] = jnp.zeros(out_ref.shape[1:], jnp.float32)
    for face in range(faces):
        for parity in range(2):
            lane = (face % 2) * WINDOW + MARGIN + parity * cy
            for xp in range(half):
                for field in range(fields):
                    row = field * half * group + xp * group + (face // 2) * levels
                    out_ref[0, row : row + levels, lane : lane + cy] = state_ref[
                        face, field, 2 * xp + parity
                    ]
                row = base + xp * pairs + face // 2
                out_ref[0, row : row + 1, lane : lane + cy] = coriolis_ref[
                    face, 2 * xp + parity : 2 * xp + parity + 1
                ]
    for copy in range(1, out_ref.shape[0]):
        out_ref[copy] = out_ref[0]


def step_kernel(
    cx, cy, count_x, parts_ref, speed_ref, edges_ref, out_ref,
    z_ref, cor_ref, pred_ref, store_ref, tile_ref, flip_ref,
):
    fields = z_ref.shape[0]
    levels = 4
    cells = cx * count_x
    faces = store_ref.shape[0] // 4
    pairs = faces // 2
    group = pairs * levels
    half = cx // 2
    index_x = lax.axis_index("tx")
    index_y = lax.axis_index("ty")

    def row_of(x):
        return (x + 4) * group

    def lanes_of(rows):
        return lax.broadcasted_iota(jnp.int32, (rows, LANES), 1)

    def unpack(source, carry):
        low = lanes_of(group) % WINDOW < MARGIN + cy
        for field in range(fields):
            for xp in range(half):
                row = field * half * group + xp * group
                south = parts_ref[0, source, row : row + group]
                north = parts_ref[1, source, row : row + group]
                even = jnp.where(low, south, pltpu.roll(north, cy, 1))
                odd = jnp.where(low, pltpu.roll(south, LANES - cy, 1), north)
                at = source * (cx * group) + row_of(2 * xp)
                z_ref[field, pl.ds(at, group)] = even
                z_ref[field, pl.ds(at + group, group)] = odd
        base = fields * half * group
        rows = half * pairs
        low = lanes_of(rows) % WINDOW < MARGIN + cy
        south = parts_ref[0, source, base : base + rows]
        north = parts_ref[1, source, base : base + rows]
        even = jnp.where(low, south, pltpu.roll(north, cy, 1))
        odd = jnp.where(low, pltpu.roll(south, LANES - cy, 1), north)
        for parity, values in enumerate((even, odd)):
            for xp in range(half):
                for pair in range(pairs):
                    at = source * (cx * group) + (2 * xp + parity) * group + pair * levels
                    line = values[xp * pairs + pair : xp * pairs + pair + 1]
                    cor_ref[pl.ds(at, levels)] = jnp.broadcast_to(line, (levels, LANES))
        return carry

    lax.fori_loop(0, count_x, unpack, 0)

    def speed_rows(rows):
        level = lax.broadcasted_iota(jnp.int32, (rows, LANES), 0) % levels
        values = jnp.full((rows, LANES), speed_ref[0], jnp.float32)
        for index in range(1, levels):
            values = jnp.where(level == index, speed_ref[index], values)
        return values

    def collect():
        lane = lanes_of(cells)
        place = lane % WINDOW

        def body(pair, carry):
            for slot, field in ((0, 0), (1, 2)):
                merged = jnp.zeros((cells, LANES), jnp.float32)
                for level in range(levels):
                    lines = z_ref[field, pl.ds(row_of(0) + pair * levels + level, cells, group)]
                    shift = (3 * level - (MARGIN + cells - 3)) % LANES
                    gap = WINDOW - cells + 3
                    here = place - 3 * level
                    wanted = ((here >= 0) & (here < 3)) | ((here >= gap) & (here < gap + 3))
                    merged = jnp.where(wanted, pltpu.roll(lines, shift, 1), merged)
                merged = jnp.concatenate(
                    [merged, jnp.zeros((LANES - cells, LANES), jnp.float32)], axis=0
                )
                flip_ref[...] = merged.T
                for side in (2, 3):
                    for odd in range(2):
                        for depth in range(3):
                            if side == 3:
                                base = odd * WINDOW + 2 - depth
                            else:
                                base = ((odd + 1) % 2) * WINDOW + gap + depth
                            at = slot * 3 * levels + depth * levels
                            store_ref[(2 * pair + odd) * 4 + side, at : at + levels] = flip_ref[
                                pl.ds(base, levels, 3)
                            ]
            for slot, field in ((0, 0), (1, 1)):
                for side in (0, 1):
                    for depth in range(3):
                        x = depth if side == 0 else cells - 1 - depth
                        lines = z_ref[field, pl.ds(row_of(x) + pair * levels, levels)]
                        at = slot * 3 * levels + depth * levels
                        for odd in range(2):
                            store_ref[(2 * pair + odd) * 4 + side, at : at + levels] = pltpu.roll(
                                lines, LANES - MARGIN - odd * WINDOW, 1
                            )
            return carry

        lax.fori_loop(0, pairs, body, 0)

    def fetch(face, side):
        at = (face * 4 + side) * 3
        neighbour = edges_ref[at]
        far_side = edges_ref[at + 1]
        flipped = edges_ref[at + 2]
        block = store_ref[neighbour * 4 + far_side]
        lane = lanes_of(block.shape[0])
        order = jnp.where((flipped == 1) & (lane < cells), cells - 1 - lane, lane)
        block = jnp.take_along_axis(block, order, axis=1)
        sign_here = 2 * (side % 2) - 1
        sign_there = 2 * (far_side % 2) - 1
        sign = (-sign_here * sign_there).astype(jnp.float32)
        normal = lax.broadcasted_iota(jnp.int32, block.shape, 0) >= 3 * levels
        return jnp.where(normal, sign * block, block)

    def rim_rows(side):
        def body(pair, carry):
            first = pltpu.roll(fetch(2 * pair, side), MARGIN, 1)
            second = pltpu.roll(fetch(2 * pair + 1, side), MARGIN + WINDOW, 1)
            both = jnp.where(lanes_of(first.shape[0]) < WINDOW, first, second)
            for slot, field in ((0, 0), (1, 1)):
                for depth in range(3):
                    x = -1 - depth if side == 0 else cells + depth
                    at = slot * 3 * levels + depth * levels
                    z_ref[field, pl.ds(row_of(x) + pair * levels, levels)] = both[at : at + levels]
            return carry

        lax.fori_loop(0, pairs, body, 0)

    def rim_columns(start, count):
        def body(pair, carry):
            for odd in range(2):
                for side in (2, 3):
                    block = fetch(2 * pair + odd, side)
                    for slot in range(2):
                        for depth in range(3):
                            at = slot * 3 * levels + depth * levels
                            if side == 3:
                                base = odd * WINDOW + depth
                            else:
                                base = ((odd + 1) % 2) * WINDOW + 15 - depth
                            tile_ref[slot, pl.ds(base, levels, 16)] = block[at : at + levels]
            place = lanes_of(count) % WINDOW
            rim = ((place >= MARGIN - 3) & (place < MARGIN)) | (
                (place >= MARGIN + cells) & (place < MARGIN + cells + 3)
            )
            for slot, field in ((0, 0), (1, 2)):
                flip_ref[...] = tile_ref[slot].T
                lines = flip_ref[pl.ds(start, count)]
                for level in range(levels):
                    rolled = pltpu.roll(lines, (MARGIN + cells - 16 * level) % LANES, 1)
                    at = pl.ds(row_of(start) + pair * levels + level, count, group)
                    z_ref[field, at] = jnp.where(rim, rolled, z_ref[field, at])
            return carry

        lax.fori_loop(0, pairs, body, 0)

    def predict(at, rows):
        speed = speed_rows(rows)
        ahead = z_ref[0, pl.ds(at + group, rows)]
        behind = z_ref[0, pl.ds(at - group, rows)]
        pred_ref[pl.ds(at, rows)] = z_ref[1, pl.ds(at, rows)] - speed * (0.5 * (ahead - behind))

    def update(at, rows):
        speed = speed_rows(rows)
        height = z_ref[0, pl.ds(at, rows)]
        north_pred = z_ref[2, pl.ds(at, rows)] - speed * (
            0.5 * (pltpu.roll(height, LANES - 1, 1) - pltpu.roll(height, 1, 1))
        )
        east_pred = pred_ref[pl.ds(at, rows)]
        flux_east = 8.0 * (
            pred_ref[pl.ds(at + group, rows)] - pred_ref[pl.ds(at - group, rows)]
        ) - (pred_ref[pl.ds(at + 2 * group, rows)] - pred_ref[pl.ds(at - 2 * group, rows)])
        flux_north = 8.0 * (
            pltpu.roll(north_pred, LANES - 1, 1) - pltpu.roll(north_pred, 1, 1)
        ) - (pltpu.roll(north_pred, LANES - 2, 1) - pltpu.roll(north_pred, 2, 1))
        height = height - speed * ((flux_east + flux_north) * (1.0 / 12.0))
        turning = cor_ref[pl.ds(at - row_of(0), rows)]
        return height, east_pred + turning * north_pred, north_pred - turning * east_pred

    collect()
    rim_rows(0)
    rim_rows(1)
    rim_columns(0, cells)
    chunk = cx * group

    def predict_all(index, carry):
        predict(row_of(-2) + index * (4 * group), 4 * group)
        return carry

    lax.fori_loop(0, (cells + 4) // 4, predict_all, 0)

    def update_all(index, carry):
        at = row_of(0) + index * chunk
        for field, values in enumerate(update(at, chunk)):
            z_ref[field, pl.ds(at, chunk)] = values
        return carry

    lax.fori_loop(0, count_x, update_all, 0)

    collect()

    @pl.when(index_x == 0)
    def _():
        rim_rows(0)

    @pl.when(index_x == count_x - 1)
    def _():
        rim_rows(1)

    rim_columns(index_x * cx, cx)
    at = row_of(0) + index_x * chunk
    predict(at - 2 * group, chunk + 4 * group)
    for field, values in enumerate(update(at, chunk)):
        for odd in range(2):
            shift = LANES - (MARGIN + odd * WINDOW) - index_y * cy
            rolled = pltpu.roll(values, shift, 1)
            for x in range(cx):
                for pair in range(pairs):
                    row = x * group + pair * levels
                    out_ref[2 * pair + odd, field, x] = rolled[row : row + levels, :cy]


def fast_on_device(state, coriolis, wave_speed, edges):
    count_x = lax.axis_size("tx")
    faces, fields, levels, cx, cy = state.shape
    pairs = faces // 2
    group = pairs * levels
    rows = fields * (cx // 2) * group + (cx // 2) * pairs
    rows = -(-rows // 8) * 8
    cells = cx * count_x
    packed = pl.pallas_call(
        functools.partial(pack_kernel, cx, cy),
        out_shape=jax.ShapeDtypeStruct((count_x, rows, LANES), jnp.float32),
        in_specs=[pl.BlockSpec(memory_space=pltpu.VMEM)] * 2,
        out_specs=pl.BlockSpec(memory_space=pltpu.VMEM),
        compiler_params=pltpu.CompilerParams(vmem_limit_bytes=VMEM_LIMIT),
        name="pack",
    )(jnp.swapaxes(state, 2, 3), coriolis)
    column = lax.all_to_all(packed, "tx", 0, 0)
    parts = lax.all_gather(column, "ty")
    z_rows = (cells + 8) * group
    out = pl.pallas_call(
        functools.partial(step_kernel, cx, cy, count_x),
        out_shape=jax.ShapeDtypeStruct((faces, fields, cx, levels, cy), jnp.float32),
        in_specs=[
            pl.BlockSpec(memory_space=pltpu.VMEM),
            pl.BlockSpec(memory_space=pltpu.SMEM),
            pl.BlockSpec(memory_space=pltpu.SMEM),
        ],
        out_specs=pl.BlockSpec(memory_space=pltpu.VMEM),
        scratch_shapes=[
            pltpu.VMEM((fields, z_rows, LANES), jnp.float32),
            pltpu.VMEM((cells * group, LANES), jnp.float32),
            pltpu.VMEM((z_rows, LANES), jnp.float32),
            pltpu.VMEM((faces * 4, 6 * levels, LANES), jnp.float32),
            pltpu.VMEM((2, LANES, LANES), jnp.float32),
            pltpu.VMEM((LANES, LANES), jnp.float32),
        ],
        compiler_params=pltpu.CompilerParams(vmem_limit_bytes=VMEM_LIMIT),
        name="substeps",
    )(parts, wave_speed, edges.reshape(-1))
    return jnp.swapaxes(out, 2, 3)


def padded_2(block, sides, width):
    for axis, dim in sides:
        count = lax.axis_size(axis)
        forward = [(i, i + 1) for i in range(count - 1)]
        backward = [(target, source) for source, target in forward]
        low = lax.ppermute(
            lax.slice_in_dim(block, block.shape[dim] - width, None, axis=dim), axis, forward
        )
        high = lax.ppermute(lax.slice_in_dim(block, 0, width, axis=dim), axis, backward)
        block = jnp.concatenate([low, block, high], axis=dim)
    return block


def spread(block, axis, owner):
    block = jnp.where(lax.axis_index(axis) == owner, block, jnp.zeros_like(block))
    return lax.psum(block, axis)


def rotate_strip(strip_data, side_index, far_side, flipped):
    normal_part = jnp.where(far_side < 2, strip_data[1], strip_data[2])
    along_part = jnp.where(far_side < 2, strip_data[2], strip_data[1])
    sign_here = 2.0 * (side_index % 2) - 1.0
    sign_there = (2 * (far_side % 2) - 1).astype(jnp.float32)
    normal_part = -sign_here * sign_there * normal_part
    along_part = (1 - 2 * flipped).astype(jnp.float32) * along_part
    if side_index < 2:
        return jnp.stack([strip_data[0], normal_part, along_part])
    return jnp.stack([strip_data[0], along_part, normal_part])


def window_strip(store, side_pick, neighbour, flipped, start, width):
    full_length = store.shape[5]
    begin = jnp.where(flipped == 1, full_length - start - width, start)
    zero = jnp.zeros((), jnp.int32)
    sizes_here = (1, 1, store.shape[2], store.shape[3], store.shape[4], width)
    piece = lax.dynamic_slice(store, (side_pick, neighbour, zero, zero, zero, begin), sizes_here)[
        0, 0
    ]
    return jnp.where(flipped == 1, jnp.flip(piece, 3), piece)


def side_halo(edge_store, edges, face_index, side_index, start, width):
    neighbour = edges[face_index, side_index, 0]
    far_side = edges[face_index, side_index, 1]
    flipped = edges[face_index, side_index, 2]
    strip_data = window_strip(edge_store, far_side, neighbour, flipped, start, width)
    return rotate_strip(strip_data, side_index, far_side, flipped)


def advance(padded, wave_speed, coriolis_part, cells_x, cells_y):
    height = padded[..., 0, :, :, :]
    wind_east = padded[..., 1, :, :, :]
    wind_north = padded[..., 2, :, :, :]
    speed = wave_speed[:, None, None]
    east_pred = wind_east[..., 1 : cells_x + 5, 3 : cells_y + 3] - speed * (
        0.5
        * (
            height[..., 2 : cells_x + 6, 3 : cells_y + 3]
            - height[..., 0 : cells_x + 4, 3 : cells_y + 3]
        )
    )
    north_pred = wind_north[..., 3 : cells_x + 3, 1 : cells_y + 5] - speed * (
        0.5
        * (
            height[..., 3 : cells_x + 3, 2 : cells_y + 6]
            - height[..., 3 : cells_x + 3, 0 : cells_y + 4]
        )
    )
    flux_east = (
        8.0 * (east_pred[..., 3 : cells_x + 3, :] - east_pred[..., 1 : cells_x + 1, :])
        - (east_pred[..., 4 : cells_x + 4, :] - east_pred[..., 0:cells_x, :])
    ) / 12.0
    flux_north = (
        8.0 * (north_pred[..., 3 : cells_y + 3] - north_pred[..., 1 : cells_y + 1])
        - (north_pred[..., 4 : cells_y + 4] - north_pred[..., 0:cells_y])
    ) / 12.0
    height_new = height[..., 3 : cells_x + 3, 3 : cells_y + 3] - speed * (flux_east + flux_north)
    east_inner = east_pred[..., 2 : cells_x + 2, :]
    north_inner = north_pred[..., 2 : cells_y + 2]
    turning = coriolis_part[..., None, :, :]
    return jnp.stack(
        [height_new, east_inner + turning * north_inner, north_inner - turning * east_inner],
        axis=-4,
    )


def one_substep(state, coriolis, wave_speed, edges, count_x, count_y, index_x, index_y):
    faces = state.shape[0]
    cells_x = state.shape[3]
    cells_y = state.shape[4]
    padded = padded_2(state, (("tx", 3), ("ty", 4)), 3)
    west_rim = state[:, :, :, 0:3, :]
    east_rim = jnp.flip(state[:, :, :, cells_x - 3 :, :], 3)
    south_rim = jnp.swapaxes(state[:, :, :, :, 0:3], 3, 4)
    north_rim = jnp.swapaxes(jnp.flip(state[:, :, :, :, cells_y - 3 :], 4), 3, 4)
    west_part = spread(west_rim, "tx", 0)
    east_part = spread(east_rim, "tx", count_x - 1)
    west_full, east_full = (
        lax.all_gather(west_part, "ty", axis=4, tiled=True),
        lax.all_gather(east_part, "ty", axis=4, tiled=True),
    )
    south_row, north_row = (
        lax.all_gather(south_rim, "tx", axis=4, tiled=True),
        lax.all_gather(north_rim, "tx", axis=4, tiled=True),
    )
    south_all, north_all = (
        lax.all_gather(south_row, "ty", axis=0, tiled=True),
        lax.all_gather(north_row, "ty", axis=0, tiled=True),
    )
    south_full = south_all[0:faces]
    north_full = north_all[(count_y - 1) * faces : count_y * faces]
    edge_store = jnp.stack([west_full, east_full, south_full, north_full])
    halos = []
    for side_index in range(4):
        if side_index < 2:
            slabs = jnp.stack(
                [
                    side_halo(edge_store, edges, face_index, side_index, index_y * cells_y, cells_y)
                    for face_index in range(faces)
                ]
            )
        else:
            slabs = jnp.stack(
                [
                    side_halo(edge_store, edges, face_index, side_index, index_x * cells_x, cells_x)
                    for face_index in range(faces)
                ]
            )
        halos.append(slabs)
    west_region = padded[:, :, :, 0:3, 3 : cells_y + 3]
    padded = padded.at[:, :, :, 0:3, 3 : cells_y + 3].set(
        jnp.where(index_x == 0, jnp.flip(halos[0], 3), west_region)
    )
    east_region = padded[:, :, :, cells_x + 3 : cells_x + 6, 3 : cells_y + 3]
    padded = padded.at[:, :, :, cells_x + 3 : cells_x + 6, 3 : cells_y + 3].set(
        jnp.where(index_x == count_x - 1, halos[1], east_region)
    )
    south_region = padded[:, :, :, 3 : cells_x + 3, 0:3]
    padded = padded.at[:, :, :, 3 : cells_x + 3, 0:3].set(
        jnp.where(index_y == 0, jnp.swapaxes(jnp.flip(halos[2], 3), 3, 4), south_region)
    )
    north_region = padded[:, :, :, 3 : cells_x + 3, cells_y + 3 : cells_y + 6]
    padded = padded.at[:, :, :, 3 : cells_x + 3, cells_y + 3 : cells_y + 6].set(
        jnp.where(index_y == count_y - 1, jnp.swapaxes(halos[3], 3, 4), north_region)
    )
    return advance(padded, wave_speed, coriolis, cells_x, cells_y)


def on_device(state, coriolis, wave_speed, edges):
    count_x = lax.axis_size("tx")
    count_y = lax.axis_size("ty")
    index_x = lax.axis_index("tx")
    index_y = lax.axis_index("ty")
    for substep_index in range(SUBSTEPS):
        state = one_substep(state, coriolis, wave_speed, edges, count_x, count_y, index_x, index_y)
    return state


def fits(state):
    count_x = lax.axis_size("tx")
    faces, fields, levels, cells_x, cells_y = state.shape
    return (
        lax.axis_size("ty") == 2
        and faces % 2 == 0
        and levels == 4
        and cells_x == 6
        and cells_x * count_x == 2 * cells_y
        and 2 * cells_y + 2 * MARGIN <= WINDOW
    )


def either(state, coriolis, wave_speed, edges):
    if fits(state):
        return fast_on_device(state, coriolis, wave_speed, edges)
    return on_device(state, coriolis, wave_speed, edges)


def solution(mesh):
    in_specs = (P("member", None, None, "tx", "ty"), P(None, "tx", "ty"), P(), P())
    out_specs = P("member", None, None, "tx", "ty")
    return jax.shard_map(
        either, mesh=mesh, in_specs=in_specs, out_specs=out_specs, check_vma=False
    )
```

```python
import functools

import jax
import jax.numpy as jnp
from jax import lax
from jax.experimental import pallas as pl
from jax.experimental.pallas import tpu as pltpu
from jax.sharding import PartitionSpec as P

SUBSTEPS = 2
LANES = 128
WINDOW = 64
MARGIN = 8
VMEM_LIMIT = 32 * 1024 * 1024


def pack_kernel(cx, cy, state_ref, coriolis_ref, out_ref):
    faces, fields = state_ref.shape[:2]
    levels = state_ref.shape[3]
    pairs = faces // 2
    group = pairs * levels
    half = cx // 2
    base = fields * half * group
    out_ref[0] = jnp.zeros(out_ref.shape[1:], jnp.float32)
    for face in range(faces):
        for parity in range(2):
            lane = (face % 2) * WINDOW + MARGIN + parity * cy
            for xp in range(half):
                for field in range(fields):
                    row = field * half * group + xp * group + (face // 2) * levels
                    out_ref[0, row : row + levels, lane : lane + cy] = state_ref[
                        face, field, 2 * xp + parity
                    ]
                row = base + xp * pairs + face // 2
                out_ref[0, row : row + 1, lane : lane + cy] = coriolis_ref[
                    face, 2 * xp + parity : 2 * xp + parity + 1
                ]
    for copy in range(1, out_ref.shape[0]):
        out_ref[copy] = out_ref[0]


def step_kernel(
    cx, cy, count_x, parts_ref, speed_ref, edges_ref, out_ref,
    z_ref, cor_ref, pred_ref, store_ref, tile_ref, flip_ref,
):
    fields = z_ref.shape[0]
    levels = 4
    cells = cx * count_x
    faces = store_ref.shape[0] // 4
    pairs = faces // 2
    group = pairs * levels
    half = cx // 2
    index_x = lax.axis_index("tx")
    index_y = lax.axis_index("ty")

    def row_of(x):
        return (x + 4) * group

    def lanes_of(rows):
        return lax.broadcasted_iota(jnp.int32, (rows, LANES), 1)

    def unpack(source, carry):
        low = lanes_of(group) % WINDOW < MARGIN + cy
        for field in range(fields):
            for xp in range(half):
                row = field * half * group + xp * group
                south = parts_ref[0, source ^ index_x, row : row + group]
                north = parts_ref[1, source ^ index_x, row : row + group]
                even = jnp.where(low, south, pltpu.roll(north, cy, 1))
                odd = jnp.where(low, pltpu.roll(south, LANES - cy, 1), north)
                at = source * (cx * group) + row_of(2 * xp)
                z_ref[field, pl.ds(at, group)] = even
                z_ref[field, pl.ds(at + group, group)] = odd
        base = fields * half * group
        rows = half * pairs
        low = lanes_of(rows) % WINDOW < MARGIN + cy
        south = parts_ref[0, source ^ index_x, base : base + rows]
        north = parts_ref[1, source ^ index_x, base : base + rows]
        even = jnp.where(low, south, pltpu.roll(north, cy, 1))
        odd = jnp.where(low, pltpu.roll(south, LANES - cy, 1), north)
        for parity, values in enumerate((even, odd)):
            for xp in range(half):
                for pair in range(pairs):
                    at = source * (cx * group) + (2 * xp + parity) * group + pair * levels
                    line = values[xp * pairs + pair : xp * pairs + pair + 1]
                    cor_ref[pl.ds(at, levels)] = jnp.broadcast_to(line, (levels, LANES))
        return carry

    lax.fori_loop(0, count_x, unpack, 0)

    def speed_rows(rows):
        level = lax.broadcasted_iota(jnp.int32, (rows, LANES), 0) % levels
        values = jnp.full((rows, LANES), speed_ref[0], jnp.float32)
        for index in range(1, levels):
            values = jnp.where(level == index, speed_ref[index], values)
        return values

    def collect():
        lane = lanes_of(cells)
        place = lane % WINDOW

        def body(pair, carry):
            for slot, field in ((0, 0), (1, 2)):
                merged = jnp.zeros((cells, LANES), jnp.float32)
                for level in range(levels):
                    lines = z_ref[field, pl.ds(row_of(0) + pair * levels + level, cells, group)]
                    shift = (3 * level - (MARGIN + cells - 3)) % LANES
                    gap = WINDOW - cells + 3
                    here = place - 3 * level
                    wanted = ((here >= 0) & (here < 3)) | ((here >= gap) & (here < gap + 3))
                    merged = jnp.where(wanted, pltpu.roll(lines, shift, 1), merged)
                merged = jnp.concatenate(
                    [merged, jnp.zeros((LANES - cells, LANES), jnp.float32)], axis=0
                )
                flip_ref[...] = merged.T
                for side in (2, 3):
                    for odd in range(2):
                        for depth in range(3):
                            if side == 3:
                                base = odd * WINDOW + 2 - depth
                            else:
                                base = ((odd + 1) % 2) * WINDOW + gap + depth
                            at = slot * 3 * levels + depth * levels
                            store_ref[(2 * pair + odd) * 4 + side, at : at + levels] = flip_ref[
                                pl.ds(base, levels, 3)
                            ]
            for slot, field in ((0, 0), (1, 1)):
                for side in (0, 1):
                    for depth in range(3):
                        x = depth if side == 0 else cells - 1 - depth
                        lines = z_ref[field, pl.ds(row_of(x) + pair * levels, levels)]
                        at = slot * 3 * levels + depth * levels
                        for odd in range(2):
                            store_ref[(2 * pair + odd) * 4 + side, at : at + levels] = pltpu.roll(
                                lines, LANES - MARGIN - odd * WINDOW, 1
                            )
            return carry

        lax.fori_loop(0, pairs, body, 0)

    def fetch(face, side):
        at = (face * 4 + side) * 3
        neighbour = edges_ref[at]
        far_side = edges_ref[at + 1]
        flipped = edges_ref[at + 2]
        block = store_ref[neighbour * 4 + far_side]
        lane = lanes_of(block.shape[0])
        order = jnp.where((flipped == 1) & (lane < cells), cells - 1 - lane, lane)
        block = jnp.take_along_axis(block, order, axis=1)
        sign_here = 2 * (side % 2) - 1
        sign_there = 2 * (far_side % 2) - 1
        sign = (-sign_here * sign_there).astype(jnp.float32)
        normal = lax.broadcasted_iota(jnp.int32, block.shape, 0) >= 3 * levels
        return jnp.where(normal, sign * block, block)

    def rim_rows(side):
        def body(pair, carry):
            first = pltpu.roll(fetch(2 * pair, side), MARGIN, 1)
            second = pltpu.roll(fetch(2 * pair + 1, side), MARGIN + WINDOW, 1)
            both = jnp.where(lanes_of(first.shape[0]) < WINDOW, first, second)
            for slot, field in ((0, 0), (1, 1)):
                for depth in range(3):
                    x = -1 - depth if side == 0 else cells + depth
                    at = slot * 3 * levels + depth * levels
                    z_ref[field, pl.ds(row_of(x) + pair * levels, levels)] = both[at : at + levels]
            return carry

        lax.fori_loop(0, pairs, body, 0)

    def rim_columns(start, count):
        def body(pair, carry):
            for odd in range(2):
                for side in (2, 3):
                    block = fetch(2 * pair + odd, side)
                    for slot in range(2):
                        for depth in range(3):
                            at = slot * 3 * levels + depth * levels
                            if side == 3:
                                base = odd * WINDOW + depth
                            else:
                                base = ((odd + 1) % 2) * WINDOW + 15 - depth
                            tile_ref[slot, pl.ds(base, levels, 16)] = block[at : at + levels]
            place = lanes_of(count) % WINDOW
            rim = ((place >= MARGIN - 3) & (place < MARGIN)) | (
                (place >= MARGIN + cells) & (place < MARGIN + cells + 3)
            )
            for slot, field in ((0, 0), (1, 2)):
                flip_ref[...] = tile_ref[slot].T
                lines = flip_ref[pl.ds(start, count)]
                for level in range(levels):
                    rolled = pltpu.roll(lines, (MARGIN + cells - 16 * level) % LANES, 1)
                    at = pl.ds(row_of(start) + pair * levels + level, count, group)
                    z_ref[field, at] = jnp.where(rim, rolled, z_ref[field, at])
            return carry

        lax.fori_loop(0, pairs, body, 0)

    def predict(at, rows):
        speed = speed_rows(rows)
        ahead = z_ref[0, pl.ds(at + group, rows)]
        behind = z_ref[0, pl.ds(at - group, rows)]
        pred_ref[pl.ds(at, rows)] = z_ref[1, pl.ds(at, rows)] - speed * (0.5 * (ahead - behind))

    def update(at, rows):
        speed = speed_rows(rows)
        height = z_ref[0, pl.ds(at, rows)]
        north_pred = z_ref[2, pl.ds(at, rows)] - speed * (
            0.5 * (pltpu.roll(height, LANES - 1, 1) - pltpu.roll(height, 1, 1))
        )
        east_pred = pred_ref[pl.ds(at, rows)]
        flux_east = 8.0 * (
            pred_ref[pl.ds(at + group, rows)] - pred_ref[pl.ds(at - group, rows)]
        ) - (pred_ref[pl.ds(at + 2 * group, rows)] - pred_ref[pl.ds(at - 2 * group, rows)])
        flux_north = 8.0 * (
            pltpu.roll(north_pred, LANES - 1, 1) - pltpu.roll(north_pred, 1, 1)
        ) - (pltpu.roll(north_pred, LANES - 2, 1) - pltpu.roll(north_pred, 2, 1))
        height = height - speed * ((flux_east + flux_north) * (1.0 / 12.0))
        turning = cor_ref[pl.ds(at - row_of(0), rows)]
        return height, east_pred + turning * north_pred, north_pred - turning * east_pred

    collect()
    rim_rows(0)
    rim_rows(1)
    rim_columns(0, cells)
    chunk = cx * group

    def predict_all(index, carry):
        predict(row_of(-2) + index * (4 * group), 4 * group)
        return carry

    lax.fori_loop(0, (cells + 4) // 4, predict_all, 0)

    def update_all(index, carry):
        at = row_of(0) + index * chunk
        for field, values in enumerate(update(at, chunk)):
            z_ref[field, pl.ds(at, chunk)] = values
        return carry

    lax.fori_loop(0, count_x, update_all, 0)

    collect()

    @pl.when(index_x == 0)
    def _():
        rim_rows(0)

    @pl.when(index_x == count_x - 1)
    def _():
        rim_rows(1)

    rim_columns(index_x * cx, cx)
    at = row_of(0) + index_x * chunk
    predict(at - 2 * group, chunk + 4 * group)
    for field, values in enumerate(update(at, chunk)):
        for odd in range(2):
            shift = LANES - (MARGIN + odd * WINDOW) - index_y * cy
            rolled = pltpu.roll(values, shift, 1)
            for x in range(cx):
                for pair in range(pairs):
                    row = x * group + pair * levels
                    out_ref[2 * pair + odd, field, x] = rolled[row : row + levels, :cy]


def fast_on_device(state, coriolis, wave_speed, edges):
    count_x = lax.axis_size("tx")
    faces, fields, levels, cx, cy = state.shape
    pairs = faces // 2
    group = pairs * levels
    rows = fields * (cx // 2) * group + (cx // 2) * pairs
    rows = -(-rows // 8) * 8
    cells = cx * count_x
    packed = pl.pallas_call(
        functools.partial(pack_kernel, cx, cy),
        out_shape=jax.ShapeDtypeStruct((1, rows, LANES), jnp.float32),
        in_specs=[pl.BlockSpec(memory_space=pltpu.VMEM)] * 2,
        out_specs=pl.BlockSpec(memory_space=pltpu.VMEM),
        compiler_params=pltpu.CompilerParams(vmem_limit_bytes=VMEM_LIMIT),
        name="pack",
    )(jnp.swapaxes(state, 2, 3), coriolis)
    chunks = [packed[0]]
    for other in range(1, count_x):
        pairs_of = [(index, index ^ other) for index in range(count_x)]
        chunks.append(lax.ppermute(packed[0], "tx", pairs_of))
    column = jnp.stack(chunks)
    parts = lax.all_gather(column, "ty")
    z_rows = (cells + 8) * group
    out = pl.pallas_call(
        functools.partial(step_kernel, cx, cy, count_x),
        out_shape=jax.ShapeDtypeStruct((faces, fields, cx, levels, cy), jnp.float32),
        in_specs=[
            pl.BlockSpec(memory_space=pltpu.VMEM),
            pl.BlockSpec(memory_space=pltpu.SMEM),
            pl.BlockSpec(memory_space=pltpu.SMEM),
        ],
        out_specs=pl.BlockSpec(memory_space=pltpu.VMEM),
        scratch_shapes=[
            pltpu.VMEM((fields, z_rows, LANES), jnp.float32),
            pltpu.VMEM((cells * group, LANES), jnp.float32),
            pltpu.VMEM((z_rows, LANES), jnp.float32),
            pltpu.VMEM((faces * 4, 6 * levels, LANES), jnp.float32),
            pltpu.VMEM((2, LANES, LANES), jnp.float32),
            pltpu.VMEM((LANES, LANES), jnp.float32),
        ],
        compiler_params=pltpu.CompilerParams(vmem_limit_bytes=VMEM_LIMIT),
        name="substeps",
    )(parts, wave_speed, edges.reshape(-1))
    return jnp.swapaxes(out, 2, 3)


def padded_2(block, sides, width):
    for axis, dim in sides:
        count = lax.axis_size(axis)
        forward = [(i, i + 1) for i in range(count - 1)]
        backward = [(target, source) for source, target in forward]
        low = lax.ppermute(
            lax.slice_in_dim(block, block.shape[dim] - width, None, axis=dim), axis, forward
        )
        high = lax.ppermute(lax.slice_in_dim(block, 0, width, axis=dim), axis, backward)
        block = jnp.concatenate([low, block, high], axis=dim)
    return block


def spread(block, axis, owner):
    block = jnp.where(lax.axis_index(axis) == owner, block, jnp.zeros_like(block))
    return lax.psum(block, axis)


def rotate_strip(strip_data, side_index, far_side, flipped):
    normal_part = jnp.where(far_side < 2, strip_data[1], strip_data[2])
    along_part = jnp.where(far_side < 2, strip_data[2], strip_data[1])
    sign_here = 2.0 * (side_index % 2) - 1.0
    sign_there = (2 * (far_side % 2) - 1).astype(jnp.float32)
    normal_part = -sign_here * sign_there * normal_part
    along_part = (1 - 2 * flipped).astype(jnp.float32) * along_part
    if side_index < 2:
        return jnp.stack([strip_data[0], normal_part, along_part])
    return jnp.stack([strip_data[0], along_part, normal_part])


def window_strip(store, side_pick, neighbour, flipped, start, width):
    full_length = store.shape[5]
    begin = jnp.where(flipped == 1, full_length - start - width, start)
    zero = jnp.zeros((), jnp.int32)
    sizes_here = (1, 1, store.shape[2], store.shape[3], store.shape[4], width)
    piece = lax.dynamic_slice(store, (side_pick, neighbour, zero, zero, zero, begin), sizes_here)[
        0, 0
    ]
    return jnp.where(flipped == 1, jnp.flip(piece, 3), piece)


def side_halo(edge_store, edges, face_index, side_index, start, width):
    neighbour = edges[face_index, side_index, 0]
    far_side = edges[face_index, side_index, 1]
    flipped = edges[face_index, side_index, 2]
    strip_data = window_strip(edge_store, far_side, neighbour, flipped, start, width)
    return rotate_strip(strip_data, side_index, far_side, flipped)


def advance(padded, wave_speed, coriolis_part, cells_x, cells_y):
    height = padded[..., 0, :, :, :]
    wind_east = padded[..., 1, :, :, :]
    wind_north = padded[..., 2, :, :, :]
    speed = wave_speed[:, None, None]
    east_pred = wind_east[..., 1 : cells_x + 5, 3 : cells_y + 3] - speed * (
        0.5
        * (
            height[..., 2 : cells_x + 6, 3 : cells_y + 3]
            - height[..., 0 : cells_x + 4, 3 : cells_y + 3]
        )
    )
    north_pred = wind_north[..., 3 : cells_x + 3, 1 : cells_y + 5] - speed * (
        0.5
        * (
            height[..., 3 : cells_x + 3, 2 : cells_y + 6]
            - height[..., 3 : cells_x + 3, 0 : cells_y + 4]
        )
    )
    flux_east = (
        8.0 * (east_pred[..., 3 : cells_x + 3, :] - east_pred[..., 1 : cells_x + 1, :])
        - (east_pred[..., 4 : cells_x + 4, :] - east_pred[..., 0:cells_x, :])
    ) / 12.0
    flux_north = (
        8.0 * (north_pred[..., 3 : cells_y + 3] - north_pred[..., 1 : cells_y + 1])
        - (north_pred[..., 4 : cells_y + 4] - north_pred[..., 0:cells_y])
    ) / 12.0
    height_new = height[..., 3 : cells_x + 3, 3 : cells_y + 3] - speed * (flux_east + flux_north)
    east_inner = east_pred[..., 2 : cells_x + 2, :]
    north_inner = north_pred[..., 2 : cells_y + 2]
    turning = coriolis_part[..., None, :, :]
    return jnp.stack(
        [height_new, east_inner + turning * north_inner, north_inner - turning * east_inner],
        axis=-4,
    )


def one_substep(state, coriolis, wave_speed, edges, count_x, count_y, index_x, index_y):
    faces = state.shape[0]
    cells_x = state.shape[3]
    cells_y = state.shape[4]
    padded = padded_2(state, (("tx", 3), ("ty", 4)), 3)
    west_rim = state[:, :, :, 0:3, :]
    east_rim = jnp.flip(state[:, :, :, cells_x - 3 :, :], 3)
    south_rim = jnp.swapaxes(state[:, :, :, :, 0:3], 3, 4)
    north_rim = jnp.swapaxes(jnp.flip(state[:, :, :, :, cells_y - 3 :], 4), 3, 4)
    west_part = spread(west_rim, "tx", 0)
    east_part = spread(east_rim, "tx", count_x - 1)
    west_full, east_full = (
        lax.all_gather(west_part, "ty", axis=4, tiled=True),
        lax.all_gather(east_part, "ty", axis=4, tiled=True),
    )
    south_row, north_row = (
        lax.all_gather(south_rim, "tx", axis=4, tiled=True),
        lax.all_gather(north_rim, "tx", axis=4, tiled=True),
    )
    south_all, north_all = (
        lax.all_gather(south_row, "ty", axis=0, tiled=True),
        lax.all_gather(north_row, "ty", axis=0, tiled=True),
    )
    south_full = south_all[0:faces]
    north_full = north_all[(count_y - 1) * faces : count_y * faces]
    edge_store = jnp.stack([west_full, east_full, south_full, north_full])
    halos = []
    for side_index in range(4):
        if side_index < 2:
            slabs = jnp.stack(
                [
                    side_halo(edge_store, edges, face_index, side_index, index_y * cells_y, cells_y)
                    for face_index in range(faces)
                ]
            )
        else:
            slabs = jnp.stack(
                [
                    side_halo(edge_store, edges, face_index, side_index, index_x * cells_x, cells_x)
                    for face_index in range(faces)
                ]
            )
        halos.append(slabs)
    west_region = padded[:, :, :, 0:3, 3 : cells_y + 3]
    padded = padded.at[:, :, :, 0:3, 3 : cells_y + 3].set(
        jnp.where(index_x == 0, jnp.flip(halos[0], 3), west_region)
    )
    east_region = padded[:, :, :, cells_x + 3 : cells_x + 6, 3 : cells_y + 3]
    padded = padded.at[:, :, :, cells_x + 3 : cells_x + 6, 3 : cells_y + 3].set(
        jnp.where(index_x == count_x - 1, halos[1], east_region)
    )
    south_region = padded[:, :, :, 3 : cells_x + 3, 0:3]
    padded = padded.at[:, :, :, 3 : cells_x + 3, 0:3].set(
        jnp.where(index_y == 0, jnp.swapaxes(jnp.flip(halos[2], 3), 3, 4), south_region)
    )
    north_region = padded[:, :, :, 3 : cells_x + 3, cells_y + 3 : cells_y + 6]
    padded = padded.at[:, :, :, 3 : cells_x + 3, cells_y + 3 : cells_y + 6].set(
        jnp.where(index_y == count_y - 1, jnp.swapaxes(halos[3], 3, 4), north_region)
    )
    return advance(padded, wave_speed, coriolis, cells_x, cells_y)


def on_device(state, coriolis, wave_speed, edges):
    count_x = lax.axis_size("tx")
    count_y = lax.axis_size("ty")
    index_x = lax.axis_index("tx")
    index_y = lax.axis_index("ty")
    for substep_index in range(SUBSTEPS):
        state = one_substep(state, coriolis, wave_speed, edges, count_x, count_y, index_x, index_y)
    return state


def fits(state):
    count_x = lax.axis_size("tx")
    faces, fields, levels, cells_x, cells_y = state.shape
    return (
        lax.axis_size("ty") == 2
        and faces % 2 == 0
        and levels == 4
        and cells_x == 6
        and cells_x * count_x == 2 * cells_y
        and 2 * cells_y + 2 * MARGIN <= WINDOW
    )


def either(state, coriolis, wave_speed, edges):
    if fits(state):
        return fast_on_device(state, coriolis, wave_speed, edges)
    return on_device(state, coriolis, wave_speed, edges)


def solution(mesh):
    in_specs = (P("member", None, None, "tx", "ty"), P(None, "tx", "ty"), P(), P())
    out_specs = P("member", None, None, "tx", "ty")
    return jax.shard_map(
        either, mesh=mesh, in_specs=in_specs, out_specs=out_specs, check_vma=False
    )
```

```python
import functools

import jax
import jax.numpy as jnp
from jax import lax
from jax.experimental import pallas as pl
from jax.experimental.pallas import tpu as pltpu
from jax.sharding import PartitionSpec as P

SUBSTEPS = 2
LANES = 128
WINDOW = 64
MARGIN = 8
VMEM_LIMIT = 32 * 1024 * 1024


def pack_kernel(cx, cy, state_hbm, coriolis_hbm, out_ref, state_ref, coriolis_ref, sems):
    copies = [
        pltpu.make_async_copy(state_hbm, state_ref, sems.at[0]),
        pltpu.make_async_copy(coriolis_hbm, coriolis_ref, sems.at[1]),
    ]
    for copy in copies:
        copy.start()
    faces, fields = state_ref.shape[:2]
    levels = state_ref.shape[3]
    pairs = faces // 2
    group = pairs * levels
    half = cx // 2
    base = fields * half * group
    out_ref[...] = jnp.zeros(out_ref.shape, jnp.float32)
    for copy in copies:
        copy.wait()
    for face in range(faces):
        for parity in range(2):
            lane = (face % 2) * WINDOW + MARGIN + parity * cy
            for xp in range(half):
                for field in range(fields):
                    row = field * half * group + xp * group + (face // 2) * levels
                    out_ref[row : row + levels, lane : lane + cy] = state_ref[
                        face, field, 2 * xp + parity
                    ]
                row = base + xp * pairs + face // 2
                out_ref[row : row + 1, lane : lane + cy] = coriolis_ref[
                    face, 2 * xp + parity : 2 * xp + parity + 1
                ]


def step_kernel(
    cx, cy, count_x, parts_ref, speed_hbm, edges_ref, out_ref,
    z_ref, cor_ref, pred_ref, store_ref, tile_ref, flip_ref, speed_ref, speed_smem, sem,
):
    fields = z_ref.shape[0]
    levels = 4
    slots = 16
    cells = cx * count_x
    faces = store_ref.shape[0] // 4
    pairs = faces // 2
    group = pairs * levels
    half = cx // 2
    chunk = cx * group
    index_x = lax.axis_index("tx")
    index_y = lax.axis_index("ty")
    speed_copy = pltpu.make_async_copy(speed_hbm, speed_smem, sem)
    speed_copy.start()

    def row_of(x):
        return (x + 4) * group

    def lanes_of(rows):
        return lax.broadcasted_iota(jnp.int32, (rows, LANES), 1)

    for place in range(count_x):
        source = place ^ index_x
        start = pl.multiple_of(source * chunk, 8)
        low = lanes_of(group) % WINDOW < MARGIN + cy
        for field in range(fields):
            for xp in range(half):
                row = field * half * group + xp * group
                south = parts_ref[0, place, row : row + group]
                north = parts_ref[1, place, row : row + group]
                even = jnp.where(low, south, pltpu.roll(north, cy, 1))
                odd = jnp.where(low, pltpu.roll(south, LANES - cy, 1), north)
                z_ref[field, pl.ds(start + row_of(2 * xp), group)] = even
                z_ref[field, pl.ds(start + row_of(2 * xp + 1), group)] = odd
        base = fields * half * group
        rows = half * pairs
        low = lanes_of(rows) % WINDOW < MARGIN + cy
        south = parts_ref[0, place, base : base + rows]
        north = parts_ref[1, place, base : base + rows]
        even = jnp.where(low, south, pltpu.roll(north, cy, 1))
        odd = jnp.where(low, pltpu.roll(south, LANES - cy, 1), north)
        for parity, values in enumerate((even, odd)):
            for xp in range(half):
                for pair in range(pairs):
                    at = start + (2 * xp + parity) * group + pair * levels
                    line = values[xp * pairs + pair : xp * pairs + pair + 1]
                    cor_ref[pl.ds(at, levels)] = jnp.broadcast_to(line, (levels, LANES))

    speed_copy.wait()
    level_of = lax.broadcasted_iota(jnp.int32, speed_ref.shape, 0) % levels
    speeds = jnp.full(speed_ref.shape, speed_smem[0], jnp.float32)
    for index in range(1, levels):
        speeds = jnp.where(level_of == index, speed_smem[index], speeds)
    speed_ref[...] = speeds

    def collect():
        position = lanes_of(cells) % WINDOW
        gap = WINDOW - cells + 3
        wide = gap + 3 * levels
        for pair in range(pairs):
            merged = jnp.zeros((cells, LANES), jnp.float32)
            for slot, field in ((0, 0), (1, 2)):
                for level in range(levels):
                    lines = z_ref[field, pl.ds(row_of(0) + pair * levels + level, cells, group)]
                    offset = slot * wide + 3 * level
                    here = position - offset
                    wanted = ((here >= 0) & (here < 3)) | ((here >= gap) & (here < gap + 3))
                    shift = (offset - (MARGIN + cells - 3)) % LANES
                    merged = jnp.where(wanted, pltpu.roll(lines, shift, 1), merged)
            merged = jnp.concatenate(
                [merged, jnp.zeros((LANES - cells, LANES), jnp.float32)], axis=0
            )
            flip_ref[pair] = merged.T
            for slot in range(2):
                for side in (2, 3):
                    for odd in range(2):
                        for depth in range(3):
                            base = slot * wide
                            if side == 3:
                                base += odd * WINDOW + 2 - depth
                            else:
                                base += ((odd + 1) % 2) * WINDOW + gap + depth
                            at = slot * slots + depth * levels
                            store_ref[(2 * pair + odd) * 4 + side, at : at + levels] = flip_ref[
                                pair, pl.ds(base, levels, 3)
                            ]
            for slot in range(2):
                for side in (0, 1):
                    for depth in range(3):
                        x = depth if side == 0 else cells - 1 - depth
                        row = row_of(x) + pair * levels
                        lines = z_ref[slot, row : row + levels]
                        at = slot * slots + depth * levels
                        for odd in range(2):
                            store_ref[(2 * pair + odd) * 4 + side, at : at + levels] = pltpu.roll(
                                lines, LANES - MARGIN - odd * WINDOW, 1
                            )

    def fetch(face, side, position):
        at = (face * 4 + side) * 3
        neighbour = edges_ref[at]
        far_side = edges_ref[at + 1]
        flipped = edges_ref[at + 2]
        block = store_ref[neighbour * 4 + far_side]
        order = jnp.where(flipped == 1, cells - 1 - position, position)
        order = jnp.where((position >= 0) & (position < cells), order, 0)
        block = jnp.take_along_axis(block, order, axis=1)
        sign_here = 2 * (side % 2) - 1
        sign_there = 2 * (far_side % 2) - 1
        sign = (-sign_here * sign_there).astype(jnp.float32)
        normal = lax.broadcasted_iota(jnp.int32, block.shape, 0) >= slots
        return jnp.where(normal, sign * block, block)

    def rim_rows(side):
        lane = lanes_of(2 * slots)
        for pair in range(pairs):
            first = fetch(2 * pair, side, lane - MARGIN)
            second = fetch(2 * pair + 1, side, lane - (MARGIN + WINDOW))
            both = jnp.where(lane < WINDOW, first, second)
            for slot in range(2):
                for depth in range(3):
                    x = -1 - depth if side == 0 else cells + depth
                    at = slot * slots + depth * levels
                    row = row_of(x) + pair * levels
                    z_ref[slot, row : row + levels] = both[at : at + levels]

    def tile_rows(odd, side, depth):
        if side == 3:
            return pl.ds(odd * WINDOW + depth, levels, 16)
        return pl.ds(((odd + 1) % 2) * WINDOW + 15 - depth, levels, 16)

    def put_columns(lines, field, start, pair):
        count = lines.shape[0]
        position = lanes_of(count) % WINDOW
        rim = ((position >= MARGIN - 3) & (position < MARGIN)) | (
            (position >= MARGIN + cells) & (position < MARGIN + cells + 3)
        )
        for level in range(levels):
            rolled = pltpu.roll(lines, (MARGIN + cells - 16 * level) % LANES, 1)
            at = pl.ds(row_of(start) + pair * levels + level, count, group)
            z_ref[field, at] = jnp.where(rim, rolled, z_ref[field, at])

    def rim_columns_all():
        for pair in range(pairs):
            for odd in range(2):
                for side in (2, 3):
                    block = fetch(2 * pair + odd, side, lanes_of(2 * slots))
                    for slot in range(2):
                        for depth in range(3):
                            at = slot * slots + depth * levels
                            tile_ref[2 * pair + slot, tile_rows(odd, side, depth)] = block[
                                at : at + levels
                            ]
            for slot, field in ((0, 0), (1, 2)):
                put_columns(tile_ref[2 * pair + slot].T[:cells], field, 0, pair)

    def rim_columns_own():
        lane = lanes_of(2 * slots)
        second = lax.broadcasted_iota(jnp.int32, lane.shape, 0) >= slots
        for odd in range(2):
            for side in (2, 3):
                total = jnp.zeros((slots, LANES), jnp.float32)
                for pair in range(pairs):
                    local = lane - jnp.where(second, 8 * (pairs + pair), 8 * pair)
                    block = fetch(2 * pair + odd, side, index_x * cx + local)
                    block = jnp.where((local >= 0) & (local < 8), block, 0.0)
                    total = total + block[:slots] + block[slots:]
                for depth in range(3):
                    at = depth * levels
                    tile_ref[0, tile_rows(odd, side, depth)] = total[at : at + levels]
        turned = tile_ref[0].T
        for slot, field in ((0, 0), (1, 2)):
            for pair in range(pairs):
                at = 8 * (slot * pairs + pair)
                put_columns(turned[at : at + cx], field, index_x * cx, pair)

    def predict(at, rows):
        speed = speed_ref[:rows]
        ahead = z_ref[0, pl.ds(at + group, rows)]
        behind = z_ref[0, pl.ds(at - group, rows)]
        pred_ref[pl.ds(at, rows)] = z_ref[1, pl.ds(at, rows)] - speed * (0.5 * (ahead - behind))

    def update(at, rows):
        speed = speed_ref[:rows]
        height = z_ref[0, pl.ds(at, rows)]
        north_pred = z_ref[2, pl.ds(at, rows)] - speed * (
            0.5 * (pltpu.roll(height, LANES - 1, 1) - pltpu.roll(height, 1, 1))
        )
        east_pred = pred_ref[pl.ds(at, rows)]
        flux_east = 8.0 * (
            pred_ref[pl.ds(at + group, rows)] - pred_ref[pl.ds(at - group, rows)]
        ) - (pred_ref[pl.ds(at + 2 * group, rows)] - pred_ref[pl.ds(at - 2 * group, rows)])
        flux_north = 8.0 * (
            pltpu.roll(north_pred, LANES - 1, 1) - pltpu.roll(north_pred, 1, 1)
        ) - (pltpu.roll(north_pred, LANES - 2, 1) - pltpu.roll(north_pred, 2, 1))
        height = height - speed * ((flux_east + flux_north) * (1.0 / 12.0))
        turning = cor_ref[pl.ds(at - row_of(0), rows)]
        return height, east_pred + turning * north_pred, north_pred - turning * east_pred

    collect()
    rim_rows(0)
    rim_rows(1)
    rim_columns_all()
    for first in range(-2, cells + 2, 4):
        predict(row_of(first), 4 * group)
    for index in range(count_x):
        at = row_of(0) + index * chunk
        for field, values in enumerate(update(at, chunk)):
            z_ref[field, at : at + chunk] = values

    collect()

    @pl.when(index_x == 0)
    def _():
        rim_rows(0)

    @pl.when(index_x == count_x - 1)
    def _():
        rim_rows(1)

    rim_columns_own()
    at = pl.multiple_of(row_of(0) + index_x * chunk, 8)
    predict(at - 2 * group, chunk + 4 * group)
    for field, values in enumerate(update(at, chunk)):
        for odd in range(2):
            shift = LANES - (MARGIN + odd * WINDOW) - index_y * cy
            rolled = pltpu.roll(values, shift, 1)
            for x in range(cx):
                for pair in range(pairs):
                    row = x * group + pair * levels
                    out_ref[2 * pair + odd, field, x] = rolled[row : row + levels, :cy]


def fast_on_device(state, coriolis, wave_speed, edges):
    count_x = lax.axis_size("tx")
    faces, fields, levels, cx, cy = state.shape
    pairs = faces // 2
    group = pairs * levels
    rows = fields * (cx // 2) * group + (cx // 2) * pairs
    rows = -(-rows // 8) * 8
    cells = cx * count_x
    packed = pl.pallas_call(
        functools.partial(pack_kernel, cx, cy),
        out_shape=jax.ShapeDtypeStruct((rows, LANES), jnp.float32),
        in_specs=[pl.BlockSpec(memory_space=pltpu.HBM)] * 2,
        out_specs=pl.BlockSpec(memory_space=pltpu.VMEM),
        scratch_shapes=[
            pltpu.VMEM((faces, fields, cx, levels, cy), jnp.float32),
            pltpu.VMEM((faces, cx, cy), jnp.float32),
            pltpu.SemaphoreType.DMA((2,)),
        ],
        compiler_params=pltpu.CompilerParams(vmem_limit_bytes=VMEM_LIMIT),
        name="pack",
    )(jnp.swapaxes(state, 2, 3), coriolis)
    chunks = [packed] * count_x
    for other in reversed(range(1, count_x)):
        partners = [(index, index ^ other) for index in range(count_x)]
        chunks[other] = lax.ppermute(packed, "tx", partners)
    parts = lax.all_gather(jnp.stack(chunks), "ty")
    z_rows = (cells + 8) * group
    return jnp.swapaxes(
        pl.pallas_call(
            functools.partial(step_kernel, cx, cy, count_x),
            out_shape=jax.ShapeDtypeStruct((faces, fields, cx, levels, cy), jnp.float32),
            in_specs=[
                pl.BlockSpec(memory_space=pltpu.VMEM),
                pl.BlockSpec(memory_space=pltpu.HBM),
                pl.BlockSpec(memory_space=pltpu.SMEM),
            ],
            out_specs=pl.BlockSpec(memory_space=pltpu.VMEM),
            scratch_shapes=[
                pltpu.VMEM((fields, z_rows, LANES), jnp.float32),
                pltpu.VMEM((cells * group, LANES), jnp.float32),
                pltpu.VMEM((z_rows, LANES), jnp.float32),
                pltpu.VMEM((faces * 4, 32, LANES), jnp.float32),
                pltpu.VMEM((faces, LANES, LANES), jnp.float32),
                pltpu.VMEM((pairs, LANES, LANES), jnp.float32),
                pltpu.VMEM(((cx + 4) * group, LANES), jnp.float32),
                pltpu.SMEM((levels,), jnp.float32),
                pltpu.SemaphoreType.DMA,
            ],
            compiler_params=pltpu.CompilerParams(vmem_limit_bytes=VMEM_LIMIT),
            name="substeps",
        )(parts, wave_speed, edges.reshape(-1)),
        2,
        3,
    )


def padded_2(block, sides, width):
    for axis, dim in sides:
        count = lax.axis_size(axis)
        forward = [(i, i + 1) for i in range(count - 1)]
        backward = [(target, source) for source, target in forward]
        low = lax.ppermute(
            lax.slice_in_dim(block, block.shape[dim] - width, None, axis=dim), axis, forward
        )
        high = lax.ppermute(lax.slice_in_dim(block, 0, width, axis=dim), axis, backward)
        block = jnp.concatenate([low, block, high], axis=dim)
    return block


def spread(block, axis, owner):
    block = jnp.where(lax.axis_index(axis) == owner, block, jnp.zeros_like(block))
    return lax.psum(block, axis)


def rotate_strip(strip_data, side_index, far_side, flipped):
    normal_part = jnp.where(far_side < 2, strip_data[1], strip_data[2])
    along_part = jnp.where(far_side < 2, strip_data[2], strip_data[1])
    sign_here = 2.0 * (side_index % 2) - 1.0
    sign_there = (2 * (far_side % 2) - 1).astype(jnp.float32)
    normal_part = -sign_here * sign_there * normal_part
    along_part = (1 - 2 * flipped).astype(jnp.float32) * along_part
    if side_index < 2:
        return jnp.stack([strip_data[0], normal_part, along_part])
    return jnp.stack([strip_data[0], along_part, normal_part])


def window_strip(store, side_pick, neighbour, flipped, start, width):
    full_length = store.shape[5]
    begin = jnp.where(flipped == 1, full_length - start - width, start)
    zero = jnp.zeros((), jnp.int32)
    sizes_here = (1, 1, store.shape[2], store.shape[3], store.shape[4], width)
    piece = lax.dynamic_slice(store, (side_pick, neighbour, zero, zero, zero, begin), sizes_here)[
        0, 0
    ]
    return jnp.where(flipped == 1, jnp.flip(piece, 3), piece)


def side_halo(edge_store, edges, face_index, side_index, start, width):
    neighbour = edges[face_index, side_index, 0]
    far_side = edges[face_index, side_index, 1]
    flipped = edges[face_index, side_index, 2]
    strip_data = window_strip(edge_store, far_side, neighbour, flipped, start, width)
    return rotate_strip(strip_data, side_index, far_side, flipped)


def advance(padded, wave_speed, coriolis_part, cells_x, cells_y):
    height = padded[..., 0, :, :, :]
    wind_east = padded[..., 1, :, :, :]
    wind_north = padded[..., 2, :, :, :]
    speed = wave_speed[:, None, None]
    east_pred = wind_east[..., 1 : cells_x + 5, 3 : cells_y + 3] - speed * (
        0.5
        * (
            height[..., 2 : cells_x + 6, 3 : cells_y + 3]
            - height[..., 0 : cells_x + 4, 3 : cells_y + 3]
        )
    )
    north_pred = wind_north[..., 3 : cells_x + 3, 1 : cells_y + 5] - speed * (
        0.5
        * (
            height[..., 3 : cells_x + 3, 2 : cells_y + 6]
            - height[..., 3 : cells_x + 3, 0 : cells_y + 4]
        )
    )
    flux_east = (
        8.0 * (east_pred[..., 3 : cells_x + 3, :] - east_pred[..., 1 : cells_x + 1, :])
        - (east_pred[..., 4 : cells_x + 4, :] - east_pred[..., 0:cells_x, :])
    ) / 12.0
    flux_north = (
        8.0 * (north_pred[..., 3 : cells_y + 3] - north_pred[..., 1 : cells_y + 1])
        - (north_pred[..., 4 : cells_y + 4] - north_pred[..., 0:cells_y])
    ) / 12.0
    height_new = height[..., 3 : cells_x + 3, 3 : cells_y + 3] - speed * (flux_east + flux_north)
    east_inner = east_pred[..., 2 : cells_x + 2, :]
    north_inner = north_pred[..., 2 : cells_y + 2]
    turning = coriolis_part[..., None, :, :]
    return jnp.stack(
        [height_new, east_inner + turning * north_inner, north_inner - turning * east_inner],
        axis=-4,
    )


def one_substep(state, coriolis, wave_speed, edges, count_x, count_y, index_x, index_y):
    faces = state.shape[0]
    cells_x = state.shape[3]
    cells_y = state.shape[4]
    padded = padded_2(state, (("tx", 3), ("ty", 4)), 3)
    west_rim = state[:, :, :, 0:3, :]
    east_rim = jnp.flip(state[:, :, :, cells_x - 3 :, :], 3)
    south_rim = jnp.swapaxes(state[:, :, :, :, 0:3], 3, 4)
    north_rim = jnp.swapaxes(jnp.flip(state[:, :, :, :, cells_y - 3 :], 4), 3, 4)
    west_part = spread(west_rim, "tx", 0)
    east_part = spread(east_rim, "tx", count_x - 1)
    west_full, east_full = (
        lax.all_gather(west_part, "ty", axis=4, tiled=True),
        lax.all_gather(east_part, "ty", axis=4, tiled=True),
    )
    south_row, north_row = (
        lax.all_gather(south_rim, "tx", axis=4, tiled=True),
        lax.all_gather(north_rim, "tx", axis=4, tiled=True),
    )
    south_all, north_all = (
        lax.all_gather(south_row, "ty", axis=0, tiled=True),
        lax.all_gather(north_row, "ty", axis=0, tiled=True),
    )
    south_full = south_all[0:faces]
    north_full = north_all[(count_y - 1) * faces : count_y * faces]
    edge_store = jnp.stack([west_full, east_full, south_full, north_full])
    halos = []
    for side_index in range(4):
        if side_index < 2:
            slabs = jnp.stack(
                [
                    side_halo(edge_store, edges, face_index, side_index, index_y * cells_y, cells_y)
                    for face_index in range(faces)
                ]
            )
        else:
            slabs = jnp.stack(
                [
                    side_halo(edge_store, edges, face_index, side_index, index_x * cells_x, cells_x)
                    for face_index in range(faces)
                ]
            )
        halos.append(slabs)
    west_region = padded[:, :, :, 0:3, 3 : cells_y + 3]
    padded = padded.at[:, :, :, 0:3, 3 : cells_y + 3].set(
        jnp.where(index_x == 0, jnp.flip(halos[0], 3), west_region)
    )
    east_region = padded[:, :, :, cells_x + 3 : cells_x + 6, 3 : cells_y + 3]
    padded = padded.at[:, :, :, cells_x + 3 : cells_x + 6, 3 : cells_y + 3].set(
        jnp.where(index_x == count_x - 1, halos[1], east_region)
    )
    south_region = padded[:, :, :, 3 : cells_x + 3, 0:3]
    padded = padded.at[:, :, :, 3 : cells_x + 3, 0:3].set(
        jnp.where(index_y == 0, jnp.swapaxes(jnp.flip(halos[2], 3), 3, 4), south_region)
    )
    north_region = padded[:, :, :, 3 : cells_x + 3, cells_y + 3 : cells_y + 6]
    padded = padded.at[:, :, :, 3 : cells_x + 3, cells_y + 3 : cells_y + 6].set(
        jnp.where(index_y == count_y - 1, jnp.swapaxes(halos[3], 3, 4), north_region)
    )
    return advance(padded, wave_speed, coriolis, cells_x, cells_y)


def on_device(state, coriolis, wave_speed, edges):
    count_x = lax.axis_size("tx")
    count_y = lax.axis_size("ty")
    index_x = lax.axis_index("tx")
    index_y = lax.axis_index("ty")
    for substep_index in range(SUBSTEPS):
        state = one_substep(state, coriolis, wave_speed, edges, count_x, count_y, index_x, index_y)
    return state


def fits(state):
    count_x = lax.axis_size("tx")
    faces, fields, levels, cells_x, cells_y = state.shape
    return (
        lax.axis_size("ty") == 2
        and faces % 2 == 0
        and levels == 4
        and cells_x == 6
        and cells_x * count_x == 2 * cells_y
        and 2 * cells_y + 2 * MARGIN <= WINDOW
    )


def either(state, coriolis, wave_speed, edges):
    if fits(state):
        return fast_on_device(state, coriolis, wave_speed, edges)
    return on_device(state, coriolis, wave_speed, edges)


def solution(mesh):
    in_specs = (P("member", None, None, "tx", "ty"), P(None, "tx", "ty"), P(), P())
    out_specs = P("member", None, None, "tx", "ty")
    return jax.shard_map(
        either, mesh=mesh, in_specs=in_specs, out_specs=out_specs, check_vma=False
    )
```

```python
import functools

import jax
import jax.numpy as jnp
from jax import lax
from jax.experimental import pallas as pl
from jax.experimental.pallas import tpu as pltpu
from jax.sharding import PartitionSpec as P

SUBSTEPS = 2
LANES = 128
WINDOW = 64
MARGIN = 8
VMEM_LIMIT = 32 * 1024 * 1024


def window_start(source, target, count_x, index_y, cx, cy, far):
    width = 2 * cx
    near = jnp.minimum(target, count_x - 1 - target)
    inward = jnp.minimum(cx * near - jnp.where(far, cx, cx // 2), cy - width)
    rim = (source == 0) | (source == count_x - 1)
    start = jnp.where(rim, jnp.maximum(inward, 0), 0)
    return jnp.where(index_y == 0, start, cy - width - start)


def windows(source, target, count_x, index_y, cx, cy):
    low_far = source == count_x - 1
    lower = window_start(source, target, count_x, index_y, cx, cy, low_far)
    upper = window_start(source, target, count_x, index_y, cx, cy, ~low_far)
    return lower, upper


def unit_place(field, x, cx, group, width):
    per_row = 60 // width
    index = field * cx + x
    return (index // per_row) * group, (index % per_row) * width


def pack_kernel(
    cx, cy, count_x, distant, state_hbm, coriolis_hbm, full_ref, *rest
):
    small_refs = rest[: len(distant)]
    state_ref, coriolis_ref, sems = rest[len(distant) :]
    copies = [
        pltpu.make_async_copy(state_hbm, state_ref, sems.at[0]),
        pltpu.make_async_copy(coriolis_hbm, coriolis_ref, sems.at[1]),
    ]
    for copy in copies:
        copy.start()
    faces, fields = state_ref.shape[:2]
    levels = state_ref.shape[3]
    pairs = faces // 2
    group = pairs * levels
    half = cx // 2
    width = 2 * cx
    base = fields * half * group
    index_x = lax.axis_index("tx")
    index_y = lax.axis_index("ty")
    full_ref[...] = jnp.zeros(full_ref.shape, jnp.float32)
    for copy in copies:
        copy.wait()
    for face in range(faces):
        for parity in range(2):
            lane = (face % 2) * WINDOW + MARGIN + parity * cy
            for xp in range(half):
                for field in range(fields):
                    row = field * half * group + xp * group + (face // 2) * levels
                    full_ref[row : row + levels, lane : lane + cy] = state_ref[
                        face, field, 2 * xp + parity
                    ]
                row = base + (2 * xp + parity) * pairs + face // 2
                lane_at = (face % 2) * WINDOW + MARGIN
                full_ref[row : row + 1, lane_at : lane_at + cy] = coriolis_ref[
                    face, 2 * xp + parity : 2 * xp + parity + 1
                ]
    for small_ref, offset in zip(small_refs, distant):
        target = (index_x + offset + count_x) % count_x
        starts = windows(index_x, target, count_x, index_y, cx, cy)
        blocks = {}

        def put(row, lane, lines):
            position = lax.broadcasted_iota(jnp.int32, lines.shape, 1) % WINDOW
            here = (position >= lane) & (position < lane + width)
            blocks[row] = jnp.where(here, lines, blocks.get(row, jnp.zeros_like(lines)))

        for field in range(fields):
            for x in range(cx):
                row = field * half * group + (x // 2) * group
                at, lane = unit_place(field, x, cx, group, width)
                shift = lane - MARGIN - (x % 2) * cy - starts[x // half] + 2 * LANES
                put(at, lane, pltpu.roll(full_ref[row : row + group], shift % LANES, 1))
        for part in range(2):
            row = base + part * half * pairs
            at, lane = unit_place(fields, part, cx, group, width)
            shift = lane - MARGIN - starts[part] + 2 * LANES
            lines = full_ref[row : row + group]
            put(at, lane, pltpu.roll(lines, shift % LANES, 1))
        for row, lines in blocks.items():
            small_ref[row : row + group] = lines


def step_kernel(
    cx, cy, count_x, near, distant, full_rows, small_rows, parts_ref, table_ref, out_ref,
    z_ref, cor_ref, pred_ref, store_ref, tile_ref, flip_ref, speed_ref,
):
    fields = z_ref.shape[0]
    levels = 4
    slots = 16
    cells = cx * count_x
    faces = store_ref.shape[0] // 4
    pairs = faces // 2
    group = pairs * levels
    half = cx // 2
    chunk = cx * group
    width = 2 * cx
    index_x = lax.axis_index("tx")
    index_y = lax.axis_index("ty")

    def row_of(x):
        return (x + 4) * group

    def lanes_of(rows):
        return lax.broadcasted_iota(jnp.int32, (rows, LANES), 1)

    south_half = lanes_of(group) % WINDOW < MARGIN + cy

    def put_coriolis(start, x, values, at):
        for pair in range(pairs):
            line = values[at + pair : at + pair + 1]
            rows = pl.ds(start + x * group + pair * levels, levels)
            cor_ref[rows] = jnp.broadcast_to(line, (levels, LANES))

    for place, offset in enumerate(near):
        source = (index_x - offset + count_x) % count_x
        start = pl.multiple_of(source * chunk, 8)
        top = place * full_rows
        for field in range(fields):
            for xp in range(half):
                row = top + field * half * group + xp * group
                south = parts_ref[0, row : row + group]
                north = parts_ref[1, row : row + group]
                even = jnp.where(south_half, south, pltpu.roll(north, cy, 1))
                odd = jnp.where(south_half, pltpu.roll(south, LANES - cy, 1), north)
                z_ref[field, pl.ds(start + row_of(2 * xp), group)] = even
                z_ref[field, pl.ds(start + row_of(2 * xp + 1), group)] = odd
        for part in range(2):
            row = top + fields * half * group + part * half * pairs
            south = parts_ref[0, row : row + group]
            north = parts_ref[1, row : row + group]
            values = jnp.where(south_half, south, pltpu.roll(north, cy, 1))
            for x in range(half):
                put_coriolis(start, part * half + x, values, x * pairs)

    for place, offset in enumerate(distant):
        source = (index_x - offset + count_x) % count_x
        start = pl.multiple_of(source * chunk, 8)
        top = len(near) * full_rows + place * small_rows
        from_south = windows(source, index_x, count_x, 0, cx, cy)
        from_north = windows(source, index_x, count_x, 1, cx, cy)

        def lines_at(at, lane, part):
            row = top + at
            south = parts_ref[0, row : row + group]
            north = parts_ref[1, row : row + group]
            south_shift = MARGIN + from_south[part] - lane + LANES
            north_shift = MARGIN + cy + from_north[part] - lane + LANES
            return jnp.where(
                south_half,
                pltpu.roll(south, south_shift % LANES, 1),
                pltpu.roll(north, north_shift % LANES, 1),
            )

        for field in range(fields):
            for x in range(cx):
                at, lane = unit_place(field, x, cx, group, width)
                z_ref[field, pl.ds(start + row_of(x), group)] = lines_at(at, lane, x // half)
        for part in range(2):
            at, lane = unit_place(fields, part, cx, group, width)
            values = lines_at(at, lane, part)
            for x in range(half):
                put_coriolis(start, part * half + x, values, x * pairs)

    level_of = lax.broadcasted_iota(jnp.int32, speed_ref.shape, 0) % levels
    speeds = jnp.full(speed_ref.shape, table_ref[0], jnp.float32)
    for index in range(1, levels):
        speeds = jnp.where(level_of == index, table_ref[index], speeds)
    speed_ref[...] = speeds

    def collect():
        position = lanes_of(cells) % WINDOW
        gap = WINDOW - cells + 3
        wide = gap + 3 * levels
        for pair in range(pairs):
            merged = jnp.zeros((cells, LANES), jnp.float32)
            for slot, field in ((0, 0), (1, 2)):
                for level in range(levels):
                    lines = z_ref[field, pl.ds(row_of(0) + pair * levels + level, cells, group)]
                    offset = slot * wide + 3 * level
                    here = position - offset
                    wanted = ((here >= 0) & (here < 3)) | ((here >= gap) & (here < gap + 3))
                    shift = (offset - (MARGIN + cells - 3)) % LANES
                    merged = jnp.where(wanted, pltpu.roll(lines, shift, 1), merged)
            merged = jnp.concatenate(
                [merged, jnp.zeros((LANES - cells, LANES), jnp.float32)], axis=0
            )
            flip_ref[pair] = merged.T
            for slot in range(2):
                for side in (2, 3):
                    for odd in range(2):
                        for depth in range(3):
                            base = slot * wide
                            if side == 3:
                                base += odd * WINDOW + 2 - depth
                            else:
                                base += ((odd + 1) % 2) * WINDOW + gap + depth
                            at = slot * slots + depth * levels
                            store_ref[(2 * pair + odd) * 4 + side, at : at + levels] = flip_ref[
                                pair, pl.ds(base, levels, 3)
                            ]
            for slot in range(2):
                for side in (0, 1):
                    for depth in range(3):
                        x = depth if side == 0 else cells - 1 - depth
                        row = row_of(x) + pair * levels
                        lines = z_ref[slot, row : row + levels]
                        at = slot * slots + depth * levels
                        for odd in range(2):
                            store_ref[(2 * pair + odd) * 4 + side, at : at + levels] = pltpu.roll(
                                lines, LANES - MARGIN - odd * WINDOW, 1
                            )

    def fetch(face, side, position):
        at = levels + (face * 4 + side) * 3
        neighbour = table_ref[at].astype(jnp.int32)
        far_side = table_ref[at + 1].astype(jnp.int32)
        flipped = table_ref[at + 2].astype(jnp.int32)
        block = store_ref[neighbour * 4 + far_side]
        order = jnp.where(flipped == 1, cells - 1 - position, position)
        order = jnp.where((position >= 0) & (position < cells), order, 0)
        block = jnp.take_along_axis(block, order, axis=1)
        sign_here = 2 * (side % 2) - 1
        sign_there = 2 * (far_side % 2) - 1
        sign = (-sign_here * sign_there).astype(jnp.float32)
        normal = lax.broadcasted_iota(jnp.int32, block.shape, 0) >= slots
        return jnp.where(normal, sign * block, block)

    def rim_rows(side):
        lane = lanes_of(2 * slots)
        for pair in range(pairs):
            first = fetch(2 * pair, side, lane - MARGIN)
            second = fetch(2 * pair + 1, side, lane - (MARGIN + WINDOW))
            both = jnp.where(lane < WINDOW, first, second)
            for slot in range(2):
                for depth in range(3):
                    x = -1 - depth if side == 0 else cells + depth
                    at = slot * slots + depth * levels
                    row = row_of(x) + pair * levels
                    z_ref[slot, row : row + levels] = both[at : at + levels]

    def tile_rows(odd, side, depth):
        if side == 3:
            return pl.ds(odd * WINDOW + depth, levels, 16)
        return pl.ds(((odd + 1) % 2) * WINDOW + 15 - depth, levels, 16)

    def put_columns(lines, field, start, pair):
        count = lines.shape[0]
        position = lanes_of(count) % WINDOW
        rim = ((position >= MARGIN - 3) & (position < MARGIN)) | (
            (position >= MARGIN + cells) & (position < MARGIN + cells + 3)
        )
        for level in range(levels):
            rolled = pltpu.roll(lines, (MARGIN + cells - 16 * level) % LANES, 1)
            at = pl.ds(row_of(start) + pair * levels + level, count, group)
            z_ref[field, at] = jnp.where(rim, rolled, z_ref[field, at])

    def rim_columns_all():
        for pair in range(pairs):
            for odd in range(2):
                for side in (2, 3):
                    block = fetch(2 * pair + odd, side, lanes_of(2 * slots))
                    for slot in range(2):
                        for depth in range(3):
                            at = slot * slots + depth * levels
                            tile_ref[2 * pair + slot, tile_rows(odd, side, depth)] = block[
                                at : at + levels
                            ]
            for slot, field in ((0, 0), (1, 2)):
                put_columns(tile_ref[2 * pair + slot].T[:cells], field, 0, pair)

    def rim_columns_own():
        lane = lanes_of(2 * slots)
        second = lax.broadcasted_iota(jnp.int32, lane.shape, 0) >= slots
        for odd in range(2):
            for side in (2, 3):
                total = jnp.zeros((slots, LANES), jnp.float32)
                for pair in range(pairs):
                    local = lane - jnp.where(second, 8 * (pairs + pair), 8 * pair)
                    block = fetch(2 * pair + odd, side, index_x * cx + local)
                    block = jnp.where((local >= 0) & (local < 8), block, 0.0)
                    total = total + block[:slots] + block[slots:]
                for depth in range(3):
                    at = depth * levels
                    tile_ref[0, tile_rows(odd, side, depth)] = total[at : at + levels]
        turned = tile_ref[0].T
        for slot, field in ((0, 0), (1, 2)):
            for pair in range(pairs):
                at = 8 * (slot * pairs + pair)
                put_columns(turned[at : at + cx], field, index_x * cx, pair)

    def predict(at, rows):
        speed = speed_ref[:rows]
        ahead = z_ref[0, pl.ds(at + group, rows)]
        behind = z_ref[0, pl.ds(at - group, rows)]
        pred_ref[pl.ds(at, rows)] = z_ref[1, pl.ds(at, rows)] - speed * (0.5 * (ahead - behind))

    def update(at, rows):
        speed = speed_ref[:rows]
        height = z_ref[0, pl.ds(at, rows)]
        north_pred = z_ref[2, pl.ds(at, rows)] - speed * (
            0.5 * (pltpu.roll(height, LANES - 1, 1) - pltpu.roll(height, 1, 1))
        )
        east_pred = pred_ref[pl.ds(at, rows)]
        flux_east = 8.0 * (
            pred_ref[pl.ds(at + group, rows)] - pred_ref[pl.ds(at - group, rows)]
        ) - (pred_ref[pl.ds(at + 2 * group, rows)] - pred_ref[pl.ds(at - 2 * group, rows)])
        flux_north = 8.0 * (
            pltpu.roll(north_pred, LANES - 1, 1) - pltpu.roll(north_pred, 1, 1)
        ) - (pltpu.roll(north_pred, LANES - 2, 1) - pltpu.roll(north_pred, 2, 1))
        height = height - speed * ((flux_east + flux_north) * (1.0 / 12.0))
        turning = cor_ref[pl.ds(at - row_of(0), rows)]
        return height, east_pred + turning * north_pred, north_pred - turning * east_pred

    collect()
    rim_rows(0)
    rim_rows(1)
    rim_columns_all()
    for first in range(-2, cells + 2, 4):
        predict(row_of(first), 4 * group)
    for index in range(count_x):
        at = row_of(0) + index * chunk
        for field, values in enumerate(update(at, chunk)):
            z_ref[field, at : at + chunk] = values

    collect()

    @pl.when(index_x == 0)
    def _():
        rim_rows(0)

    @pl.when(index_x == count_x - 1)
    def _():
        rim_rows(1)

    rim_columns_own()
    at = pl.multiple_of(row_of(0) + index_x * chunk, 8)
    predict(at - 2 * group, chunk + 4 * group)
    for field, values in enumerate(update(at, chunk)):
        for odd in range(2):
            shift = LANES - (MARGIN + odd * WINDOW) - index_y * cy
            rolled = pltpu.roll(values, shift, 1)
            for x in range(cx):
                for pair in range(pairs):
                    row = x * group + pair * levels
                    out_ref[2 * pair + odd, field, x] = rolled[row : row + levels, :cy]


def fast_on_device(state, coriolis, wave_speed, edges):
    count_x = lax.axis_size("tx")
    faces, fields, levels, cx, cy = state.shape
    pairs = faces // 2
    group = pairs * levels
    cells = cx * count_x
    near = (0, 1, -1)
    distant = (4, 3, -3, 2, -2)
    full_rows = fields * (cx // 2) * group + (cx // 2) * pairs + group
    full_rows = -(-full_rows // 8) * 8
    small_rows = unit_place(fields, 1, cx, group, 2 * cx)[0] + group
    packed = pl.pallas_call(
        functools.partial(pack_kernel, cx, cy, count_x, distant),
        out_shape=[jax.ShapeDtypeStruct((full_rows, LANES), jnp.float32)]
        + [jax.ShapeDtypeStruct((small_rows, LANES), jnp.float32)] * len(distant),
        in_specs=[pl.BlockSpec(memory_space=pltpu.HBM)] * 2,
        out_specs=[pl.BlockSpec(memory_space=pltpu.VMEM)] * (1 + len(distant)),
        scratch_shapes=[
            pltpu.VMEM((faces, fields, cx, levels, cy), jnp.float32),
            pltpu.VMEM((faces, cx, cy), jnp.float32),
            pltpu.SemaphoreType.DMA((2,)),
        ],
        compiler_params=pltpu.CompilerParams(vmem_limit_bytes=VMEM_LIMIT),
        name="pack",
    )(jnp.swapaxes(state, 2, 3), coriolis)

    def moved(block, offset):
        return lax.ppermute(
            block, "tx", [(index, (index + offset) % count_x) for index in range(count_x)]
        )

    chunks = [packed[0]] + [moved(packed[0], offset) for offset in near[1:]]
    chunks += [moved(block, offset) for block, offset in zip(packed[1:], distant)]
    parts = lax.all_gather(jnp.concatenate(chunks), "ty")
    table = jnp.concatenate([wave_speed, edges.reshape(-1).astype(jnp.float32)])
    z_rows = (cells + 8) * group
    out = pl.pallas_call(
        functools.partial(
            step_kernel, cx, cy, count_x, near, distant, full_rows, small_rows
        ),
        out_shape=jax.ShapeDtypeStruct((faces, fields, cx, levels, cy), jnp.float32),
        in_specs=[
            pl.BlockSpec(memory_space=pltpu.VMEM),
            pl.BlockSpec(memory_space=pltpu.SMEM),
        ],
        out_specs=pl.BlockSpec(memory_space=pltpu.VMEM),
        scratch_shapes=[
            pltpu.VMEM((fields, z_rows, LANES), jnp.float32),
            pltpu.VMEM((cells * group, LANES), jnp.float32),
            pltpu.VMEM((z_rows, LANES), jnp.float32),
            pltpu.VMEM((faces * 4, 32, LANES), jnp.float32),
            pltpu.VMEM((faces, LANES, LANES), jnp.float32),
            pltpu.VMEM((pairs, LANES, LANES), jnp.float32),
            pltpu.VMEM(((cx + 4) * group, LANES), jnp.float32),
        ],
        compiler_params=pltpu.CompilerParams(vmem_limit_bytes=VMEM_LIMIT),
        name="substeps",
    )(parts, table)
    return jnp.swapaxes(out, 2, 3)


def padded_2(block, sides, width):
    for axis, dim in sides:
        count = lax.axis_size(axis)
        forward = [(i, i + 1) for i in range(count - 1)]
        backward = [(target, source) for source, target in forward]
        low = lax.ppermute(
            lax.slice_in_dim(block, block.shape[dim] - width, None, axis=dim), axis, forward
        )
        high = lax.ppermute(lax.slice_in_dim(block, 0, width, axis=dim), axis, backward)
        block = jnp.concatenate([low, block, high], axis=dim)
    return block


def spread(block, axis, owner):
    block = jnp.where(lax.axis_index(axis) == owner, block, jnp.zeros_like(block))
    return lax.psum(block, axis)


def rotate_strip(strip_data, side_index, far_side, flipped):
    normal_part = jnp.where(far_side < 2, strip_data[1], strip_data[2])
    along_part = jnp.where(far_side < 2, strip_data[2], strip_data[1])
    sign_here = 2.0 * (side_index % 2) - 1.0
    sign_there = (2 * (far_side % 2) - 1).astype(jnp.float32)
    normal_part = -sign_here * sign_there * normal_part
    along_part = (1 - 2 * flipped).astype(jnp.float32) * along_part
    if side_index < 2:
        return jnp.stack([strip_data[0], normal_part, along_part])
    return jnp.stack([strip_data[0], along_part, normal_part])


def window_strip(store, side_pick, neighbour, flipped, start, width):
    full_length = store.shape[5]
    begin = jnp.where(flipped == 1, full_length - start - width, start)
    zero = jnp.zeros((), jnp.int32)
    sizes_here = (1, 1, store.shape[2], store.shape[3], store.shape[4], width)
    piece = lax.dynamic_slice(store, (side_pick, neighbour, zero, zero, zero, begin), sizes_here)[
        0, 0
    ]
    return jnp.where(flipped == 1, jnp.flip(piece, 3), piece)


def side_halo(edge_store, edges, face_index, side_index, start, width):
    neighbour = edges[face_index, side_index, 0]
    far_side = edges[face_index, side_index, 1]
    flipped = edges[face_index, side_index, 2]
    strip_data = window_strip(edge_store, far_side, neighbour, flipped, start, width)
    return rotate_strip(strip_data, side_index, far_side, flipped)


def advance(padded, wave_speed, coriolis_part, cells_x, cells_y):
    height = padded[..., 0, :, :, :]
    wind_east = padded[..., 1, :, :, :]
    wind_north = padded[..., 2, :, :, :]
    speed = wave_speed[:, None, None]
    east_pred = wind_east[..., 1 : cells_x + 5, 3 : cells_y + 3] - speed * (
        0.5
        * (
            height[..., 2 : cells_x + 6, 3 : cells_y + 3]
            - height[..., 0 : cells_x + 4, 3 : cells_y + 3]
        )
    )
    north_pred = wind_north[..., 3 : cells_x + 3, 1 : cells_y + 5] - speed * (
        0.5
        * (
            height[..., 3 : cells_x + 3, 2 : cells_y + 6]
            - height[..., 3 : cells_x + 3, 0 : cells_y + 4]
        )
    )
    flux_east = (
        8.0 * (east_pred[..., 3 : cells_x + 3, :] - east_pred[..., 1 : cells_x + 1, :])
        - (east_pred[..., 4 : cells_x + 4, :] - east_pred[..., 0:cells_x, :])
    ) / 12.0
    flux_north = (
        8.0 * (north_pred[..., 3 : cells_y + 3] - north_pred[..., 1 : cells_y + 1])
        - (north_pred[..., 4 : cells_y + 4] - north_pred[..., 0:cells_y])
    ) / 12.0
    height_new = height[..., 3 : cells_x + 3, 3 : cells_y + 3] - speed * (flux_east + flux_north)
    east_inner = east_pred[..., 2 : cells_x + 2, :]
    north_inner = north_pred[..., 2 : cells_y + 2]
    turning = coriolis_part[..., None, :, :]
    return jnp.stack(
        [height_new, east_inner + turning * north_inner, north_inner - turning * east_inner],
        axis=-4,
    )


def one_substep(state, coriolis, wave_speed, edges, count_x, count_y, index_x, index_y):
    faces = state.shape[0]
    cells_x = state.shape[3]
    cells_y = state.shape[4]
    padded = padded_2(state, (("tx", 3), ("ty", 4)), 3)
    west_rim = state[:, :, :, 0:3, :]
    east_rim = jnp.flip(state[:, :, :, cells_x - 3 :, :], 3)
    south_rim = jnp.swapaxes(state[:, :, :, :, 0:3], 3, 4)
    north_rim = jnp.swapaxes(jnp.flip(state[:, :, :, :, cells_y - 3 :], 4), 3, 4)
    west_part = spread(west_rim, "tx", 0)
    east_part = spread(east_rim, "tx", count_x - 1)
    west_full, east_full = (
        lax.all_gather(west_part, "ty", axis=4, tiled=True),
        lax.all_gather(east_part, "ty", axis=4, tiled=True),
    )
    south_row, north_row = (
        lax.all_gather(south_rim, "tx", axis=4, tiled=True),
        lax.all_gather(north_rim, "tx", axis=4, tiled=True),
    )
    south_all, north_all = (
        lax.all_gather(south_row, "ty", axis=0, tiled=True),
        lax.all_gather(north_row, "ty", axis=0, tiled=True),
    )
    south_full = south_all[0:faces]
    north_full = north_all[(count_y - 1) * faces : count_y * faces]
    edge_store = jnp.stack([west_full, east_full, south_full, north_full])
    halos = []
    for side_index in range(4):
        if side_index < 2:
            slabs = jnp.stack(
                [
                    side_halo(edge_store, edges, face_index, side_index, index_y * cells_y, cells_y)
                    for face_index in range(faces)
                ]
            )
        else:
            slabs = jnp.stack(
                [
                    side_halo(edge_store, edges, face_index, side_index, index_x * cells_x, cells_x)
                    for face_index in range(faces)
                ]
            )
        halos.append(slabs)
    west_region = padded[:, :, :, 0:3, 3 : cells_y + 3]
    padded = padded.at[:, :, :, 0:3, 3 : cells_y + 3].set(
        jnp.where(index_x == 0, jnp.flip(halos[0], 3), west_region)
    )
    east_region = padded[:, :, :, cells_x + 3 : cells_x + 6, 3 : cells_y + 3]
    padded = padded.at[:, :, :, cells_x + 3 : cells_x + 6, 3 : cells_y + 3].set(
        jnp.where(index_x == count_x - 1, halos[1], east_region)
    )
    south_region = padded[:, :, :, 3 : cells_x + 3, 0:3]
    padded = padded.at[:, :, :, 3 : cells_x + 3, 0:3].set(
        jnp.where(index_y == 0, jnp.swapaxes(jnp.flip(halos[2], 3), 3, 4), south_region)
    )
    north_region = padded[:, :, :, 3 : cells_x + 3, cells_y + 3 : cells_y + 6]
    padded = padded.at[:, :, :, 3 : cells_x + 3, cells_y + 3 : cells_y + 6].set(
        jnp.where(index_y == count_y - 1, jnp.swapaxes(halos[3], 3, 4), north_region)
    )
    return advance(padded, wave_speed, coriolis, cells_x, cells_y)


def on_device(state, coriolis, wave_speed, edges):
    count_x = lax.axis_size("tx")
    count_y = lax.axis_size("ty")
    index_x = lax.axis_index("tx")
    index_y = lax.axis_index("ty")
    for substep_index in range(SUBSTEPS):
        state = one_substep(state, coriolis, wave_speed, edges, count_x, count_y, index_x, index_y)
    return state


def fits(state):
    count_x = lax.axis_size("tx")
    faces, fields, levels, cells_x, cells_y = state.shape
    return (
        lax.axis_size("ty") == 2
        and faces % 2 == 0
        and levels == 4
        and cells_x == 6
        and cells_y == 24
        and count_x == 8
        and cells_x * count_x == 2 * cells_y
        and 2 * cells_y + 2 * MARGIN <= WINDOW
    )


def either(state, coriolis, wave_speed, edges):
    if fits(state):
        return fast_on_device(state, coriolis, wave_speed, edges)
    return on_device(state, coriolis, wave_speed, edges)


def solution(mesh):
    in_specs = (P("member", None, None, "tx", "ty"), P(None, "tx", "ty"), P(), P())
    out_specs = P("member", None, None, "tx", "ty")
    return jax.shard_map(
        either, mesh=mesh, in_specs=in_specs, out_specs=out_specs, check_vma=False
    )
```

```python
import functools

import jax
import jax.numpy as jnp
from jax import lax
from jax.experimental import pallas as pl
from jax.experimental.pallas import tpu as pltpu
from jax.sharding import PartitionSpec as P

SUBSTEPS = 2
LANES = 128
WINDOW = 64
MARGIN = 8
VMEM_LIMIT = 32 * 1024 * 1024


def window_start(source, target, count_x, index_y, cx, cy, far):
    width = 2 * cx
    near = jnp.minimum(target, count_x - 1 - target)
    inward = jnp.minimum(cx * near - jnp.where(far, cx, cx // 2), cy - width)
    rim = (source == 0) | (source == count_x - 1)
    start = jnp.where(rim, jnp.maximum(inward, 0), 0)
    return jnp.where(index_y == 0, start, cy - width - start)


def windows(source, target, count_x, index_y, cx, cy):
    low_far = source == count_x - 1
    lower = window_start(source, target, count_x, index_y, cx, cy, low_far)
    upper = window_start(source, target, count_x, index_y, cx, cy, ~low_far)
    return lower, upper


def unit_place(field, x, cx, group, width):
    per_row = 60 // width
    index = field * cx + x
    return (index // per_row) * group, (index % per_row) * width


def pack_kernel(
    cx, cy, count_x, full_rows, small_rows, state_hbm, coriolis_hbm,
    swap_ref, keep_ref, middle_ref, state_ref, coriolis_ref, sems,
):
    full_ref = swap_ref.at[pl.ds(0, full_rows)]
    copies = [
        pltpu.make_async_copy(state_hbm, state_ref, sems.at[0]),
        pltpu.make_async_copy(coriolis_hbm, coriolis_ref, sems.at[1]),
    ]
    for copy in copies:
        copy.start()
    faces, fields = state_ref.shape[:2]
    levels = state_ref.shape[3]
    pairs = faces // 2
    group = pairs * levels
    half = cx // 2
    width = 2 * cx
    base = fields * half * group
    index_x = lax.axis_index("tx")
    index_y = lax.axis_index("ty")
    full_ref[...] = jnp.zeros(full_ref.shape, jnp.float32)
    for copy in copies:
        copy.wait()
    for face in range(faces):
        for parity in range(2):
            lane = (face % 2) * WINDOW + MARGIN + parity * cy
            for xp in range(half):
                for field in range(fields):
                    row = field * half * group + xp * group + (face // 2) * levels
                    full_ref[row : row + levels, lane : lane + cy] = state_ref[
                        face, field, 2 * xp + parity
                    ]
                row = base + (2 * xp + parity) * pairs + face // 2
                lane_at = (face % 2) * WINDOW + MARGIN
                full_ref[row : row + 1, lane_at : lane_at + cy] = coriolis_ref[
                    face, 2 * xp + parity : 2 * xp + parity + 1
                ]
    sense = 1 - 2 * index_y
    wanted = [(middle_ref, 0, count_x // 2)]
    for place, distance in enumerate((2, 3)):
        wanted.append((keep_ref, place * small_rows, sense * distance))
        wanted.append((swap_ref, full_rows + place * small_rows, -sense * distance))
    for small_ref, top, offset in wanted:
        target = (index_x + offset + count_x) % count_x
        starts = windows(index_x, target, count_x, index_y, cx, cy)
        blocks = {}

        def put(row, lane, lines):
            position = lax.broadcasted_iota(jnp.int32, lines.shape, 1) % WINDOW
            here = (position >= lane) & (position < lane + width)
            blocks[row] = jnp.where(here, lines, blocks.get(row, jnp.zeros_like(lines)))

        for field in range(fields):
            for x in range(cx):
                row = field * half * group + (x // 2) * group
                at, lane = unit_place(field, x, cx, group, width)
                shift = lane - MARGIN - (x % 2) * cy - starts[x // half] + 2 * LANES
                put(at, lane, pltpu.roll(full_ref[row : row + group], shift % LANES, 1))
        for part in range(2):
            row = base + part * half * pairs
            at, lane = unit_place(fields, part, cx, group, width)
            shift = lane - MARGIN - starts[part] + 2 * LANES
            lines = full_ref[row : row + group]
            put(at, lane, pltpu.roll(lines, shift % LANES, 1))
        for row, lines in blocks.items():
            small_ref[top + row : top + row + group] = lines


def step_kernel(
    cx, cy, count_x, full_rows, small_rows, parts_ref, table_ref, out_ref,
    z_ref, cor_ref, pred_ref, store_ref, tile_ref, flip_ref, speed_ref,
):
    fields = z_ref.shape[0]
    levels = 4
    slots = 16
    cells = cx * count_x
    faces = store_ref.shape[0] // 4
    pairs = faces // 2
    group = pairs * levels
    half = cx // 2
    chunk = cx * group
    width = 2 * cx
    index_x = lax.axis_index("tx")
    index_y = lax.axis_index("ty")

    def row_of(x):
        return (x + 4) * group

    def lanes_of(rows):
        return lax.broadcasted_iota(jnp.int32, (rows, LANES), 1)

    south_half = lanes_of(group) % WINDOW < MARGIN + cy

    def put_coriolis(start, x, values, at):
        for pair in range(pairs):
            line = values[at + pair : at + pair + 1]
            rows = pl.ds(start + x * group + pair * levels, levels)
            cor_ref[rows] = jnp.broadcast_to(line, (levels, LANES))

    near = [(0, (0, 0), (1, 0))]
    distant = []
    for core in range(2):
        sense = 1 - 2 * core
        places = [(core, full_rows), (core, 2 * full_rows)]
        near.append((sense, places[core], places[1 - core]))
        for place, distance in enumerate((2, 3)):
            top = 3 * full_rows + 2 * place * small_rows
            places = [(core, top), (core, top + small_rows)]
            distant.append((sense * distance, places[core], places[1 - core]))
    top = 3 * full_rows + 4 * small_rows
    distant.append((count_x // 2, (0, top), (1, top)))

    for offset, (south_core, south_top), (north_core, north_top) in near:
        source = (index_x - offset + count_x) % count_x
        start = pl.multiple_of(source * chunk, 8)
        for field in range(fields):
            for xp in range(half):
                row = field * half * group + xp * group
                south = parts_ref[south_core, south_top + row : south_top + row + group]
                north = parts_ref[north_core, north_top + row : north_top + row + group]
                even = jnp.where(south_half, south, pltpu.roll(north, cy, 1))
                odd = jnp.where(south_half, pltpu.roll(south, LANES - cy, 1), north)
                z_ref[field, pl.ds(start + row_of(2 * xp), group)] = even
                z_ref[field, pl.ds(start + row_of(2 * xp + 1), group)] = odd
        for part in range(2):
            row = fields * half * group + part * half * pairs
            south = parts_ref[south_core, south_top + row : south_top + row + group]
            north = parts_ref[north_core, north_top + row : north_top + row + group]
            values = jnp.where(south_half, south, pltpu.roll(north, cy, 1))
            for x in range(half):
                put_coriolis(start, part * half + x, values, x * pairs)

    for offset, south_place, north_place in distant:
        source = (index_x - offset + count_x) % count_x
        start = pl.multiple_of(source * chunk, 8)
        from_south = windows(source, index_x, count_x, 0, cx, cy)
        from_north = windows(source, index_x, count_x, 1, cx, cy)

        def lines_at(at, lane, part):
            south = parts_ref[south_place[0], south_place[1] + at : south_place[1] + at + group]
            north = parts_ref[north_place[0], north_place[1] + at : north_place[1] + at + group]
            south_shift = MARGIN + from_south[part] - lane + LANES
            north_shift = MARGIN + cy + from_north[part] - lane + LANES
            return jnp.where(
                south_half,
                pltpu.roll(south, south_shift % LANES, 1),
                pltpu.roll(north, north_shift % LANES, 1),
            )

        for field in range(fields):
            for x in range(cx):
                at, lane = unit_place(field, x, cx, group, width)
                z_ref[field, pl.ds(start + row_of(x), group)] = lines_at(at, lane, x // half)
        for part in range(2):
            at, lane = unit_place(fields, part, cx, group, width)
            values = lines_at(at, lane, part)
            for x in range(half):
                put_coriolis(start, part * half + x, values, x * pairs)

    level_of = lax.broadcasted_iota(jnp.int32, speed_ref.shape, 0) % levels
    speeds = jnp.full(speed_ref.shape, table_ref[0], jnp.float32)
    for index in range(1, levels):
        speeds = jnp.where(level_of == index, table_ref[index], speeds)
    speed_ref[...] = speeds

    def collect():
        position = lanes_of(cells) % WINDOW
        gap = WINDOW - cells + 3
        wide = gap + 3 * levels
        for pair in range(pairs):
            merged = jnp.zeros((cells, LANES), jnp.float32)
            for slot, field in ((0, 0), (1, 2)):
                for level in range(levels):
                    lines = z_ref[field, pl.ds(row_of(0) + pair * levels + level, cells, group)]
                    offset = slot * wide + 3 * level
                    here = position - offset
                    wanted = ((here >= 0) & (here < 3)) | ((here >= gap) & (here < gap + 3))
                    shift = (offset - (MARGIN + cells - 3)) % LANES
                    merged = jnp.where(wanted, pltpu.roll(lines, shift, 1), merged)
            merged = jnp.concatenate(
                [merged, jnp.zeros((LANES - cells, LANES), jnp.float32)], axis=0
            )
            flip_ref[pair] = merged.T
            for slot in range(2):
                for side in (2, 3):
                    for odd in range(2):
                        for depth in range(3):
                            base = slot * wide
                            if side == 3:
                                base += odd * WINDOW + 2 - depth
                            else:
                                base += ((odd + 1) % 2) * WINDOW + gap + depth
                            at = slot * slots + depth * levels
                            store_ref[(2 * pair + odd) * 4 + side, at : at + levels] = flip_ref[
                                pair, pl.ds(base, levels, 3)
                            ]
            for slot in range(2):
                for side in (0, 1):
                    for depth in range(3):
                        x = depth if side == 0 else cells - 1 - depth
                        row = row_of(x) + pair * levels
                        lines = z_ref[slot, row : row + levels]
                        at = slot * slots + depth * levels
                        for odd in range(2):
                            store_ref[(2 * pair + odd) * 4 + side, at : at + levels] = pltpu.roll(
                                lines, LANES - MARGIN - odd * WINDOW, 1
                            )

    def fetch(face, side, position):
        at = levels + (face * 4 + side) * 3
        neighbour = table_ref[at].astype(jnp.int32)
        far_side = table_ref[at + 1].astype(jnp.int32)
        flipped = table_ref[at + 2].astype(jnp.int32)
        block = store_ref[neighbour * 4 + far_side]
        order = jnp.where(flipped == 1, cells - 1 - position, position)
        order = jnp.where((position >= 0) & (position < cells), order, 0)
        block = jnp.take_along_axis(block, order, axis=1)
        sign_here = 2 * (side % 2) - 1
        sign_there = 2 * (far_side % 2) - 1
        sign = (-sign_here * sign_there).astype(jnp.float32)
        normal = lax.broadcasted_iota(jnp.int32, block.shape, 0) >= slots
        return jnp.where(normal, sign * block, block)

    def rim_rows(side):
        lane = lanes_of(2 * slots)
        for pair in range(pairs):
            first = fetch(2 * pair, side, lane - MARGIN)
            second = fetch(2 * pair + 1, side, lane - (MARGIN + WINDOW))
            both = jnp.where(lane < WINDOW, first, second)
            for slot in range(2):
                for depth in range(3):
                    x = -1 - depth if side == 0 else cells + depth
                    at = slot * slots + depth * levels
                    row = row_of(x) + pair * levels
                    z_ref[slot, row : row + levels] = both[at : at + levels]

    def tile_rows(odd, side, depth):
        if side == 3:
            return pl.ds(odd * WINDOW + depth, levels, 16)
        return pl.ds(((odd + 1) % 2) * WINDOW + 15 - depth, levels, 16)

    def put_columns(lines, field, start, pair):
        count = lines.shape[0]
        position = lanes_of(count) % WINDOW
        rim = ((position >= MARGIN - 3) & (position < MARGIN)) | (
            (position >= MARGIN + cells) & (position < MARGIN + cells + 3)
        )
        for level in range(levels):
            rolled = pltpu.roll(lines, (MARGIN + cells - 16 * level) % LANES, 1)
            at = pl.ds(row_of(start) + pair * levels + level, count, group)
            z_ref[field, at] = jnp.where(rim, rolled, z_ref[field, at])

    def rim_columns_all():
        for pair in range(pairs):
            for odd in range(2):
                for side in (2, 3):
                    block = fetch(2 * pair + odd, side, lanes_of(2 * slots))
                    for slot in range(2):
                        for depth in range(3):
                            at = slot * slots + depth * levels
                            tile_ref[2 * pair + slot, tile_rows(odd, side, depth)] = block[
                                at : at + levels
                            ]
            for slot, field in ((0, 0), (1, 2)):
                put_columns(tile_ref[2 * pair + slot].T[:cells], field, 0, pair)

    def rim_columns_own():
        lane = lanes_of(2 * slots)
        second = lax.broadcasted_iota(jnp.int32, lane.shape, 0) >= slots
        for odd in range(2):
            for side in (2, 3):
                total = jnp.zeros((slots, LANES), jnp.float32)
                for pair in range(pairs):
                    local = lane - jnp.where(second, 8 * (pairs + pair), 8 * pair)
                    block = fetch(2 * pair + odd, side, index_x * cx + local)
                    block = jnp.where((local >= 0) & (local < 8), block, 0.0)
                    total = total + block[:slots] + block[slots:]
                for depth in range(3):
                    at = depth * levels
                    tile_ref[0, tile_rows(odd, side, depth)] = total[at : at + levels]
        turned = tile_ref[0].T
        for slot, field in ((0, 0), (1, 2)):
            for pair in range(pairs):
                at = 8 * (slot * pairs + pair)
                put_columns(turned[at : at + cx], field, index_x * cx, pair)

    def predict(at, rows):
        speed = speed_ref[:rows]
        ahead = z_ref[0, pl.ds(at + group, rows)]
        behind = z_ref[0, pl.ds(at - group, rows)]
        pred_ref[pl.ds(at, rows)] = z_ref[1, pl.ds(at, rows)] - speed * (0.5 * (ahead - behind))

    def update(at, rows):
        speed = speed_ref[:rows]
        height = z_ref[0, pl.ds(at, rows)]
        north_pred = z_ref[2, pl.ds(at, rows)] - speed * (
            0.5 * (pltpu.roll(height, LANES - 1, 1) - pltpu.roll(height, 1, 1))
        )
        east_pred = pred_ref[pl.ds(at, rows)]
        flux_east = 8.0 * (
            pred_ref[pl.ds(at + group, rows)] - pred_ref[pl.ds(at - group, rows)]
        ) - (pred_ref[pl.ds(at + 2 * group, rows)] - pred_ref[pl.ds(at - 2 * group, rows)])
        flux_north = 8.0 * (
            pltpu.roll(north_pred, LANES - 1, 1) - pltpu.roll(north_pred, 1, 1)
        ) - (pltpu.roll(north_pred, LANES - 2, 1) - pltpu.roll(north_pred, 2, 1))
        height = height - speed * ((flux_east + flux_north) * (1.0 / 12.0))
        turning = cor_ref[pl.ds(at - row_of(0), rows)]
        return height, east_pred + turning * north_pred, north_pred - turning * east_pred

    collect()
    rim_rows(0)
    rim_rows(1)
    rim_columns_all()
    for first in range(-2, cells + 2, 4):
        predict(row_of(first), 4 * group)
    for index in range(count_x):
        at = row_of(0) + index * chunk
        for field, values in enumerate(update(at, chunk)):
            z_ref[field, at : at + chunk] = values

    collect()

    @pl.when(index_x == 0)
    def _():
        rim_rows(0)

    @pl.when(index_x == count_x - 1)
    def _():
        rim_rows(1)

    rim_columns_own()
    at = pl.multiple_of(row_of(0) + index_x * chunk, 8)
    predict(at - 2 * group, chunk + 4 * group)
    for field, values in enumerate(update(at, chunk)):
        for odd in range(2):
            shift = LANES - (MARGIN + odd * WINDOW) - index_y * cy
            rolled = pltpu.roll(values, shift, 1)
            for x in range(cx):
                for pair in range(pairs):
                    row = x * group + pair * levels
                    out_ref[2 * pair + odd, field, x] = rolled[row : row + levels, :cy]


def fast_on_device(state, coriolis, wave_speed, edges):
    count_x = lax.axis_size("tx")
    faces, fields, levels, cx, cy = state.shape
    pairs = faces // 2
    group = pairs * levels
    cells = cx * count_x
    full_rows = fields * (cx // 2) * group + (cx // 2) * pairs + group
    full_rows = -(-full_rows // 8) * 8
    small_rows = unit_place(fields, 1, cx, group, 2 * cx)[0] + group
    swap, keep, middle = pl.pallas_call(
        functools.partial(pack_kernel, cx, cy, count_x, full_rows, small_rows),
        out_shape=[
            jax.ShapeDtypeStruct((full_rows + 2 * small_rows, LANES), jnp.float32),
            jax.ShapeDtypeStruct((2 * small_rows, LANES), jnp.float32),
            jax.ShapeDtypeStruct((small_rows, LANES), jnp.float32),
        ],
        in_specs=[pl.BlockSpec(memory_space=pltpu.HBM)] * 2,
        out_specs=[pl.BlockSpec(memory_space=pltpu.VMEM)] * 3,
        scratch_shapes=[
            pltpu.VMEM((faces, fields, cx, levels, cy), jnp.float32),
            pltpu.VMEM((faces, cx, cy), jnp.float32),
            pltpu.SemaphoreType.DMA((2,)),
        ],
        compiler_params=pltpu.CompilerParams(vmem_limit_bytes=VMEM_LIMIT),
        name="pack",
    )(jnp.swapaxes(state, 2, 3), coriolis)

    def moved(block, distance):
        pairs_of = []
        for index in range(count_x):
            for core in range(2):
                target = (index + distance * (1 - 2 * core)) % count_x
                pairs_of.append((2 * index + core, 2 * target + core))
        return lax.ppermute(block, ("tx", "ty"), pairs_of)

    own = swap[:full_rows]
    other = lax.ppermute(swap, "ty", [(0, 1), (1, 0)])
    first = moved(jnp.concatenate([own, other[:full_rows]]), 1)
    seconds = [
        moved(
            jnp.concatenate(
                [
                    keep[place * small_rows : (place + 1) * small_rows],
                    other[full_rows + place * small_rows : full_rows + (place + 1) * small_rows],
                ]
            ),
            distance,
        )
        for place, distance in enumerate((2, 3))
    ]
    last = moved(middle, count_x // 2)
    parts = lax.all_gather(jnp.concatenate([own, first, *seconds, last]), "ty")
    table = jnp.concatenate([wave_speed, edges.reshape(-1).astype(jnp.float32)])
    z_rows = (cells + 8) * group
    out = pl.pallas_call(
        functools.partial(
            step_kernel, cx, cy, count_x, full_rows, small_rows
        ),
        out_shape=jax.ShapeDtypeStruct((faces, fields, cx, levels, cy), jnp.float32),
        in_specs=[
            pl.BlockSpec(memory_space=pltpu.VMEM),
            pl.BlockSpec(memory_space=pltpu.SMEM),
        ],
        out_specs=pl.BlockSpec(memory_space=pltpu.VMEM),
        scratch_shapes=[
            pltpu.VMEM((fields, z_rows, LANES), jnp.float32),
            pltpu.VMEM((cells * group, LANES), jnp.float32),
            pltpu.VMEM((z_rows, LANES), jnp.float32),
            pltpu.VMEM((faces * 4, 32, LANES), jnp.float32),
            pltpu.VMEM((faces, LANES, LANES), jnp.float32),
            pltpu.VMEM((pairs, LANES, LANES), jnp.float32),
            pltpu.VMEM(((cx + 4) * group, LANES), jnp.float32),
        ],
        compiler_params=pltpu.CompilerParams(vmem_limit_bytes=VMEM_LIMIT),
        name="substeps",
    )(parts, table)
    return jnp.swapaxes(out, 2, 3)


def padded_2(block, sides, width):
    for axis, dim in sides:
        count = lax.axis_size(axis)
        forward = [(i, i + 1) for i in range(count - 1)]
        backward = [(target, source) for source, target in forward]
        low = lax.ppermute(
            lax.slice_in_dim(block, block.shape[dim] - width, None, axis=dim), axis, forward
        )
        high = lax.ppermute(lax.slice_in_dim(block, 0, width, axis=dim), axis, backward)
        block = jnp.concatenate([low, block, high], axis=dim)
    return block


def spread(block, axis, owner):
    block = jnp.where(lax.axis_index(axis) == owner, block, jnp.zeros_like(block))
    return lax.psum(block, axis)


def rotate_strip(strip_data, side_index, far_side, flipped):
    normal_part = jnp.where(far_side < 2, strip_data[1], strip_data[2])
    along_part = jnp.where(far_side < 2, strip_data[2], strip_data[1])
    sign_here = 2.0 * (side_index % 2) - 1.0
    sign_there = (2 * (far_side % 2) - 1).astype(jnp.float32)
    normal_part = -sign_here * sign_there * normal_part
    along_part = (1 - 2 * flipped).astype(jnp.float32) * along_part
    if side_index < 2:
        return jnp.stack([strip_data[0], normal_part, along_part])
    return jnp.stack([strip_data[0], along_part, normal_part])


def window_strip(store, side_pick, neighbour, flipped, start, width):
    full_length = store.shape[5]
    begin = jnp.where(flipped == 1, full_length - start - width, start)
    zero = jnp.zeros((), jnp.int32)
    sizes_here = (1, 1, store.shape[2], store.shape[3], store.shape[4], width)
    piece = lax.dynamic_slice(store, (side_pick, neighbour, zero, zero, zero, begin), sizes_here)[
        0, 0
    ]
    return jnp.where(flipped == 1, jnp.flip(piece, 3), piece)


def side_halo(edge_store, edges, face_index, side_index, start, width):
    neighbour = edges[face_index, side_index, 0]
    far_side = edges[face_index, side_index, 1]
    flipped = edges[face_index, side_index, 2]
    strip_data = window_strip(edge_store, far_side, neighbour, flipped, start, width)
    return rotate_strip(strip_data, side_index, far_side, flipped)


def advance(padded, wave_speed, coriolis_part, cells_x, cells_y):
    height = padded[..., 0, :, :, :]
    wind_east = padded[..., 1, :, :, :]
    wind_north = padded[..., 2, :, :, :]
    speed = wave_speed[:, None, None]
    east_pred = wind_east[..., 1 : cells_x + 5, 3 : cells_y + 3] - speed * (
        0.5
        * (
            height[..., 2 : cells_x + 6, 3 : cells_y + 3]
            - height[..., 0 : cells_x + 4, 3 : cells_y + 3]
        )
    )
    north_pred = wind_north[..., 3 : cells_x + 3, 1 : cells_y + 5] - speed * (
        0.5
        * (
            height[..., 3 : cells_x + 3, 2 : cells_y + 6]
            - height[..., 3 : cells_x + 3, 0 : cells_y + 4]
        )
    )
    flux_east = (
        8.0 * (east_pred[..., 3 : cells_x + 3, :] - east_pred[..., 1 : cells_x + 1, :])
        - (east_pred[..., 4 : cells_x + 4, :] - east_pred[..., 0:cells_x, :])
    ) / 12.0
    flux_north = (
        8.0 * (north_pred[..., 3 : cells_y + 3] - north_pred[..., 1 : cells_y + 1])
        - (north_pred[..., 4 : cells_y + 4] - north_pred[..., 0:cells_y])
    ) / 12.0
    height_new = height[..., 3 : cells_x + 3, 3 : cells_y + 3] - speed * (flux_east + flux_north)
    east_inner = east_pred[..., 2 : cells_x + 2, :]
    north_inner = north_pred[..., 2 : cells_y + 2]
    turning = coriolis_part[..., None, :, :]
    return jnp.stack(
        [height_new, east_inner + turning * north_inner, north_inner - turning * east_inner],
        axis=-4,
    )


def one_substep(state, coriolis, wave_speed, edges, count_x, count_y, index_x, index_y):
    faces = state.shape[0]
    cells_x = state.shape[3]
    cells_y = state.shape[4]
    padded = padded_2(state, (("tx", 3), ("ty", 4)), 3)
    west_rim = state[:, :, :, 0:3, :]
    east_rim = jnp.flip(state[:, :, :, cells_x - 3 :, :], 3)
    south_rim = jnp.swapaxes(state[:, :, :, :, 0:3], 3, 4)
    north_rim = jnp.swapaxes(jnp.flip(state[:, :, :, :, cells_y - 3 :], 4), 3, 4)
    west_part = spread(west_rim, "tx", 0)
    east_part = spread(east_rim, "tx", count_x - 1)
    west_full, east_full = (
        lax.all_gather(west_part, "ty", axis=4, tiled=True),
        lax.all_gather(east_part, "ty", axis=4, tiled=True),
    )
    south_row, north_row = (
        lax.all_gather(south_rim, "tx", axis=4, tiled=True),
        lax.all_gather(north_rim, "tx", axis=4, tiled=True),
    )
    south_all, north_all = (
        lax.all_gather(south_row, "ty", axis=0, tiled=True),
        lax.all_gather(north_row, "ty", axis=0, tiled=True),
    )
    south_full = south_all[0:faces]
    north_full = north_all[(count_y - 1) * faces : count_y * faces]
    edge_store = jnp.stack([west_full, east_full, south_full, north_full])
    halos = []
    for side_index in range(4):
        if side_index < 2:
            slabs = jnp.stack(
                [
                    side_halo(edge_store, edges, face_index, side_index, index_y * cells_y, cells_y)
                    for face_index in range(faces)
                ]
            )
        else:
            slabs = jnp.stack(
                [
                    side_halo(edge_store, edges, face_index, side_index, index_x * cells_x, cells_x)
                    for face_index in range(faces)
                ]
            )
        halos.append(slabs)
    west_region = padded[:, :, :, 0:3, 3 : cells_y + 3]
    padded = padded.at[:, :, :, 0:3, 3 : cells_y + 3].set(
        jnp.where(index_x == 0, jnp.flip(halos[0], 3), west_region)
    )
    east_region = padded[:, :, :, cells_x + 3 : cells_x + 6, 3 : cells_y + 3]
    padded = padded.at[:, :, :, cells_x + 3 : cells_x + 6, 3 : cells_y + 3].set(
        jnp.where(index_x == count_x - 1, halos[1], east_region)
    )
    south_region = padded[:, :, :, 3 : cells_x + 3, 0:3]
    padded = padded.at[:, :, :, 3 : cells_x + 3, 0:3].set(
        jnp.where(index_y == 0, jnp.swapaxes(jnp.flip(halos[2], 3), 3, 4), south_region)
    )
    north_region = padded[:, :, :, 3 : cells_x + 3, cells_y + 3 : cells_y + 6]
    padded = padded.at[:, :, :, 3 : cells_x + 3, cells_y + 3 : cells_y + 6].set(
        jnp.where(index_y == count_y - 1, jnp.swapaxes(halos[3], 3, 4), north_region)
    )
    return advance(padded, wave_speed, coriolis, cells_x, cells_y)


def on_device(state, coriolis, wave_speed, edges):
    count_x = lax.axis_size("tx")
    count_y = lax.axis_size("ty")
    index_x = lax.axis_index("tx")
    index_y = lax.axis_index("ty")
    for substep_index in range(SUBSTEPS):
        state = one_substep(state, coriolis, wave_speed, edges, count_x, count_y, index_x, index_y)
    return state


def fits(state):
    count_x = lax.axis_size("tx")
    faces, fields, levels, cells_x, cells_y = state.shape
    return (
        lax.axis_size("ty") == 2
        and faces % 2 == 0
        and levels == 4
        and cells_x == 6
        and cells_y == 24
        and count_x == 8
        and cells_x * count_x == 2 * cells_y
        and 2 * cells_y + 2 * MARGIN <= WINDOW
    )


def either(state, coriolis, wave_speed, edges):
    if fits(state):
        return fast_on_device(state, coriolis, wave_speed, edges)
    return on_device(state, coriolis, wave_speed, edges)


def solution(mesh):
    in_specs = (P("member", None, None, "tx", "ty"), P(None, "tx", "ty"), P(), P())
    out_specs = P("member", None, None, "tx", "ty")
    return jax.shard_map(
        either, mesh=mesh, in_specs=in_specs, out_specs=out_specs, check_vma=False
    )
```

```python
import functools

import jax
import jax.numpy as jnp
from jax import lax
from jax.experimental import pallas as pl
from jax.experimental.pallas import tpu as pltpu
from jax.sharding import PartitionSpec as P

SUBSTEPS = 2
LANES = 128
WINDOW = 64
MARGIN = 8
VMEM_LIMIT = 32 * 1024 * 1024


def window_start(source, target, count_x, index_y, cx, cy, far):
    width = 2 * cx
    near = jnp.minimum(target, count_x - 1 - target)
    inward = jnp.minimum(cx * near - jnp.where(far, cx, cx // 2), cy - width)
    rim = (source == 0) | (source == count_x - 1)
    start = jnp.where(rim, jnp.maximum(inward, 0), 0)
    return jnp.where(index_y == 0, start, cy - width - start)


def windows(source, target, count_x, index_y, cx, cy):
    low_far = source == count_x - 1
    lower = window_start(source, target, count_x, index_y, cx, cy, low_far)
    upper = window_start(source, target, count_x, index_y, cx, cy, ~low_far)
    return lower, upper


def unit_place(field, x, cx, group, width):
    per_row = 60 // width
    index = field * cx + x
    return (index // per_row) * group, (index % per_row) * width


def pack_kernel(
    cx, cy, count_x, full_rows, small_rows, state_hbm, coriolis_hbm,
    swap_ref, keep_ref, middle_ref, state_ref, coriolis_ref, line_ref, sems,
):
    full_ref = swap_ref.at[pl.ds(0, full_rows)]
    copies = [
        pltpu.make_async_copy(state_hbm, state_ref, sems.at[0]),
        pltpu.make_async_copy(coriolis_hbm, coriolis_ref, sems.at[1]),
    ]
    for copy in copies:
        copy.start()
    faces, fields = state_ref.shape[:2]
    levels = state_ref.shape[3]
    pairs = faces // 2
    group = pairs * levels
    half = cx // 2
    width = 2 * cx
    base = fields * half * group
    index_x = lax.axis_index("tx")
    index_y = lax.axis_index("ty")
    full_ref[...] = jnp.zeros(full_ref.shape, jnp.float32)
    line_ref[...] = jnp.zeros(line_ref.shape, jnp.float32)
    for copy in copies:
        copy.wait()
    for face in range(faces):
        for parity in range(2):
            lane = (face % 2) * WINDOW + MARGIN + parity * cy
            for xp in range(half):
                for field in range(fields):
                    row = field * half * group + xp * group + (face // 2) * levels
                    full_ref[row : row + levels, lane : lane + cy] = state_ref[
                        face, field, 2 * xp + parity
                    ]
                x = 2 * xp + parity
                row = base + xp * pairs + face // 2
                full_ref[row : row + 1, lane : lane + cy] = coriolis_ref[face, x : x + 1]
                row = (x // half) * 16 + (x % half) * pairs + face // 2
                lane_at = (face % 2) * WINDOW + MARGIN
                line_ref[row : row + 1, lane_at : lane_at + cy] = coriolis_ref[face, x : x + 1]
    sense = 1 - 2 * index_y
    wanted = [(middle_ref, 0, count_x // 2)]
    for place, distance in enumerate((2, 3)):
        wanted.append((keep_ref, place * small_rows, sense * distance))
        wanted.append((swap_ref, full_rows + place * small_rows, -sense * distance))
    for small_ref, top, offset in wanted:
        target = (index_x + offset + count_x) % count_x
        starts = windows(index_x, target, count_x, index_y, cx, cy)
        blocks = {}

        def put(row, lane, lines):
            position = lax.broadcasted_iota(jnp.int32, lines.shape, 1) % WINDOW
            here = (position >= lane) & (position < lane + width)
            blocks[row] = jnp.where(here, lines, blocks.get(row, jnp.zeros_like(lines)))

        for field in range(fields):
            for x in range(cx):
                row = field * half * group + (x // 2) * group
                at, lane = unit_place(field, x, cx, group, width)
                shift = lane - MARGIN - (x % 2) * cy - starts[x // half] + 2 * LANES
                put(at, lane, pltpu.roll(full_ref[row : row + group], shift % LANES, 1))
        for part in range(2):
            at, lane = unit_place(fields, part, cx, group, width)
            shift = lane - MARGIN - starts[part] + 2 * LANES
            lines = line_ref[16 * part : 16 * part + group]
            put(at, lane, pltpu.roll(lines, shift % LANES, 1))
        for row, lines in blocks.items():
            small_ref[top + row : top + row + group] = lines


def step_kernel(
    cx, cy, count_x, full_rows, small_rows, own_ref, other_ref, near_ref, near_other_ref,
    far_ref, far_other_ref, table_ref, out_ref, z_ref, cor_ref, pred_ref, store_ref, tile_ref, flip_ref, speed_ref,
):
    fields = z_ref.shape[0]
    levels = 4
    slots = 16
    cells = cx * count_x
    faces = store_ref.shape[0] // 4
    pairs = faces // 2
    group = pairs * levels
    half = cx // 2
    chunk = cx * group
    width = 2 * cx
    index_x = lax.axis_index("tx")
    index_y = lax.axis_index("ty")

    def row_of(x):
        return (x + 4) * group

    def lanes_of(rows):
        return lax.broadcasted_iota(jnp.int32, (rows, LANES), 1)

    south_half = lanes_of(group) % WINDOW < MARGIN + cy
    south_is_own = index_y == 0
    own_half = south_half == south_is_own

    def from_owner(offset):
        source = (index_x - offset + 2 * count_x) % count_x
        return source, pl.multiple_of(source * chunk, 8)

    def put_coriolis(start, x, values, at):
        for pair in range(pairs):
            line = values[at + pair : at + pair + 1]
            rows = pl.ds(start + x * group + pair * levels, levels)
            cor_ref[rows] = jnp.broadcast_to(line, (levels, LANES))

    def put_block(start, lines_of):
        base = fields * half * group
        for field in range(fields):
            for xp in range(half):
                even, odd = lines_of(field * half * group + xp * group, group)
                z_ref[field, pl.ds(start + row_of(2 * xp), group)] = even
                z_ref[field, pl.ds(start + row_of(2 * xp + 1), group)] = odd
        for parity, values in enumerate(lines_of(base, half * pairs)):
            for xp in range(half):
                put_coriolis(start, 2 * xp + parity, values, xp * pairs)

    def put_distant(source, start, lines_of):
        starts_south = windows(source, index_x, count_x, 0, cx, cy)
        starts_north = windows(source, index_x, count_x, 1, cx, cy)

        def lines_at(field, x, part):
            at, lane = unit_place(field, x, cx, group, width)
            south_shift = (MARGIN + starts_south[part] - lane + LANES) % LANES
            north_shift = (MARGIN + cy + starts_north[part] - lane + LANES) % LANES
            return lines_of(at, south_shift, north_shift)

        for field in range(fields):
            for x in range(cx):
                z_ref[field, pl.ds(start + row_of(x), group)] = lines_at(field, x, x // half)
        for part in range(2):
            values = lines_at(fields, part, part)
            for x in range(half):
                put_coriolis(start, part * half + x, values, x * pairs)

    def own_lines(row, rows):
        mine = own_ref[row : row + rows]
        theirs = other_ref[row : row + rows]
        up, down = index_y * cy, (1 - index_y) * cy
        even = jnp.where(own_half[:rows], pltpu.roll(mine, up, 1), pltpu.roll(theirs, down, 1))
        mine = pltpu.roll(mine, (LANES - down) % LANES, 1)
        theirs = pltpu.roll(theirs, (LANES - up) % LANES, 1)
        return even, jnp.where(own_half[:rows], mine, theirs)

    put_block(from_owner(0)[1], own_lines)

    sense = 1 - 2 * index_y
    for block_ref, far_block_ref, toward, south_first in (
        (near_ref, far_ref, sense, index_y),
        (near_other_ref, far_other_ref, -sense, 1 - index_y),
    ):
        south_top = pl.multiple_of(south_first * full_rows, 8)
        north_top = pl.multiple_of((1 - south_first) * full_rows, 8)

        def near_lines(row, rows, block_ref=block_ref, south_top=south_top, north_top=north_top):
            south = block_ref[pl.ds(south_top + row, rows)]
            north = block_ref[pl.ds(north_top + row, rows)]
            low = south_half[:rows]
            even = jnp.where(low, south, pltpu.roll(north, cy, 1))
            return even, jnp.where(low, pltpu.roll(south, LANES - cy, 1), north)

        put_block(from_owner(toward)[1], near_lines)
        for place, distance in enumerate((2, 3)):
            top = 2 * place * small_rows
            south_top = pl.multiple_of(top + south_first * small_rows, 8)
            north_top = pl.multiple_of(top + (1 - south_first) * small_rows, 8)

            def far_lines(
                at, south_shift, north_shift,
                block_ref=far_block_ref, south_top=south_top, north_top=north_top,
            ):
                south = block_ref[pl.ds(south_top + at, group)]
                north = block_ref[pl.ds(north_top + at, group)]
                south = pltpu.roll(south, south_shift, 1)
                return jnp.where(south_half, south, pltpu.roll(north, north_shift, 1))

            put_distant(*from_owner(toward * distance), far_lines)

    def middle_lines(at, south_shift, north_shift):
        row = 4 * small_rows + at
        mine_shift = jnp.where(south_is_own, south_shift, north_shift)
        other_shift = jnp.where(south_is_own, north_shift, south_shift)
        mine = pltpu.roll(far_ref[row : row + group], mine_shift, 1)
        return jnp.where(own_half, mine, pltpu.roll(far_other_ref[row : row + group], other_shift, 1))

    put_distant(*from_owner(count_x // 2), middle_lines)

    level_of = lax.broadcasted_iota(jnp.int32, speed_ref.shape, 0) % levels
    speeds = jnp.full(speed_ref.shape, table_ref[0], jnp.float32)
    for index in range(1, levels):
        speeds = jnp.where(level_of == index, table_ref[index], speeds)
    speed_ref[...] = speeds

    def collect():
        position = lanes_of(cells) % WINDOW
        gap = WINDOW - cells + 3
        wide = gap + 3 * levels
        for pair in range(pairs):
            merged = jnp.zeros((cells, LANES), jnp.float32)
            for slot, field in ((0, 0), (1, 2)):
                for level in range(levels):
                    lines = z_ref[field, pl.ds(row_of(0) + pair * levels + level, cells, group)]
                    offset = slot * wide + 3 * level
                    here = position - offset
                    wanted = ((here >= 0) & (here < 3)) | ((here >= gap) & (here < gap + 3))
                    shift = (offset - (MARGIN + cells - 3)) % LANES
                    merged = jnp.where(wanted, pltpu.roll(lines, shift, 1), merged)
            merged = jnp.concatenate(
                [merged, jnp.zeros((LANES - cells, LANES), jnp.float32)], axis=0
            )
            flip_ref[pair] = merged.T
            for slot in range(2):
                for side in (2, 3):
                    for odd in range(2):
                        for depth in range(3):
                            base = slot * wide
                            if side == 3:
                                base += odd * WINDOW + 2 - depth
                            else:
                                base += ((odd + 1) % 2) * WINDOW + gap + depth
                            at = slot * slots + depth * levels
                            store_ref[(2 * pair + odd) * 4 + side, at : at + levels] = flip_ref[
                                pair, pl.ds(base, levels, 3)
                            ]
            for slot in range(2):
                for side in (0, 1):
                    for depth in range(3):
                        x = depth if side == 0 else cells - 1 - depth
                        row = row_of(x) + pair * levels
                        lines = z_ref[slot, row : row + levels]
                        at = slot * slots + depth * levels
                        for odd in range(2):
                            store_ref[(2 * pair + odd) * 4 + side, at : at + levels] = pltpu.roll(
                                lines, LANES - MARGIN - odd * WINDOW, 1
                            )

    def fetch(face, side, position):
        at = levels + (face * 4 + side) * 3
        neighbour = table_ref[at].astype(jnp.int32)
        far_side = table_ref[at + 1].astype(jnp.int32)
        flipped = table_ref[at + 2].astype(jnp.int32)
        block = store_ref[neighbour * 4 + far_side]
        order = jnp.where(flipped == 1, cells - 1 - position, position)
        order = jnp.where((position >= 0) & (position < cells), order, 0)
        block = jnp.take_along_axis(block, order, axis=1)
        sign_here = 2 * (side % 2) - 1
        sign_there = 2 * (far_side % 2) - 1
        sign = (-sign_here * sign_there).astype(jnp.float32)
        normal = lax.broadcasted_iota(jnp.int32, block.shape, 0) >= slots
        return jnp.where(normal, sign * block, block)

    def rim_rows(side):
        lane = lanes_of(2 * slots)
        for pair in range(pairs):
            first = fetch(2 * pair, side, lane - MARGIN)
            second = fetch(2 * pair + 1, side, lane - (MARGIN + WINDOW))
            both = jnp.where(lane < WINDOW, first, second)
            for slot in range(2):
                for depth in range(3):
                    x = -1 - depth if side == 0 else cells + depth
                    at = slot * slots + depth * levels
                    row = row_of(x) + pair * levels
                    z_ref[slot, row : row + levels] = both[at : at + levels]

    def tile_rows(odd, side, depth):
        if side == 3:
            return pl.ds(odd * WINDOW + depth, levels, 16)
        return pl.ds(((odd + 1) % 2) * WINDOW + 15 - depth, levels, 16)

    def put_columns(lines, field, start, pair):
        count = lines.shape[0]
        position = lanes_of(count) % WINDOW
        rim = ((position >= MARGIN - 3) & (position < MARGIN)) | (
            (position >= MARGIN + cells) & (position < MARGIN + cells + 3)
        )
        for level in range(levels):
            rolled = pltpu.roll(lines, (MARGIN + cells - 16 * level) % LANES, 1)
            at = pl.ds(row_of(start) + pair * levels + level, count, group)
            z_ref[field, at] = jnp.where(rim, rolled, z_ref[field, at])

    def rim_columns_all():
        for pair in range(pairs):
            for odd in range(2):
                for side in (2, 3):
                    block = fetch(2 * pair + odd, side, lanes_of(2 * slots))
                    for slot in range(2):
                        for depth in range(3):
                            at = slot * slots + depth * levels
                            tile_ref[2 * pair + slot, tile_rows(odd, side, depth)] = block[
                                at : at + levels
                            ]
            for slot, field in ((0, 0), (1, 2)):
                put_columns(tile_ref[2 * pair + slot].T[:cells], field, 0, pair)

    def rim_columns_own():
        lane = lanes_of(2 * slots)
        second = lax.broadcasted_iota(jnp.int32, lane.shape, 0) >= slots
        for odd in range(2):
            for side in (2, 3):
                total = jnp.zeros((slots, LANES), jnp.float32)
                for pair in range(pairs):
                    local = lane - jnp.where(second, 8 * (pairs + pair), 8 * pair)
                    block = fetch(2 * pair + odd, side, index_x * cx + local)
                    block = jnp.where((local >= 0) & (local < 8), block, 0.0)
                    total = total + block[:slots] + block[slots:]
                for depth in range(3):
                    at = depth * levels
                    tile_ref[0, tile_rows(odd, side, depth)] = total[at : at + levels]
        turned = tile_ref[0].T
        for slot, field in ((0, 0), (1, 2)):
            for pair in range(pairs):
                at = 8 * (slot * pairs + pair)
                put_columns(turned[at : at + cx], field, index_x * cx, pair)

    def predict(at, rows):
        speed = speed_ref[:rows]
        ahead = z_ref[0, pl.ds(at + group, rows)]
        behind = z_ref[0, pl.ds(at - group, rows)]
        pred_ref[pl.ds(at, rows)] = z_ref[1, pl.ds(at, rows)] - speed * (0.5 * (ahead - behind))

    def update(at, rows):
        speed = speed_ref[:rows]
        height = z_ref[0, pl.ds(at, rows)]
        north_pred = z_ref[2, pl.ds(at, rows)] - speed * (
            0.5 * (pltpu.roll(height, LANES - 1, 1) - pltpu.roll(height, 1, 1))
        )
        east_pred = pred_ref[pl.ds(at, rows)]
        flux_east = 8.0 * (
            pred_ref[pl.ds(at + group, rows)] - pred_ref[pl.ds(at - group, rows)]
        ) - (pred_ref[pl.ds(at + 2 * group, rows)] - pred_ref[pl.ds(at - 2 * group, rows)])
        flux_north = 8.0 * (
            pltpu.roll(north_pred, LANES - 1, 1) - pltpu.roll(north_pred, 1, 1)
        ) - (pltpu.roll(north_pred, LANES - 2, 1) - pltpu.roll(north_pred, 2, 1))
        height = height - speed * ((flux_east + flux_north) * (1.0 / 12.0))
        turning = cor_ref[pl.ds(at - row_of(0), rows)]
        return height, east_pred + turning * north_pred, north_pred - turning * east_pred

    collect()
    rim_rows(0)
    rim_rows(1)
    rim_columns_all()
    for first in range(-2, cells + 2, 4):
        predict(row_of(first), 4 * group)
    for index in range(count_x):
        at = row_of(0) + index * chunk
        for field, values in enumerate(update(at, chunk)):
            z_ref[field, at : at + chunk] = values

    collect()

    @pl.when(index_x == 0)
    def _():
        rim_rows(0)

    @pl.when(index_x == count_x - 1)
    def _():
        rim_rows(1)

    rim_columns_own()
    at = pl.multiple_of(row_of(0) + index_x * chunk, 8)
    predict(at - 2 * group, chunk + 4 * group)
    for field, values in enumerate(update(at, chunk)):
        for odd in range(2):
            shift = LANES - (MARGIN + odd * WINDOW) - index_y * cy
            rolled = pltpu.roll(values, shift, 1)
            for x in range(cx):
                for pair in range(pairs):
                    row = x * group + pair * levels
                    out_ref[2 * pair + odd, field, x] = rolled[row : row + levels, :cy]


def fast_on_device(state, coriolis, wave_speed, edges):
    count_x = lax.axis_size("tx")
    faces, fields, levels, cx, cy = state.shape
    pairs = faces // 2
    group = pairs * levels
    cells = cx * count_x
    full_rows = fields * (cx // 2) * group + (cx // 2) * pairs
    full_rows = -(-full_rows // 8) * 8
    small_rows = unit_place(fields, 1, cx, group, 2 * cx)[0] + group
    swap, keep, middle = pl.pallas_call(
        functools.partial(pack_kernel, cx, cy, count_x, full_rows, small_rows),
        out_shape=[
            jax.ShapeDtypeStruct((full_rows + 2 * small_rows, LANES), jnp.float32),
            jax.ShapeDtypeStruct((2 * small_rows, LANES), jnp.float32),
            jax.ShapeDtypeStruct((small_rows, LANES), jnp.float32),
        ],
        in_specs=[pl.BlockSpec(memory_space=pltpu.HBM)] * 2,
        out_specs=[pl.BlockSpec(memory_space=pltpu.VMEM)] * 3,
        scratch_shapes=[
            pltpu.VMEM((faces, fields, cx, levels, cy), jnp.float32),
            pltpu.VMEM((faces, cx, cy), jnp.float32),
            pltpu.VMEM((32, LANES), jnp.float32),
            pltpu.SemaphoreType.DMA((2,)),
        ],
        compiler_params=pltpu.CompilerParams(vmem_limit_bytes=VMEM_LIMIT),
        name="pack",
    )(jnp.swapaxes(state, 2, 3), coriolis)

    def moved(block, distance):
        pairs_of = []
        for index in range(count_x):
            for core in range(2):
                target = (index + distance * (1 - 2 * core)) % count_x
                pairs_of.append((2 * index + core, 2 * target + core))
        return lax.ppermute(block, ("tx", "ty"), pairs_of)

    def across(block):
        return lax.ppermute(block, "ty", [(0, 1), (1, 0)])

    own = swap[:full_rows]
    other = across(swap)
    wave_speed, edges, other = lax.optimization_barrier((wave_speed, edges, other))
    first = moved(jnp.concatenate([own, other[:full_rows]]), 1)
    seconds = [
        moved(
            jnp.concatenate(
                [
                    keep[place * small_rows : (place + 1) * small_rows],
                    other[full_rows + place * small_rows : full_rows + (place + 1) * small_rows],
                ]
            ),
            distance,
        )
        for place, distance in enumerate((2, 3))
    ]
    far = jnp.concatenate([*seconds, moved(middle, count_x // 2)])
    pieces = (own, other, first, across(first), far, across(far))
    table = jnp.concatenate([wave_speed, edges.reshape(-1).astype(jnp.float32)])
    z_rows = (cells + 8) * group
    out = pl.pallas_call(
        functools.partial(
            step_kernel, cx, cy, count_x, full_rows, small_rows
        ),
        out_shape=jax.ShapeDtypeStruct((faces, fields, cx, levels, cy), jnp.float32),
        in_specs=[pl.BlockSpec(memory_space=pltpu.VMEM)] * 6
        + [pl.BlockSpec(memory_space=pltpu.SMEM)],
        out_specs=pl.BlockSpec(memory_space=pltpu.VMEM),
        scratch_shapes=[
            pltpu.VMEM((fields, z_rows, LANES), jnp.float32),
            pltpu.VMEM((cells * group, LANES), jnp.float32),
            pltpu.VMEM((z_rows, LANES), jnp.float32),
            pltpu.VMEM((faces * 4, 32, LANES), jnp.float32),
            pltpu.VMEM((faces, LANES, LANES), jnp.float32),
            pltpu.VMEM((pairs, LANES, LANES), jnp.float32),
            pltpu.VMEM(((cx + 4) * group, LANES), jnp.float32),
        ],
        compiler_params=pltpu.CompilerParams(vmem_limit_bytes=VMEM_LIMIT),
        name="substeps",
    )(*pieces, table)
    return jnp.swapaxes(out, 2, 3)


def padded_2(block, sides, width):
    for axis, dim in sides:
        count = lax.axis_size(axis)
        forward = [(i, i + 1) for i in range(count - 1)]
        backward = [(target, source) for source, target in forward]
        low = lax.ppermute(
            lax.slice_in_dim(block, block.shape[dim] - width, None, axis=dim), axis, forward
        )
        high = lax.ppermute(lax.slice_in_dim(block, 0, width, axis=dim), axis, backward)
        block = jnp.concatenate([low, block, high], axis=dim)
    return block


def spread(block, axis, owner):
    block = jnp.where(lax.axis_index(axis) == owner, block, jnp.zeros_like(block))
    return lax.psum(block, axis)


def rotate_strip(strip_data, side_index, far_side, flipped):
    normal_part = jnp.where(far_side < 2, strip_data[1], strip_data[2])
    along_part = jnp.where(far_side < 2, strip_data[2], strip_data[1])
    sign_here = 2.0 * (side_index % 2) - 1.0
    sign_there = (2 * (far_side % 2) - 1).astype(jnp.float32)
    normal_part = -sign_here * sign_there * normal_part
    along_part = (1 - 2 * flipped).astype(jnp.float32) * along_part
    if side_index < 2:
        return jnp.stack([strip_data[0], normal_part, along_part])
    return jnp.stack([strip_data[0], along_part, normal_part])


def window_strip(store, side_pick, neighbour, flipped, start, width):
    full_length = store.shape[5]
    begin = jnp.where(flipped == 1, full_length - start - width, start)
    zero = jnp.zeros((), jnp.int32)
    sizes_here = (1, 1, store.shape[2], store.shape[3], store.shape[4], width)
    piece = lax.dynamic_slice(store, (side_pick, neighbour, zero, zero, zero, begin), sizes_here)[
        0, 0
    ]
    return jnp.where(flipped == 1, jnp.flip(piece, 3), piece)


def side_halo(edge_store, edges, face_index, side_index, start, width):
    neighbour = edges[face_index, side_index, 0]
    far_side = edges[face_index, side_index, 1]
    flipped = edges[face_index, side_index, 2]
    strip_data = window_strip(edge_store, far_side, neighbour, flipped, start, width)
    return rotate_strip(strip_data, side_index, far_side, flipped)


def advance(padded, wave_speed, coriolis_part, cells_x, cells_y):
    height = padded[..., 0, :, :, :]
    wind_east = padded[..., 1, :, :, :]
    wind_north = padded[..., 2, :, :, :]
    speed = wave_speed[:, None, None]
    east_pred = wind_east[..., 1 : cells_x + 5, 3 : cells_y + 3] - speed * (
        0.5
        * (
            height[..., 2 : cells_x + 6, 3 : cells_y + 3]
            - height[..., 0 : cells_x + 4, 3 : cells_y + 3]
        )
    )
    north_pred = wind_north[..., 3 : cells_x + 3, 1 : cells_y + 5] - speed * (
        0.5
        * (
            height[..., 3 : cells_x + 3, 2 : cells_y + 6]
            - height[..., 3 : cells_x + 3, 0 : cells_y + 4]
        )
    )
    flux_east = (
        8.0 * (east_pred[..., 3 : cells_x + 3, :] - east_pred[..., 1 : cells_x + 1, :])
        - (east_pred[..., 4 : cells_x + 4, :] - east_pred[..., 0:cells_x, :])
    ) / 12.0
    flux_north = (
        8.0 * (north_pred[..., 3 : cells_y + 3] - north_pred[..., 1 : cells_y + 1])
        - (north_pred[..., 4 : cells_y + 4] - north_pred[..., 0:cells_y])
    ) / 12.0
    height_new = height[..., 3 : cells_x + 3, 3 : cells_y + 3] - speed * (flux_east + flux_north)
    east_inner = east_pred[..., 2 : cells_x + 2, :]
    north_inner = north_pred[..., 2 : cells_y + 2]
    turning = coriolis_part[..., None, :, :]
    return jnp.stack(
        [height_new, east_inner + turning * north_inner, north_inner - turning * east_inner],
        axis=-4,
    )


def one_substep(state, coriolis, wave_speed, edges, count_x, count_y, index_x, index_y):
    faces = state.shape[0]
    cells_x = state.shape[3]
    cells_y = state.shape[4]
    padded = padded_2(state, (("tx", 3), ("ty", 4)), 3)
    west_rim = state[:, :, :, 0:3, :]
    east_rim = jnp.flip(state[:, :, :, cells_x - 3 :, :], 3)
    south_rim = jnp.swapaxes(state[:, :, :, :, 0:3], 3, 4)
    north_rim = jnp.swapaxes(jnp.flip(state[:, :, :, :, cells_y - 3 :], 4), 3, 4)
    west_part = spread(west_rim, "tx", 0)
    east_part = spread(east_rim, "tx", count_x - 1)
    west_full, east_full = (
        lax.all_gather(west_part, "ty", axis=4, tiled=True),
        lax.all_gather(east_part, "ty", axis=4, tiled=True),
    )
    south_row, north_row = (
        lax.all_gather(south_rim, "tx", axis=4, tiled=True),
        lax.all_gather(north_rim, "tx", axis=4, tiled=True),
    )
    south_all, north_all = (
        lax.all_gather(south_row, "ty", axis=0, tiled=True),
        lax.all_gather(north_row, "ty", axis=0, tiled=True),
    )
    south_full = south_all[0:faces]
    north_full = north_all[(count_y - 1) * faces : count_y * faces]
    edge_store = jnp.stack([west_full, east_full, south_full, north_full])
    halos = []
    for side_index in range(4):
        if side_index < 2:
            slabs = jnp.stack(
                [
                    side_halo(edge_store, edges, face_index, side_index, index_y * cells_y, cells_y)
                    for face_index in range(faces)
                ]
            )
        else:
            slabs = jnp.stack(
                [
                    side_halo(edge_store, edges, face_index, side_index, index_x * cells_x, cells_x)
                    for face_index in range(faces)
                ]
            )
        halos.append(slabs)
    west_region = padded[:, :, :, 0:3, 3 : cells_y + 3]
    padded = padded.at[:, :, :, 0:3, 3 : cells_y + 3].set(
        jnp.where(index_x == 0, jnp.flip(halos[0], 3), west_region)
    )
    east_region = padded[:, :, :, cells_x + 3 : cells_x + 6, 3 : cells_y + 3]
    padded = padded.at[:, :, :, cells_x + 3 : cells_x + 6, 3 : cells_y + 3].set(
        jnp.where(index_x == count_x - 1, halos[1], east_region)
    )
    south_region = padded[:, :, :, 3 : cells_x + 3, 0:3]
    padded = padded.at[:, :, :, 3 : cells_x + 3, 0:3].set(
        jnp.where(index_y == 0, jnp.swapaxes(jnp.flip(halos[2], 3), 3, 4), south_region)
    )
    north_region = padded[:, :, :, 3 : cells_x + 3, cells_y + 3 : cells_y + 6]
    padded = padded.at[:, :, :, 3 : cells_x + 3, cells_y + 3 : cells_y + 6].set(
        jnp.where(index_y == count_y - 1, jnp.swapaxes(halos[3], 3, 4), north_region)
    )
    return advance(padded, wave_speed, coriolis, cells_x, cells_y)


def on_device(state, coriolis, wave_speed, edges):
    count_x = lax.axis_size("tx")
    count_y = lax.axis_size("ty")
    index_x = lax.axis_index("tx")
    index_y = lax.axis_index("ty")
    for substep_index in range(SUBSTEPS):
        state = one_substep(state, coriolis, wave_speed, edges, count_x, count_y, index_x, index_y)
    return state


def fits(state):
    count_x = lax.axis_size("tx")
    faces, fields, levels, cells_x, cells_y = state.shape
    return (
        lax.axis_size("ty") == 2
        and faces % 2 == 0
        and levels == 4
        and cells_x == 6
        and cells_y == 24
        and count_x == 8
        and cells_x * count_x == 2 * cells_y
        and 2 * cells_y + 2 * MARGIN <= WINDOW
    )


def either(state, coriolis, wave_speed, edges):
    if fits(state):
        return fast_on_device(state, coriolis, wave_speed, edges)
    return on_device(state, coriolis, wave_speed, edges)


def solution(mesh):
    in_specs = (P("member", None, None, "tx", "ty"), P(None, "tx", "ty"), P(), P())
    out_specs = P("member", None, None, "tx", "ty")
    return jax.shard_map(
        either, mesh=mesh, in_specs=in_specs, out_specs=out_specs, check_vma=False
    )
```

```python
import functools

import jax
import jax.numpy as jnp
from jax import lax
from jax.experimental import pallas as pl
from jax.experimental.pallas import tpu as pltpu
from jax.sharding import PartitionSpec as P

SUBSTEPS = 2
LANES = 128
WINDOW = 64
MARGIN = 8
VMEM_LIMIT = 32 * 1024 * 1024


def window_start(source, target, count_x, index_y, cx, cy, far):
    width = 2 * cx
    near = jnp.minimum(target, count_x - 1 - target)
    inward = jnp.minimum(cx * near - jnp.where(far, cx, cx // 2), cy - width)
    rim = (source == 0) | (source == count_x - 1)
    start = jnp.where(rim, jnp.maximum(inward, 0), 0)
    return jnp.where(index_y == 0, start, cy - width - start)


def windows(source, target, count_x, index_y, cx, cy):
    low_far = source == count_x - 1
    lower = window_start(source, target, count_x, index_y, cx, cy, low_far)
    upper = window_start(source, target, count_x, index_y, cx, cy, ~low_far)
    return lower, upper


def unit_place(field, x, cx, group, width):
    per_row = 60 // width
    index = field * cx + x
    return (index // per_row) * group, (index % per_row) * width


def pack_kernel(
    cx, cy, count_x, full_rows, small_rows, state_hbm, coriolis_hbm,
    swap_ref, keep_ref, middle_ref, state_ref, coriolis_ref, line_ref, sems,
):
    full_ref = swap_ref.at[pl.ds(0, full_rows)]
    copies = [
        pltpu.make_async_copy(state_hbm, state_ref, sems.at[0]),
        pltpu.make_async_copy(coriolis_hbm, coriolis_ref, sems.at[1]),
    ]
    for copy in copies:
        copy.start()
    faces, fields = state_ref.shape[:2]
    levels = state_ref.shape[3]
    pairs = faces // 2
    group = pairs * levels
    half = cx // 2
    width = 2 * cx
    base = fields * half * group
    index_x = lax.axis_index("tx")
    index_y = lax.axis_index("ty")
    full_ref[...] = jnp.zeros(full_ref.shape, jnp.float32)
    line_ref[...] = jnp.zeros(line_ref.shape, jnp.float32)
    for copy in copies:
        copy.wait()
    for face in range(faces):
        for parity in range(2):
            lane = (face % 2) * WINDOW + MARGIN + parity * cy
            for xp in range(half):
                for field in range(fields):
                    row = field * half * group + xp * group + (face // 2) * levels
                    full_ref[row : row + levels, lane : lane + cy] = state_ref[
                        face, field, 2 * xp + parity
                    ]
                x = 2 * xp + parity
                row = base + xp * pairs + face // 2
                full_ref[row : row + 1, lane : lane + cy] = coriolis_ref[face, x : x + 1]
                row = (x // half) * 16 + (x % half) * pairs + face // 2
                lane_at = (face % 2) * WINDOW + MARGIN
                line_ref[row : row + 1, lane_at : lane_at + cy] = coriolis_ref[face, x : x + 1]
    sense = 1 - 2 * index_y
    wanted = [(middle_ref, 0, count_x // 2)]
    for place, distance in enumerate((2, 3)):
        wanted.append((keep_ref, place * small_rows, sense * distance))
        wanted.append((swap_ref, full_rows + place * small_rows, -sense * distance))
    for small_ref, top, offset in wanted:
        target = (index_x + offset + count_x) % count_x
        starts = windows(index_x, target, count_x, index_y, cx, cy)
        blocks = {}

        def put(row, lane, lines):
            position = lax.broadcasted_iota(jnp.int32, lines.shape, 1) % WINDOW
            here = (position >= lane) & (position < lane + width)
            blocks[row] = jnp.where(here, lines, blocks.get(row, jnp.zeros_like(lines)))

        for field in range(fields):
            for x in range(cx):
                row = field * half * group + (x // 2) * group
                at, lane = unit_place(field, x, cx, group, width)
                shift = lane - MARGIN - (x % 2) * cy - starts[x // half] + 2 * LANES
                put(at, lane, pltpu.roll(full_ref[row : row + group], shift % LANES, 1))
        for part in range(2):
            at, lane = unit_place(fields, part, cx, group, width)
            shift = lane - MARGIN - starts[part] + 2 * LANES
            lines = line_ref[16 * part : 16 * part + group]
            put(at, lane, pltpu.roll(lines, shift % LANES, 1))
        for row, lines in blocks.items():
            small_ref[top + row : top + row + group] = lines


def mix_kernel(full_rows, small_rows, swap_ref, other_ref, keep_ref, near_ref, second_ref, third_ref):
    near_ref[:full_rows] = swap_ref[:full_rows]
    near_ref[full_rows:] = other_ref[:full_rows]
    for place, far_ref in enumerate((second_ref, third_ref)):
        at = place * small_rows
        far_ref[:small_rows] = keep_ref[at : at + small_rows]
        at += full_rows
        far_ref[small_rows:] = other_ref[at : at + small_rows]


def step_kernel(
    cx, cy, count_x, full_rows, small_rows, own_ref, other_ref, got_ref, got_other_ref,
    table_ref, out_ref, z_ref, cor_ref, pred_ref, store_ref, tile_ref, flip_ref, speed_ref,
):
    fields = z_ref.shape[0]
    levels = 4
    slots = 16
    cells = cx * count_x
    faces = store_ref.shape[0] // 4
    pairs = faces // 2
    group = pairs * levels
    half = cx // 2
    chunk = cx * group
    width = 2 * cx
    index_x = lax.axis_index("tx")
    index_y = lax.axis_index("ty")

    def row_of(x):
        return (x + 4) * group

    def lanes_of(rows):
        return lax.broadcasted_iota(jnp.int32, (rows, LANES), 1)

    south_half = lanes_of(group) % WINDOW < MARGIN + cy
    south_is_own = index_y == 0
    own_half = south_half == south_is_own

    def from_owner(offset):
        source = (index_x - offset + 2 * count_x) % count_x
        return source, pl.multiple_of(source * chunk, 8)

    def put_coriolis(start, x, values, at):
        for pair in range(pairs):
            line = values[at + pair : at + pair + 1]
            rows = pl.ds(start + x * group + pair * levels, levels)
            cor_ref[rows] = jnp.broadcast_to(line, (levels, LANES))

    def put_block(start, lines_of):
        base = fields * half * group
        for field in range(fields):
            for xp in range(half):
                even, odd = lines_of(field * half * group + xp * group, group)
                z_ref[field, pl.ds(start + row_of(2 * xp), group)] = even
                z_ref[field, pl.ds(start + row_of(2 * xp + 1), group)] = odd
        for parity, values in enumerate(lines_of(base, half * pairs)):
            for xp in range(half):
                put_coriolis(start, 2 * xp + parity, values, xp * pairs)

    def put_distant(source, start, lines_of):
        starts_south = windows(source, index_x, count_x, 0, cx, cy)
        starts_north = windows(source, index_x, count_x, 1, cx, cy)

        def lines_at(field, x, part):
            at, lane = unit_place(field, x, cx, group, width)
            south_shift = (MARGIN + starts_south[part] - lane + LANES) % LANES
            north_shift = (MARGIN + cy + starts_north[part] - lane + LANES) % LANES
            return lines_of(at, south_shift, north_shift)

        for field in range(fields):
            for x in range(cx):
                z_ref[field, pl.ds(start + row_of(x), group)] = lines_at(field, x, x // half)
        for part in range(2):
            values = lines_at(fields, part, part)
            for x in range(half):
                put_coriolis(start, part * half + x, values, x * pairs)

    def own_lines(row, rows):
        mine = own_ref[row : row + rows]
        theirs = other_ref[row : row + rows]
        up, down = index_y * cy, (1 - index_y) * cy
        even = jnp.where(own_half[:rows], pltpu.roll(mine, up, 1), pltpu.roll(theirs, down, 1))
        mine = pltpu.roll(mine, (LANES - down) % LANES, 1)
        theirs = pltpu.roll(theirs, (LANES - up) % LANES, 1)
        return even, jnp.where(own_half[:rows], mine, theirs)

    put_block(from_owner(0)[1], own_lines)

    sense = 1 - 2 * index_y
    for block_ref, toward, south_first in (
        (got_ref, sense, index_y),
        (got_other_ref, -sense, 1 - index_y),
    ):
        south_top = pl.multiple_of(south_first * full_rows, 8)
        north_top = pl.multiple_of((1 - south_first) * full_rows, 8)

        def near_lines(row, rows, block_ref=block_ref, south_top=south_top, north_top=north_top):
            south = block_ref[pl.ds(south_top + row, rows)]
            north = block_ref[pl.ds(north_top + row, rows)]
            low = south_half[:rows]
            even = jnp.where(low, south, pltpu.roll(north, cy, 1))
            return even, jnp.where(low, pltpu.roll(south, LANES - cy, 1), north)

        put_block(from_owner(toward)[1], near_lines)
        for place, distance in enumerate((2, 3)):
            top = 2 * full_rows + 2 * place * small_rows
            south_top = pl.multiple_of(top + south_first * small_rows, 8)
            north_top = pl.multiple_of(top + (1 - south_first) * small_rows, 8)

            def far_lines(
                at, south_shift, north_shift,
                block_ref=block_ref, south_top=south_top, north_top=north_top,
            ):
                south = block_ref[pl.ds(south_top + at, group)]
                north = block_ref[pl.ds(north_top + at, group)]
                south = pltpu.roll(south, south_shift, 1)
                return jnp.where(south_half, south, pltpu.roll(north, north_shift, 1))

            put_distant(*from_owner(toward * distance), far_lines)

    def middle_lines(at, south_shift, north_shift):
        row = 2 * full_rows + 4 * small_rows + at
        mine_shift = jnp.where(south_is_own, south_shift, north_shift)
        other_shift = jnp.where(south_is_own, north_shift, south_shift)
        mine = pltpu.roll(got_ref[row : row + group], mine_shift, 1)
        theirs = pltpu.roll(got_other_ref[row : row + group], other_shift, 1)
        return jnp.where(own_half, mine, theirs)

    put_distant(*from_owner(count_x // 2), middle_lines)

    level_of = lax.broadcasted_iota(jnp.int32, speed_ref.shape, 0) % levels
    speeds = jnp.full(speed_ref.shape, table_ref[0], jnp.float32)
    for index in range(1, levels):
        speeds = jnp.where(level_of == index, table_ref[index], speeds)
    speed_ref[...] = speeds

    def collect():
        position = lanes_of(cells) % WINDOW
        gap = WINDOW - cells + 3
        wide = gap + 3 * levels
        for pair in range(pairs):
            merged = jnp.zeros((cells, LANES), jnp.float32)
            for slot, field in ((0, 0), (1, 2)):
                for level in range(levels):
                    lines = z_ref[field, pl.ds(row_of(0) + pair * levels + level, cells, group)]
                    offset = slot * wide + 3 * level
                    here = position - offset
                    wanted = ((here >= 0) & (here < 3)) | ((here >= gap) & (here < gap + 3))
                    shift = (offset - (MARGIN + cells - 3)) % LANES
                    merged = jnp.where(wanted, pltpu.roll(lines, shift, 1), merged)
            merged = jnp.concatenate(
                [merged, jnp.zeros((LANES - cells, LANES), jnp.float32)], axis=0
            )
            flip_ref[pair] = merged.T
            for slot in range(2):
                for side in (2, 3):
                    for odd in range(2):
                        for depth in range(3):
                            base = slot * wide
                            if side == 3:
                                base += odd * WINDOW + 2 - depth
                            else:
                                base += ((odd + 1) % 2) * WINDOW + gap + depth
                            at = slot * slots + depth * levels
                            store_ref[(2 * pair + odd) * 4 + side, at : at + levels] = flip_ref[
                                pair, pl.ds(base, levels, 3)
                            ]
            for slot in range(2):
                for side in (0, 1):
                    for depth in range(3):
                        x = depth if side == 0 else cells - 1 - depth
                        row = row_of(x) + pair * levels
                        lines = z_ref[slot, row : row + levels]
                        at = slot * slots + depth * levels
                        for odd in range(2):
                            store_ref[(2 * pair + odd) * 4 + side, at : at + levels] = pltpu.roll(
                                lines, LANES - MARGIN - odd * WINDOW, 1
                            )

    def fetch(face, side, position):
        at = levels + (face * 4 + side) * 3
        neighbour = table_ref[at].astype(jnp.int32)
        far_side = table_ref[at + 1].astype(jnp.int32)
        flipped = table_ref[at + 2].astype(jnp.int32)
        block = store_ref[neighbour * 4 + far_side]
        order = jnp.where(flipped == 1, cells - 1 - position, position)
        order = jnp.where((position >= 0) & (position < cells), order, 0)
        block = jnp.take_along_axis(block, order, axis=1)
        sign_here = 2 * (side % 2) - 1
        sign_there = 2 * (far_side % 2) - 1
        sign = (-sign_here * sign_there).astype(jnp.float32)
        normal = lax.broadcasted_iota(jnp.int32, block.shape, 0) >= slots
        return jnp.where(normal, sign * block, block)

    def rim_rows(side):
        lane = lanes_of(2 * slots)
        for pair in range(pairs):
            first = fetch(2 * pair, side, lane - MARGIN)
            second = fetch(2 * pair + 1, side, lane - (MARGIN + WINDOW))
            both = jnp.where(lane < WINDOW, first, second)
            for slot in range(2):
                for depth in range(3):
                    x = -1 - depth if side == 0 else cells + depth
                    at = slot * slots + depth * levels
                    row = row_of(x) + pair * levels
                    z_ref[slot, row : row + levels] = both[at : at + levels]

    def tile_rows(odd, side, depth):
        if side == 3:
            return pl.ds(odd * WINDOW + depth, levels, 16)
        return pl.ds(((odd + 1) % 2) * WINDOW + 15 - depth, levels, 16)

    def put_columns(lines, field, start, pair):
        count = lines.shape[0]
        position = lanes_of(count) % WINDOW
        rim = ((position >= MARGIN - 3) & (position < MARGIN)) | (
            (position >= MARGIN + cells) & (position < MARGIN + cells + 3)
        )
        for level in range(levels):
            rolled = pltpu.roll(lines, (MARGIN + cells - 16 * level) % LANES, 1)
            at = pl.ds(row_of(start) + pair * levels + level, count, group)
            z_ref[field, at] = jnp.where(rim, rolled, z_ref[field, at])

    def rim_columns_all():
        for pair in range(pairs):
            for odd in range(2):
                for side in (2, 3):
                    block = fetch(2 * pair + odd, side, lanes_of(2 * slots))
                    for slot in range(2):
                        for depth in range(3):
                            at = slot * slots + depth * levels
                            tile_ref[2 * pair + slot, tile_rows(odd, side, depth)] = block[
                                at : at + levels
                            ]
            for slot, field in ((0, 0), (1, 2)):
                put_columns(tile_ref[2 * pair + slot].T[:cells], field, 0, pair)

    def rim_columns_own():
        lane = lanes_of(2 * slots)
        second = lax.broadcasted_iota(jnp.int32, lane.shape, 0) >= slots
        for odd in range(2):
            for side in (2, 3):
                total = jnp.zeros((slots, LANES), jnp.float32)
                for pair in range(pairs):
                    local = lane - jnp.where(second, 8 * (pairs + pair), 8 * pair)
                    block = fetch(2 * pair + odd, side, index_x * cx + local)
                    block = jnp.where((local >= 0) & (local < 8), block, 0.0)
                    total = total + block[:slots] + block[slots:]
                for depth in range(3):
                    at = depth * levels
                    tile_ref[0, tile_rows(odd, side, depth)] = total[at : at + levels]
        turned = tile_ref[0].T
        for slot, field in ((0, 0), (1, 2)):
            for pair in range(pairs):
                at = 8 * (slot * pairs + pair)
                put_columns(turned[at : at + cx], field, index_x * cx, pair)

    def predict(at, rows):
        speed = speed_ref[:rows]
        ahead = z_ref[0, pl.ds(at + group, rows)]
        behind = z_ref[0, pl.ds(at - group, rows)]
        pred_ref[pl.ds(at, rows)] = z_ref[1, pl.ds(at, rows)] - speed * (0.5 * (ahead - behind))

    def update(at, rows):
        speed = speed_ref[:rows]
        height = z_ref[0, pl.ds(at, rows)]
        north_pred = z_ref[2, pl.ds(at, rows)] - speed * (
            0.5 * (pltpu.roll(height, LANES - 1, 1) - pltpu.roll(height, 1, 1))
        )
        east_pred = pred_ref[pl.ds(at, rows)]
        flux_east = 8.0 * (
            pred_ref[pl.ds(at + group, rows)] - pred_ref[pl.ds(at - group, rows)]
        ) - (pred_ref[pl.ds(at + 2 * group, rows)] - pred_ref[pl.ds(at - 2 * group, rows)])
        flux_north = 8.0 * (
            pltpu.roll(north_pred, LANES - 1, 1) - pltpu.roll(north_pred, 1, 1)
        ) - (pltpu.roll(north_pred, LANES - 2, 1) - pltpu.roll(north_pred, 2, 1))
        height = height - speed * ((flux_east + flux_north) * (1.0 / 12.0))
        turning = cor_ref[pl.ds(at - row_of(0), rows)]
        return height, east_pred + turning * north_pred, north_pred - turning * east_pred

    collect()
    rim_rows(0)
    rim_rows(1)
    rim_columns_all()
    for first in range(-2, cells + 2, 4):
        predict(row_of(first), 4 * group)
    for index in range(count_x):
        at = row_of(0) + index * chunk
        for field, values in enumerate(update(at, chunk)):
            z_ref[field, at : at + chunk] = values

    collect()

    @pl.when(index_x == 0)
    def _():
        rim_rows(0)

    @pl.when(index_x == count_x - 1)
    def _():
        rim_rows(1)

    rim_columns_own()
    at = pl.multiple_of(row_of(0) + index_x * chunk, 8)
    predict(at - 2 * group, chunk + 4 * group)
    for field, values in enumerate(update(at, chunk)):
        for odd in range(2):
            shift = LANES - (MARGIN + odd * WINDOW) - index_y * cy
            rolled = pltpu.roll(values, shift, 1)
            for x in range(cx):
                for pair in range(pairs):
                    row = x * group + pair * levels
                    out_ref[2 * pair + odd, field, x] = rolled[row : row + levels, :cy]


def fast_on_device(state, coriolis, wave_speed, edges):
    count_x = lax.axis_size("tx")
    faces, fields, levels, cx, cy = state.shape
    pairs = faces // 2
    group = pairs * levels
    cells = cx * count_x
    full_rows = fields * (cx // 2) * group + (cx // 2) * pairs
    full_rows = -(-full_rows // 8) * 8
    small_rows = unit_place(fields, 1, cx, group, 2 * cx)[0] + group
    swap, keep, middle = pl.pallas_call(
        functools.partial(pack_kernel, cx, cy, count_x, full_rows, small_rows),
        out_shape=[
            jax.ShapeDtypeStruct((full_rows + 2 * small_rows, LANES), jnp.float32),
            jax.ShapeDtypeStruct((2 * small_rows, LANES), jnp.float32),
            jax.ShapeDtypeStruct((small_rows, LANES), jnp.float32),
        ],
        in_specs=[pl.BlockSpec(memory_space=pltpu.HBM)] * 2,
        out_specs=[pl.BlockSpec(memory_space=pltpu.VMEM)] * 3,
        scratch_shapes=[
            pltpu.VMEM((faces, fields, cx, levels, cy), jnp.float32),
            pltpu.VMEM((faces, cx, cy), jnp.float32),
            pltpu.VMEM((32, LANES), jnp.float32),
            pltpu.SemaphoreType.DMA((2,)),
        ],
        compiler_params=pltpu.CompilerParams(vmem_limit_bytes=VMEM_LIMIT),
        name="pack",
    )(jnp.swapaxes(state, 2, 3), coriolis)

    def moved(block, distance):
        pairs_of = []
        for index in range(count_x):
            for core in range(2):
                target = (index + distance * (1 - 2 * core)) % count_x
                pairs_of.append((2 * index + core, 2 * target + core))
        return lax.ppermute(block, ("tx", "ty"), pairs_of)

    def across(block):
        return lax.ppermute(block, "ty", [(0, 1), (1, 0)])

    other = across(swap)
    wave_speed, edges, other = lax.optimization_barrier((wave_speed, edges, other))
    messages = pl.pallas_call(
        functools.partial(mix_kernel, full_rows, small_rows),
        out_shape=[
            jax.ShapeDtypeStruct((2 * rows, LANES), jnp.float32)
            for rows in (full_rows, small_rows, small_rows)
        ],
        in_specs=[pl.BlockSpec(memory_space=pltpu.VMEM)] * 3,
        out_specs=[pl.BlockSpec(memory_space=pltpu.VMEM)] * 3,
        name="messages",
    )(swap, other, keep)
    got = [moved(block, place + 1) for place, block in enumerate(messages)]
    got = jnp.concatenate([*got, moved(middle, count_x // 2)])
    pieces = (swap, other, got, across(got))
    table = jnp.concatenate([wave_speed, edges.reshape(-1).astype(jnp.float32)])
    z_rows = (cells + 8) * group
    out = pl.pallas_call(
        functools.partial(
            step_kernel, cx, cy, count_x, full_rows, small_rows
        ),
        out_shape=jax.ShapeDtypeStruct((faces, fields, cx, levels, cy), jnp.float32),
        in_specs=[pl.BlockSpec(memory_space=pltpu.VMEM)] * 4
        + [pl.BlockSpec(memory_space=pltpu.SMEM)],
        out_specs=pl.BlockSpec(memory_space=pltpu.VMEM),
        scratch_shapes=[
            pltpu.VMEM((fields, z_rows, LANES), jnp.float32),
            pltpu.VMEM((cells * group, LANES), jnp.float32),
            pltpu.VMEM((z_rows, LANES), jnp.float32),
            pltpu.VMEM((faces * 4, 32, LANES), jnp.float32),
            pltpu.VMEM((faces, LANES, LANES), jnp.float32),
            pltpu.VMEM((pairs, LANES, LANES), jnp.float32),
            pltpu.VMEM(((cx + 4) * group, LANES), jnp.float32),
        ],
        compiler_params=pltpu.CompilerParams(vmem_limit_bytes=VMEM_LIMIT),
        name="substeps",
    )(*pieces, table)
    return jnp.swapaxes(out, 2, 3)


def padded_2(block, sides, width):
    for axis, dim in sides:
        count = lax.axis_size(axis)
        forward = [(i, i + 1) for i in range(count - 1)]
        backward = [(target, source) for source, target in forward]
        low = lax.ppermute(
            lax.slice_in_dim(block, block.shape[dim] - width, None, axis=dim), axis, forward
        )
        high = lax.ppermute(lax.slice_in_dim(block, 0, width, axis=dim), axis, backward)
        block = jnp.concatenate([low, block, high], axis=dim)
    return block


def spread(block, axis, owner):
    block = jnp.where(lax.axis_index(axis) == owner, block, jnp.zeros_like(block))
    return lax.psum(block, axis)


def rotate_strip(strip_data, side_index, far_side, flipped):
    normal_part = jnp.where(far_side < 2, strip_data[1], strip_data[2])
    along_part = jnp.where(far_side < 2, strip_data[2], strip_data[1])
    sign_here = 2.0 * (side_index % 2) - 1.0
    sign_there = (2 * (far_side % 2) - 1).astype(jnp.float32)
    normal_part = -sign_here * sign_there * normal_part
    along_part = (1 - 2 * flipped).astype(jnp.float32) * along_part
    if side_index < 2:
        return jnp.stack([strip_data[0], normal_part, along_part])
    return jnp.stack([strip_data[0], along_part, normal_part])


def window_strip(store, side_pick, neighbour, flipped, start, width):
    full_length = store.shape[5]
    begin = jnp.where(flipped == 1, full_length - start - width, start)
    zero = jnp.zeros((), jnp.int32)
    sizes_here = (1, 1, store.shape[2], store.shape[3], store.shape[4], width)
    piece = lax.dynamic_slice(store, (side_pick, neighbour, zero, zero, zero, begin), sizes_here)[
        0, 0
    ]
    return jnp.where(flipped == 1, jnp.flip(piece, 3), piece)


def side_halo(edge_store, edges, face_index, side_index, start, width):
    neighbour = edges[face_index, side_index, 0]
    far_side = edges[face_index, side_index, 1]
    flipped = edges[face_index, side_index, 2]
    strip_data = window_strip(edge_store, far_side, neighbour, flipped, start, width)
    return rotate_strip(strip_data, side_index, far_side, flipped)


def advance(padded, wave_speed, coriolis_part, cells_x, cells_y):
    height = padded[..., 0, :, :, :]
    wind_east = padded[..., 1, :, :, :]
    wind_north = padded[..., 2, :, :, :]
    speed = wave_speed[:, None, None]
    east_pred = wind_east[..., 1 : cells_x + 5, 3 : cells_y + 3] - speed * (
        0.5
        * (
            height[..., 2 : cells_x + 6, 3 : cells_y + 3]
            - height[..., 0 : cells_x + 4, 3 : cells_y + 3]
        )
    )
    north_pred = wind_north[..., 3 : cells_x + 3, 1 : cells_y + 5] - speed * (
        0.5
        * (
            height[..., 3 : cells_x + 3, 2 : cells_y + 6]
            - height[..., 3 : cells_x + 3, 0 : cells_y + 4]
        )
    )
    flux_east = (
        8.0 * (east_pred[..., 3 : cells_x + 3, :] - east_pred[..., 1 : cells_x + 1, :])
        - (east_pred[..., 4 : cells_x + 4, :] - east_pred[..., 0:cells_x, :])
    ) / 12.0
    flux_north = (
        8.0 * (north_pred[..., 3 : cells_y + 3] - north_pred[..., 1 : cells_y + 1])
        - (north_pred[..., 4 : cells_y + 4] - north_pred[..., 0:cells_y])
    ) / 12.0
    height_new = height[..., 3 : cells_x + 3, 3 : cells_y + 3] - speed * (flux_east + flux_north)
    east_inner = east_pred[..., 2 : cells_x + 2, :]
    north_inner = north_pred[..., 2 : cells_y + 2]
    turning = coriolis_part[..., None, :, :]
    return jnp.stack(
        [height_new, east_inner + turning * north_inner, north_inner - turning * east_inner],
        axis=-4,
    )


def one_substep(state, coriolis, wave_speed, edges, count_x, count_y, index_x, index_y):
    faces = state.shape[0]
    cells_x = state.shape[3]
    cells_y = state.shape[4]
    padded = padded_2(state, (("tx", 3), ("ty", 4)), 3)
    west_rim = state[:, :, :, 0:3, :]
    east_rim = jnp.flip(state[:, :, :, cells_x - 3 :, :], 3)
    south_rim = jnp.swapaxes(state[:, :, :, :, 0:3], 3, 4)
    north_rim = jnp.swapaxes(jnp.flip(state[:, :, :, :, cells_y - 3 :], 4), 3, 4)
    west_part = spread(west_rim, "tx", 0)
    east_part = spread(east_rim, "tx", count_x - 1)
    west_full, east_full = (
        lax.all_gather(west_part, "ty", axis=4, tiled=True),
        lax.all_gather(east_part, "ty", axis=4, tiled=True),
    )
    south_row, north_row = (
        lax.all_gather(south_rim, "tx", axis=4, tiled=True),
        lax.all_gather(north_rim, "tx", axis=4, tiled=True),
    )
    south_all, north_all = (
        lax.all_gather(south_row, "ty", axis=0, tiled=True),
        lax.all_gather(north_row, "ty", axis=0, tiled=True),
    )
    south_full = south_all[0:faces]
    north_full = north_all[(count_y - 1) * faces : count_y * faces]
    edge_store = jnp.stack([west_full, east_full, south_full, north_full])
    halos = []
    for side_index in range(4):
        if side_index < 2:
            slabs = jnp.stack(
                [
                    side_halo(edge_store, edges, face_index, side_index, index_y * cells_y, cells_y)
                    for face_index in range(faces)
                ]
            )
        else:
            slabs = jnp.stack(
                [
                    side_halo(edge_store, edges, face_index, side_index, index_x * cells_x, cells_x)
                    for face_index in range(faces)
                ]
            )
        halos.append(slabs)
    west_region = padded[:, :, :, 0:3, 3 : cells_y + 3]
    padded = padded.at[:, :, :, 0:3, 3 : cells_y + 3].set(
        jnp.where(index_x == 0, jnp.flip(halos[0], 3), west_region)
    )
    east_region = padded[:, :, :, cells_x + 3 : cells_x + 6, 3 : cells_y + 3]
    padded = padded.at[:, :, :, cells_x + 3 : cells_x + 6, 3 : cells_y + 3].set(
        jnp.where(index_x == count_x - 1, halos[1], east_region)
    )
    south_region = padded[:, :, :, 3 : cells_x + 3, 0:3]
    padded = padded.at[:, :, :, 3 : cells_x + 3, 0:3].set(
        jnp.where(index_y == 0, jnp.swapaxes(jnp.flip(halos[2], 3), 3, 4), south_region)
    )
    north_region = padded[:, :, :, 3 : cells_x + 3, cells_y + 3 : cells_y + 6]
    padded = padded.at[:, :, :, 3 : cells_x + 3, cells_y + 3 : cells_y + 6].set(
        jnp.where(index_y == count_y - 1, jnp.swapaxes(halos[3], 3, 4), north_region)
    )
    return advance(padded, wave_speed, coriolis, cells_x, cells_y)


def on_device(state, coriolis, wave_speed, edges):
    count_x = lax.axis_size("tx")
    count_y = lax.axis_size("ty")
    index_x = lax.axis_index("tx")
    index_y = lax.axis_index("ty")
    for substep_index in range(SUBSTEPS):
        state = one_substep(state, coriolis, wave_speed, edges, count_x, count_y, index_x, index_y)
    return state


def fits(state):
    count_x = lax.axis_size("tx")
    faces, fields, levels, cells_x, cells_y = state.shape
    return (
        lax.axis_size("ty") == 2
        and faces % 2 == 0
        and levels == 4
        and cells_x == 6
        and cells_y == 24
        and count_x == 8
        and cells_x * count_x == 2 * cells_y
        and 2 * cells_y + 2 * MARGIN <= WINDOW
    )


def either(state, coriolis, wave_speed, edges):
    if fits(state):
        return fast_on_device(state, coriolis, wave_speed, edges)
    return on_device(state, coriolis, wave_speed, edges)


def solution(mesh):
    in_specs = (P("member", None, None, "tx", "ty"), P(None, "tx", "ty"), P(), P())
    out_specs = P("member", None, None, "tx", "ty")
    return jax.shard_map(
        either, mesh=mesh, in_specs=in_specs, out_specs=out_specs, check_vma=False
    )
```

```python
import functools

import jax
import jax.numpy as jnp
from jax import lax
from jax.experimental import pallas as pl
from jax.experimental.pallas import tpu as pltpu
from jax.sharding import PartitionSpec as P

SUBSTEPS = 2
LANES = 128
WINDOW = 64
MARGIN = 8
VMEM_LIMIT = 32 * 1024 * 1024
SMALL_VMEM_LIMIT = 8 * 1024 * 1024


def window_start(source, target, count_x, index_y, cx, cy, far):
    width = 2 * cx
    near = jnp.minimum(target, count_x - 1 - target)
    inward = jnp.minimum(cx * near - jnp.where(far, cx, cx // 2), cy - width)
    rim = (source == 0) | (source == count_x - 1)
    start = jnp.where(rim, jnp.maximum(inward, 0), 0)
    return jnp.where(index_y == 0, start, cy - width - start)


def windows(source, target, count_x, index_y, cx, cy):
    low_far = source == count_x - 1
    lower = window_start(source, target, count_x, index_y, cx, cy, low_far)
    upper = window_start(source, target, count_x, index_y, cx, cy, ~low_far)
    return lower, upper


def unit_place(field, x, cx, group, width):
    per_row = 60 // width
    index = field * cx + x
    return (index // per_row) * group, (index % per_row) * width


def pack_kernel(
    cx, cy, count_x, full_rows, small_rows, state_hbm, coriolis_hbm,
    swap_ref, line_ref, state_ref, coriolis_ref, sems,
):
    copies = [
        pltpu.make_async_copy(state_hbm, state_ref, sems.at[0]),
        pltpu.make_async_copy(coriolis_hbm, coriolis_ref, sems.at[1]),
    ]
    for copy in copies:
        copy.start()
    faces, fields = state_ref.shape[:2]
    levels = state_ref.shape[3]
    pairs = faces // 2
    group = pairs * levels
    half = cx // 2
    base = fields * half * group
    swap_ref[:full_rows] = jnp.zeros((full_rows, LANES), jnp.float32)
    line_ref[...] = jnp.zeros(line_ref.shape, jnp.float32)
    for copy in copies:
        copy.wait()
    for face in range(faces):
        for parity in range(2):
            lane = (face % 2) * WINDOW + MARGIN + parity * cy
            for xp in range(half):
                for field in range(fields):
                    row = field * half * group + xp * group + (face // 2) * levels
                    swap_ref[row : row + levels, lane : lane + cy] = state_ref[
                        face, field, 2 * xp + parity
                    ]
                x = 2 * xp + parity
                row = base + xp * pairs + face // 2
                swap_ref[row : row + 1, lane : lane + cy] = coriolis_ref[face, x : x + 1]
                row = (x // half) * 16 + (x % half) * pairs + face // 2
                lane_at = (face % 2) * WINDOW + MARGIN
                line_ref[row : row + 1, lane_at : lane_at + cy] = coriolis_ref[face, x : x + 1]
    sense = 1 - 2 * lax.axis_index("ty")
    for place, distance in enumerate((2, 3)):
        top = full_rows + place * small_rows
        put_chunk(cx, cy, count_x, swap_ref, line_ref, swap_ref, top, -sense * distance)


def put_chunk(cx, cy, count_x, block_ref, line_ref, out_ref, top, offset):
    pairs = 3
    group = 4 * pairs
    fields = 3
    half = cx // 2
    width = 2 * cx
    index_x = lax.axis_index("tx")
    index_y = lax.axis_index("ty")
    target = (index_x + offset + count_x) % count_x
    starts = windows(index_x, target, count_x, index_y, cx, cy)
    blocks = {}

    def put(row, lane, lines):
        position = lax.broadcasted_iota(jnp.int32, lines.shape, 1) % WINDOW
        here = (position >= lane) & (position < lane + width)
        blocks[row] = jnp.where(here, lines, blocks.get(row, jnp.zeros_like(lines)))

    for field in range(fields):
        for x in range(cx):
            row = field * half * group + (x // 2) * group
            at, lane = unit_place(field, x, cx, group, width)
            shift = lane - MARGIN - (x % 2) * cy - starts[x // half] + 2 * LANES
            put(at, lane, pltpu.roll(block_ref[row : row + group], shift % LANES, 1))
    for part in range(2):
        at, lane = unit_place(fields, part, cx, group, width)
        shift = lane - MARGIN - starts[part] + 2 * LANES
        lines = line_ref[16 * part : 16 * part + group]
        put(at, lane, pltpu.roll(lines, shift % LANES, 1))
    for row, lines in blocks.items():
        out_ref[top + row : top + row + group] = lines


def keep_kernel(cx, cy, count_x, small_rows, swap_ref, line_ref, keep_ref, middle_ref):
    sense = 1 - 2 * lax.axis_index("ty")
    put_chunk(cx, cy, count_x, swap_ref, line_ref, middle_ref, 0, count_x // 2)
    for place, distance in enumerate((2, 3)):
        top = place * small_rows
        put_chunk(cx, cy, count_x, swap_ref, line_ref, keep_ref, top, sense * distance)


def mix_kernel(full_rows, small_rows, swap_ref, other_ref, keep_ref, near_ref, second_ref, third_ref):
    near_ref[:full_rows] = swap_ref[:full_rows]
    near_ref[full_rows:] = other_ref[:full_rows]
    for place, far_ref in enumerate((second_ref, third_ref)):
        at = place * small_rows
        far_ref[:small_rows] = keep_ref[at : at + small_rows]
        at += full_rows
        far_ref[small_rows:] = other_ref[at : at + small_rows]


def step_kernel(
    cx, cy, count_x, full_rows, small_rows, own_ref, other_ref, got_ref, got_other_ref,
    table_ref, out_ref, z_ref, cor_ref, pred_ref, store_ref, tile_ref, flip_ref, speed_ref,
):
    fields = z_ref.shape[0]
    levels = 4
    slots = 16
    cells = cx * count_x
    faces = store_ref.shape[0] // 4
    pairs = faces // 2
    group = pairs * levels
    half = cx // 2
    chunk = cx * group
    width = 2 * cx
    index_x = lax.axis_index("tx")
    index_y = lax.axis_index("ty")

    def row_of(x):
        return (x + 4) * group

    def lanes_of(rows):
        return lax.broadcasted_iota(jnp.int32, (rows, LANES), 1)

    south_half = lanes_of(group) % WINDOW < MARGIN + cy
    south_is_own = index_y == 0
    own_half = south_half == south_is_own

    def from_owner(offset):
        source = (index_x - offset + 2 * count_x) % count_x
        return source, pl.multiple_of(source * chunk, 8)

    def put_coriolis(start, x, values, at):
        for pair in range(pairs):
            line = values[at + pair : at + pair + 1]
            rows = pl.ds(start + x * group + pair * levels, levels)
            cor_ref[rows] = jnp.broadcast_to(line, (levels, LANES))

    def put_block(start, lines_of):
        base = fields * half * group
        for field in range(fields):
            for xp in range(half):
                even, odd = lines_of(field * half * group + xp * group, group)
                z_ref[field, pl.ds(start + row_of(2 * xp), group)] = even
                z_ref[field, pl.ds(start + row_of(2 * xp + 1), group)] = odd
        for parity, values in enumerate(lines_of(base, half * pairs)):
            for xp in range(half):
                put_coriolis(start, 2 * xp + parity, values, xp * pairs)

    def put_distant(source, start, lines_of):
        starts_south = windows(source, index_x, count_x, 0, cx, cy)
        starts_north = windows(source, index_x, count_x, 1, cx, cy)

        def lines_at(field, x, part):
            at, lane = unit_place(field, x, cx, group, width)
            south_shift = (MARGIN + starts_south[part] - lane + LANES) % LANES
            north_shift = (MARGIN + cy + starts_north[part] - lane + LANES) % LANES
            return lines_of(at, south_shift, north_shift)

        for field in range(fields):
            for x in range(cx):
                z_ref[field, pl.ds(start + row_of(x), group)] = lines_at(field, x, x // half)
        for part in range(2):
            values = lines_at(fields, part, part)
            for x in range(half):
                put_coriolis(start, part * half + x, values, x * pairs)

    def own_lines(row, rows):
        mine = own_ref[row : row + rows]
        theirs = other_ref[row : row + rows]
        up, down = index_y * cy, (1 - index_y) * cy
        even = jnp.where(own_half[:rows], pltpu.roll(mine, up, 1), pltpu.roll(theirs, down, 1))
        mine = pltpu.roll(mine, (LANES - down) % LANES, 1)
        theirs = pltpu.roll(theirs, (LANES - up) % LANES, 1)
        return even, jnp.where(own_half[:rows], mine, theirs)

    put_block(from_owner(0)[1], own_lines)

    sense = 1 - 2 * index_y
    for block_ref, toward, south_first in (
        (got_ref, sense, index_y),
        (got_other_ref, -sense, 1 - index_y),
    ):
        south_top = pl.multiple_of(south_first * full_rows, 8)
        north_top = pl.multiple_of((1 - south_first) * full_rows, 8)

        def near_lines(row, rows, block_ref=block_ref, south_top=south_top, north_top=north_top):
            south = block_ref[pl.ds(south_top + row, rows)]
            north = block_ref[pl.ds(north_top + row, rows)]
            low = south_half[:rows]
            even = jnp.where(low, south, pltpu.roll(north, cy, 1))
            return even, jnp.where(low, pltpu.roll(south, LANES - cy, 1), north)

        put_block(from_owner(toward)[1], near_lines)
        for place, distance in enumerate((2, 3)):
            top = 2 * full_rows + 2 * place * small_rows
            south_top = pl.multiple_of(top + south_first * small_rows, 8)
            north_top = pl.multiple_of(top + (1 - south_first) * small_rows, 8)

            def far_lines(
                at, south_shift, north_shift,
                block_ref=block_ref, south_top=south_top, north_top=north_top,
            ):
                south = block_ref[pl.ds(south_top + at, group)]
                north = block_ref[pl.ds(north_top + at, group)]
                south = pltpu.roll(south, south_shift, 1)
                return jnp.where(south_half, south, pltpu.roll(north, north_shift, 1))

            put_distant(*from_owner(toward * distance), far_lines)

    def middle_lines(at, south_shift, north_shift):
        row = 2 * full_rows + 4 * small_rows + at
        mine_shift = jnp.where(south_is_own, south_shift, north_shift)
        other_shift = jnp.where(south_is_own, north_shift, south_shift)
        mine = pltpu.roll(got_ref[row : row + group], mine_shift, 1)
        theirs = pltpu.roll(got_other_ref[row : row + group], other_shift, 1)
        return jnp.where(own_half, mine, theirs)

    put_distant(*from_owner(count_x // 2), middle_lines)

    level_of = lax.broadcasted_iota(jnp.int32, speed_ref.shape, 0) % levels
    speeds = jnp.full(speed_ref.shape, table_ref[0], jnp.float32)
    for index in range(1, levels):
        speeds = jnp.where(level_of == index, table_ref[index], speeds)
    speed_ref[...] = speeds

    def collect():
        position = lanes_of(cells) % WINDOW
        gap = WINDOW - cells + 3
        wide = gap + 3 * levels
        for pair in range(pairs):
            merged = jnp.zeros((cells, LANES), jnp.float32)
            for slot, field in ((0, 0), (1, 2)):
                for level in range(levels):
                    lines = z_ref[field, pl.ds(row_of(0) + pair * levels + level, cells, group)]
                    offset = slot * wide + 3 * level
                    here = position - offset
                    wanted = ((here >= 0) & (here < 3)) | ((here >= gap) & (here < gap + 3))
                    shift = (offset - (MARGIN + cells - 3)) % LANES
                    merged = jnp.where(wanted, pltpu.roll(lines, shift, 1), merged)
            merged = jnp.concatenate(
                [merged, jnp.zeros((LANES - cells, LANES), jnp.float32)], axis=0
            )
            flip_ref[pair] = merged.T
            for slot in range(2):
                for side in (2, 3):
                    for odd in range(2):
                        for depth in range(3):
                            base = slot * wide
                            if side == 3:
                                base += odd * WINDOW + 2 - depth
                            else:
                                base += ((odd + 1) % 2) * WINDOW + gap + depth
                            at = slot * slots + depth * levels
                            store_ref[(2 * pair + odd) * 4 + side, at : at + levels] = flip_ref[
                                pair, pl.ds(base, levels, 3)
                            ]
            for slot in range(2):
                for side in (0, 1):
                    for depth in range(3):
                        x = depth if side == 0 else cells - 1 - depth
                        row = row_of(x) + pair * levels
                        lines = z_ref[slot, row : row + levels]
                        at = slot * slots + depth * levels
                        for odd in range(2):
                            store_ref[(2 * pair + odd) * 4 + side, at : at + levels] = pltpu.roll(
                                lines, LANES - MARGIN - odd * WINDOW, 1
                            )

    def fetch(face, side, position):
        at = levels + (face * 4 + side) * 3
        neighbour = table_ref[at].astype(jnp.int32)
        far_side = table_ref[at + 1].astype(jnp.int32)
        flipped = table_ref[at + 2].astype(jnp.int32)
        block = store_ref[neighbour * 4 + far_side]
        order = jnp.where(flipped == 1, cells - 1 - position, position)
        order = jnp.where((position >= 0) & (position < cells), order, 0)
        block = jnp.take_along_axis(block, order, axis=1)
        sign_here = 2 * (side % 2) - 1
        sign_there = 2 * (far_side % 2) - 1
        sign = (-sign_here * sign_there).astype(jnp.float32)
        normal = lax.broadcasted_iota(jnp.int32, block.shape, 0) >= slots
        return jnp.where(normal, sign * block, block)

    def rim_rows(side):
        lane = lanes_of(2 * slots)
        for pair in range(pairs):
            first = fetch(2 * pair, side, lane - MARGIN)
            second = fetch(2 * pair + 1, side, lane - (MARGIN + WINDOW))
            both = jnp.where(lane < WINDOW, first, second)
            for slot in range(2):
                for depth in range(3):
                    x = -1 - depth if side == 0 else cells + depth
                    at = slot * slots + depth * levels
                    row = row_of(x) + pair * levels
                    z_ref[slot, row : row + levels] = both[at : at + levels]

    def tile_rows(odd, side, depth):
        if side == 3:
            return pl.ds(odd * WINDOW + depth, levels, 16)
        return pl.ds(((odd + 1) % 2) * WINDOW + 15 - depth, levels, 16)

    def put_columns(lines, field, start, pair):
        count = lines.shape[0]
        position = lanes_of(count) % WINDOW
        rim = ((position >= MARGIN - 3) & (position < MARGIN)) | (
            (position >= MARGIN + cells) & (position < MARGIN + cells + 3)
        )
        for level in range(levels):
            rolled = pltpu.roll(lines, (MARGIN + cells - 16 * level) % LANES, 1)
            at = pl.ds(row_of(start) + pair * levels + level, count, group)
            z_ref[field, at] = jnp.where(rim, rolled, z_ref[field, at])

    def rim_columns_all():
        for pair in range(pairs):
            for odd in range(2):
                for side in (2, 3):
                    block = fetch(2 * pair + odd, side, lanes_of(2 * slots))
                    for slot in range(2):
                        for depth in range(3):
                            at = slot * slots + depth * levels
                            tile_ref[2 * pair + slot, tile_rows(odd, side, depth)] = block[
                                at : at + levels
                            ]
            for slot, field in ((0, 0), (1, 2)):
                put_columns(tile_ref[2 * pair + slot].T[:cells], field, 0, pair)

    def rim_columns_own():
        lane = lanes_of(2 * slots)
        second = lax.broadcasted_iota(jnp.int32, lane.shape, 0) >= slots
        for odd in range(2):
            for side in (2, 3):
                total = jnp.zeros((slots, LANES), jnp.float32)
                for pair in range(pairs):
                    local = lane - jnp.where(second, 8 * (pairs + pair), 8 * pair)
                    block = fetch(2 * pair + odd, side, index_x * cx + local)
                    block = jnp.where((local >= 0) & (local < 8), block, 0.0)
                    total = total + block[:slots] + block[slots:]
                for depth in range(3):
                    at = depth * levels
                    tile_ref[0, tile_rows(odd, side, depth)] = total[at : at + levels]
        turned = tile_ref[0].T
        for slot, field in ((0, 0), (1, 2)):
            for pair in range(pairs):
                at = 8 * (slot * pairs + pair)
                put_columns(turned[at : at + cx], field, index_x * cx, pair)

    def predict(at, rows):
        speed = speed_ref[:rows]
        ahead = z_ref[0, pl.ds(at + group, rows)]
        behind = z_ref[0, pl.ds(at - group, rows)]
        pred_ref[pl.ds(at, rows)] = z_ref[1, pl.ds(at, rows)] - speed * (0.5 * (ahead - behind))

    def update(at, rows):
        speed = speed_ref[:rows]
        height = z_ref[0, pl.ds(at, rows)]
        north_pred = z_ref[2, pl.ds(at, rows)] - speed * (
            0.5 * (pltpu.roll(height, LANES - 1, 1) - pltpu.roll(height, 1, 1))
        )
        east_pred = pred_ref[pl.ds(at, rows)]
        flux_east = 8.0 * (
            pred_ref[pl.ds(at + group, rows)] - pred_ref[pl.ds(at - group, rows)]
        ) - (pred_ref[pl.ds(at + 2 * group, rows)] - pred_ref[pl.ds(at - 2 * group, rows)])
        flux_north = 8.0 * (
            pltpu.roll(north_pred, LANES - 1, 1) - pltpu.roll(north_pred, 1, 1)
        ) - (pltpu.roll(north_pred, LANES - 2, 1) - pltpu.roll(north_pred, 2, 1))
        height = height - speed * ((flux_east + flux_north) * (1.0 / 12.0))
        turning = cor_ref[pl.ds(at - row_of(0), rows)]
        return height, east_pred + turning * north_pred, north_pred - turning * east_pred

    collect()
    rim_rows(0)
    rim_rows(1)
    rim_columns_all()
    for first in range(-2, cells + 2, 4):
        predict(row_of(first), 4 * group)
    for index in range(count_x):
        at = row_of(0) + index * chunk
        for field, values in enumerate(update(at, chunk)):
            z_ref[field, at : at + chunk] = values

    collect()

    @pl.when(index_x == 0)
    def _():
        rim_rows(0)

    @pl.when(index_x == count_x - 1)
    def _():
        rim_rows(1)

    rim_columns_own()
    at = pl.multiple_of(row_of(0) + index_x * chunk, 8)
    predict(at - 2 * group, chunk + 4 * group)
    for field, values in enumerate(update(at, chunk)):
        for odd in range(2):
            shift = LANES - (MARGIN + odd * WINDOW) - index_y * cy
            rolled = pltpu.roll(values, shift, 1)
            for x in range(cx):
                for pair in range(pairs):
                    row = x * group + pair * levels
                    out_ref[2 * pair + odd, field, x] = rolled[row : row + levels, :cy]


def fast_on_device(state, coriolis, wave_speed, edges):
    count_x = lax.axis_size("tx")
    faces, fields, levels, cx, cy = state.shape
    pairs = faces // 2
    group = pairs * levels
    cells = cx * count_x
    full_rows = fields * (cx // 2) * group + (cx // 2) * pairs
    full_rows = -(-full_rows // 8) * 8
    small_rows = unit_place(fields, 1, cx, group, 2 * cx)[0] + group
    swap, lines = pl.pallas_call(
        functools.partial(pack_kernel, cx, cy, count_x, full_rows, small_rows),
        out_shape=[
            jax.ShapeDtypeStruct((full_rows + 2 * small_rows, LANES), jnp.float32),
            jax.ShapeDtypeStruct((32, LANES), jnp.float32),
        ],
        in_specs=[pl.BlockSpec(memory_space=pltpu.HBM)] * 2,
        out_specs=[pl.BlockSpec(memory_space=pltpu.VMEM)] * 2,
        scratch_shapes=[
            pltpu.VMEM((faces, fields, cx, levels, cy), jnp.float32),
            pltpu.VMEM((faces, cx, cy), jnp.float32),
            pltpu.SemaphoreType.DMA((2,)),
        ],
        compiler_params=pltpu.CompilerParams(vmem_limit_bytes=VMEM_LIMIT),
        name="pack",
    )(jnp.swapaxes(state, 2, 3), coriolis)
    keep, middle = pl.pallas_call(
        functools.partial(keep_kernel, cx, cy, count_x, small_rows),
        out_shape=[
            jax.ShapeDtypeStruct((2 * small_rows, LANES), jnp.float32),
            jax.ShapeDtypeStruct((small_rows, LANES), jnp.float32),
        ],
        in_specs=[pl.BlockSpec(memory_space=pltpu.VMEM)] * 2,
        out_specs=[pl.BlockSpec(memory_space=pltpu.VMEM)] * 2,
        compiler_params=pltpu.CompilerParams(vmem_limit_bytes=SMALL_VMEM_LIMIT),
        name="keep",
    )(swap, lines)

    def moved(block, distance):
        pairs_of = []
        for index in range(count_x):
            for core in range(2):
                target = (index + distance * (1 - 2 * core)) % count_x
                pairs_of.append((2 * index + core, 2 * target + core))
        return lax.ppermute(block, ("tx", "ty"), pairs_of)

    def across(block):
        return lax.ppermute(block, "ty", [(0, 1), (1, 0)])

    other = across(swap)
    messages = pl.pallas_call(
        functools.partial(mix_kernel, full_rows, small_rows),
        out_shape=[
            jax.ShapeDtypeStruct((2 * rows, LANES), jnp.float32)
            for rows in (full_rows, small_rows, small_rows)
        ],
        in_specs=[pl.BlockSpec(memory_space=pltpu.VMEM)] * 3,
        out_specs=[pl.BlockSpec(memory_space=pltpu.VMEM)] * 3,
        compiler_params=pltpu.CompilerParams(vmem_limit_bytes=SMALL_VMEM_LIMIT),
        name="messages",
    )(swap, other, keep)
    got = [moved(block, place + 1) for place, block in enumerate(messages)]
    got = jnp.concatenate([*got, moved(middle, count_x // 2)])
    table = jnp.concatenate([wave_speed, edges.reshape(-1).astype(jnp.float32)])
    got, table = lax.optimization_barrier((got, table))
    pieces = (swap, other, got, across(got))
    z_rows = (cells + 8) * group
    out = pl.pallas_call(
        functools.partial(
            step_kernel, cx, cy, count_x, full_rows, small_rows
        ),
        out_shape=jax.ShapeDtypeStruct((faces, fields, cx, levels, cy), jnp.float32),
        in_specs=[pl.BlockSpec(memory_space=pltpu.VMEM)] * 4
        + [pl.BlockSpec(memory_space=pltpu.SMEM)],
        out_specs=pl.BlockSpec(memory_space=pltpu.VMEM),
        scratch_shapes=[
            pltpu.VMEM((fields, z_rows, LANES), jnp.float32),
            pltpu.VMEM((cells * group, LANES), jnp.float32),
            pltpu.VMEM((z_rows, LANES), jnp.float32),
            pltpu.VMEM((faces * 4, 32, LANES), jnp.float32),
            pltpu.VMEM((faces, LANES, LANES), jnp.float32),
            pltpu.VMEM((pairs, LANES, LANES), jnp.float32),
            pltpu.VMEM(((cx + 4) * group, LANES), jnp.float32),
        ],
        compiler_params=pltpu.CompilerParams(vmem_limit_bytes=VMEM_LIMIT),
        name="substeps",
    )(*pieces, table)
    return jnp.swapaxes(out, 2, 3)


def padded_2(block, sides, width):
    for axis, dim in sides:
        count = lax.axis_size(axis)
        forward = [(i, i + 1) for i in range(count - 1)]
        backward = [(target, source) for source, target in forward]
        low = lax.ppermute(
            lax.slice_in_dim(block, block.shape[dim] - width, None, axis=dim), axis, forward
        )
        high = lax.ppermute(lax.slice_in_dim(block, 0, width, axis=dim), axis, backward)
        block = jnp.concatenate([low, block, high], axis=dim)
    return block


def spread(block, axis, owner):
    block = jnp.where(lax.axis_index(axis) == owner, block, jnp.zeros_like(block))
    return lax.psum(block, axis)


def rotate_strip(strip_data, side_index, far_side, flipped):
    normal_part = jnp.where(far_side < 2, strip_data[1], strip_data[2])
    along_part = jnp.where(far_side < 2, strip_data[2], strip_data[1])
    sign_here = 2.0 * (side_index % 2) - 1.0
    sign_there = (2 * (far_side % 2) - 1).astype(jnp.float32)
    normal_part = -sign_here * sign_there * normal_part
    along_part = (1 - 2 * flipped).astype(jnp.float32) * along_part
    if side_index < 2:
        return jnp.stack([strip_data[0], normal_part, along_part])
    return jnp.stack([strip_data[0], along_part, normal_part])


def window_strip(store, side_pick, neighbour, flipped, start, width):
    full_length = store.shape[5]
    begin = jnp.where(flipped == 1, full_length - start - width, start)
    zero = jnp.zeros((), jnp.int32)
    sizes_here = (1, 1, store.shape[2], store.shape[3], store.shape[4], width)
    piece = lax.dynamic_slice(store, (side_pick, neighbour, zero, zero, zero, begin), sizes_here)[
        0, 0
    ]
    return jnp.where(flipped == 1, jnp.flip(piece, 3), piece)


def side_halo(edge_store, edges, face_index, side_index, start, width):
    neighbour = edges[face_index, side_index, 0]
    far_side = edges[face_index, side_index, 1]
    flipped = edges[face_index, side_index, 2]
    strip_data = window_strip(edge_store, far_side, neighbour, flipped, start, width)
    return rotate_strip(strip_data, side_index, far_side, flipped)


def advance(padded, wave_speed, coriolis_part, cells_x, cells_y):
    height = padded[..., 0, :, :, :]
    wind_east = padded[..., 1, :, :, :]
    wind_north = padded[..., 2, :, :, :]
    speed = wave_speed[:, None, None]
    east_pred = wind_east[..., 1 : cells_x + 5, 3 : cells_y + 3] - speed * (
        0.5
        * (
            height[..., 2 : cells_x + 6, 3 : cells_y + 3]
            - height[..., 0 : cells_x + 4, 3 : cells_y + 3]
        )
    )
    north_pred = wind_north[..., 3 : cells_x + 3, 1 : cells_y + 5] - speed * (
        0.5
        * (
            height[..., 3 : cells_x + 3, 2 : cells_y + 6]
            - height[..., 3 : cells_x + 3, 0 : cells_y + 4]
        )
    )
    flux_east = (
        8.0 * (east_pred[..., 3 : cells_x + 3, :] - east_pred[..., 1 : cells_x + 1, :])
        - (east_pred[..., 4 : cells_x + 4, :] - east_pred[..., 0:cells_x, :])
    ) / 12.0
    flux_north = (
        8.0 * (north_pred[..., 3 : cells_y + 3] - north_pred[..., 1 : cells_y + 1])
        - (north_pred[..., 4 : cells_y + 4] - north_pred[..., 0:cells_y])
    ) / 12.0
    height_new = height[..., 3 : cells_x + 3, 3 : cells_y + 3] - speed * (flux_east + flux_north)
    east_inner = east_pred[..., 2 : cells_x + 2, :]
    north_inner = north_pred[..., 2 : cells_y + 2]
    turning = coriolis_part[..., None, :, :]
    return jnp.stack(
        [height_new, east_inner + turning * north_inner, north_inner - turning * east_inner],
        axis=-4,
    )


def one_substep(state, coriolis, wave_speed, edges, count_x, count_y, index_x, index_y):
    faces = state.shape[0]
    cells_x = state.shape[3]
    cells_y = state.shape[4]
    padded = padded_2(state, (("tx", 3), ("ty", 4)), 3)
    west_rim = state[:, :, :, 0:3, :]
    east_rim = jnp.flip(state[:, :, :, cells_x - 3 :, :], 3)
    south_rim = jnp.swapaxes(state[:, :, :, :, 0:3], 3, 4)
    north_rim = jnp.swapaxes(jnp.flip(state[:, :, :, :, cells_y - 3 :], 4), 3, 4)
    west_part = spread(west_rim, "tx", 0)
    east_part = spread(east_rim, "tx", count_x - 1)
    west_full, east_full = (
        lax.all_gather(west_part, "ty", axis=4, tiled=True),
        lax.all_gather(east_part, "ty", axis=4, tiled=True),
    )
    south_row, north_row = (
        lax.all_gather(south_rim, "tx", axis=4, tiled=True),
        lax.all_gather(north_rim, "tx", axis=4, tiled=True),
    )
    south_all, north_all = (
        lax.all_gather(south_row, "ty", axis=0, tiled=True),
        lax.all_gather(north_row, "ty", axis=0, tiled=True),
    )
    south_full = south_all[0:faces]
    north_full = north_all[(count_y - 1) * faces : count_y * faces]
    edge_store = jnp.stack([west_full, east_full, south_full, north_full])
    halos = []
    for side_index in range(4):
        if side_index < 2:
            slabs = jnp.stack(
                [
                    side_halo(edge_store, edges, face_index, side_index, index_y * cells_y, cells_y)
                    for face_index in range(faces)
                ]
            )
        else:
            slabs = jnp.stack(
                [
                    side_halo(edge_store, edges, face_index, side_index, index_x * cells_x, cells_x)
                    for face_index in range(faces)
                ]
            )
        halos.append(slabs)
    west_region = padded[:, :, :, 0:3, 3 : cells_y + 3]
    padded = padded.at[:, :, :, 0:3, 3 : cells_y + 3].set(
        jnp.where(index_x == 0, jnp.flip(halos[0], 3), west_region)
    )
    east_region = padded[:, :, :, cells_x + 3 : cells_x + 6, 3 : cells_y + 3]
    padded = padded.at[:, :, :, cells_x + 3 : cells_x + 6, 3 : cells_y + 3].set(
        jnp.where(index_x == count_x - 1, halos[1], east_region)
    )
    south_region = padded[:, :, :, 3 : cells_x + 3, 0:3]
    padded = padded.at[:, :, :, 3 : cells_x + 3, 0:3].set(
        jnp.where(index_y == 0, jnp.swapaxes(jnp.flip(halos[2], 3), 3, 4), south_region)
    )
    north_region = padded[:, :, :, 3 : cells_x + 3, cells_y + 3 : cells_y + 6]
    padded = padded.at[:, :, :, 3 : cells_x + 3, cells_y + 3 : cells_y + 6].set(
        jnp.where(index_y == count_y - 1, jnp.swapaxes(halos[3], 3, 4), north_region)
    )
    return advance(padded, wave_speed, coriolis, cells_x, cells_y)


def on_device(state, coriolis, wave_speed, edges):
    count_x = lax.axis_size("tx")
    count_y = lax.axis_size("ty")
    index_x = lax.axis_index("tx")
    index_y = lax.axis_index("ty")
    for substep_index in range(SUBSTEPS):
        state = one_substep(state, coriolis, wave_speed, edges, count_x, count_y, index_x, index_y)
    return state


def fits(state):
    count_x = lax.axis_size("tx")
    faces, fields, levels, cells_x, cells_y = state.shape
    return (
        lax.axis_size("ty") == 2
        and faces % 2 == 0
        and levels == 4
        and cells_x == 6
        and cells_y == 24
        and count_x == 8
        and cells_x * count_x == 2 * cells_y
        and 2 * cells_y + 2 * MARGIN <= WINDOW
    )


def either(state, coriolis, wave_speed, edges):
    if fits(state):
        return fast_on_device(state, coriolis, wave_speed, edges)
    return on_device(state, coriolis, wave_speed, edges)


def solution(mesh):
    in_specs = (P("member", None, None, "tx", "ty"), P(None, "tx", "ty"), P(), P())
    out_specs = P("member", None, None, "tx", "ty")
    return jax.shard_map(
        either, mesh=mesh, in_specs=in_specs, out_specs=out_specs, check_vma=False
    )
```

```python
import functools

import jax
import jax.numpy as jnp
from jax import lax
from jax.experimental import pallas as pl
from jax.experimental.pallas import tpu as pltpu
from jax.sharding import PartitionSpec as P

SUBSTEPS = 2
LANES = 128
WINDOW = 64
MARGIN = 8
VMEM_LIMIT = 32 * 1024 * 1024
SMALL_VMEM_LIMIT = 8 * 1024 * 1024


def window_start(source, target, count_x, index_y, cx, cy, far):
    width = 2 * cx
    near = jnp.minimum(target, count_x - 1 - target)
    inward = jnp.minimum(cx * near - jnp.where(far, cx, cx // 2), cy - width)
    rim = (source == 0) | (source == count_x - 1)
    start = jnp.where(rim, jnp.maximum(inward, 0), 0)
    return jnp.where(index_y == 0, start, cy - width - start)


def windows(source, target, count_x, index_y, cx, cy):
    low_far = source == count_x - 1
    lower = window_start(source, target, count_x, index_y, cx, cy, low_far)
    upper = window_start(source, target, count_x, index_y, cx, cy, ~low_far)
    return lower, upper


def unit_place(field, x, cx, group, width):
    per_row = 60 // width
    index = field * cx + x
    return (index // per_row) * group, (index % per_row) * width


def pack_kernel(
    cx, cy, count_x, full_rows, small_rows, state_hbm, coriolis_hbm,
    swap_ref, line_ref, state_ref, coriolis_ref, sems,
):
    copies = [
        pltpu.make_async_copy(state_hbm, state_ref, sems.at[0]),
        pltpu.make_async_copy(coriolis_hbm, coriolis_ref, sems.at[1]),
    ]
    for copy in copies:
        copy.start()
    faces, fields = state_ref.shape[:2]
    levels = state_ref.shape[3]
    pairs = faces // 2
    group = pairs * levels
    half = cx // 2
    base = fields * half * group
    swap_ref[:full_rows] = jnp.zeros((full_rows, LANES), jnp.float32)
    line_ref[...] = jnp.zeros(line_ref.shape, jnp.float32)
    for copy in copies:
        copy.wait()
    for face in range(faces):
        for parity in range(2):
            lane = (face % 2) * WINDOW + MARGIN + parity * cy
            for xp in range(half):
                for field in range(fields):
                    row = field * half * group + xp * group + (face // 2) * levels
                    swap_ref[row : row + levels, lane : lane + cy] = state_ref[
                        face, field, 2 * xp + parity
                    ]
                x = 2 * xp + parity
                row = base + xp * pairs + face // 2
                swap_ref[row : row + 1, lane : lane + cy] = coriolis_ref[face, x : x + 1]
                row = (x // half) * 16 + (x % half) * pairs + face // 2
                lane_at = (face % 2) * WINDOW + MARGIN
                line_ref[row : row + 1, lane_at : lane_at + cy] = coriolis_ref[face, x : x + 1]
    sense = 1 - 2 * lax.axis_index("ty")
    for place, distance in enumerate((2, 3)):
        top = full_rows + place * small_rows
        put_chunk(cx, cy, count_x, swap_ref, line_ref, swap_ref, top, -sense * distance)


def put_chunk(cx, cy, count_x, block_ref, line_ref, out_ref, top, offset):
    pairs = 3
    group = 4 * pairs
    fields = 3
    half = cx // 2
    width = 2 * cx
    index_x = lax.axis_index("tx")
    index_y = lax.axis_index("ty")
    target = (index_x + offset + count_x) % count_x
    starts = windows(index_x, target, count_x, index_y, cx, cy)
    blocks = {}

    def put(row, lane, lines):
        position = lax.broadcasted_iota(jnp.int32, lines.shape, 1) % WINDOW
        here = (position >= lane) & (position < lane + width)
        blocks[row] = jnp.where(here, lines, blocks.get(row, jnp.zeros_like(lines)))

    for field in range(fields):
        for x in range(cx):
            row = field * half * group + (x // 2) * group
            at, lane = unit_place(field, x, cx, group, width)
            shift = lane - MARGIN - (x % 2) * cy - starts[x // half] + 2 * LANES
            put(at, lane, pltpu.roll(block_ref[row : row + group], shift % LANES, 1))
    for part in range(2):
        at, lane = unit_place(fields, part, cx, group, width)
        shift = lane - MARGIN - starts[part] + 2 * LANES
        lines = line_ref[16 * part : 16 * part + group]
        put(at, lane, pltpu.roll(lines, shift % LANES, 1))
    for row, lines in blocks.items():
        out_ref[top + row : top + row + group] = lines


def keep_kernel(cx, cy, count_x, small_rows, swap_ref, line_ref, keep_ref, middle_ref):
    sense = 1 - 2 * lax.axis_index("ty")
    put_chunk(cx, cy, count_x, swap_ref, line_ref, middle_ref, 0, count_x // 2)
    for place, distance in enumerate((2, 3)):
        top = place * small_rows
        put_chunk(cx, cy, count_x, swap_ref, line_ref, keep_ref, top, sense * distance)


def mix_kernel(full_rows, small_rows, swap_ref, other_ref, keep_ref, near_ref, second_ref, third_ref):
    near_ref[:full_rows] = swap_ref[:full_rows]
    near_ref[full_rows:] = other_ref[:full_rows]
    for place, far_ref in enumerate((second_ref, third_ref)):
        at = place * small_rows
        far_ref[:small_rows] = keep_ref[at : at + small_rows]
        at += full_rows
        far_ref[small_rows:] = other_ref[at : at + small_rows]


def placer(cx, cy, count_x, full_rows, small_rows, z_ref, cor_ref):
    fields = z_ref.shape[0]
    levels = 4
    group = z_ref.shape[1] // (cx * count_x + 8)
    pairs = group // levels
    half = cx // 2
    chunk = cx * group
    index_x = lax.axis_index("tx")
    index_y = lax.axis_index("ty")
    south_half = lax.broadcasted_iota(jnp.int32, (group, LANES), 1) % WINDOW < MARGIN + cy
    south_is_own = index_y == 0
    own_half = south_half == south_is_own

    def row_of(x):
        return (x + 4) * group

    def from_owner(offset):
        source = (index_x - offset + 2 * count_x) % count_x
        return source, pl.multiple_of(source * chunk, 8)

    def put_coriolis(start, x, values, at):
        for pair in range(pairs):
            line = values[at + pair : at + pair + 1]
            rows = pl.ds(start + x * group + pair * levels, levels)
            cor_ref[rows] = jnp.broadcast_to(line, (levels, LANES))

    def put_block(start, lines_of):
        base = fields * half * group
        for field in range(fields):
            for xp in range(half):
                even, odd = lines_of(field * half * group + xp * group, group)
                z_ref[field, pl.ds(start + row_of(2 * xp), group)] = even
                z_ref[field, pl.ds(start + row_of(2 * xp + 1), group)] = odd
        for parity, values in enumerate(lines_of(base, half * pairs)):
            for xp in range(half):
                put_coriolis(start, 2 * xp + parity, values, xp * pairs)

    def put_distant(source, start, lines_of):
        starts_south = windows(source, index_x, count_x, 0, cx, cy)
        starts_north = windows(source, index_x, count_x, 1, cx, cy)

        def lines_at(field, x, part):
            at, lane = unit_place(field, x, cx, group, 2 * cx)
            south_shift = (MARGIN + starts_south[part] - lane + LANES) % LANES
            north_shift = (MARGIN + cy + starts_north[part] - lane + LANES) % LANES
            return lines_of(at, south_shift, north_shift)

        for field in range(fields):
            for x in range(cx):
                z_ref[field, pl.ds(start + row_of(x), group)] = lines_at(field, x, x // half)
        for part in range(2):
            values = lines_at(fields, part, part)
            for x in range(half):
                put_coriolis(start, part * half + x, values, x * pairs)

    def place_own(own_ref, other_ref):
        def own_lines(row, rows):
            mine = own_ref[row : row + rows]
            theirs = other_ref[row : row + rows]
            up, down = index_y * cy, (1 - index_y) * cy
            keep = own_half[:rows]
            even = jnp.where(keep, pltpu.roll(mine, up, 1), pltpu.roll(theirs, down, 1))
            mine = pltpu.roll(mine, (LANES - down) % LANES, 1)
            theirs = pltpu.roll(theirs, (LANES - up) % LANES, 1)
            return even, jnp.where(keep, mine, theirs)

        put_block(from_owner(0)[1], own_lines)

    def place_got(block_ref, toward, south_first):
        south_top = pl.multiple_of(south_first * full_rows, 8)
        north_top = pl.multiple_of((1 - south_first) * full_rows, 8)

        def near_lines(row, rows):
            south = block_ref[pl.ds(south_top + row, rows)]
            north = block_ref[pl.ds(north_top + row, rows)]
            low = south_half[:rows]
            even = jnp.where(low, south, pltpu.roll(north, cy, 1))
            return even, jnp.where(low, pltpu.roll(south, LANES - cy, 1), north)

        put_block(from_owner(toward)[1], near_lines)
        for place, distance in enumerate((2, 3)):
            top = 2 * full_rows + 2 * place * small_rows
            south_at = pl.multiple_of(top + south_first * small_rows, 8)
            north_at = pl.multiple_of(top + (1 - south_first) * small_rows, 8)

            def far_lines(at, south_shift, north_shift, south_at=south_at, north_at=north_at):
                south = pltpu.roll(block_ref[pl.ds(south_at + at, group)], south_shift, 1)
                north = pltpu.roll(block_ref[pl.ds(north_at + at, group)], north_shift, 1)
                return jnp.where(south_half, south, north)

            put_distant(*from_owner(toward * distance), far_lines)

    def place_middle(got_ref, got_other_ref):
        def middle_lines(at, south_shift, north_shift):
            row = 2 * full_rows + 4 * small_rows + at
            mine_shift = jnp.where(south_is_own, south_shift, north_shift)
            other_shift = jnp.where(south_is_own, north_shift, south_shift)
            mine = pltpu.roll(got_ref[row : row + group], mine_shift, 1)
            theirs = pltpu.roll(got_other_ref[row : row + group], other_shift, 1)
            return jnp.where(own_half, mine, theirs)

        put_distant(*from_owner(count_x // 2), middle_lines)

    return place_own, place_got, place_middle


def own_kernel(sizes, own_ref, other_ref, z_ref, cor_ref):
    placer(*sizes, z_ref, cor_ref)[0](own_ref, other_ref)


def got_kernel(sizes, got_ref, z_in, cor_in, z_ref, cor_ref):
    index_y = lax.axis_index("ty")
    placer(*sizes, z_ref, cor_ref)[1](got_ref, 1 - 2 * index_y, index_y)


def step_kernel(
    sizes, got_ref, got_other_ref, table_ref, z_in, cor_in, out_ref, z_ref, cor_ref,
    pred_ref, store_ref, tile_ref, flip_ref, speed_ref,
):
    cx, cy, count_x = sizes[:3]
    levels = 4
    slots = 16
    cells = cx * count_x
    faces = store_ref.shape[0] // 4
    pairs = faces // 2
    group = pairs * levels
    chunk = cx * group
    index_x = lax.axis_index("tx")
    index_y = lax.axis_index("ty")

    def row_of(x):
        return (x + 4) * group

    def lanes_of(rows):
        return lax.broadcasted_iota(jnp.int32, (rows, LANES), 1)

    _, place_got, place_middle = placer(*sizes, z_ref, cor_ref)
    place_got(got_other_ref, 2 * index_y - 1, 1 - index_y)
    place_middle(got_ref, got_other_ref)

    level_of = lax.broadcasted_iota(jnp.int32, speed_ref.shape, 0) % levels
    speeds = jnp.full(speed_ref.shape, table_ref[0], jnp.float32)
    for index in range(1, levels):
        speeds = jnp.where(level_of == index, table_ref[index], speeds)
    speed_ref[...] = speeds

    def collect():
        position = lanes_of(cells) % WINDOW
        gap = WINDOW - cells + 3
        wide = gap + 3 * levels
        for pair in range(pairs):
            merged = jnp.zeros((cells, LANES), jnp.float32)
            for slot, field in ((0, 0), (1, 2)):
                for level in range(levels):
                    lines = z_ref[field, pl.ds(row_of(0) + pair * levels + level, cells, group)]
                    offset = slot * wide + 3 * level
                    here = position - offset
                    wanted = ((here >= 0) & (here < 3)) | ((here >= gap) & (here < gap + 3))
                    shift = (offset - (MARGIN + cells - 3)) % LANES
                    merged = jnp.where(wanted, pltpu.roll(lines, shift, 1), merged)
            merged = jnp.concatenate(
                [merged, jnp.zeros((LANES - cells, LANES), jnp.float32)], axis=0
            )
            flip_ref[pair] = merged.T
            for slot in range(2):
                for side in (2, 3):
                    for odd in range(2):
                        for depth in range(3):
                            base = slot * wide
                            if side == 3:
                                base += odd * WINDOW + 2 - depth
                            else:
                                base += ((odd + 1) % 2) * WINDOW + gap + depth
                            at = slot * slots + depth * levels
                            store_ref[(2 * pair + odd) * 4 + side, at : at + levels] = flip_ref[
                                pair, pl.ds(base, levels, 3)
                            ]
            for slot in range(2):
                for side in (0, 1):
                    for depth in range(3):
                        x = depth if side == 0 else cells - 1 - depth
                        row = row_of(x) + pair * levels
                        lines = z_ref[slot, row : row + levels]
                        at = slot * slots + depth * levels
                        for odd in range(2):
                            store_ref[(2 * pair + odd) * 4 + side, at : at + levels] = pltpu.roll(
                                lines, LANES - MARGIN - odd * WINDOW, 1
                            )

    def fetch(face, side, position):
        at = levels + (face * 4 + side) * 3
        neighbour = table_ref[at].astype(jnp.int32)
        far_side = table_ref[at + 1].astype(jnp.int32)
        flipped = table_ref[at + 2].astype(jnp.int32)
        block = store_ref[neighbour * 4 + far_side]
        order = jnp.where(flipped == 1, cells - 1 - position, position)
        order = jnp.where((position >= 0) & (position < cells), order, 0)
        block = jnp.take_along_axis(block, order, axis=1)
        sign_here = 2 * (side % 2) - 1
        sign_there = 2 * (far_side % 2) - 1
        sign = (-sign_here * sign_there).astype(jnp.float32)
        normal = lax.broadcasted_iota(jnp.int32, block.shape, 0) >= slots
        return jnp.where(normal, sign * block, block)

    def rim_rows(side):
        lane = lanes_of(2 * slots)
        for pair in range(pairs):
            first = fetch(2 * pair, side, lane - MARGIN)
            second = fetch(2 * pair + 1, side, lane - (MARGIN + WINDOW))
            both = jnp.where(lane < WINDOW, first, second)
            for slot in range(2):
                for depth in range(3):
                    x = -1 - depth if side == 0 else cells + depth
                    at = slot * slots + depth * levels
                    row = row_of(x) + pair * levels
                    z_ref[slot, row : row + levels] = both[at : at + levels]

    def tile_rows(odd, side, depth):
        if side == 3:
            return pl.ds(odd * WINDOW + depth, levels, 16)
        return pl.ds(((odd + 1) % 2) * WINDOW + 15 - depth, levels, 16)

    def put_columns(lines, field, start, pair):
        count = lines.shape[0]
        position = lanes_of(count) % WINDOW
        rim = ((position >= MARGIN - 3) & (position < MARGIN)) | (
            (position >= MARGIN + cells) & (position < MARGIN + cells + 3)
        )
        for level in range(levels):
            rolled = pltpu.roll(lines, (MARGIN + cells - 16 * level) % LANES, 1)
            at = pl.ds(row_of(start) + pair * levels + level, count, group)
            z_ref[field, at] = jnp.where(rim, rolled, z_ref[field, at])

    def rim_columns_all():
        for pair in range(pairs):
            for odd in range(2):
                for side in (2, 3):
                    block = fetch(2 * pair + odd, side, lanes_of(2 * slots))
                    for slot in range(2):
                        for depth in range(3):
                            at = slot * slots + depth * levels
                            tile_ref[2 * pair + slot, tile_rows(odd, side, depth)] = block[
                                at : at + levels
                            ]
            for slot, field in ((0, 0), (1, 2)):
                put_columns(tile_ref[2 * pair + slot].T[:cells], field, 0, pair)

    def rim_columns_own():
        lane = lanes_of(2 * slots)
        second = lax.broadcasted_iota(jnp.int32, lane.shape, 0) >= slots
        for odd in range(2):
            for side in (2, 3):
                total = jnp.zeros((slots, LANES), jnp.float32)
                for pair in range(pairs):
                    local = lane - jnp.where(second, 8 * (pairs + pair), 8 * pair)
                    block = fetch(2 * pair + odd, side, index_x * cx + local)
                    block = jnp.where((local >= 0) & (local < 8), block, 0.0)
                    total = total + block[:slots] + block[slots:]
                for depth in range(3):
                    at = depth * levels
                    tile_ref[0, tile_rows(odd, side, depth)] = total[at : at + levels]
        turned = tile_ref[0].T
        for slot, field in ((0, 0), (1, 2)):
            for pair in range(pairs):
                at = 8 * (slot * pairs + pair)
                put_columns(turned[at : at + cx], field, index_x * cx, pair)

    def predict(at, rows):
        speed = speed_ref[:rows]
        ahead = z_ref[0, pl.ds(at + group, rows)]
        behind = z_ref[0, pl.ds(at - group, rows)]
        pred_ref[pl.ds(at, rows)] = z_ref[1, pl.ds(at, rows)] - speed * (0.5 * (ahead - behind))

    def update(at, rows):
        speed = speed_ref[:rows]
        height = z_ref[0, pl.ds(at, rows)]
        north_pred = z_ref[2, pl.ds(at, rows)] - speed * (
            0.5 * (pltpu.roll(height, LANES - 1, 1) - pltpu.roll(height, 1, 1))
        )
        east_pred = pred_ref[pl.ds(at, rows)]
        flux_east = 8.0 * (
            pred_ref[pl.ds(at + group, rows)] - pred_ref[pl.ds(at - group, rows)]
        ) - (pred_ref[pl.ds(at + 2 * group, rows)] - pred_ref[pl.ds(at - 2 * group, rows)])
        flux_north = 8.0 * (
            pltpu.roll(north_pred, LANES - 1, 1) - pltpu.roll(north_pred, 1, 1)
        ) - (pltpu.roll(north_pred, LANES - 2, 1) - pltpu.roll(north_pred, 2, 1))
        height = height - speed * ((flux_east + flux_north) * (1.0 / 12.0))
        turning = cor_ref[pl.ds(at - row_of(0), rows)]
        return height, east_pred + turning * north_pred, north_pred - turning * east_pred

    collect()
    rim_rows(0)
    rim_rows(1)
    rim_columns_all()
    for first in range(-2, cells + 2, 4):
        predict(row_of(first), 4 * group)
    for index in range(count_x):
        at = row_of(0) + index * chunk
        for field, values in enumerate(update(at, chunk)):
            z_ref[field, at : at + chunk] = values

    collect()

    @pl.when(index_x == 0)
    def _():
        rim_rows(0)

    @pl.when(index_x == count_x - 1)
    def _():
        rim_rows(1)

    rim_columns_own()
    at = pl.multiple_of(row_of(0) + index_x * chunk, 8)
    predict(at - 2 * group, chunk + 4 * group)
    for field, values in enumerate(update(at, chunk)):
        for odd in range(2):
            shift = LANES - (MARGIN + odd * WINDOW) - index_y * cy
            rolled = pltpu.roll(values, shift, 1)
            for x in range(cx):
                for pair in range(pairs):
                    row = x * group + pair * levels
                    out_ref[2 * pair + odd, field, x] = rolled[row : row + levels, :cy]


def fast_on_device(state, coriolis, wave_speed, edges):
    count_x = lax.axis_size("tx")
    faces, fields, levels, cx, cy = state.shape
    pairs = faces // 2
    group = pairs * levels
    cells = cx * count_x
    full_rows = fields * (cx // 2) * group + (cx // 2) * pairs
    full_rows = -(-full_rows // 8) * 8
    small_rows = unit_place(fields, 1, cx, group, 2 * cx)[0] + group
    swap, lines = pl.pallas_call(
        functools.partial(pack_kernel, cx, cy, count_x, full_rows, small_rows),
        out_shape=[
            jax.ShapeDtypeStruct((full_rows + 2 * small_rows, LANES), jnp.float32),
            jax.ShapeDtypeStruct((32, LANES), jnp.float32),
        ],
        in_specs=[pl.BlockSpec(memory_space=pltpu.HBM)] * 2,
        out_specs=[pl.BlockSpec(memory_space=pltpu.VMEM)] * 2,
        scratch_shapes=[
            pltpu.VMEM((faces, fields, cx, levels, cy), jnp.float32),
            pltpu.VMEM((faces, cx, cy), jnp.float32),
            pltpu.SemaphoreType.DMA((2,)),
        ],
        compiler_params=pltpu.CompilerParams(vmem_limit_bytes=VMEM_LIMIT),
        name="pack",
    )(jnp.swapaxes(state, 2, 3), coriolis)
    keep, middle = pl.pallas_call(
        functools.partial(keep_kernel, cx, cy, count_x, small_rows),
        out_shape=[
            jax.ShapeDtypeStruct((2 * small_rows, LANES), jnp.float32),
            jax.ShapeDtypeStruct((small_rows, LANES), jnp.float32),
        ],
        in_specs=[pl.BlockSpec(memory_space=pltpu.VMEM)] * 2,
        out_specs=[pl.BlockSpec(memory_space=pltpu.VMEM)] * 2,
        compiler_params=pltpu.CompilerParams(vmem_limit_bytes=SMALL_VMEM_LIMIT),
        name="keep",
    )(swap, lines)

    def moved(block, distance):
        pairs_of = []
        for index in range(count_x):
            for core in range(2):
                target = (index + distance * (1 - 2 * core)) % count_x
                pairs_of.append((2 * index + core, 2 * target + core))
        return lax.ppermute(block, ("tx", "ty"), pairs_of)

    def across(block):
        return lax.ppermute(block, "ty", [(0, 1), (1, 0)])

    other = across(swap)
    messages = pl.pallas_call(
        functools.partial(mix_kernel, full_rows, small_rows),
        out_shape=[
            jax.ShapeDtypeStruct((2 * rows, LANES), jnp.float32)
            for rows in (full_rows, small_rows, small_rows)
        ],
        in_specs=[pl.BlockSpec(memory_space=pltpu.VMEM)] * 3,
        out_specs=[pl.BlockSpec(memory_space=pltpu.VMEM)] * 3,
        compiler_params=pltpu.CompilerParams(vmem_limit_bytes=SMALL_VMEM_LIMIT),
        name="messages",
    )(swap, other, keep)
    got = [moved(block, place + 1) for place, block in enumerate(messages)]
    got = jnp.concatenate([*got, moved(middle, count_x // 2)])
    table = jnp.concatenate([wave_speed, edges.reshape(-1).astype(jnp.float32)])
    got, table = lax.optimization_barrier((got, table))
    passed = across(got)

    sizes = (cx, cy, count_x, full_rows, small_rows)
    state_rows = [
        jax.ShapeDtypeStruct((fields, (cells + 8) * group, LANES), jnp.float32),
        jax.ShapeDtypeStruct((cells * group, LANES), jnp.float32),
    ]
    in_vmem = pl.BlockSpec(memory_space=pltpu.VMEM)
    params = pltpu.CompilerParams(vmem_limit_bytes=SMALL_VMEM_LIMIT)
    rows = pl.pallas_call(
        functools.partial(own_kernel, sizes),
        out_shape=state_rows,
        in_specs=[in_vmem] * 2,
        out_specs=[in_vmem] * 2,
        compiler_params=params,
        name="place_own",
    )(swap, other)
    rows = pl.pallas_call(
        functools.partial(got_kernel, sizes),
        out_shape=state_rows,
        in_specs=[in_vmem] * 3,
        out_specs=[in_vmem] * 2,
        input_output_aliases={1: 0, 2: 1},
        compiler_params=params,
        name="place_got",
    )(got, *rows)
    out, _, _ = pl.pallas_call(
        functools.partial(step_kernel, sizes),
        out_shape=[jax.ShapeDtypeStruct((faces, fields, cx, levels, cy), jnp.float32)]
        + state_rows,
        in_specs=[in_vmem] * 2 + [pl.BlockSpec(memory_space=pltpu.SMEM)] + [in_vmem] * 2,
        out_specs=[in_vmem] * 3,
        input_output_aliases={3: 1, 4: 2},
        scratch_shapes=[
            pltpu.VMEM(((cells + 8) * group, LANES), jnp.float32),
            pltpu.VMEM((faces * 4, 32, LANES), jnp.float32),
            pltpu.VMEM((faces, LANES, LANES), jnp.float32),
            pltpu.VMEM((pairs, LANES, LANES), jnp.float32),
            pltpu.VMEM(((cx + 4) * group, LANES), jnp.float32),
        ],
        compiler_params=pltpu.CompilerParams(vmem_limit_bytes=VMEM_LIMIT),
        name="substeps",
    )(got, passed, table, *rows)
    return jnp.swapaxes(out, 2, 3)


def padded_2(block, sides, width):
    for axis, dim in sides:
        count = lax.axis_size(axis)
        forward = [(i, i + 1) for i in range(count - 1)]
        backward = [(target, source) for source, target in forward]
        low = lax.ppermute(
            lax.slice_in_dim(block, block.shape[dim] - width, None, axis=dim), axis, forward
        )
        high = lax.ppermute(lax.slice_in_dim(block, 0, width, axis=dim), axis, backward)
        block = jnp.concatenate([low, block, high], axis=dim)
    return block


def spread(block, axis, owner):
    block = jnp.where(lax.axis_index(axis) == owner, block, jnp.zeros_like(block))
    return lax.psum(block, axis)


def rotate_strip(strip_data, side_index, far_side, flipped):
    normal_part = jnp.where(far_side < 2, strip_data[1], strip_data[2])
    along_part = jnp.where(far_side < 2, strip_data[2], strip_data[1])
    sign_here = 2.0 * (side_index % 2) - 1.0
    sign_there = (2 * (far_side % 2) - 1).astype(jnp.float32)
    normal_part = -sign_here * sign_there * normal_part
    along_part = (1 - 2 * flipped).astype(jnp.float32) * along_part
    if side_index < 2:
        return jnp.stack([strip_data[0], normal_part, along_part])
    return jnp.stack([strip_data[0], along_part, normal_part])


def window_strip(store, side_pick, neighbour, flipped, start, width):
    full_length = store.shape[5]
    begin = jnp.where(flipped == 1, full_length - start - width, start)
    zero = jnp.zeros((), jnp.int32)
    sizes_here = (1, 1, store.shape[2], store.shape[3], store.shape[4], width)
    piece = lax.dynamic_slice(store, (side_pick, neighbour, zero, zero, zero, begin), sizes_here)[
        0, 0
    ]
    return jnp.where(flipped == 1, jnp.flip(piece, 3), piece)


def side_halo(edge_store, edges, face_index, side_index, start, width):
    neighbour = edges[face_index, side_index, 0]
    far_side = edges[face_index, side_index, 1]
    flipped = edges[face_index, side_index, 2]
    strip_data = window_strip(edge_store, far_side, neighbour, flipped, start, width)
    return rotate_strip(strip_data, side_index, far_side, flipped)


def advance(padded, wave_speed, coriolis_part, cells_x, cells_y):
    height = padded[..., 0, :, :, :]
    wind_east = padded[..., 1, :, :, :]
    wind_north = padded[..., 2, :, :, :]
    speed = wave_speed[:, None, None]
    east_pred = wind_east[..., 1 : cells_x + 5, 3 : cells_y + 3] - speed * (
        0.5
        * (
            height[..., 2 : cells_x + 6, 3 : cells_y + 3]
            - height[..., 0 : cells_x + 4, 3 : cells_y + 3]
        )
    )
    north_pred = wind_north[..., 3 : cells_x + 3, 1 : cells_y + 5] - speed * (
        0.5
        * (
            height[..., 3 : cells_x + 3, 2 : cells_y + 6]
            - height[..., 3 : cells_x + 3, 0 : cells_y + 4]
        )
    )
    flux_east = (
        8.0 * (east_pred[..., 3 : cells_x + 3, :] - east_pred[..., 1 : cells_x + 1, :])
        - (east_pred[..., 4 : cells_x + 4, :] - east_pred[..., 0:cells_x, :])
    ) / 12.0
    flux_north = (
        8.0 * (north_pred[..., 3 : cells_y + 3] - north_pred[..., 1 : cells_y + 1])
        - (north_pred[..., 4 : cells_y + 4] - north_pred[..., 0:cells_y])
    ) / 12.0
    height_new = height[..., 3 : cells_x + 3, 3 : cells_y + 3] - speed * (flux_east + flux_north)
    east_inner = east_pred[..., 2 : cells_x + 2, :]
    north_inner = north_pred[..., 2 : cells_y + 2]
    turning = coriolis_part[..., None, :, :]
    return jnp.stack(
        [height_new, east_inner + turning * north_inner, north_inner - turning * east_inner],
        axis=-4,
    )


def one_substep(state, coriolis, wave_speed, edges, count_x, count_y, index_x, index_y):
    faces = state.shape[0]
    cells_x = state.shape[3]
    cells_y = state.shape[4]
    padded = padded_2(state, (("tx", 3), ("ty", 4)), 3)
    west_rim = state[:, :, :, 0:3, :]
    east_rim = jnp.flip(state[:, :, :, cells_x - 3 :, :], 3)
    south_rim = jnp.swapaxes(state[:, :, :, :, 0:3], 3, 4)
    north_rim = jnp.swapaxes(jnp.flip(state[:, :, :, :, cells_y - 3 :], 4), 3, 4)
    west_part = spread(west_rim, "tx", 0)
    east_part = spread(east_rim, "tx", count_x - 1)
    west_full, east_full = (
        lax.all_gather(west_part, "ty", axis=4, tiled=True),
        lax.all_gather(east_part, "ty", axis=4, tiled=True),
    )
    south_row, north_row = (
        lax.all_gather(south_rim, "tx", axis=4, tiled=True),
        lax.all_gather(north_rim, "tx", axis=4, tiled=True),
    )
    south_all, north_all = (
        lax.all_gather(south_row, "ty", axis=0, tiled=True),
        lax.all_gather(north_row, "ty", axis=0, tiled=True),
    )
    south_full = south_all[0:faces]
    north_full = north_all[(count_y - 1) * faces : count_y * faces]
    edge_store = jnp.stack([west_full, east_full, south_full, north_full])
    halos = []
    for side_index in range(4):
        if side_index < 2:
            slabs = jnp.stack(
                [
                    side_halo(edge_store, edges, face_index, side_index, index_y * cells_y, cells_y)
                    for face_index in range(faces)
                ]
            )
        else:
            slabs = jnp.stack(
                [
                    side_halo(edge_store, edges, face_index, side_index, index_x * cells_x, cells_x)
                    for face_index in range(faces)
                ]
            )
        halos.append(slabs)
    west_region = padded[:, :, :, 0:3, 3 : cells_y + 3]
    padded = padded.at[:, :, :, 0:3, 3 : cells_y + 3].set(
        jnp.where(index_x == 0, jnp.flip(halos[0], 3), west_region)
    )
    east_region = padded[:, :, :, cells_x + 3 : cells_x + 6, 3 : cells_y + 3]
    padded = padded.at[:, :, :, cells_x + 3 : cells_x + 6, 3 : cells_y + 3].set(
        jnp.where(index_x == count_x - 1, halos[1], east_region)
    )
    south_region = padded[:, :, :, 3 : cells_x + 3, 0:3]
    padded = padded.at[:, :, :, 3 : cells_x + 3, 0:3].set(
        jnp.where(index_y == 0, jnp.swapaxes(jnp.flip(halos[2], 3), 3, 4), south_region)
    )
    north_region = padded[:, :, :, 3 : cells_x + 3, cells_y + 3 : cells_y + 6]
    padded = padded.at[:, :, :, 3 : cells_x + 3, cells_y + 3 : cells_y + 6].set(
        jnp.where(index_y == count_y - 1, jnp.swapaxes(halos[3], 3, 4), north_region)
    )
    return advance(padded, wave_speed, coriolis, cells_x, cells_y)


def on_device(state, coriolis, wave_speed, edges):
    count_x = lax.axis_size("tx")
    count_y = lax.axis_size("ty")
    index_x = lax.axis_index("tx")
    index_y = lax.axis_index("ty")
    for substep_index in range(SUBSTEPS):
        state = one_substep(state, coriolis, wave_speed, edges, count_x, count_y, index_x, index_y)
    return state


def fits(state):
    count_x = lax.axis_size("tx")
    faces, fields, levels, cells_x, cells_y = state.shape
    return (
        lax.axis_size("ty") == 2
        and faces % 2 == 0
        and levels == 4
        and cells_x == 6
        and cells_y == 24
        and count_x == 8
        and cells_x * count_x == 2 * cells_y
        and 2 * cells_y + 2 * MARGIN <= WINDOW
    )


def either(state, coriolis, wave_speed, edges):
    if fits(state):
        return fast_on_device(state, coriolis, wave_speed, edges)
    return on_device(state, coriolis, wave_speed, edges)


def solution(mesh):
    in_specs = (P("member", None, None, "tx", "ty"), P(None, "tx", "ty"), P(), P())
    out_specs = P("member", None, None, "tx", "ty")
    return jax.shard_map(
        either, mesh=mesh, in_specs=in_specs, out_specs=out_specs, check_vma=False
    )
```

```python
import functools

import jax
import jax.numpy as jnp
from jax import lax
from jax.experimental import pallas as pl
from jax.experimental.pallas import tpu as pltpu
from jax.sharding import PartitionSpec as P

SUBSTEPS = 2
LANES = 128
WINDOW = 64
MARGIN = 8
STRIDE = 13
VMEM_LIMIT = 32 * 1024 * 1024
SMALL_VMEM_LIMIT = 8 * 1024 * 1024


def window_start(source, target, count_x, index_y, cx, cy, far):
    width = 2 * cx
    near = jnp.minimum(target, count_x - 1 - target)
    inward = jnp.minimum(cx * near - jnp.where(far, cx, cx // 2), cy - width)
    rim = (source == 0) | (source == count_x - 1)
    start = jnp.where(rim, jnp.maximum(inward, 0), 0)
    return jnp.where(index_y == 0, start, cy - width - start)


def windows(source, target, count_x, index_y, cx, cy):
    low_far = source == count_x - 1
    lower = window_start(source, target, count_x, index_y, cx, cy, low_far)
    upper = window_start(source, target, count_x, index_y, cx, cy, ~low_far)
    return lower, upper


def unit_place(field, x, cx, group, width):
    per_row = 60 // width
    index = field * cx + x
    return (index // per_row) * group, (index % per_row) * width


def pack_kernel(
    cx, cy, count_x, full_rows, small_rows, state_hbm, coriolis_hbm,
    swap_ref, line_ref, state_ref, coriolis_ref, sems,
):
    copies = [
        pltpu.make_async_copy(state_hbm, state_ref, sems.at[0]),
        pltpu.make_async_copy(coriolis_hbm, coriolis_ref, sems.at[1]),
    ]
    for copy in copies:
        copy.start()
    faces, fields = state_ref.shape[:2]
    levels = state_ref.shape[3]
    pairs = faces // 2
    group = pairs * levels
    half = cx // 2
    base = fields * half * group
    swap_ref[:full_rows] = jnp.zeros((full_rows, LANES), jnp.float32)
    line_ref[...] = jnp.zeros(line_ref.shape, jnp.float32)
    for copy in copies:
        copy.wait()
    for face in range(faces):
        for parity in range(2):
            lane = (face % 2) * WINDOW + MARGIN + parity * cy
            for xp in range(half):
                for field in range(fields):
                    row = field * half * group + xp * group + (face // 2) * levels
                    swap_ref[row : row + levels, lane : lane + cy] = state_ref[
                        face, field, 2 * xp + parity
                    ]
                x = 2 * xp + parity
                row = base + xp * pairs + face // 2
                swap_ref[row : row + 1, lane : lane + cy] = coriolis_ref[face, x : x + 1]
                row = (x // half) * 16 + (x % half) * pairs + face // 2
                lane_at = (face % 2) * WINDOW + MARGIN
                line_ref[row : row + 1, lane_at : lane_at + cy] = coriolis_ref[face, x : x + 1]
    sense = 1 - 2 * lax.axis_index("ty")
    for place, distance in enumerate((2, 3)):
        top = full_rows + place * small_rows
        put_chunk(cx, cy, count_x, swap_ref, line_ref, swap_ref, top, -sense * distance)


def put_chunk(cx, cy, count_x, block_ref, line_ref, out_ref, top, offset):
    pairs = 3
    group = 4 * pairs
    fields = 3
    half = cx // 2
    width = 2 * cx
    index_x = lax.axis_index("tx")
    index_y = lax.axis_index("ty")
    target = (index_x + offset + count_x) % count_x
    starts = windows(index_x, target, count_x, index_y, cx, cy)
    blocks = {}

    def put(row, lane, lines):
        position = lax.broadcasted_iota(jnp.int32, lines.shape, 1) % WINDOW
        here = (position >= lane) & (position < lane + width)
        blocks[row] = jnp.where(here, lines, blocks.get(row, jnp.zeros_like(lines)))

    for field in range(fields):
        for x in range(cx):
            row = field * half * group + (x // 2) * group
            at, lane = unit_place(field, x, cx, group, width)
            shift = lane - MARGIN - (x % 2) * cy - starts[x // half] + 2 * LANES
            put(at, lane, pltpu.roll(block_ref[row : row + group], shift % LANES, 1))
    for part in range(2):
        at, lane = unit_place(fields, part, cx, group, width)
        shift = lane - MARGIN - starts[part] + 2 * LANES
        lines = line_ref[16 * part : 16 * part + group]
        put(at, lane, pltpu.roll(lines, shift % LANES, 1))
    for row, lines in blocks.items():
        out_ref[top + row : top + row + group] = lines


def keep_kernel(cx, cy, count_x, small_rows, swap_ref, line_ref, keep_ref, middle_ref):
    sense = 1 - 2 * lax.axis_index("ty")
    put_chunk(cx, cy, count_x, swap_ref, line_ref, middle_ref, 0, count_x // 2)
    for place, distance in enumerate((2, 3)):
        top = place * small_rows
        put_chunk(cx, cy, count_x, swap_ref, line_ref, keep_ref, top, sense * distance)


def mix_kernel(full_rows, small_rows, swap_ref, other_ref, keep_ref, near_ref, second_ref, third_ref):
    near_ref[:full_rows] = swap_ref[:full_rows]
    near_ref[full_rows:] = other_ref[:full_rows]
    for place, far_ref in enumerate((second_ref, third_ref)):
        at = place * small_rows
        far_ref[:small_rows] = keep_ref[at : at + small_rows]
        at += full_rows
        far_ref[small_rows:] = other_ref[at : at + small_rows]


def placer(cx, cy, count_x, full_rows, small_rows, z_ref, cor_ref):
    fields = z_ref.shape[0]
    levels = 4
    pairs = 3
    group = pairs * levels
    half = cx // 2
    index_x = lax.axis_index("tx")
    index_y = lax.axis_index("ty")
    south_half = lax.broadcasted_iota(jnp.int32, (group, LANES), 1) % WINDOW < MARGIN + cy
    south_is_own = index_y == 0
    own_half = south_half == south_is_own

    def row_of(x):
        return (x + 4) * STRIDE

    def from_owner(offset):
        source = (index_x - offset + 2 * count_x) % count_x
        return source, source * (cx * STRIDE)

    def put_coriolis(start, x, values, at):
        for pair in range(pairs):
            line = values[at + pair : at + pair + 1]
            rows = pl.ds(start + x * STRIDE + pair * levels, levels)
            cor_ref[rows] = jnp.broadcast_to(line, (levels, LANES))

    def put_block(start, lines_of):
        base = fields * half * group
        for field in range(fields):
            for xp in range(half):
                even, odd = lines_of(field * half * group + xp * group, group)
                z_ref[field, pl.ds(start + row_of(2 * xp), group)] = even
                z_ref[field, pl.ds(start + row_of(2 * xp + 1), group)] = odd
        for parity, values in enumerate(lines_of(base, half * pairs)):
            for xp in range(half):
                put_coriolis(start, 2 * xp + parity, values, xp * pairs)

    def put_distant(source, start, lines_of):
        starts_south = windows(source, index_x, count_x, 0, cx, cy)
        starts_north = windows(source, index_x, count_x, 1, cx, cy)

        def lines_at(field, x, part):
            at, lane = unit_place(field, x, cx, group, 2 * cx)
            south_shift = (MARGIN + starts_south[part] - lane + LANES) % LANES
            north_shift = (MARGIN + cy + starts_north[part] - lane + LANES) % LANES
            return lines_of(at, south_shift, north_shift)

        for field in range(fields):
            for x in range(cx):
                z_ref[field, pl.ds(start + row_of(x), group)] = lines_at(field, x, x // half)
        for part in range(2):
            values = lines_at(fields, part, part)
            for x in range(half):
                put_coriolis(start, part * half + x, values, x * pairs)

    def place_own(own_ref, other_ref):
        def own_lines(row, rows):
            mine = own_ref[row : row + rows]
            theirs = other_ref[row : row + rows]
            up, down = index_y * cy, (1 - index_y) * cy
            keep = own_half[:rows]
            even = jnp.where(keep, pltpu.roll(mine, up, 1), pltpu.roll(theirs, down, 1))
            mine = pltpu.roll(mine, (LANES - down) % LANES, 1)
            theirs = pltpu.roll(theirs, (LANES - up) % LANES, 1)
            return even, jnp.where(keep, mine, theirs)

        put_block(from_owner(0)[1], own_lines)

    def place_got(block_ref, toward, south_first):
        south_top = pl.multiple_of(south_first * full_rows, 8)
        north_top = pl.multiple_of((1 - south_first) * full_rows, 8)

        def near_lines(row, rows):
            south = block_ref[pl.ds(south_top + row, rows)]
            north = block_ref[pl.ds(north_top + row, rows)]
            low = south_half[:rows]
            even = jnp.where(low, south, pltpu.roll(north, cy, 1))
            return even, jnp.where(low, pltpu.roll(south, LANES - cy, 1), north)

        put_block(from_owner(toward)[1], near_lines)
        for place, distance in enumerate((2, 3)):
            top = 2 * full_rows + 2 * place * small_rows
            south_at = pl.multiple_of(top + south_first * small_rows, 8)
            north_at = pl.multiple_of(top + (1 - south_first) * small_rows, 8)

            def far_lines(at, south_shift, north_shift, south_at=south_at, north_at=north_at):
                south = pltpu.roll(block_ref[pl.ds(south_at + at, group)], south_shift, 1)
                north = pltpu.roll(block_ref[pl.ds(north_at + at, group)], north_shift, 1)
                return jnp.where(south_half, south, north)

            put_distant(*from_owner(toward * distance), far_lines)

    def place_middle(got_ref, got_other_ref):
        def middle_lines(at, south_shift, north_shift):
            row = 2 * full_rows + 4 * small_rows + at
            mine_shift = jnp.where(south_is_own, south_shift, north_shift)
            other_shift = jnp.where(south_is_own, north_shift, south_shift)
            mine = pltpu.roll(got_ref[row : row + group], mine_shift, 1)
            theirs = pltpu.roll(got_other_ref[row : row + group], other_shift, 1)
            return jnp.where(own_half, mine, theirs)

        put_distant(*from_owner(count_x // 2), middle_lines)

    return place_own, place_got, place_middle


def own_kernel(sizes, own_ref, other_ref, z_ref, cor_ref):
    placer(*sizes, z_ref, cor_ref)[0](own_ref, other_ref)


def got_kernel(sizes, got_ref, z_in, cor_in, z_ref, cor_ref):
    index_y = lax.axis_index("ty")
    placer(*sizes, z_ref, cor_ref)[1](got_ref, 1 - 2 * index_y, index_y)


def step_kernel(
    sizes, got_ref, got_other_ref, table_ref, z_in, cor_in, out_ref, z_ref, cor_ref,
    pred_ref, store_ref, tile_ref, flip_ref, speed_ref,
):
    cx, cy, count_x = sizes[:3]
    levels = 4
    slots = 16
    cells = cx * count_x
    faces = store_ref.shape[0] // 4
    pairs = faces // 2
    group = STRIDE
    chunk = cx * group
    index_x = lax.axis_index("tx")
    index_y = lax.axis_index("ty")

    def row_of(x):
        return (x + 4) * group

    def lanes_of(rows):
        return lax.broadcasted_iota(jnp.int32, (rows, LANES), 1)

    _, place_got, place_middle = placer(*sizes, z_ref, cor_ref)
    place_got(got_other_ref, 2 * index_y - 1, 1 - index_y)
    place_middle(got_ref, got_other_ref)

    level_of = lax.broadcasted_iota(jnp.int32, speed_ref.shape, 0) % group % levels
    speeds = jnp.full(speed_ref.shape, table_ref[0], jnp.float32)
    for index in range(1, levels):
        speeds = jnp.where(level_of == index, table_ref[index], speeds)
    speed_ref[...] = speeds

    def collect():
        position = lanes_of(cells) % WINDOW
        gap = WINDOW - cells + 3
        wide = gap + 3 * levels
        for pair in range(pairs):
            merged = jnp.zeros((cells, LANES), jnp.float32)
            for slot, field in ((0, 0), (1, 2)):
                for level in range(levels):
                    lines = z_ref[field, pl.ds(row_of(0) + pair * levels + level, cells, group)]
                    offset = slot * wide + 3 * level
                    here = position - offset
                    wanted = ((here >= 0) & (here < 3)) | ((here >= gap) & (here < gap + 3))
                    shift = (offset - (MARGIN + cells - 3)) % LANES
                    merged = jnp.where(wanted, pltpu.roll(lines, shift, 1), merged)
            merged = jnp.concatenate(
                [merged, jnp.zeros((LANES - cells, LANES), jnp.float32)], axis=0
            )
            flip_ref[pair] = merged.T
            for slot in range(2):
                for side in (2, 3):
                    for odd in range(2):
                        for depth in range(3):
                            base = slot * wide
                            if side == 3:
                                base += odd * WINDOW + 2 - depth
                            else:
                                base += ((odd + 1) % 2) * WINDOW + gap + depth
                            at = slot * slots + depth * levels
                            store_ref[(2 * pair + odd) * 4 + side, at : at + levels] = flip_ref[
                                pair, pl.ds(base, levels, 3)
                            ]
            for slot in range(2):
                for side in (0, 1):
                    for depth in range(3):
                        x = depth if side == 0 else cells - 1 - depth
                        row = row_of(x) + pair * levels
                        lines = z_ref[slot, row : row + levels]
                        at = slot * slots + depth * levels
                        for odd in range(2):
                            store_ref[(2 * pair + odd) * 4 + side, at : at + levels] = pltpu.roll(
                                lines, LANES - MARGIN - odd * WINDOW, 1
                            )

    def fetch(face, side, position):
        at = levels + (face * 4 + side) * 3
        neighbour = table_ref[at].astype(jnp.int32)
        far_side = table_ref[at + 1].astype(jnp.int32)
        flipped = table_ref[at + 2].astype(jnp.int32)
        block = store_ref[neighbour * 4 + far_side]
        order = jnp.where(flipped == 1, cells - 1 - position, position)
        order = jnp.where((position >= 0) & (position < cells), order, 0)
        block = jnp.take_along_axis(block, order, axis=1)
        sign_here = 2 * (side % 2) - 1
        sign_there = 2 * (far_side % 2) - 1
        sign = (-sign_here * sign_there).astype(jnp.float32)
        normal = lax.broadcasted_iota(jnp.int32, block.shape, 0) >= slots
        return jnp.where(normal, sign * block, block)

    def rim_rows(side):
        lane = lanes_of(2 * slots)
        for pair in range(pairs):
            first = fetch(2 * pair, side, lane - MARGIN)
            second = fetch(2 * pair + 1, side, lane - (MARGIN + WINDOW))
            both = jnp.where(lane < WINDOW, first, second)
            for slot in range(2):
                for depth in range(3):
                    x = -1 - depth if side == 0 else cells + depth
                    at = slot * slots + depth * levels
                    row = row_of(x) + pair * levels
                    z_ref[slot, row : row + levels] = both[at : at + levels]

    wide = WINDOW - cells - 3 + 3 * levels

    def tile_rows(odd, side, depth, base=0):
        if side == 3:
            return pl.ds(base + odd * WINDOW + depth, levels, 3)
        return pl.ds(base + ((odd + 1) % 2) * WINDOW + wide - 3 * levels + 2 - depth, levels, 3)

    def put_columns(lines, field, start, pair, base=0):
        count = lines.shape[0]
        position = lanes_of(count) % WINDOW
        rim = ((position >= MARGIN - 3) & (position < MARGIN)) | (
            (position >= MARGIN + cells) & (position < MARGIN + cells + 3)
        )
        for level in range(levels):
            rolled = pltpu.roll(lines, (MARGIN + cells - base - 3 * level) % LANES, 1)
            at = pl.ds(row_of(start) + pair * levels + level, count, group)
            z_ref[field, at] = jnp.where(rim, rolled, z_ref[field, at])

    def rim_columns_all():
        for pair in range(pairs):
            for odd in range(2):
                for side in (2, 3):
                    block = fetch(2 * pair + odd, side, lanes_of(2 * slots))
                    for slot in range(2):
                        for depth in range(3):
                            at = slot * slots + depth * levels
                            rows = tile_rows(odd, side, depth, slot * wide)
                            tile_ref[pair, rows] = block[at : at + levels]
            turned = tile_ref[pair].T[:cells]
            for slot, field in ((0, 0), (1, 2)):
                put_columns(turned, field, 0, pair, slot * wide)

    def rim_columns_own():
        lane = lanes_of(2 * slots)
        second = lax.broadcasted_iota(jnp.int32, lane.shape, 0) >= slots
        for odd in range(2):
            for side in (2, 3):
                total = jnp.zeros((slots, LANES), jnp.float32)
                for pair in range(pairs):
                    local = lane - jnp.where(second, 8 * (pairs + pair), 8 * pair)
                    block = fetch(2 * pair + odd, side, index_x * cx + local)
                    block = jnp.where((local >= 0) & (local < 8), block, 0.0)
                    total = total + block[:slots] + block[slots:]
                for depth in range(3):
                    at = depth * levels
                    tile_ref[0, tile_rows(odd, side, depth)] = total[at : at + levels]
        turned = tile_ref[0].T
        for slot, field in ((0, 0), (1, 2)):
            for pair in range(pairs):
                at = 8 * (slot * pairs + pair)
                put_columns(turned[at : at + cx], field, index_x * cx, pair)

    def predict(at, rows):
        speed = speed_ref[:rows]
        ahead = z_ref[0, pl.ds(at + group, rows)]
        behind = z_ref[0, pl.ds(at - group, rows)]
        pred_ref[pl.ds(at, rows)] = z_ref[1, pl.ds(at, rows)] - speed * (0.5 * (ahead - behind))

    def update(at, rows):
        speed = speed_ref[:rows]
        height = z_ref[0, pl.ds(at, rows)]
        north_pred = z_ref[2, pl.ds(at, rows)] - speed * (
            0.5 * (pltpu.roll(height, LANES - 1, 1) - pltpu.roll(height, 1, 1))
        )
        east_pred = pred_ref[pl.ds(at, rows)]
        flux_east = 8.0 * (
            pred_ref[pl.ds(at + group, rows)] - pred_ref[pl.ds(at - group, rows)]
        ) - (pred_ref[pl.ds(at + 2 * group, rows)] - pred_ref[pl.ds(at - 2 * group, rows)])
        flux_north = 8.0 * (
            pltpu.roll(north_pred, LANES - 1, 1) - pltpu.roll(north_pred, 1, 1)
        ) - (pltpu.roll(north_pred, LANES - 2, 1) - pltpu.roll(north_pred, 2, 1))
        height = height - speed * ((flux_east + flux_north) * (1.0 / 12.0))
        turning = cor_ref[pl.ds(at - row_of(0), rows)]
        return height, east_pred + turning * north_pred, north_pred - turning * east_pred

    collect()
    rim_rows(0)
    rim_rows(1)
    rim_columns_all()
    for first in range(-2, cells + 2, 4):
        predict(row_of(first), 4 * group)
    for index in range(count_x):
        at = row_of(0) + index * chunk
        for field, values in enumerate(update(at, chunk)):
            z_ref[field, at : at + chunk] = values

    collect()

    @pl.when(index_x == 0)
    def _():
        rim_rows(0)

    @pl.when(index_x == count_x - 1)
    def _():
        rim_rows(1)

    rim_columns_own()
    at = row_of(0) + index_x * chunk
    predict(at - 2 * group, chunk + 4 * group)
    for field, values in enumerate(update(at, chunk)):
        for odd in range(2):
            shift = LANES - (MARGIN + odd * WINDOW) - index_y * cy
            rolled = pltpu.roll(values, shift, 1)
            for x in range(cx):
                for pair in range(pairs):
                    row = x * group + pair * levels
                    out_ref[2 * pair + odd, field, x] = rolled[row : row + levels, :cy]


def fast_on_device(state, coriolis, wave_speed, edges):
    count_x = lax.axis_size("tx")
    faces, fields, levels, cx, cy = state.shape
    pairs = faces // 2
    group = pairs * levels
    cells = cx * count_x
    full_rows = fields * (cx // 2) * group + (cx // 2) * pairs
    full_rows = -(-full_rows // 8) * 8
    small_rows = unit_place(fields, 1, cx, group, 2 * cx)[0] + group
    swap, lines = pl.pallas_call(
        functools.partial(pack_kernel, cx, cy, count_x, full_rows, small_rows),
        out_shape=[
            jax.ShapeDtypeStruct((full_rows + 2 * small_rows, LANES), jnp.float32),
            jax.ShapeDtypeStruct((32, LANES), jnp.float32),
        ],
        in_specs=[pl.BlockSpec(memory_space=pltpu.HBM)] * 2,
        out_specs=[pl.BlockSpec(memory_space=pltpu.VMEM)] * 2,
        scratch_shapes=[
            pltpu.VMEM((faces, fields, cx, levels, cy), jnp.float32),
            pltpu.VMEM((faces, cx, cy), jnp.float32),
            pltpu.SemaphoreType.DMA((2,)),
        ],
        compiler_params=pltpu.CompilerParams(vmem_limit_bytes=VMEM_LIMIT),
        name="pack",
    )(jnp.swapaxes(state, 2, 3), coriolis)
    keep, middle = pl.pallas_call(
        functools.partial(keep_kernel, cx, cy, count_x, small_rows),
        out_shape=[
            jax.ShapeDtypeStruct((2 * small_rows, LANES), jnp.float32),
            jax.ShapeDtypeStruct((small_rows, LANES), jnp.float32),
        ],
        in_specs=[pl.BlockSpec(memory_space=pltpu.VMEM)] * 2,
        out_specs=[pl.BlockSpec(memory_space=pltpu.VMEM)] * 2,
        compiler_params=pltpu.CompilerParams(vmem_limit_bytes=SMALL_VMEM_LIMIT),
        name="keep",
    )(swap, lines)

    def moved(block, distance):
        pairs_of = []
        for index in range(count_x):
            for core in range(2):
                target = (index + distance * (1 - 2 * core)) % count_x
                pairs_of.append((2 * index + core, 2 * target + core))
        return lax.ppermute(block, ("tx", "ty"), pairs_of)

    def across(block):
        return lax.ppermute(block, "ty", [(0, 1), (1, 0)])

    other = across(swap)
    messages = pl.pallas_call(
        functools.partial(mix_kernel, full_rows, small_rows),
        out_shape=[
            jax.ShapeDtypeStruct((2 * rows, LANES), jnp.float32)
            for rows in (full_rows, small_rows, small_rows)
        ],
        in_specs=[pl.BlockSpec(memory_space=pltpu.VMEM)] * 3,
        out_specs=[pl.BlockSpec(memory_space=pltpu.VMEM)] * 3,
        compiler_params=pltpu.CompilerParams(vmem_limit_bytes=SMALL_VMEM_LIMIT),
        name="messages",
    )(swap, other, keep)
    got = [moved(block, place + 1) for place, block in enumerate(messages)]
    got = jnp.concatenate([*got, moved(middle, count_x // 2)])
    table = jnp.concatenate([wave_speed, edges.reshape(-1).astype(jnp.float32)])
    got, table = lax.optimization_barrier((got, table))
    passed = across(got)

    sizes = (cx, cy, count_x, full_rows, small_rows)
    state_rows = [
        jax.ShapeDtypeStruct((fields, (cells + 8) * STRIDE, LANES), jnp.float32),
        jax.ShapeDtypeStruct((cells * STRIDE, LANES), jnp.float32),
    ]
    in_vmem = pl.BlockSpec(memory_space=pltpu.VMEM)
    params = pltpu.CompilerParams(vmem_limit_bytes=SMALL_VMEM_LIMIT)
    rows = pl.pallas_call(
        functools.partial(own_kernel, sizes),
        out_shape=state_rows,
        in_specs=[in_vmem] * 2,
        out_specs=[in_vmem] * 2,
        compiler_params=params,
        name="place_own",
    )(swap, other)
    rows = pl.pallas_call(
        functools.partial(got_kernel, sizes),
        out_shape=state_rows,
        in_specs=[in_vmem] * 3,
        out_specs=[in_vmem] * 2,
        input_output_aliases={1: 0, 2: 1},
        compiler_params=params,
        name="place_got",
    )(got, *rows)
    out, _, _ = pl.pallas_call(
        functools.partial(step_kernel, sizes),
        out_shape=[jax.ShapeDtypeStruct((faces, fields, cx, levels, cy), jnp.float32)]
        + state_rows,
        in_specs=[in_vmem] * 2 + [pl.BlockSpec(memory_space=pltpu.SMEM)] + [in_vmem] * 2,
        out_specs=[in_vmem] * 3,
        input_output_aliases={3: 1, 4: 2},
        scratch_shapes=[
            pltpu.VMEM(((cells + 8) * STRIDE, LANES), jnp.float32),
            pltpu.VMEM((faces * 4, 32, LANES), jnp.float32),
            pltpu.VMEM((pairs, LANES, LANES), jnp.float32),
            pltpu.VMEM((pairs, LANES, LANES), jnp.float32),
            pltpu.VMEM(((cx + 4) * STRIDE, LANES), jnp.float32),
        ],
        compiler_params=pltpu.CompilerParams(vmem_limit_bytes=VMEM_LIMIT),
        name="substeps",
    )(got, passed, table, *rows)
    return jnp.swapaxes(out, 2, 3)


def padded_2(block, sides, width):
    for axis, dim in sides:
        count = lax.axis_size(axis)
        forward = [(i, i + 1) for i in range(count - 1)]
        backward = [(target, source) for source, target in forward]
        low = lax.ppermute(
            lax.slice_in_dim(block, block.shape[dim] - width, None, axis=dim), axis, forward
        )
        high = lax.ppermute(lax.slice_in_dim(block, 0, width, axis=dim), axis, backward)
        block = jnp.concatenate([low, block, high], axis=dim)
    return block


def spread(block, axis, owner):
    block = jnp.where(lax.axis_index(axis) == owner, block, jnp.zeros_like(block))
    return lax.psum(block, axis)


def rotate_strip(strip_data, side_index, far_side, flipped):
    normal_part = jnp.where(far_side < 2, strip_data[1], strip_data[2])
    along_part = jnp.where(far_side < 2, strip_data[2], strip_data[1])
    sign_here = 2.0 * (side_index % 2) - 1.0
    sign_there = (2 * (far_side % 2) - 1).astype(jnp.float32)
    normal_part = -sign_here * sign_there * normal_part
    along_part = (1 - 2 * flipped).astype(jnp.float32) * along_part
    if side_index < 2:
        return jnp.stack([strip_data[0], normal_part, along_part])
    return jnp.stack([strip_data[0], along_part, normal_part])


def window_strip(store, side_pick, neighbour, flipped, start, width):
    full_length = store.shape[5]
    begin = jnp.where(flipped == 1, full_length - start - width, start)
    zero = jnp.zeros((), jnp.int32)
    sizes_here = (1, 1, store.shape[2], store.shape[3], store.shape[4], width)
    piece = lax.dynamic_slice(store, (side_pick, neighbour, zero, zero, zero, begin), sizes_here)[
        0, 0
    ]
    return jnp.where(flipped == 1, jnp.flip(piece, 3), piece)


def side_halo(edge_store, edges, face_index, side_index, start, width):
    neighbour = edges[face_index, side_index, 0]
    far_side = edges[face_index, side_index, 1]
    flipped = edges[face_index, side_index, 2]
    strip_data = window_strip(edge_store, far_side, neighbour, flipped, start, width)
    return rotate_strip(strip_data, side_index, far_side, flipped)


def advance(padded, wave_speed, coriolis_part, cells_x, cells_y):
    height = padded[..., 0, :, :, :]
    wind_east = padded[..., 1, :, :, :]
    wind_north = padded[..., 2, :, :, :]
    speed = wave_speed[:, None, None]
    east_pred = wind_east[..., 1 : cells_x + 5, 3 : cells_y + 3] - speed * (
        0.5
        * (
            height[..., 2 : cells_x + 6, 3 : cells_y + 3]
            - height[..., 0 : cells_x + 4, 3 : cells_y + 3]
        )
    )
    north_pred = wind_north[..., 3 : cells_x + 3, 1 : cells_y + 5] - speed * (
        0.5
        * (
            height[..., 3 : cells_x + 3, 2 : cells_y + 6]
            - height[..., 3 : cells_x + 3, 0 : cells_y + 4]
        )
    )
    flux_east = (
        8.0 * (east_pred[..., 3 : cells_x + 3, :] - east_pred[..., 1 : cells_x + 1, :])
        - (east_pred[..., 4 : cells_x + 4, :] - east_pred[..., 0:cells_x, :])
    ) / 12.0
    flux_north = (
        8.0 * (north_pred[..., 3 : cells_y + 3] - north_pred[..., 1 : cells_y + 1])
        - (north_pred[..., 4 : cells_y + 4] - north_pred[..., 0:cells_y])
    ) / 12.0
    height_new = height[..., 3 : cells_x + 3, 3 : cells_y + 3] - speed * (flux_east + flux_north)
    east_inner = east_pred[..., 2 : cells_x + 2, :]
    north_inner = north_pred[..., 2 : cells_y + 2]
    turning = coriolis_part[..., None, :, :]
    return jnp.stack(
        [height_new, east_inner + turning * north_inner, north_inner - turning * east_inner],
        axis=-4,
    )


def one_substep(state, coriolis, wave_speed, edges, count_x, count_y, index_x, index_y):
    faces = state.shape[0]
    cells_x = state.shape[3]
    cells_y = state.shape[4]
    padded = padded_2(state, (("tx", 3), ("ty", 4)), 3)
    west_rim = state[:, :, :, 0:3, :]
    east_rim = jnp.flip(state[:, :, :, cells_x - 3 :, :], 3)
    south_rim = jnp.swapaxes(state[:, :, :, :, 0:3], 3, 4)
    north_rim = jnp.swapaxes(jnp.flip(state[:, :, :, :, cells_y - 3 :], 4), 3, 4)
    west_part = spread(west_rim, "tx", 0)
    east_part = spread(east_rim, "tx", count_x - 1)
    west_full, east_full = (
        lax.all_gather(west_part, "ty", axis=4, tiled=True),
        lax.all_gather(east_part, "ty", axis=4, tiled=True),
    )
    south_row, north_row = (
        lax.all_gather(south_rim, "tx", axis=4, tiled=True),
        lax.all_gather(north_rim, "tx", axis=4, tiled=True),
    )
    south_all, north_all = (
        lax.all_gather(south_row, "ty", axis=0, tiled=True),
        lax.all_gather(north_row, "ty", axis=0, tiled=True),
    )
    south_full = south_all[0:faces]
    north_full = north_all[(count_y - 1) * faces : count_y * faces]
    edge_store = jnp.stack([west_full, east_full, south_full, north_full])
    halos = []
    for side_index in range(4):
        if side_index < 2:
            slabs = jnp.stack(
                [
                    side_halo(edge_store, edges, face_index, side_index, index_y * cells_y, cells_y)
                    for face_index in range(faces)
                ]
            )
        else:
            slabs = jnp.stack(
                [
                    side_halo(edge_store, edges, face_index, side_index, index_x * cells_x, cells_x)
                    for face_index in range(faces)
                ]
            )
        halos.append(slabs)
    west_region = padded[:, :, :, 0:3, 3 : cells_y + 3]
    padded = padded.at[:, :, :, 0:3, 3 : cells_y + 3].set(
        jnp.where(index_x == 0, jnp.flip(halos[0], 3), west_region)
    )
    east_region = padded[:, :, :, cells_x + 3 : cells_x + 6, 3 : cells_y + 3]
    padded = padded.at[:, :, :, cells_x + 3 : cells_x + 6, 3 : cells_y + 3].set(
        jnp.where(index_x == count_x - 1, halos[1], east_region)
    )
    south_region = padded[:, :, :, 3 : cells_x + 3, 0:3]
    padded = padded.at[:, :, :, 3 : cells_x + 3, 0:3].set(
        jnp.where(index_y == 0, jnp.swapaxes(jnp.flip(halos[2], 3), 3, 4), south_region)
    )
    north_region = padded[:, :, :, 3 : cells_x + 3, cells_y + 3 : cells_y + 6]
    padded = padded.at[:, :, :, 3 : cells_x + 3, cells_y + 3 : cells_y + 6].set(
        jnp.where(index_y == count_y - 1, jnp.swapaxes(halos[3], 3, 4), north_region)
    )
    return advance(padded, wave_speed, coriolis, cells_x, cells_y)


def on_device(state, coriolis, wave_speed, edges):
    count_x = lax.axis_size("tx")
    count_y = lax.axis_size("ty")
    index_x = lax.axis_index("tx")
    index_y = lax.axis_index("ty")
    for substep_index in range(SUBSTEPS):
        state = one_substep(state, coriolis, wave_speed, edges, count_x, count_y, index_x, index_y)
    return state


def fits(state):
    count_x = lax.axis_size("tx")
    faces, fields, levels, cells_x, cells_y = state.shape
    return (
        lax.axis_size("ty") == 2
        and faces % 2 == 0
        and levels == 4
        and cells_x == 6
        and cells_y == 24
        and count_x == 8
        and cells_x * count_x == 2 * cells_y
        and 2 * cells_y + 2 * MARGIN <= WINDOW
    )


def either(state, coriolis, wave_speed, edges):
    if fits(state):
        return fast_on_device(state, coriolis, wave_speed, edges)
    return on_device(state, coriolis, wave_speed, edges)


def solution(mesh):
    in_specs = (P("member", None, None, "tx", "ty"), P(None, "tx", "ty"), P(), P())
    out_specs = P("member", None, None, "tx", "ty")
    return jax.shard_map(
        either, mesh=mesh, in_specs=in_specs, out_specs=out_specs, check_vma=False
    )
```

```python
import functools

import jax
import jax.numpy as jnp
from jax import lax
from jax.experimental import pallas as pl
from jax.experimental.pallas import tpu as pltpu
from jax.sharding import PartitionSpec as P

SUBSTEPS = 2
LANES = 128
WINDOW = 64
MARGIN = 8
ROWS = 64
EDGE = 8
VMEM_LIMIT = 32 * 1024 * 1024
SMALL_VMEM_LIMIT = 8 * 1024 * 1024


def window_start(source, target, count_x, index_y, cx, cy, far):
    width = 2 * cx
    near = jnp.minimum(target, count_x - 1 - target)
    inward = jnp.minimum(cx * near - jnp.where(far, cx, cx // 2), cy - width)
    rim = (source == 0) | (source == count_x - 1)
    start = jnp.where(rim, jnp.maximum(inward, 0), 0)
    return jnp.where(index_y == 0, start, cy - width - start)


def windows(source, target, count_x, index_y, cx, cy):
    low_far = source == count_x - 1
    lower = window_start(source, target, count_x, index_y, cx, cy, low_far)
    upper = window_start(source, target, count_x, index_y, cx, cy, ~low_far)
    return lower, upper


def unit_place(field, x, cx, group, width):
    per_row = 60 // width
    index = field * cx + x
    return (index // per_row) * group, (index % per_row) * width


def pack_kernel(
    cx, cy, count_x, full_rows, small_rows, state_hbm, coriolis_hbm,
    swap_ref, line_ref, state_ref, coriolis_ref, sems,
):
    copies = [
        pltpu.make_async_copy(state_hbm, state_ref, sems.at[0]),
        pltpu.make_async_copy(coriolis_hbm, coriolis_ref, sems.at[1]),
    ]
    for copy in copies:
        copy.start()
    faces, fields = state_ref.shape[:2]
    levels = state_ref.shape[3]
    pairs = faces // 2
    group = pairs * levels
    half = cx // 2
    base = fields * half * group
    swap_ref[:full_rows] = jnp.zeros((full_rows, LANES), jnp.float32)
    line_ref[...] = jnp.zeros(line_ref.shape, jnp.float32)
    for copy in copies:
        copy.wait()
    for face in range(faces):
        for parity in range(2):
            lane = (face % 2) * WINDOW + MARGIN + parity * cy
            for xp in range(half):
                for field in range(fields):
                    row = field * half * group + xp * group + (face // 2) * levels
                    swap_ref[row : row + levels, lane : lane + cy] = state_ref[
                        face, field, 2 * xp + parity
                    ]
                x = 2 * xp + parity
                row = base + xp * pairs + face // 2
                swap_ref[row : row + 1, lane : lane + cy] = coriolis_ref[face, x : x + 1]
                row = (x // half) * 16 + (x % half) * pairs + face // 2
                lane_at = (face % 2) * WINDOW + MARGIN
                line_ref[row : row + 1, lane_at : lane_at + cy] = coriolis_ref[face, x : x + 1]
    sense = 1 - 2 * lax.axis_index("ty")
    for place, distance in enumerate((2, 3)):
        top = full_rows + place * small_rows
        put_chunk(cx, cy, count_x, swap_ref, line_ref, swap_ref, top, -sense * distance)


def put_chunk(cx, cy, count_x, block_ref, line_ref, out_ref, top, offset):
    pairs = 3
    group = 4 * pairs
    fields = 3
    half = cx // 2
    width = 2 * cx
    index_x = lax.axis_index("tx")
    index_y = lax.axis_index("ty")
    target = (index_x + offset + count_x) % count_x
    starts = windows(index_x, target, count_x, index_y, cx, cy)
    blocks = {}

    def put(row, lane, lines):
        position = lax.broadcasted_iota(jnp.int32, lines.shape, 1) % WINDOW
        here = (position >= lane) & (position < lane + width)
        blocks[row] = jnp.where(here, lines, blocks.get(row, jnp.zeros_like(lines)))

    for field in range(fields):
        for x in range(cx):
            row = field * half * group + (x // 2) * group
            at, lane = unit_place(field, x, cx, group, width)
            shift = lane - MARGIN - (x % 2) * cy - starts[x // half] + 2 * LANES
            put(at, lane, pltpu.roll(block_ref[row : row + group], shift % LANES, 1))
    for part in range(2):
        at, lane = unit_place(fields, part, cx, group, width)
        shift = lane - MARGIN - starts[part] + 2 * LANES
        lines = line_ref[16 * part : 16 * part + group]
        put(at, lane, pltpu.roll(lines, shift % LANES, 1))
    for row, lines in blocks.items():
        out_ref[top + row : top + row + group] = lines


def keep_kernel(cx, cy, count_x, small_rows, swap_ref, line_ref, keep_ref, middle_ref):
    sense = 1 - 2 * lax.axis_index("ty")
    put_chunk(cx, cy, count_x, swap_ref, line_ref, middle_ref, 0, count_x // 2)
    for place, distance in enumerate((2, 3)):
        top = place * small_rows
        put_chunk(cx, cy, count_x, swap_ref, line_ref, keep_ref, top, sense * distance)


def mix_kernel(full_rows, small_rows, swap_ref, other_ref, keep_ref, near_ref, second_ref, third_ref):
    near_ref[:full_rows] = swap_ref[:full_rows]
    near_ref[full_rows:] = other_ref[:full_rows]
    for place, far_ref in enumerate((second_ref, third_ref)):
        at = place * small_rows
        far_ref[:small_rows] = keep_ref[at : at + small_rows]
        at += full_rows
        far_ref[small_rows:] = other_ref[at : at + small_rows]


def placer(cx, cy, count_x, full_rows, small_rows, z_ref, cor_ref):
    fields = z_ref.shape[0]
    levels = 4
    pairs = cor_ref.shape[0]
    group = pairs * levels
    half = cx // 2
    index_x = lax.axis_index("tx")
    index_y = lax.axis_index("ty")
    south_half = lax.broadcasted_iota(jnp.int32, (group, LANES), 1) % WINDOW < MARGIN + cy
    south_is_own = index_y == 0
    own_half = south_half == south_is_own

    def from_owner(offset):
        source = (index_x - offset + 2 * count_x) % count_x
        return source, source * cx

    def put_state(field, x, values):
        z_ref[field, pl.ds(x + EDGE, group, ROWS)] = values

    def put_coriolis(x, values, at):
        for pair in range(pairs):
            cor_ref[pair, pl.ds(x, 1)] = values[at + pair : at + pair + 1]

    def put_block(start, lines_of):
        base = fields * half * group
        for field in range(fields):
            for xp in range(half):
                even, odd = lines_of(field * half * group + xp * group, group)
                put_state(field, start + 2 * xp, even)
                put_state(field, start + 2 * xp + 1, odd)
        for parity, values in enumerate(lines_of(base, half * pairs)):
            for xp in range(half):
                put_coriolis(start + 2 * xp + parity, values, xp * pairs)

    def put_distant(source, start, lines_of):
        starts_south = windows(source, index_x, count_x, 0, cx, cy)
        starts_north = windows(source, index_x, count_x, 1, cx, cy)

        def lines_at(field, x, part):
            at, lane = unit_place(field, x, cx, group, 2 * cx)
            south_shift = (MARGIN + starts_south[part] - lane + LANES) % LANES
            north_shift = (MARGIN + cy + starts_north[part] - lane + LANES) % LANES
            return lines_of(at, south_shift, north_shift)

        for field in range(fields):
            for x in range(cx):
                put_state(field, start + x, lines_at(field, x, x // half))
        for part in range(2):
            values = lines_at(fields, part, part)
            for x in range(half):
                put_coriolis(start + part * half + x, values, x * pairs)

    def place_own(own_ref, other_ref):
        def own_lines(row, rows):
            mine = own_ref[row : row + rows]
            theirs = other_ref[row : row + rows]
            up, down = index_y * cy, (1 - index_y) * cy
            keep = own_half[:rows]
            even = jnp.where(keep, pltpu.roll(mine, up, 1), pltpu.roll(theirs, down, 1))
            mine = pltpu.roll(mine, (LANES - down) % LANES, 1)
            theirs = pltpu.roll(theirs, (LANES - up) % LANES, 1)
            return even, jnp.where(keep, mine, theirs)

        put_block(from_owner(0)[1], own_lines)

    def place_got(block_ref, toward, south_first):
        south_top = pl.multiple_of(south_first * full_rows, 8)
        north_top = pl.multiple_of((1 - south_first) * full_rows, 8)

        def near_lines(row, rows):
            south = block_ref[pl.ds(south_top + row, rows)]
            north = block_ref[pl.ds(north_top + row, rows)]
            low = south_half[:rows]
            even = jnp.where(low, south, pltpu.roll(north, cy, 1))
            return even, jnp.where(low, pltpu.roll(south, LANES - cy, 1), north)

        put_block(from_owner(toward)[1], near_lines)
        for place, distance in enumerate((2, 3)):
            top = 2 * full_rows + 2 * place * small_rows
            south_at = pl.multiple_of(top + south_first * small_rows, 8)
            north_at = pl.multiple_of(top + (1 - south_first) * small_rows, 8)

            def far_lines(at, south_shift, north_shift, south_at=south_at, north_at=north_at):
                south = pltpu.roll(block_ref[pl.ds(south_at + at, group)], south_shift, 1)
                north = pltpu.roll(block_ref[pl.ds(north_at + at, group)], north_shift, 1)
                return jnp.where(south_half, south, north)

            put_distant(*from_owner(toward * distance), far_lines)

    def place_middle(got_ref, got_other_ref):
        def middle_lines(at, south_shift, north_shift):
            row = 2 * full_rows + 4 * small_rows + at
            mine_shift = jnp.where(south_is_own, south_shift, north_shift)
            other_shift = jnp.where(south_is_own, north_shift, south_shift)
            mine = pltpu.roll(got_ref[row : row + group], mine_shift, 1)
            theirs = pltpu.roll(got_other_ref[row : row + group], other_shift, 1)
            return jnp.where(own_half, mine, theirs)

        put_distant(*from_owner(count_x // 2), middle_lines)

    return place_own, place_got, place_middle


def own_kernel(sizes, own_ref, other_ref, z_ref, cor_ref):
    placer(*sizes, z_ref, cor_ref)[0](own_ref, other_ref)


def got_kernel(sizes, got_ref, z_in, cor_in, z_ref, cor_ref):
    index_y = lax.axis_index("ty")
    placer(*sizes, z_ref, cor_ref)[1](got_ref, 1 - 2 * index_y, index_y)


def step_kernel(
    sizes, got_ref, got_other_ref, table_ref, z_in, cor_in, out_ref, z_ref, cor_ref,
    pred_ref, store_ref, tile_ref, flip_ref, result_ref,
):
    cx, cy, count_x = sizes[:3]
    levels = 4
    slots = 4 * levels
    cells = cx * count_x
    faces = store_ref.shape[0] // 4
    pairs = faces // 2
    index_x = lax.axis_index("tx")
    index_y = lax.axis_index("ty")

    def lanes_of(rows):
        return lax.broadcasted_iota(jnp.int32, (rows, LANES), 1)

    def rows_of(rows):
        return lax.broadcasted_iota(jnp.int32, (rows, LANES), 0)

    def top_of(pair, level):
        return (pair * levels + level) * ROWS

    _, place_got, place_middle = placer(*sizes, z_ref, cor_ref)
    place_got(got_other_ref, 2 * index_y - 1, 1 - index_y)
    place_middle(got_ref, got_other_ref)

    def collect():
        position = lanes_of(cells) % WINDOW
        gap = WINDOW - cells + 3
        for pair in range(pairs):
            for slot, field in ((0, 0), (1, 2)):
                merged = jnp.zeros((cells, LANES), jnp.float32)
                for level in range(levels):
                    at = top_of(pair, level) + EDGE
                    here = position - 4 * level
                    wanted = ((here >= 0) & (here < 3)) | ((here >= gap) & (here < gap + 3))
                    shift = (4 * level - (MARGIN + cells - 3)) % LANES
                    lines = pltpu.roll(z_ref[field, at : at + cells], shift, 1)
                    merged = jnp.where(wanted, lines, merged)
                merged = jnp.concatenate(
                    [merged, jnp.zeros((LANES - cells, LANES), jnp.float32)], axis=0
                )
                flip = 2 * pair + slot
                flip_ref[flip] = merged.T
                for odd in range(2):
                    for side in (2, 3):
                        if side == 3:
                            base = odd * WINDOW
                        else:
                            base = ((odd + 1) % 2) * WINDOW + gap
                        store_ref[(2 * pair + odd) * 4 + side, slot * slots : (slot + 1) * slots] = (
                            flip_ref[flip, base : base + slots]
                        )
            for slot in range(2):
                for level in range(levels):
                    for side in (0, 1):
                        at = top_of(pair, level) + EDGE + (0 if side == 0 else cells - 3)
                        lines = z_ref[slot, at : at + 4]
                        row = slot * slots + 4 * level
                        for odd in range(2):
                            store_ref[(2 * pair + odd) * 4 + side, row : row + 4] = lines

    def fetch(face, side, position):
        at = levels + (face * 4 + side) * 3
        neighbour = table_ref[at].astype(jnp.int32)
        far_side = table_ref[at + 1].astype(jnp.int32)
        flipped = table_ref[at + 2].astype(jnp.int32)
        block = store_ref[neighbour * 4 + far_side]
        order = jnp.where(flipped == 1, cells - 1 - position, position)
        order = jnp.where((position >= 0) & (position < cells), order, 0)
        order = order + jnp.where(far_side < 2, MARGIN + WINDOW * (neighbour % 2), 0)
        block = jnp.take_along_axis(block, order, axis=1)
        turned = far_side % 2 == side % 2
        place = rows_of(8) % 4
        parts = []
        for part in range(4):
            lines = block[8 * part : 8 * part + 8]
            swapped = jnp.where(place == 0, pltpu.roll(lines, 6, 0), pltpu.roll(lines, 2, 0))
            parts.append(jnp.where(turned & (place != 1), swapped, lines))
        sign_here = 2 * (side % 2) - 1
        sign_there = 2 * (far_side % 2) - 1
        sign = (-sign_here * sign_there).astype(jnp.float32)
        return parts[:2], [sign * lines for lines in parts[2:]]

    def level_rows(parts, level, rows):
        at = 4 * (level % 2)
        return parts[level // 2][at : at + rows]

    def rim_rows(side):
        lane = lanes_of(2 * slots)
        left = lanes_of(8) < WINDOW
        for pair in range(pairs):
            first = fetch(2 * pair, side, lane - MARGIN)
            second = fetch(2 * pair + 1, side, lane - (MARGIN + WINDOW))
            for slot in range(2):
                both = [jnp.where(left, a, b) for a, b in zip(first[slot], second[slot])]
                for level in range(levels):
                    at = top_of(pair, level) + EDGE + (-3 if side == 0 else cells)
                    z_ref[slot, at : at + 3] = level_rows(both, level, 3)

    def put_tile(tile, parts, odd, side):
        for level in range(levels):
            if side == 3:
                at = odd * WINDOW + 16 * level
            else:
                at = ((odd + 1) % 2) * WINDOW + 16 * level + 13
            tile_ref[tile, at : at + 3] = level_rows(parts, level, 3)

    def put_columns(lines, field, start, pair):
        count = lines.shape[0]
        position = lanes_of(count) % WINDOW
        rim = ((position >= MARGIN - 3) & (position < MARGIN)) | (
            (position >= MARGIN + cells) & (position < MARGIN + cells + 3)
        )
        for level in range(levels):
            rolled = pltpu.roll(lines, (MARGIN + cells - 16 * level) % LANES, 1)
            at = pl.ds(start + top_of(pair, level) + EDGE, count)
            z_ref[field, at] = jnp.where(rim, rolled, z_ref[field, at])

    def rim_columns_all():
        for pair in range(pairs):
            for odd in range(2):
                for side in (2, 3):
                    for slot, parts in enumerate(fetch(2 * pair + odd, side, lanes_of(2 * slots))):
                        put_tile(2 * pair + slot, parts, odd, side)
            for slot, field in ((0, 0), (1, 2)):
                put_columns(tile_ref[2 * pair + slot].T[:cells], field, 0, pair)

    def rim_columns_own():
        lane = lanes_of(2 * slots)
        second = rows_of(2 * slots) >= slots
        for odd in range(2):
            for side in (2, 3):
                total = [jnp.zeros((8, LANES), jnp.float32)] * 2
                for pair in range(pairs):
                    local = lane - jnp.where(second, 8 * (pairs + pair), 8 * pair)
                    fetched = fetch(2 * pair + odd, side, index_x * cx + local)
                    for slot, parts in enumerate(fetched):
                        local = lanes_of(8) - 8 * (slot * pairs + pair)
                        here = (local >= 0) & (local < 8)
                        total = [jnp.where(here, a, b) for a, b in zip(parts, total)]
                put_tile(0, total, odd, side)
        turned = tile_ref[0].T
        for slot, field in ((0, 0), (1, 2)):
            for pair in range(pairs):
                at = 8 * (slot * pairs + pair)
                put_columns(turned[at : at + 8], field, index_x * cx, pair)

    def advance_rows(pair, level, start, count, before, rows):
        top = top_of(pair, level) + EDGE + start
        speed = table_ref[level]
        ahead = z_ref[0, pl.ds(top - before + 1, rows)]
        behind = z_ref[0, pl.ds(top - before - 1, rows)]
        east = z_ref[1, pl.ds(top - before, rows)]
        pred_ref[pl.ds(top - before, rows)] = east - speed * (0.5 * (ahead - behind))
        height = z_ref[0, pl.ds(top, count)]
        north_pred = z_ref[2, pl.ds(top, count)] - speed * (
            0.5 * (pltpu.roll(height, LANES - 1, 1) - pltpu.roll(height, 1, 1))
        )
        east_pred = pred_ref[pl.ds(top, count)]
        flux_east = 8.0 * (pred_ref[pl.ds(top + 1, count)] - pred_ref[pl.ds(top - 1, count)]) - (
            pred_ref[pl.ds(top + 2, count)] - pred_ref[pl.ds(top - 2, count)]
        )
        flux_north = 8.0 * (
            pltpu.roll(north_pred, LANES - 1, 1) - pltpu.roll(north_pred, 1, 1)
        ) - (pltpu.roll(north_pred, LANES - 2, 1) - pltpu.roll(north_pred, 2, 1))
        height = height - speed * ((flux_east + flux_north) * (1.0 / 12.0))
        turning = cor_ref[pair, pl.ds(start, count)]
        return height, east_pred + turning * north_pred, north_pred - turning * east_pred

    collect()
    rim_rows(0)
    rim_rows(1)
    rim_columns_all()
    for pair in range(pairs):
        for level in range(levels):
            at = top_of(pair, level) + EDGE
            for field, values in enumerate(advance_rows(pair, level, 0, cells, 4, cells + 8)):
                z_ref[field, at : at + cells] = values

    collect()

    @pl.when(index_x == 0)
    def _():
        rim_rows(0)

    @pl.when(index_x == count_x - 1)
    def _():
        rim_rows(1)

    rim_columns_own()
    for pair in range(pairs):
        for level in range(levels):
            fields = advance_rows(pair, level, index_x * cx, 8, 2, 16)
            at = 8 * (pair * levels + level)
            for field, values in enumerate(fields):
                for odd in range(2):
                    shift = LANES - (MARGIN + odd * WINDOW) - index_y * cy
                    result_ref[2 * field + odd, at : at + 8] = pltpu.roll(values, shift, 1)
    for field in range(3):
        for face in range(faces):
            for x in range(cx):
                rows = pl.ds((face // 2) * levels * 8 + x, levels, 8)
                out_ref[face, field, x] = result_ref[2 * field + face % 2, rows][:, :cy]


def fast_on_device(state, coriolis, wave_speed, edges):
    count_x = lax.axis_size("tx")
    faces, fields, levels, cx, cy = state.shape
    pairs = faces // 2
    group = pairs * levels
    cells = cx * count_x
    full_rows = fields * (cx // 2) * group + (cx // 2) * pairs
    full_rows = -(-full_rows // 8) * 8
    small_rows = unit_place(fields, 1, cx, group, 2 * cx)[0] + group
    swap, lines = pl.pallas_call(
        functools.partial(pack_kernel, cx, cy, count_x, full_rows, small_rows),
        out_shape=[
            jax.ShapeDtypeStruct((full_rows + 2 * small_rows, LANES), jnp.float32),
            jax.ShapeDtypeStruct((32, LANES), jnp.float32),
        ],
        in_specs=[pl.BlockSpec(memory_space=pltpu.HBM)] * 2,
        out_specs=[pl.BlockSpec(memory_space=pltpu.VMEM)] * 2,
        scratch_shapes=[
            pltpu.VMEM((faces, fields, cx, levels, cy), jnp.float32),
            pltpu.VMEM((faces, cx, cy), jnp.float32),
            pltpu.SemaphoreType.DMA((2,)),
        ],
        compiler_params=pltpu.CompilerParams(vmem_limit_bytes=VMEM_LIMIT),
        name="pack",
    )(jnp.swapaxes(state, 2, 3), coriolis)
    keep, middle = pl.pallas_call(
        functools.partial(keep_kernel, cx, cy, count_x, small_rows),
        out_shape=[
            jax.ShapeDtypeStruct((2 * small_rows, LANES), jnp.float32),
            jax.ShapeDtypeStruct((small_rows, LANES), jnp.float32),
        ],
        in_specs=[pl.BlockSpec(memory_space=pltpu.VMEM)] * 2,
        out_specs=[pl.BlockSpec(memory_space=pltpu.VMEM)] * 2,
        compiler_params=pltpu.CompilerParams(vmem_limit_bytes=SMALL_VMEM_LIMIT),
        name="keep",
    )(swap, lines)

    def moved(block, distance):
        pairs_of = []
        for index in range(count_x):
            for core in range(2):
                target = (index + distance * (1 - 2 * core)) % count_x
                pairs_of.append((2 * index + core, 2 * target + core))
        return lax.ppermute(block, ("tx", "ty"), pairs_of)

    def across(block):
        return lax.ppermute(block, "ty", [(0, 1), (1, 0)])

    other = across(swap)
    messages = pl.pallas_call(
        functools.partial(mix_kernel, full_rows, small_rows),
        out_shape=[
            jax.ShapeDtypeStruct((2 * rows, LANES), jnp.float32)
            for rows in (full_rows, small_rows, small_rows)
        ],
        in_specs=[pl.BlockSpec(memory_space=pltpu.VMEM)] * 3,
        out_specs=[pl.BlockSpec(memory_space=pltpu.VMEM)] * 3,
        compiler_params=pltpu.CompilerParams(vmem_limit_bytes=SMALL_VMEM_LIMIT),
        name="messages",
    )(swap, other, keep)
    got = [moved(block, place + 1) for place, block in enumerate(messages)]
    got = jnp.concatenate([*got, moved(middle, count_x // 2)])
    table = jnp.concatenate([wave_speed, edges.reshape(-1).astype(jnp.float32)])
    got, table = lax.optimization_barrier((got, table))
    passed = across(got)

    sizes = (cx, cy, count_x, full_rows, small_rows)
    state_rows = [
        jax.ShapeDtypeStruct((fields, group * ROWS + 8, LANES), jnp.float32),
        jax.ShapeDtypeStruct((pairs, cells + 8, LANES), jnp.float32),
    ]
    in_vmem = pl.BlockSpec(memory_space=pltpu.VMEM)
    params = pltpu.CompilerParams(vmem_limit_bytes=SMALL_VMEM_LIMIT)
    rows = pl.pallas_call(
        functools.partial(own_kernel, sizes),
        out_shape=state_rows,
        in_specs=[in_vmem] * 2,
        out_specs=[in_vmem] * 2,
        compiler_params=params,
        name="place_own",
    )(swap, other)
    rows = pl.pallas_call(
        functools.partial(got_kernel, sizes),
        out_shape=state_rows,
        in_specs=[in_vmem] * 3,
        out_specs=[in_vmem] * 2,
        input_output_aliases={1: 0, 2: 1},
        compiler_params=params,
        name="place_got",
    )(got, *rows)
    out, _, _ = pl.pallas_call(
        functools.partial(step_kernel, sizes),
        out_shape=[jax.ShapeDtypeStruct((faces, fields, cx, levels, cy), jnp.float32)]
        + state_rows,
        in_specs=[in_vmem] * 2 + [pl.BlockSpec(memory_space=pltpu.SMEM)] + [in_vmem] * 2,
        out_specs=[in_vmem] * 3,
        input_output_aliases={3: 1, 4: 2},
        scratch_shapes=[
            pltpu.VMEM((group * ROWS + 8, LANES), jnp.float32),
            pltpu.VMEM((faces * 4, 32, LANES), jnp.float32),
            pltpu.VMEM((faces, LANES, LANES), jnp.float32),
            pltpu.VMEM((faces, LANES, LANES), jnp.float32),
            pltpu.VMEM((2 * fields, 8 * group, LANES), jnp.float32),
        ],
        compiler_params=pltpu.CompilerParams(vmem_limit_bytes=VMEM_LIMIT),
        name="substeps",
    )(got, passed, table, *rows)
    return jnp.swapaxes(out, 2, 3)


def padded_2(block, sides, width):
    for axis, dim in sides:
        count = lax.axis_size(axis)
        forward = [(i, i + 1) for i in range(count - 1)]
        backward = [(target, source) for source, target in forward]
        low = lax.ppermute(
            lax.slice_in_dim(block, block.shape[dim] - width, None, axis=dim), axis, forward
        )
        high = lax.ppermute(lax.slice_in_dim(block, 0, width, axis=dim), axis, backward)
        block = jnp.concatenate([low, block, high], axis=dim)
    return block


def spread(block, axis, owner):
    block = jnp.where(lax.axis_index(axis) == owner, block, jnp.zeros_like(block))
    return lax.psum(block, axis)


def rotate_strip(strip_data, side_index, far_side, flipped):
    normal_part = jnp.where(far_side < 2, strip_data[1], strip_data[2])
    along_part = jnp.where(far_side < 2, strip_data[2], strip_data[1])
    sign_here = 2.0 * (side_index % 2) - 1.0
    sign_there = (2 * (far_side % 2) - 1).astype(jnp.float32)
    normal_part = -sign_here * sign_there * normal_part
    along_part = (1 - 2 * flipped).astype(jnp.float32) * along_part
    if side_index < 2:
        return jnp.stack([strip_data[0], normal_part, along_part])
    return jnp.stack([strip_data[0], along_part, normal_part])


def window_strip(store, side_pick, neighbour, flipped, start, width):
    full_length = store.shape[5]
    begin = jnp.where(flipped == 1, full_length - start - width, start)
    zero = jnp.zeros((), jnp.int32)
    sizes_here = (1, 1, store.shape[2], store.shape[3], store.shape[4], width)
    piece = lax.dynamic_slice(store, (side_pick, neighbour, zero, zero, zero, begin), sizes_here)[
        0, 0
    ]
    return jnp.where(flipped == 1, jnp.flip(piece, 3), piece)


def side_halo(edge_store, edges, face_index, side_index, start, width):
    neighbour = edges[face_index, side_index, 0]
    far_side = edges[face_index, side_index, 1]
    flipped = edges[face_index, side_index, 2]
    strip_data = window_strip(edge_store, far_side, neighbour, flipped, start, width)
    return rotate_strip(strip_data, side_index, far_side, flipped)


def advance(padded, wave_speed, coriolis_part, cells_x, cells_y):
    height = padded[..., 0, :, :, :]
    wind_east = padded[..., 1, :, :, :]
    wind_north = padded[..., 2, :, :, :]
    speed = wave_speed[:, None, None]
    east_pred = wind_east[..., 1 : cells_x + 5, 3 : cells_y + 3] - speed * (
        0.5
        * (
            height[..., 2 : cells_x + 6, 3 : cells_y + 3]
            - height[..., 0 : cells_x + 4, 3 : cells_y + 3]
        )
    )
    north_pred = wind_north[..., 3 : cells_x + 3, 1 : cells_y + 5] - speed * (
        0.5
        * (
            height[..., 3 : cells_x + 3, 2 : cells_y + 6]
            - height[..., 3 : cells_x + 3, 0 : cells_y + 4]
        )
    )
    flux_east = (
        8.0 * (east_pred[..., 3 : cells_x + 3, :] - east_pred[..., 1 : cells_x + 1, :])
        - (east_pred[..., 4 : cells_x + 4, :] - east_pred[..., 0:cells_x, :])
    ) / 12.0
    flux_north = (
        8.0 * (north_pred[..., 3 : cells_y + 3] - north_pred[..., 1 : cells_y + 1])
        - (north_pred[..., 4 : cells_y + 4] - north_pred[..., 0:cells_y])
    ) / 12.0
    height_new = height[..., 3 : cells_x + 3, 3 : cells_y + 3] - speed * (flux_east + flux_north)
    east_inner = east_pred[..., 2 : cells_x + 2, :]
    north_inner = north_pred[..., 2 : cells_y + 2]
    turning = coriolis_part[..., None, :, :]
    return jnp.stack(
        [height_new, east_inner + turning * north_inner, north_inner - turning * east_inner],
        axis=-4,
    )


def one_substep(state, coriolis, wave_speed, edges, count_x, count_y, index_x, index_y):
    faces = state.shape[0]
    cells_x = state.shape[3]
    cells_y = state.shape[4]
    padded = padded_2(state, (("tx", 3), ("ty", 4)), 3)
    west_rim = state[:, :, :, 0:3, :]
    east_rim = jnp.flip(state[:, :, :, cells_x - 3 :, :], 3)
    south_rim = jnp.swapaxes(state[:, :, :, :, 0:3], 3, 4)
    north_rim = jnp.swapaxes(jnp.flip(state[:, :, :, :, cells_y - 3 :], 4), 3, 4)
    west_part = spread(west_rim, "tx", 0)
    east_part = spread(east_rim, "tx", count_x - 1)
    west_full, east_full = (
        lax.all_gather(west_part, "ty", axis=4, tiled=True),
        lax.all_gather(east_part, "ty", axis=4, tiled=True),
    )
    south_row, north_row = (
        lax.all_gather(south_rim, "tx", axis=4, tiled=True),
        lax.all_gather(north_rim, "tx", axis=4, tiled=True),
    )
    south_all, north_all = (
        lax.all_gather(south_row, "ty", axis=0, tiled=True),
        lax.all_gather(north_row, "ty", axis=0, tiled=True),
    )
    south_full = south_all[0:faces]
    north_full = north_all[(count_y - 1) * faces : count_y * faces]
    edge_store = jnp.stack([west_full, east_full, south_full, north_full])
    halos = []
    for side_index in range(4):
        if side_index < 2:
            slabs = jnp.stack(
                [
                    side_halo(edge_store, edges, face_index, side_index, index_y * cells_y, cells_y)
                    for face_index in range(faces)
                ]
            )
        else:
            slabs = jnp.stack(
                [
                    side_halo(edge_store, edges, face_index, side_index, index_x * cells_x, cells_x)
                    for face_index in range(faces)
                ]
            )
        halos.append(slabs)
    west_region = padded[:, :, :, 0:3, 3 : cells_y + 3]
    padded = padded.at[:, :, :, 0:3, 3 : cells_y + 3].set(
        jnp.where(index_x == 0, jnp.flip(halos[0], 3), west_region)
    )
    east_region = padded[:, :, :, cells_x + 3 : cells_x + 6, 3 : cells_y + 3]
    padded = padded.at[:, :, :, cells_x + 3 : cells_x + 6, 3 : cells_y + 3].set(
        jnp.where(index_x == count_x - 1, halos[1], east_region)
    )
    south_region = padded[:, :, :, 3 : cells_x + 3, 0:3]
    padded = padded.at[:, :, :, 3 : cells_x + 3, 0:3].set(
        jnp.where(index_y == 0, jnp.swapaxes(jnp.flip(halos[2], 3), 3, 4), south_region)
    )
    north_region = padded[:, :, :, 3 : cells_x + 3, cells_y + 3 : cells_y + 6]
    padded = padded.at[:, :, :, 3 : cells_x + 3, cells_y + 3 : cells_y + 6].set(
        jnp.where(index_y == count_y - 1, jnp.swapaxes(halos[3], 3, 4), north_region)
    )
    return advance(padded, wave_speed, coriolis, cells_x, cells_y)


def on_device(state, coriolis, wave_speed, edges):
    count_x = lax.axis_size("tx")
    count_y = lax.axis_size("ty")
    index_x = lax.axis_index("tx")
    index_y = lax.axis_index("ty")
    for substep_index in range(SUBSTEPS):
        state = one_substep(state, coriolis, wave_speed, edges, count_x, count_y, index_x, index_y)
    return state


def fits(state):
    count_x = lax.axis_size("tx")
    faces, fields, levels, cells_x, cells_y = state.shape
    return (
        lax.axis_size("ty") == 2
        and faces % 2 == 0
        and levels == 4
        and cells_x == 6
        and cells_y == 24
        and count_x == 8
        and cells_x * count_x == 2 * cells_y
        and 2 * cells_y + 2 * MARGIN <= WINDOW
    )


def either(state, coriolis, wave_speed, edges):
    if fits(state):
        return fast_on_device(state, coriolis, wave_speed, edges)
    return on_device(state, coriolis, wave_speed, edges)


def solution(mesh):
    in_specs = (P("member", None, None, "tx", "ty"), P(None, "tx", "ty"), P(), P())
    out_specs = P("member", None, None, "tx", "ty")
    return jax.shard_map(
        either, mesh=mesh, in_specs=in_specs, out_specs=out_specs, check_vma=False
    )
```

```python
import functools

import jax
import jax.numpy as jnp
from jax import lax
from jax.experimental import pallas as pl
from jax.experimental.pallas import tpu as pltpu
from jax.sharding import PartitionSpec as P

SUBSTEPS = 2
LANES = 128
WINDOW = 64
MARGIN = 8
VMEM_LIMIT = 32 * 1024 * 1024
SMALL_VMEM_LIMIT = 8 * 1024 * 1024


def window_start(source, target, count_x, index_y, cx, cy, far):
    width = 2 * cx
    near = jnp.minimum(target, count_x - 1 - target)
    inward = jnp.minimum(cx * near - jnp.where(far, cx, cx // 2), cy - width)
    rim = (source == 0) | (source == count_x - 1)
    start = jnp.where(rim, jnp.maximum(inward, 0), 0)
    return jnp.where(index_y == 0, start, cy - width - start)


def windows(source, target, count_x, index_y, cx, cy):
    low_far = source == count_x - 1
    lower = window_start(source, target, count_x, index_y, cx, cy, low_far)
    upper = window_start(source, target, count_x, index_y, cx, cy, ~low_far)
    return lower, upper


def unit_place(field, x, cx, group, width):
    per_row = 60 // width
    index = field * cx + x
    return (index // per_row) * group, (index % per_row) * width


def pack_kernel(
    cx, cy, count_x, full_rows, small_rows, state_hbm, coriolis_hbm,
    swap_ref, line_ref, state_ref, coriolis_ref, sems,
):
    copies = [
        pltpu.make_async_copy(state_hbm, state_ref, sems.at[0]),
        pltpu.make_async_copy(coriolis_hbm, coriolis_ref, sems.at[1]),
    ]
    for copy in copies:
        copy.start()
    faces, fields = state_ref.shape[:2]
    levels = state_ref.shape[3]
    pairs = faces // 2
    group = pairs * levels
    half = cx // 2
    base = fields * half * group
    swap_ref[:full_rows] = jnp.zeros((full_rows, LANES), jnp.float32)
    line_ref[...] = jnp.zeros(line_ref.shape, jnp.float32)
    for copy in copies:
        copy.wait()
    for face in range(faces):
        for parity in range(2):
            lane = (face % 2) * WINDOW + MARGIN + parity * cy
            for xp in range(half):
                for field in range(fields):
                    row = field * half * group + xp * group + (face // 2) * levels
                    swap_ref[row : row + levels, lane : lane + cy] = state_ref[
                        face, field, 2 * xp + parity
                    ]
                x = 2 * xp + parity
                row = base + xp * pairs + face // 2
                swap_ref[row : row + 1, lane : lane + cy] = coriolis_ref[face, x : x + 1]
                row = (x // half) * 16 + (x % half) * pairs + face // 2
                lane_at = (face % 2) * WINDOW + MARGIN
                line_ref[row : row + 1, lane_at : lane_at + cy] = coriolis_ref[face, x : x + 1]
    sense = 1 - 2 * lax.axis_index("ty")
    for place, distance in enumerate((2, 3)):
        top = full_rows + place * small_rows
        put_chunk(cx, cy, count_x, swap_ref, line_ref, swap_ref, top, -sense * distance)


def put_chunk(cx, cy, count_x, block_ref, line_ref, out_ref, top, offset):
    pairs = 3
    group = 4 * pairs
    fields = 3
    half = cx // 2
    width = 2 * cx
    index_x = lax.axis_index("tx")
    index_y = lax.axis_index("ty")
    target = (index_x + offset + count_x) % count_x
    starts = windows(index_x, target, count_x, index_y, cx, cy)
    blocks = {}

    def put(row, lane, lines):
        position = lax.broadcasted_iota(jnp.int32, lines.shape, 1) % WINDOW
        here = (position >= lane) & (position < lane + width)
        blocks[row] = jnp.where(here, lines, blocks.get(row, jnp.zeros_like(lines)))

    for field in range(fields):
        for x in range(cx):
            row = field * half * group + (x // 2) * group
            at, lane = unit_place(field, x, cx, group, width)
            shift = lane - MARGIN - (x % 2) * cy - starts[x // half] + 2 * LANES
            put(at, lane, pltpu.roll(block_ref[row : row + group], shift % LANES, 1))
    for part in range(2):
        at, lane = unit_place(fields, part, cx, group, width)
        shift = lane - MARGIN - starts[part] + 2 * LANES
        lines = line_ref[16 * part : 16 * part + group]
        put(at, lane, pltpu.roll(lines, shift % LANES, 1))
    for row, lines in blocks.items():
        out_ref[top + row : top + row + group] = lines


def keep_kernel(cx, cy, count_x, small_rows, swap_ref, line_ref, keep_ref, middle_ref):
    sense = 1 - 2 * lax.axis_index("ty")
    put_chunk(cx, cy, count_x, swap_ref, line_ref, middle_ref, 0, count_x // 2)
    for place, distance in enumerate((2, 3)):
        top = place * small_rows
        put_chunk(cx, cy, count_x, swap_ref, line_ref, keep_ref, top, sense * distance)


def mix_kernel(full_rows, small_rows, swap_ref, other_ref, keep_ref, near_ref, second_ref, third_ref):
    near_ref[:full_rows] = swap_ref[:full_rows]
    near_ref[full_rows:] = other_ref[:full_rows]
    for place, far_ref in enumerate((second_ref, third_ref)):
        at = place * small_rows
        far_ref[:small_rows] = keep_ref[at : at + small_rows]
        at += full_rows
        far_ref[small_rows:] = other_ref[at : at + small_rows]


def placer(cx, cy, count_x, full_rows, small_rows, z_ref, cor_ref):
    fields = z_ref.shape[0]
    levels = 4
    group = z_ref.shape[1] // (cx * count_x + 8)
    pairs = group // levels
    half = cx // 2
    chunk = cx * group
    index_x = lax.axis_index("tx")
    index_y = lax.axis_index("ty")
    south_half = lax.broadcasted_iota(jnp.int32, (group, LANES), 1) % WINDOW < MARGIN + cy
    south_is_own = index_y == 0
    own_half = south_half == south_is_own

    def row_of(x):
        return (x + 4) * group

    def from_owner(offset):
        source = (index_x - offset + 2 * count_x) % count_x
        return source, pl.multiple_of(source * chunk, 8)

    def put_coriolis(start, x, values, at):
        for pair in range(pairs):
            line = values[at + pair : at + pair + 1]
            rows = pl.ds(start + x * group + pair * levels, levels)
            cor_ref[rows] = jnp.broadcast_to(line, (levels, LANES))

    def put_block(start, lines_of):
        base = fields * half * group
        for field in range(fields):
            for xp in range(half):
                even, odd = lines_of(field * half * group + xp * group, group)
                z_ref[field, pl.ds(start + row_of(2 * xp), group)] = even
                z_ref[field, pl.ds(start + row_of(2 * xp + 1), group)] = odd
        for parity, values in enumerate(lines_of(base, half * pairs)):
            for xp in range(half):
                put_coriolis(start, 2 * xp + parity, values, xp * pairs)

    def put_distant(source, start, lines_of):
        starts_south = windows(source, index_x, count_x, 0, cx, cy)
        starts_north = windows(source, index_x, count_x, 1, cx, cy)

        def lines_at(field, x, part):
            at, lane = unit_place(field, x, cx, group, 2 * cx)
            south_shift = (MARGIN + starts_south[part] - lane + LANES) % LANES
            north_shift = (MARGIN + cy + starts_north[part] - lane + LANES) % LANES
            return lines_of(at, south_shift, north_shift)

        for field in range(fields):
            for x in range(cx):
                z_ref[field, pl.ds(start + row_of(x), group)] = lines_at(field, x, x // half)
        for part in range(2):
            values = lines_at(fields, part, part)
            for x in range(half):
                put_coriolis(start, part * half + x, values, x * pairs)

    def place_own(own_ref, other_ref):
        def own_lines(row, rows):
            mine = own_ref[row : row + rows]
            theirs = other_ref[row : row + rows]
            up, down = index_y * cy, (1 - index_y) * cy
            keep = own_half[:rows]
            even = jnp.where(keep, pltpu.roll(mine, up, 1), pltpu.roll(theirs, down, 1))
            mine = pltpu.roll(mine, (LANES - down) % LANES, 1)
            theirs = pltpu.roll(theirs, (LANES - up) % LANES, 1)
            return even, jnp.where(keep, mine, theirs)

        put_block(from_owner(0)[1], own_lines)

    def place_got(block_ref, toward, south_first):
        south_top = pl.multiple_of(south_first * full_rows, 8)
        north_top = pl.multiple_of((1 - south_first) * full_rows, 8)

        def near_lines(row, rows):
            south = block_ref[pl.ds(south_top + row, rows)]
            north = block_ref[pl.ds(north_top + row, rows)]
            low = south_half[:rows]
            even = jnp.where(low, south, pltpu.roll(north, cy, 1))
            return even, jnp.where(low, pltpu.roll(south, LANES - cy, 1), north)

        put_block(from_owner(toward)[1], near_lines)
        for place, distance in enumerate((2, 3)):
            top = 2 * full_rows + 2 * place * small_rows
            south_at = pl.multiple_of(top + south_first * small_rows, 8)
            north_at = pl.multiple_of(top + (1 - south_first) * small_rows, 8)

            def far_lines(at, south_shift, north_shift, south_at=south_at, north_at=north_at):
                south = pltpu.roll(block_ref[pl.ds(south_at + at, group)], south_shift, 1)
                north = pltpu.roll(block_ref[pl.ds(north_at + at, group)], north_shift, 1)
                return jnp.where(south_half, south, north)

            put_distant(*from_owner(toward * distance), far_lines)

    def place_middle(got_ref, got_other_ref):
        def middle_lines(at, south_shift, north_shift):
            row = 2 * full_rows + 4 * small_rows + at
            mine_shift = jnp.where(south_is_own, south_shift, north_shift)
            other_shift = jnp.where(south_is_own, north_shift, south_shift)
            mine = pltpu.roll(got_ref[row : row + group], mine_shift, 1)
            theirs = pltpu.roll(got_other_ref[row : row + group], other_shift, 1)
            return jnp.where(own_half, mine, theirs)

        put_distant(*from_owner(count_x // 2), middle_lines)

    return place_own, place_got, place_middle


def own_kernel(sizes, own_ref, other_ref, z_ref, cor_ref):
    placer(*sizes, z_ref, cor_ref)[0](own_ref, other_ref)


def got_kernel(sizes, got_ref, z_in, cor_in, z_ref, cor_ref):
    index_y = lax.axis_index("ty")
    placer(*sizes, z_ref, cor_ref)[1](got_ref, 1 - 2 * index_y, index_y)


def step_kernel(
    sizes, got_ref, got_other_ref, table_in, z_in, cor_in, out_hbm, z_ref, cor_ref,
    pred_ref, store_ref, tile_ref, flip_ref, speed_ref, table_ref, out_ref, sems,
):
    table_copy = pltpu.make_async_copy(table_in, table_ref, sems.at[0])
    table_copy.start()
    cx, cy, count_x = sizes[:3]
    levels = 4
    slots = 16
    cells = cx * count_x
    faces = store_ref.shape[0] // 4
    pairs = faces // 2
    group = pairs * levels
    chunk = cx * group
    index_x = lax.axis_index("tx")
    index_y = lax.axis_index("ty")

    def row_of(x):
        return (x + 4) * group

    def lanes_of(rows):
        return lax.broadcasted_iota(jnp.int32, (rows, LANES), 1)

    _, place_got, place_middle = placer(*sizes, z_ref, cor_ref)
    place_got(got_other_ref, 2 * index_y - 1, 1 - index_y)
    place_middle(got_ref, got_other_ref)

    table_copy.wait()
    level_of = lax.broadcasted_iota(jnp.int32, speed_ref.shape, 0) % levels
    speeds = jnp.full(speed_ref.shape, table_ref[0], jnp.float32)
    for index in range(1, levels):
        speeds = jnp.where(level_of == index, table_ref[index], speeds)
    speed_ref[...] = speeds

    def collect():
        position = lanes_of(cells) % WINDOW
        gap = WINDOW - cells + 3
        wide = gap + 3 * levels
        for pair in range(pairs):
            merged = jnp.zeros((cells, LANES), jnp.float32)
            for slot, field in ((0, 0), (1, 2)):
                for level in range(levels):
                    lines = z_ref[field, pl.ds(row_of(0) + pair * levels + level, cells, group)]
                    offset = slot * wide + 3 * level
                    here = position - offset
                    wanted = ((here >= 0) & (here < 3)) | ((here >= gap) & (here < gap + 3))
                    shift = (offset - (MARGIN + cells - 3)) % LANES
                    merged = jnp.where(wanted, pltpu.roll(lines, shift, 1), merged)
            flip_ref[pair, :, :cells] = merged.T
            for slot in range(2):
                for side in (2, 3):
                    for odd in range(2):
                        for depth in range(3):
                            base = slot * wide
                            if side == 3:
                                base += odd * WINDOW + 2 - depth
                            else:
                                base += ((odd + 1) % 2) * WINDOW + gap + depth
                            at = slot * slots + depth * levels
                            store_ref[(2 * pair + odd) * 4 + side, at : at + levels] = flip_ref[
                                pair, pl.ds(base, levels, 3)
                            ]
            for slot in range(2):
                for side in (0, 1):
                    for depth in range(3):
                        x = depth if side == 0 else cells - 1 - depth
                        row = row_of(x) + pair * levels
                        lines = z_ref[slot, row : row + levels]
                        at = slot * slots + depth * levels
                        for odd in range(2):
                            store_ref[(2 * pair + odd) * 4 + side, at : at + levels] = pltpu.roll(
                                lines, LANES - MARGIN - odd * WINDOW, 1
                            )

    def fetch(face, side, position):
        at = levels + (face * 4 + side) * 3
        neighbour = table_ref[at].astype(jnp.int32)
        far_side = table_ref[at + 1].astype(jnp.int32)
        flipped = table_ref[at + 2].astype(jnp.int32)
        block = store_ref[neighbour * 4 + far_side]
        order = jnp.where(flipped == 1, cells - 1 - position, position)
        order = jnp.where((position >= 0) & (position < cells), order, 0)
        block = jnp.take_along_axis(block, order, axis=1)
        sign_here = 2 * (side % 2) - 1
        sign_there = 2 * (far_side % 2) - 1
        sign = (-sign_here * sign_there).astype(jnp.float32)
        normal = lax.broadcasted_iota(jnp.int32, block.shape, 0) >= slots
        return jnp.where(normal, sign * block, block)

    def rim_rows(side):
        lane = lanes_of(2 * slots)
        for pair in range(pairs):
            first = fetch(2 * pair, side, lane - MARGIN)
            second = fetch(2 * pair + 1, side, lane - (MARGIN + WINDOW))
            both = jnp.where(lane < WINDOW, first, second)
            for slot in range(2):
                for depth in range(3):
                    x = -1 - depth if side == 0 else cells + depth
                    at = slot * slots + depth * levels
                    row = row_of(x) + pair * levels
                    z_ref[slot, row : row + levels] = both[at : at + levels]

    wide = WINDOW - cells - 3 + 3 * levels

    def tile_rows(odd, side, depth, base=0):
        if side == 3:
            return pl.ds(base + odd * WINDOW + depth, levels, 3)
        return pl.ds(base + ((odd + 1) % 2) * WINDOW + wide - 3 * levels + 2 - depth, levels, 3)

    def put_columns(lines, field, start, pair, base=0):
        count = lines.shape[0]
        position = lanes_of(count) % WINDOW
        rim = ((position >= MARGIN - 3) & (position < MARGIN)) | (
            (position >= MARGIN + cells) & (position < MARGIN + cells + 3)
        )
        for level in range(levels):
            rolled = pltpu.roll(lines, (MARGIN + cells - base - 3 * level) % LANES, 1)
            at = pl.ds(row_of(start) + pair * levels + level, count, group)
            z_ref[field, at] = jnp.where(rim, rolled, z_ref[field, at])

    def rim_columns_all():
        for pair in range(pairs):
            for odd in range(2):
                for side in (2, 3):
                    block = fetch(2 * pair + odd, side, lanes_of(2 * slots))
                    for slot in range(2):
                        for depth in range(3):
                            at = slot * slots + depth * levels
                            rows = tile_rows(odd, side, depth, slot * wide)
                            tile_ref[pair, rows] = block[at : at + levels]
            turned = tile_ref[pair].T[:cells]
            for slot, field in ((0, 0), (1, 2)):
                put_columns(turned, field, 0, pair, slot * wide)

    def rim_columns_own():
        lane = lanes_of(2 * slots)
        second = lax.broadcasted_iota(jnp.int32, lane.shape, 0) >= slots
        for odd in range(2):
            for side in (2, 3):
                total = jnp.zeros((slots, LANES), jnp.float32)
                for pair in range(pairs):
                    local = lane - jnp.where(second, 8 * (pairs + pair), 8 * pair)
                    block = fetch(2 * pair + odd, side, index_x * cx + local)
                    block = jnp.where((local >= 0) & (local < 8), block, 0.0)
                    total = total + block[:slots] + block[slots:]
                for depth in range(3):
                    at = depth * levels
                    tile_ref[0, tile_rows(odd, side, depth)] = total[at : at + levels]
        turned = tile_ref[0].T
        for slot, field in ((0, 0), (1, 2)):
            for pair in range(pairs):
                at = 8 * (slot * pairs + pair)
                put_columns(turned[at : at + cx], field, index_x * cx, pair)

    def predict(at, rows):
        speed = speed_ref[:rows]
        ahead = z_ref[0, pl.ds(at + group, rows)]
        behind = z_ref[0, pl.ds(at - group, rows)]
        pred_ref[pl.ds(at, rows)] = z_ref[1, pl.ds(at, rows)] - speed * (0.5 * (ahead - behind))

    def update(at, rows):
        speed = speed_ref[:rows]
        height = z_ref[0, pl.ds(at, rows)]
        north_pred = z_ref[2, pl.ds(at, rows)] - speed * (
            0.5 * (pltpu.roll(height, LANES - 1, 1) - pltpu.roll(height, 1, 1))
        )
        east_pred = pred_ref[pl.ds(at, rows)]
        flux_east = 8.0 * (
            pred_ref[pl.ds(at + group, rows)] - pred_ref[pl.ds(at - group, rows)]
        ) - (pred_ref[pl.ds(at + 2 * group, rows)] - pred_ref[pl.ds(at - 2 * group, rows)])
        flux_north = 8.0 * (
            pltpu.roll(north_pred, LANES - 1, 1) - pltpu.roll(north_pred, 1, 1)
        ) - (pltpu.roll(north_pred, LANES - 2, 1) - pltpu.roll(north_pred, 2, 1))
        height = height - speed * ((flux_east + flux_north) * (1.0 / 12.0))
        turning = cor_ref[pl.ds(at - row_of(0), rows)]
        return height, east_pred + turning * north_pred, north_pred - turning * east_pred

    collect()
    rim_rows(0)
    rim_rows(1)
    rim_columns_all()
    for first in range(-2, cells + 2, 4):
        predict(row_of(first), 4 * group)
    for index in range(count_x):
        at = row_of(0) + index * chunk
        for field, values in enumerate(update(at, chunk)):
            z_ref[field, at : at + chunk] = values

    collect()

    @pl.when(index_x == 0)
    def _():
        rim_rows(0)

    @pl.when(index_x == count_x - 1)
    def _():
        rim_rows(1)

    rim_columns_own()
    at = pl.multiple_of(row_of(0) + index_x * chunk, 8)
    predict(at - 2 * group, chunk + 4 * group)
    copies = []
    for field, values in enumerate(update(at, chunk)):
        for odd in range(2):
            shift = LANES - (MARGIN + odd * WINDOW) - index_y * cy
            rolled = pltpu.roll(values, shift, 1)
            for x in range(cx):
                for pair in range(pairs):
                    row = x * group + pair * levels
                    out_ref[field, 2 * pair + odd, x] = rolled[row : row + levels, :cy]
        copy = pltpu.make_async_copy(out_ref.at[field], out_hbm.at[:, field], sems.at[1 + field])
        copy.start()
        copies.append(copy)
    for copy in copies:
        copy.wait()


def fast_on_device(state, coriolis, wave_speed, edges):
    count_x = lax.axis_size("tx")
    faces, fields, levels, cx, cy = state.shape
    pairs = faces // 2
    group = pairs * levels
    cells = cx * count_x
    full_rows = fields * (cx // 2) * group + (cx // 2) * pairs
    full_rows = -(-full_rows // 8) * 8
    small_rows = unit_place(fields, 1, cx, group, 2 * cx)[0] + group
    swap, lines = pl.pallas_call(
        functools.partial(pack_kernel, cx, cy, count_x, full_rows, small_rows),
        out_shape=[
            jax.ShapeDtypeStruct((full_rows + 2 * small_rows, LANES), jnp.float32),
            jax.ShapeDtypeStruct((32, LANES), jnp.float32),
        ],
        in_specs=[pl.BlockSpec(memory_space=pltpu.HBM)] * 2,
        out_specs=[pl.BlockSpec(memory_space=pltpu.VMEM)] * 2,
        scratch_shapes=[
            pltpu.VMEM((faces, fields, cx, levels, cy), jnp.float32),
            pltpu.VMEM((faces, cx, cy), jnp.float32),
            pltpu.SemaphoreType.DMA((2,)),
        ],
        compiler_params=pltpu.CompilerParams(vmem_limit_bytes=VMEM_LIMIT),
        name="pack",
    )(jnp.swapaxes(state, 2, 3), coriolis)
    keep, middle = pl.pallas_call(
        functools.partial(keep_kernel, cx, cy, count_x, small_rows),
        out_shape=[
            jax.ShapeDtypeStruct((2 * small_rows, LANES), jnp.float32),
            jax.ShapeDtypeStruct((small_rows, LANES), jnp.float32),
        ],
        in_specs=[pl.BlockSpec(memory_space=pltpu.VMEM)] * 2,
        out_specs=[pl.BlockSpec(memory_space=pltpu.VMEM)] * 2,
        compiler_params=pltpu.CompilerParams(vmem_limit_bytes=SMALL_VMEM_LIMIT),
        name="keep",
    )(swap, lines)

    def moved(block, distance):
        pairs_of = []
        for index in range(count_x):
            for core in range(2):
                target = (index + distance * (1 - 2 * core)) % count_x
                pairs_of.append((2 * index + core, 2 * target + core))
        return lax.ppermute(block, ("tx", "ty"), pairs_of)

    def across(block):
        return lax.ppermute(block, "ty", [(0, 1), (1, 0)])

    other = across(swap)
    messages = pl.pallas_call(
        functools.partial(mix_kernel, full_rows, small_rows),
        out_shape=[
            jax.ShapeDtypeStruct((2 * rows, LANES), jnp.float32)
            for rows in (full_rows, small_rows, small_rows)
        ],
        in_specs=[pl.BlockSpec(memory_space=pltpu.VMEM)] * 3,
        out_specs=[pl.BlockSpec(memory_space=pltpu.VMEM)] * 3,
        compiler_params=pltpu.CompilerParams(vmem_limit_bytes=SMALL_VMEM_LIMIT),
        name="messages",
    )(swap, other, keep)
    got = [moved(block, place + 1) for place, block in enumerate(messages)]
    got = jnp.concatenate([*got, moved(middle, count_x // 2)])
    table = jnp.concatenate([wave_speed, edges.reshape(-1).astype(jnp.float32)])
    got, table = lax.optimization_barrier((got, table))
    passed = across(got)

    sizes = (cx, cy, count_x, full_rows, small_rows)
    state_rows = [
        jax.ShapeDtypeStruct((fields, (cells + 8) * group, LANES), jnp.float32),
        jax.ShapeDtypeStruct((cells * group, LANES), jnp.float32),
    ]
    in_vmem = pl.BlockSpec(memory_space=pltpu.VMEM)
    params = pltpu.CompilerParams(vmem_limit_bytes=SMALL_VMEM_LIMIT)
    rows = pl.pallas_call(
        functools.partial(own_kernel, sizes),
        out_shape=state_rows,
        in_specs=[in_vmem] * 2,
        out_specs=[in_vmem] * 2,
        compiler_params=params,
        name="place_own",
    )(swap, other)
    rows = pl.pallas_call(
        functools.partial(got_kernel, sizes),
        out_shape=state_rows,
        in_specs=[in_vmem] * 3,
        out_specs=[in_vmem] * 2,
        input_output_aliases={1: 0, 2: 1},
        compiler_params=params,
        name="place_got",
    )(got, *rows)
    out, _, _ = pl.pallas_call(
        functools.partial(step_kernel, sizes),
        out_shape=[jax.ShapeDtypeStruct((faces, fields, cx, levels, cy), jnp.float32)]
        + state_rows,
        in_specs=[in_vmem] * 5,
        out_specs=[pl.BlockSpec(memory_space=pltpu.HBM)] + [in_vmem] * 2,
        input_output_aliases={3: 1, 4: 2},
        scratch_shapes=[
            pltpu.VMEM(((cells + 8) * group, LANES), jnp.float32),
            pltpu.VMEM((faces * 4, 32, LANES), jnp.float32),
            pltpu.VMEM((pairs, LANES, LANES), jnp.float32),
            pltpu.VMEM((pairs, LANES, LANES), jnp.float32),
            pltpu.VMEM(((cx + 4) * group, LANES), jnp.float32),
            pltpu.SMEM(table.shape, jnp.float32),
            pltpu.VMEM((fields, faces, cx, levels, cy), jnp.float32),
            pltpu.SemaphoreType.DMA((1 + fields,)),
        ],
        compiler_params=pltpu.CompilerParams(vmem_limit_bytes=VMEM_LIMIT),
        name="substeps",
    )(got, passed, table, *rows)
    return jnp.swapaxes(out, 2, 3)


def padded_2(block, sides, width):
    for axis, dim in sides:
        count = lax.axis_size(axis)
        forward = [(i, i + 1) for i in range(count - 1)]
        backward = [(target, source) for source, target in forward]
        low = lax.ppermute(
            lax.slice_in_dim(block, block.shape[dim] - width, None, axis=dim), axis, forward
        )
        high = lax.ppermute(lax.slice_in_dim(block, 0, width, axis=dim), axis, backward)
        block = jnp.concatenate([low, block, high], axis=dim)
    return block


def spread(block, axis, owner):
    block = jnp.where(lax.axis_index(axis) == owner, block, jnp.zeros_like(block))
    return lax.psum(block, axis)


def rotate_strip(strip_data, side_index, far_side, flipped):
    normal_part = jnp.where(far_side < 2, strip_data[1], strip_data[2])
    along_part = jnp.where(far_side < 2, strip_data[2], strip_data[1])
    sign_here = 2.0 * (side_index % 2) - 1.0
    sign_there = (2 * (far_side % 2) - 1).astype(jnp.float32)
    normal_part = -sign_here * sign_there * normal_part
    along_part = (1 - 2 * flipped).astype(jnp.float32) * along_part
    if side_index < 2:
        return jnp.stack([strip_data[0], normal_part, along_part])
    return jnp.stack([strip_data[0], along_part, normal_part])


def window_strip(store, side_pick, neighbour, flipped, start, width):
    full_length = store.shape[5]
    begin = jnp.where(flipped == 1, full_length - start - width, start)
    zero = jnp.zeros((), jnp.int32)
    sizes_here = (1, 1, store.shape[2], store.shape[3], store.shape[4], width)
    piece = lax.dynamic_slice(store, (side_pick, neighbour, zero, zero, zero, begin), sizes_here)[
        0, 0
    ]
    return jnp.where(flipped == 1, jnp.flip(piece, 3), piece)


def side_halo(edge_store, edges, face_index, side_index, start, width):
    neighbour = edges[face_index, side_index, 0]
    far_side = edges[face_index, side_index, 1]
    flipped = edges[face_index, side_index, 2]
    strip_data = window_strip(edge_store, far_side, neighbour, flipped, start, width)
    return rotate_strip(strip_data, side_index, far_side, flipped)


def advance(padded, wave_speed, coriolis_part, cells_x, cells_y):
    height = padded[..., 0, :, :, :]
    wind_east = padded[..., 1, :, :, :]
    wind_north = padded[..., 2, :, :, :]
    speed = wave_speed[:, None, None]
    east_pred = wind_east[..., 1 : cells_x + 5, 3 : cells_y + 3] - speed * (
        0.5
        * (
            height[..., 2 : cells_x + 6, 3 : cells_y + 3]
            - height[..., 0 : cells_x + 4, 3 : cells_y + 3]
        )
    )
    north_pred = wind_north[..., 3 : cells_x + 3, 1 : cells_y + 5] - speed * (
        0.5
        * (
            height[..., 3 : cells_x + 3, 2 : cells_y + 6]
            - height[..., 3 : cells_x + 3, 0 : cells_y + 4]
        )
    )
    flux_east = (
        8.0 * (east_pred[..., 3 : cells_x + 3, :] - east_pred[..., 1 : cells_x + 1, :])
        - (east_pred[..., 4 : cells_x + 4, :] - east_pred[..., 0:cells_x, :])
    ) / 12.0
    flux_north = (
        8.0 * (north_pred[..., 3 : cells_y + 3] - north_pred[..., 1 : cells_y + 1])
        - (north_pred[..., 4 : cells_y + 4] - north_pred[..., 0:cells_y])
    ) / 12.0
    height_new = height[..., 3 : cells_x + 3, 3 : cells_y + 3] - speed * (flux_east + flux_north)
    east_inner = east_pred[..., 2 : cells_x + 2, :]
    north_inner = north_pred[..., 2 : cells_y + 2]
    turning = coriolis_part[..., None, :, :]
    return jnp.stack(
        [height_new, east_inner + turning * north_inner, north_inner - turning * east_inner],
        axis=-4,
    )


def one_substep(state, coriolis, wave_speed, edges, count_x, count_y, index_x, index_y):
    faces = state.shape[0]
    cells_x = state.shape[3]
    cells_y = state.shape[4]
    padded = padded_2(state, (("tx", 3), ("ty", 4)), 3)
    west_rim = state[:, :, :, 0:3, :]
    east_rim = jnp.flip(state[:, :, :, cells_x - 3 :, :], 3)
    south_rim = jnp.swapaxes(state[:, :, :, :, 0:3], 3, 4)
    north_rim = jnp.swapaxes(jnp.flip(state[:, :, :, :, cells_y - 3 :], 4), 3, 4)
    west_part = spread(west_rim, "tx", 0)
    east_part = spread(east_rim, "tx", count_x - 1)
    west_full, east_full = (
        lax.all_gather(west_part, "ty", axis=4, tiled=True),
        lax.all_gather(east_part, "ty", axis=4, tiled=True),
    )
    south_row, north_row = (
        lax.all_gather(south_rim, "tx", axis=4, tiled=True),
        lax.all_gather(north_rim, "tx", axis=4, tiled=True),
    )
    south_all, north_all = (
        lax.all_gather(south_row, "ty", axis=0, tiled=True),
        lax.all_gather(north_row, "ty", axis=0, tiled=True),
    )
    south_full = south_all[0:faces]
    north_full = north_all[(count_y - 1) * faces : count_y * faces]
    edge_store = jnp.stack([west_full, east_full, south_full, north_full])
    halos = []
    for side_index in range(4):
        if side_index < 2:
            slabs = jnp.stack(
                [
                    side_halo(edge_store, edges, face_index, side_index, index_y * cells_y, cells_y)
                    for face_index in range(faces)
                ]
            )
        else:
            slabs = jnp.stack(
                [
                    side_halo(edge_store, edges, face_index, side_index, index_x * cells_x, cells_x)
                    for face_index in range(faces)
                ]
            )
        halos.append(slabs)
    west_region = padded[:, :, :, 0:3, 3 : cells_y + 3]
    padded = padded.at[:, :, :, 0:3, 3 : cells_y + 3].set(
        jnp.where(index_x == 0, jnp.flip(halos[0], 3), west_region)
    )
    east_region = padded[:, :, :, cells_x + 3 : cells_x + 6, 3 : cells_y + 3]
    padded = padded.at[:, :, :, cells_x + 3 : cells_x + 6, 3 : cells_y + 3].set(
        jnp.where(index_x == count_x - 1, halos[1], east_region)
    )
    south_region = padded[:, :, :, 3 : cells_x + 3, 0:3]
    padded = padded.at[:, :, :, 3 : cells_x + 3, 0:3].set(
        jnp.where(index_y == 0, jnp.swapaxes(jnp.flip(halos[2], 3), 3, 4), south_region)
    )
    north_region = padded[:, :, :, 3 : cells_x + 3, cells_y + 3 : cells_y + 6]
    padded = padded.at[:, :, :, 3 : cells_x + 3, cells_y + 3 : cells_y + 6].set(
        jnp.where(index_y == count_y - 1, jnp.swapaxes(halos[3], 3, 4), north_region)
    )
    return advance(padded, wave_speed, coriolis, cells_x, cells_y)


def on_device(state, coriolis, wave_speed, edges):
    count_x = lax.axis_size("tx")
    count_y = lax.axis_size("ty")
    index_x = lax.axis_index("tx")
    index_y = lax.axis_index("ty")
    for substep_index in range(SUBSTEPS):
        state = one_substep(state, coriolis, wave_speed, edges, count_x, count_y, index_x, index_y)
    return state


def fits(state):
    count_x = lax.axis_size("tx")
    faces, fields, levels, cells_x, cells_y = state.shape
    return (
        lax.axis_size("ty") == 2
        and faces % 2 == 0
        and levels == 4
        and cells_x == 6
        and cells_y == 24
        and count_x == 8
        and cells_x * count_x == 2 * cells_y
        and 2 * cells_y + 2 * MARGIN <= WINDOW
    )


def either(state, coriolis, wave_speed, edges):
    if fits(state):
        return fast_on_device(state, coriolis, wave_speed, edges)
    return on_device(state, coriolis, wave_speed, edges)


def solution(mesh):
    in_specs = (P("member", None, None, "tx", "ty"), P(None, "tx", "ty"), P(), P())
    out_specs = P("member", None, None, "tx", "ty")
    return jax.shard_map(
        either, mesh=mesh, in_specs=in_specs, out_specs=out_specs, check_vma=False
    )
```

```python
import functools

import jax
import jax.numpy as jnp
from jax import lax
from jax.experimental import pallas as pl
from jax.experimental.pallas import tpu as pltpu
from jax.sharding import PartitionSpec as P

SUBSTEPS = 2
LANES = 128
WINDOW = 64
MARGIN = 8
VMEM_LIMIT = 32 * 1024 * 1024
SMALL_VMEM_LIMIT = 8 * 1024 * 1024


def window_start(source, target, count_x, index_y, cx, cy, far):
    width = 2 * cx
    near = jnp.minimum(target, count_x - 1 - target)
    inward = jnp.minimum(cx * near - jnp.where(far, cx, cx // 2), cy - width)
    rim = (source == 0) | (source == count_x - 1)
    start = jnp.where(rim, jnp.maximum(inward, 0), 0)
    return jnp.where(index_y == 0, start, cy - width - start)


def windows(source, target, count_x, index_y, cx, cy):
    low_far = source == count_x - 1
    lower = window_start(source, target, count_x, index_y, cx, cy, low_far)
    upper = window_start(source, target, count_x, index_y, cx, cy, ~low_far)
    return lower, upper


def unit_place(field, x, cx, group, width):
    per_row = 60 // width
    index = field * cx + x
    return (index // per_row) * group, (index % per_row) * width


def pack_kernel(
    cx, cy, count_x, full_rows, small_rows, state_hbm, coriolis_hbm,
    swap_ref, line_ref, state_ref, coriolis_ref, sems,
):
    copies = [
        pltpu.make_async_copy(state_hbm, state_ref, sems.at[0]),
        pltpu.make_async_copy(coriolis_hbm, coriolis_ref, sems.at[1]),
    ]
    for copy in copies:
        copy.start()
    faces, fields = state_ref.shape[:2]
    levels = state_ref.shape[3]
    pairs = faces // 2
    group = pairs * levels
    half = cx // 2
    base = fields * half * group
    swap_ref[:full_rows] = jnp.zeros((full_rows, LANES), jnp.float32)
    line_ref[...] = jnp.zeros(line_ref.shape, jnp.float32)
    for copy in copies:
        copy.wait()
    for face in range(faces):
        for parity in range(2):
            lane = (face % 2) * WINDOW + MARGIN + parity * cy
            for xp in range(half):
                for field in range(fields):
                    row = field * half * group + xp * group + (face // 2) * levels
                    swap_ref[row : row + levels, lane : lane + cy] = state_ref[
                        face, field, 2 * xp + parity
                    ]
                x = 2 * xp + parity
                row = base + xp * pairs + face // 2
                swap_ref[row : row + 1, lane : lane + cy] = coriolis_ref[face, x : x + 1]
                row = (x // half) * 16 + (x % half) * pairs + face // 2
                lane_at = (face % 2) * WINDOW + MARGIN
                line_ref[row : row + 1, lane_at : lane_at + cy] = coriolis_ref[face, x : x + 1]
    sense = 1 - 2 * lax.axis_index("ty")
    for place, distance in enumerate((2, 3)):
        top = full_rows + place * small_rows
        put_chunk(cx, cy, count_x, swap_ref, line_ref, swap_ref, top, -sense * distance)


def put_chunk(cx, cy, count_x, block_ref, line_ref, out_ref, top, offset):
    pairs = 3
    group = 4 * pairs
    fields = 3
    half = cx // 2
    width = 2 * cx
    index_x = lax.axis_index("tx")
    index_y = lax.axis_index("ty")
    target = (index_x + offset + count_x) % count_x
    starts = windows(index_x, target, count_x, index_y, cx, cy)
    blocks = {}

    def put(row, lane, lines):
        position = lax.broadcasted_iota(jnp.int32, lines.shape, 1) % WINDOW
        here = (position >= lane) & (position < lane + width)
        blocks[row] = jnp.where(here, lines, blocks.get(row, jnp.zeros_like(lines)))

    for field in range(fields):
        for x in range(cx):
            row = field * half * group + (x // 2) * group
            at, lane = unit_place(field, x, cx, group, width)
            shift = lane - MARGIN - (x % 2) * cy - starts[x // half] + 2 * LANES
            put(at, lane, pltpu.roll(block_ref[row : row + group], shift % LANES, 1))
    for part in range(2):
        at, lane = unit_place(fields, part, cx, group, width)
        shift = lane - MARGIN - starts[part] + 2 * LANES
        lines = line_ref[16 * part : 16 * part + group]
        put(at, lane, pltpu.roll(lines, shift % LANES, 1))
    for row, lines in blocks.items():
        out_ref[top + row : top + row + group] = lines


def keep_kernel(cx, cy, count_x, small_rows, swap_ref, line_ref, keep_ref, middle_ref):
    sense = 1 - 2 * lax.axis_index("ty")
    put_chunk(cx, cy, count_x, swap_ref, line_ref, middle_ref, 0, count_x // 2)
    for place, distance in enumerate((2, 3)):
        top = place * small_rows
        put_chunk(cx, cy, count_x, swap_ref, line_ref, keep_ref, top, sense * distance)


def mix_kernel(full_rows, small_rows, swap_ref, other_ref, keep_ref, near_ref, second_ref, third_ref):
    near_ref[:full_rows] = swap_ref[:full_rows]
    near_ref[full_rows:] = other_ref[:full_rows]
    for place, far_ref in enumerate((second_ref, third_ref)):
        at = place * small_rows
        far_ref[:small_rows] = keep_ref[at : at + small_rows]
        at += full_rows
        far_ref[small_rows:] = other_ref[at : at + small_rows]


def placer(cx, cy, count_x, full_rows, small_rows, z_ref, cor_ref):
    fields = z_ref.shape[0]
    levels = 4
    group = z_ref.shape[1] // (cx * count_x + 8)
    pairs = group // levels
    half = cx // 2
    chunk = cx * group
    index_x = lax.axis_index("tx")
    index_y = lax.axis_index("ty")
    south_half = lax.broadcasted_iota(jnp.int32, (group, LANES), 1) % WINDOW < MARGIN + cy
    south_is_own = index_y == 0
    own_half = south_half == south_is_own

    def row_of(x):
        return (x + 4) * group

    def from_owner(offset):
        source = (index_x - offset + 2 * count_x) % count_x
        return source, pl.multiple_of(source * chunk, 8)

    def put_coriolis(start, x, values, at):
        for pair in range(pairs):
            line = values[at + pair : at + pair + 1]
            rows = pl.ds(start + x * group + pair * levels, levels)
            cor_ref[rows] = jnp.broadcast_to(line, (levels, LANES))

    def put_block(start, lines_of):
        base = fields * half * group
        for field in range(fields):
            for xp in range(half):
                even, odd = lines_of(field * half * group + xp * group, group)
                z_ref[field, pl.ds(start + row_of(2 * xp), group)] = even
                z_ref[field, pl.ds(start + row_of(2 * xp + 1), group)] = odd
        for parity, values in enumerate(lines_of(base, half * pairs)):
            for xp in range(half):
                put_coriolis(start, 2 * xp + parity, values, xp * pairs)

    def put_distant(source, start, lines_of):
        starts_south = windows(source, index_x, count_x, 0, cx, cy)
        starts_north = windows(source, index_x, count_x, 1, cx, cy)

        def lines_at(field, x, part):
            at, lane = unit_place(field, x, cx, group, 2 * cx)
            south_shift = (MARGIN + starts_south[part] - lane + LANES) % LANES
            north_shift = (MARGIN + cy + starts_north[part] - lane + LANES) % LANES
            return lines_of(at, south_shift, north_shift)

        for field in range(fields):
            for x in range(cx):
                z_ref[field, pl.ds(start + row_of(x), group)] = lines_at(field, x, x // half)
        for part in range(2):
            values = lines_at(fields, part, part)
            for x in range(half):
                put_coriolis(start, part * half + x, values, x * pairs)

    def place_own(own_ref, other_ref):
        def own_lines(row, rows):
            mine = own_ref[row : row + rows]
            theirs = other_ref[row : row + rows]
            up, down = index_y * cy, (1 - index_y) * cy
            keep = own_half[:rows]
            even = jnp.where(keep, pltpu.roll(mine, up, 1), pltpu.roll(theirs, down, 1))
            mine = pltpu.roll(mine, (LANES - down) % LANES, 1)
            theirs = pltpu.roll(theirs, (LANES - up) % LANES, 1)
            return even, jnp.where(keep, mine, theirs)

        put_block(from_owner(0)[1], own_lines)

    def place_got(block_ref, toward, south_first):
        south_top = pl.multiple_of(south_first * full_rows, 8)
        north_top = pl.multiple_of((1 - south_first) * full_rows, 8)

        def near_lines(row, rows):
            south = block_ref[pl.ds(south_top + row, rows)]
            north = block_ref[pl.ds(north_top + row, rows)]
            low = south_half[:rows]
            even = jnp.where(low, south, pltpu.roll(north, cy, 1))
            return even, jnp.where(low, pltpu.roll(south, LANES - cy, 1), north)

        put_block(from_owner(toward)[1], near_lines)
        for place, distance in enumerate((2, 3)):
            top = 2 * full_rows + 2 * place * small_rows
            south_at = pl.multiple_of(top + south_first * small_rows, 8)
            north_at = pl.multiple_of(top + (1 - south_first) * small_rows, 8)

            def far_lines(at, south_shift, north_shift, south_at=south_at, north_at=north_at):
                south = pltpu.roll(block_ref[pl.ds(south_at + at, group)], south_shift, 1)
                north = pltpu.roll(block_ref[pl.ds(north_at + at, group)], north_shift, 1)
                return jnp.where(south_half, south, north)

            put_distant(*from_owner(toward * distance), far_lines)

    def place_middle(got_ref, got_other_ref):
        def middle_lines(at, south_shift, north_shift):
            row = 2 * full_rows + 4 * small_rows + at
            mine_shift = jnp.where(south_is_own, south_shift, north_shift)
            other_shift = jnp.where(south_is_own, north_shift, south_shift)
            mine = pltpu.roll(got_ref[row : row + group], mine_shift, 1)
            theirs = pltpu.roll(got_other_ref[row : row + group], other_shift, 1)
            return jnp.where(own_half, mine, theirs)

        put_distant(*from_owner(count_x // 2), middle_lines)

    return place_own, place_got, place_middle


def own_kernel(sizes, own_ref, other_ref, z_ref, cor_ref):
    placer(*sizes, z_ref, cor_ref)[0](own_ref, other_ref)


def got_kernel(sizes, got_ref, z_in, cor_in, z_ref, cor_ref):
    index_y = lax.axis_index("ty")
    placer(*sizes, z_ref, cor_ref)[1](got_ref, 1 - 2 * index_y, index_y)


def step_kernel(
    sizes, got_ref, got_other_ref, table_in, z_in, cor_in, out_hbm, z_ref, cor_ref,
    pred_ref, store_ref, tile_ref, flip_ref, speed_ref, table_ref, out_ref, sems,
):
    table_copy = pltpu.make_async_copy(table_in, table_ref, sems.at[0])
    table_copy.start()
    cx, cy, count_x = sizes[:3]
    levels = 4
    slots = 16
    cells = cx * count_x
    faces = store_ref.shape[0] // 4
    pairs = faces // 2
    group = pairs * levels
    chunk = cx * group
    index_x = lax.axis_index("tx")
    index_y = lax.axis_index("ty")

    def row_of(x):
        return (x + 4) * group

    def lanes_of(rows):
        return lax.broadcasted_iota(jnp.int32, (rows, LANES), 1)

    _, place_got, place_middle = placer(*sizes, z_ref, cor_ref)
    place_got(got_other_ref, 2 * index_y - 1, 1 - index_y)
    place_middle(got_ref, got_other_ref)

    table_copy.wait()
    level_of = lax.broadcasted_iota(jnp.int32, speed_ref.shape, 0) % levels
    speeds = jnp.full(speed_ref.shape, table_ref[0], jnp.float32)
    for index in range(1, levels):
        speeds = jnp.where(level_of == index, table_ref[index], speeds)
    speed_ref[...] = speeds

    def collect():
        position = lanes_of(cells) % WINDOW
        gap = WINDOW - cells + 3
        wide = gap + 3 * levels
        for pair in range(pairs):
            merged = jnp.zeros((cells, LANES), jnp.float32)
            for slot, field in ((0, 0), (1, 2)):
                for level in range(levels):
                    lines = z_ref[field, pl.ds(row_of(0) + pair * levels + level, cells, group)]
                    offset = slot * wide + 3 * level
                    here = position - offset
                    wanted = ((here >= 0) & (here < 3)) | ((here >= gap) & (here < gap + 3))
                    shift = (offset - (MARGIN + cells - 3)) % LANES
                    merged = jnp.where(wanted, pltpu.roll(lines, shift, 1), merged)
            flip_ref[pair, :, :cells] = merged.T
            for slot in range(2):
                for side in (2, 3):
                    for odd in range(2):
                        for depth in range(3):
                            base = slot * wide
                            if side == 3:
                                base += odd * WINDOW + 2 - depth
                            else:
                                base += ((odd + 1) % 2) * WINDOW + gap + depth
                            at = slot * slots + depth * levels
                            store_ref[(2 * pair + odd) * 4 + side, at : at + levels] = flip_ref[
                                pair, pl.ds(base, levels, 3)
                            ]
            for slot in range(2):
                for side in (0, 1):
                    for depth in range(3):
                        x = depth if side == 0 else cells - 1 - depth
                        row = row_of(x) + pair * levels
                        lines = z_ref[slot, row : row + levels]
                        at = slot * slots + depth * levels
                        for odd in range(2):
                            store_ref[(2 * pair + odd) * 4 + side, at : at + levels] = pltpu.roll(
                                lines, LANES - MARGIN - odd * WINDOW, 1
                            )

    def fetch(face, side, position):
        at = levels + (face * 4 + side) * 3
        neighbour = table_ref[at].astype(jnp.int32)
        far_side = table_ref[at + 1].astype(jnp.int32)
        flipped = table_ref[at + 2].astype(jnp.int32)
        block = store_ref[neighbour * 4 + far_side]
        order = jnp.where(flipped == 1, cells - 1 - position, position)
        order = jnp.where((position >= 0) & (position < cells), order, 0)
        block = jnp.take_along_axis(block, order, axis=1)
        sign_here = 2 * (side % 2) - 1
        sign_there = 2 * (far_side % 2) - 1
        sign = (-sign_here * sign_there).astype(jnp.float32)
        normal = lax.broadcasted_iota(jnp.int32, block.shape, 0) >= slots
        return jnp.where(normal, sign * block, block)

    def rim_rows(side):
        lane = lanes_of(2 * slots)
        for pair in range(pairs):
            first = fetch(2 * pair, side, lane - MARGIN)
            second = fetch(2 * pair + 1, side, lane - (MARGIN + WINDOW))
            both = jnp.where(lane < WINDOW, first, second)
            for slot in range(2):
                for depth in range(3):
                    x = -1 - depth if side == 0 else cells + depth
                    at = slot * slots + depth * levels
                    row = row_of(x) + pair * levels
                    z_ref[slot, row : row + levels] = both[at : at + levels]

    wide = WINDOW - cells - 3 + 3 * levels

    def tile_rows(odd, side, depth, base=0):
        if side == 3:
            return pl.ds(base + odd * WINDOW + depth, levels, 3)
        return pl.ds(base + ((odd + 1) % 2) * WINDOW + wide - 3 * levels + 2 - depth, levels, 3)

    def put_columns(lines, field, start, pair, base=0):
        count = lines.shape[0]
        position = lanes_of(count) % WINDOW
        rim = ((position >= MARGIN - 3) & (position < MARGIN)) | (
            (position >= MARGIN + cells) & (position < MARGIN + cells + 3)
        )
        for level in range(levels):
            rolled = pltpu.roll(lines, (MARGIN + cells - base - 3 * level) % LANES, 1)
            at = pl.ds(row_of(start) + pair * levels + level, count, group)
            z_ref[field, at] = jnp.where(rim, rolled, z_ref[field, at])

    def rim_columns_all():
        for pair in range(pairs):
            for odd in range(2):
                for side in (2, 3):
                    block = fetch(2 * pair + odd, side, lanes_of(2 * slots))
                    for slot in range(2):
                        for depth in range(3):
                            at = slot * slots + depth * levels
                            rows = tile_rows(odd, side, depth, slot * wide)
                            tile_ref[pair, rows] = block[at : at + levels]
            turned = tile_ref[pair].T[:cells]
            for slot, field in ((0, 0), (1, 2)):
                put_columns(turned, field, 0, pair, slot * wide)

    def rim_columns_own():
        lane = lanes_of(2 * slots)
        second = lax.broadcasted_iota(jnp.int32, lane.shape, 0) >= slots
        for odd in range(2):
            for side in (2, 3):
                total = jnp.zeros((slots, LANES), jnp.float32)
                for pair in range(pairs):
                    local = lane - jnp.where(second, 8 * (pairs + pair), 8 * pair)
                    block = fetch(2 * pair + odd, side, index_x * cx + local)
                    block = jnp.where((local >= 0) & (local < 8), block, 0.0)
                    total = total + block[:slots] + block[slots:]
                for depth in range(3):
                    at = depth * levels
                    tile_ref[0, tile_rows(odd, side, depth)] = total[at : at + levels]
        turned = tile_ref[0].T
        for slot, field in ((0, 0), (1, 2)):
            for pair in range(pairs):
                at = 8 * (slot * pairs + pair)
                put_columns(turned[at : at + cx], field, index_x * cx, pair)

    def predict(at, rows):
        speed = speed_ref[:rows]
        ahead = z_ref[0, pl.ds(at + group, rows)]
        behind = z_ref[0, pl.ds(at - group, rows)]
        pred_ref[pl.ds(at, rows)] = z_ref[1, pl.ds(at, rows)] - speed * (0.5 * (ahead - behind))

    def update(at, rows):
        speed = speed_ref[:rows]
        height = z_ref[0, pl.ds(at, rows)]
        north_pred = z_ref[2, pl.ds(at, rows)] - speed * (
            0.5 * (pltpu.roll(height, LANES - 1, 1) - pltpu.roll(height, 1, 1))
        )
        east_pred = pred_ref[pl.ds(at, rows)]
        flux_east = 8.0 * (
            pred_ref[pl.ds(at + group, rows)] - pred_ref[pl.ds(at - group, rows)]
        ) - (pred_ref[pl.ds(at + 2 * group, rows)] - pred_ref[pl.ds(at - 2 * group, rows)])
        flux_north = 8.0 * (
            pltpu.roll(north_pred, LANES - 1, 1) - pltpu.roll(north_pred, 1, 1)
        ) - (pltpu.roll(north_pred, LANES - 2, 1) - pltpu.roll(north_pred, 2, 1))
        height = height - speed * ((flux_east + flux_north) * (1.0 / 12.0))
        turning = cor_ref[pl.ds(at - row_of(0), rows)]
        return height, east_pred + turning * north_pred, north_pred - turning * east_pred

    collect()
    rim_rows(0)
    rim_rows(1)
    rim_columns_all()
    for first in range(-2, cells + 2, 4):
        predict(row_of(first), 4 * group)
    for index in range(count_x):
        at = row_of(0) + index * chunk
        for field, values in enumerate(update(at, chunk)):
            z_ref[field, at : at + chunk] = values

    collect()

    @pl.when(index_x == 0)
    def _():
        rim_rows(0)

    @pl.when(index_x == count_x - 1)
    def _():
        rim_rows(1)

    rim_columns_own()
    at = pl.multiple_of(row_of(0) + index_x * chunk, 8)
    predict(at - 2 * group, chunk + 4 * group)
    copies = []
    for field, values in enumerate(update(at, chunk)):
        for odd in range(2):
            shift = LANES - (MARGIN + odd * WINDOW) - index_y * cy
            rolled = pltpu.roll(values, shift, 1)
            for x in range(cx):
                for pair in range(pairs):
                    row = x * group + pair * levels
                    out_ref[field, 2 * pair + odd, x] = rolled[row : row + levels, :cy]
        copy = pltpu.make_async_copy(out_ref.at[field], out_hbm.at[:, field], sems.at[1 + field])
        copy.start()
        copies.append(copy)
    for copy in copies:
        copy.wait()


def fast_on_device(state, coriolis, wave_speed, edges):
    count_x = lax.axis_size("tx")
    faces, fields, levels, cx, cy = state.shape
    pairs = faces // 2
    group = pairs * levels
    cells = cx * count_x
    full_rows = fields * (cx // 2) * group + (cx // 2) * pairs
    full_rows = -(-full_rows // 8) * 8
    small_rows = unit_place(fields, 1, cx, group, 2 * cx)[0] + group
    swap, lines = pl.pallas_call(
        functools.partial(pack_kernel, cx, cy, count_x, full_rows, small_rows),
        out_shape=[
            jax.ShapeDtypeStruct((full_rows + 2 * small_rows, LANES), jnp.float32),
            jax.ShapeDtypeStruct((32, LANES), jnp.float32),
        ],
        in_specs=[pl.BlockSpec(memory_space=pltpu.HBM)] * 2,
        out_specs=[pl.BlockSpec(memory_space=pltpu.VMEM)] * 2,
        scratch_shapes=[
            pltpu.VMEM((faces, fields, cx, levels, cy), jnp.float32),
            pltpu.VMEM((faces, cx, cy), jnp.float32),
            pltpu.SemaphoreType.DMA((2,)),
        ],
        compiler_params=pltpu.CompilerParams(vmem_limit_bytes=VMEM_LIMIT),
        name="pack",
    )(jnp.swapaxes(state, 2, 3), coriolis)
    keep, middle = pl.pallas_call(
        functools.partial(keep_kernel, cx, cy, count_x, small_rows),
        out_shape=[
            jax.ShapeDtypeStruct((2 * small_rows, LANES), jnp.float32),
            jax.ShapeDtypeStruct((small_rows, LANES), jnp.float32),
        ],
        in_specs=[pl.BlockSpec(memory_space=pltpu.VMEM)] * 2,
        out_specs=[pl.BlockSpec(memory_space=pltpu.VMEM)] * 2,
        compiler_params=pltpu.CompilerParams(vmem_limit_bytes=SMALL_VMEM_LIMIT),
        name="keep",
    )(swap, lines)

    def read(source, target):
        ends = (0, count_x - 1)
        return source in ends or target in ends or abs(source + target - ends[1]) <= 1

    def moved(block, distance):
        pairs_of = []
        for index in range(count_x):
            for core in range(2):
                target = (index + distance * (1 - 2 * core)) % count_x
                if distance == 1 or read(index, target):
                    pairs_of.append((2 * index + core, 2 * target + core))
        return lax.ppermute(block, ("tx", "ty"), pairs_of)

    def across(block):
        return lax.ppermute(block, "ty", [(0, 1), (1, 0)])

    other = across(swap)
    messages = pl.pallas_call(
        functools.partial(mix_kernel, full_rows, small_rows),
        out_shape=[
            jax.ShapeDtypeStruct((2 * rows, LANES), jnp.float32)
            for rows in (full_rows, small_rows, small_rows)
        ],
        in_specs=[pl.BlockSpec(memory_space=pltpu.VMEM)] * 3,
        out_specs=[pl.BlockSpec(memory_space=pltpu.VMEM)] * 3,
        compiler_params=pltpu.CompilerParams(vmem_limit_bytes=SMALL_VMEM_LIMIT),
        name="messages",
    )(swap, other, keep)
    got = [moved(block, place + 1) for place, block in enumerate(messages)]
    got = jnp.concatenate([*got, moved(middle, count_x // 2)])
    table = jnp.concatenate([wave_speed, edges.reshape(-1).astype(jnp.float32)])
    got, table = lax.optimization_barrier((got, table))
    passed = across(got)

    sizes = (cx, cy, count_x, full_rows, small_rows)
    state_rows = [
        jax.ShapeDtypeStruct((fields, (cells + 8) * group, LANES), jnp.float32),
        jax.ShapeDtypeStruct((cells * group, LANES), jnp.float32),
    ]
    in_vmem = pl.BlockSpec(memory_space=pltpu.VMEM)
    params = pltpu.CompilerParams(vmem_limit_bytes=SMALL_VMEM_LIMIT)
    rows = pl.pallas_call(
        functools.partial(own_kernel, sizes),
        out_shape=state_rows,
        in_specs=[in_vmem] * 2,
        out_specs=[in_vmem] * 2,
        compiler_params=params,
        name="place_own",
    )(swap, other)
    rows = pl.pallas_call(
        functools.partial(got_kernel, sizes),
        out_shape=state_rows,
        in_specs=[in_vmem] * 3,
        out_specs=[in_vmem] * 2,
        input_output_aliases={1: 0, 2: 1},
        compiler_params=params,
        name="place_got",
    )(got, *rows)
    out, _, _ = pl.pallas_call(
        functools.partial(step_kernel, sizes),
        out_shape=[jax.ShapeDtypeStruct((faces, fields, cx, levels, cy), jnp.float32)]
        + state_rows,
        in_specs=[in_vmem] * 5,
        out_specs=[pl.BlockSpec(memory_space=pltpu.HBM)] + [in_vmem] * 2,
        input_output_aliases={3: 1, 4: 2},
        scratch_shapes=[
            pltpu.VMEM(((cells + 8) * group, LANES), jnp.float32),
            pltpu.VMEM((faces * 4, 32, LANES), jnp.float32),
            pltpu.VMEM((pairs, LANES, LANES), jnp.float32),
            pltpu.VMEM((pairs, LANES, LANES), jnp.float32),
            pltpu.VMEM(((cx + 4) * group, LANES), jnp.float32),
            pltpu.SMEM(table.shape, jnp.float32),
            pltpu.VMEM((fields, faces, cx, levels, cy), jnp.float32),
            pltpu.SemaphoreType.DMA((1 + fields,)),
        ],
        compiler_params=pltpu.CompilerParams(vmem_limit_bytes=VMEM_LIMIT),
        name="substeps",
    )(got, passed, table, *rows)
    return jnp.swapaxes(out, 2, 3)


def padded_2(block, sides, width):
    for axis, dim in sides:
        count = lax.axis_size(axis)
        forward = [(i, i + 1) for i in range(count - 1)]
        backward = [(target, source) for source, target in forward]
        low = lax.ppermute(
            lax.slice_in_dim(block, block.shape[dim] - width, None, axis=dim), axis, forward
        )
        high = lax.ppermute(lax.slice_in_dim(block, 0, width, axis=dim), axis, backward)
        block = jnp.concatenate([low, block, high], axis=dim)
    return block


def spread(block, axis, owner):
    block = jnp.where(lax.axis_index(axis) == owner, block, jnp.zeros_like(block))
    return lax.psum(block, axis)


def rotate_strip(strip_data, side_index, far_side, flipped):
    normal_part = jnp.where(far_side < 2, strip_data[1], strip_data[2])
    along_part = jnp.where(far_side < 2, strip_data[2], strip_data[1])
    sign_here = 2.0 * (side_index % 2) - 1.0
    sign_there = (2 * (far_side % 2) - 1).astype(jnp.float32)
    normal_part = -sign_here * sign_there * normal_part
    along_part = (1 - 2 * flipped).astype(jnp.float32) * along_part
    if side_index < 2:
        return jnp.stack([strip_data[0], normal_part, along_part])
    return jnp.stack([strip_data[0], along_part, normal_part])


def window_strip(store, side_pick, neighbour, flipped, start, width):
    full_length = store.shape[5]
    begin = jnp.where(flipped == 1, full_length - start - width, start)
    zero = jnp.zeros((), jnp.int32)
    sizes_here = (1, 1, store.shape[2], store.shape[3], store.shape[4], width)
    piece = lax.dynamic_slice(store, (side_pick, neighbour, zero, zero, zero, begin), sizes_here)[
        0, 0
    ]
    return jnp.where(flipped == 1, jnp.flip(piece, 3), piece)


def side_halo(edge_store, edges, face_index, side_index, start, width):
    neighbour = edges[face_index, side_index, 0]
    far_side = edges[face_index, side_index, 1]
    flipped = edges[face_index, side_index, 2]
    strip_data = window_strip(edge_store, far_side, neighbour, flipped, start, width)
    return rotate_strip(strip_data, side_index, far_side, flipped)


def advance(padded, wave_speed, coriolis_part, cells_x, cells_y):
    height = padded[..., 0, :, :, :]
    wind_east = padded[..., 1, :, :, :]
    wind_north = padded[..., 2, :, :, :]
    speed = wave_speed[:, None, None]
    east_pred = wind_east[..., 1 : cells_x + 5, 3 : cells_y + 3] - speed * (
        0.5
        * (
            height[..., 2 : cells_x + 6, 3 : cells_y + 3]
            - height[..., 0 : cells_x + 4, 3 : cells_y + 3]
        )
    )
    north_pred = wind_north[..., 3 : cells_x + 3, 1 : cells_y + 5] - speed * (
        0.5
        * (
            height[..., 3 : cells_x + 3, 2 : cells_y + 6]
            - height[..., 3 : cells_x + 3, 0 : cells_y + 4]
        )
    )
    flux_east = (
        8.0 * (east_pred[..., 3 : cells_x + 3, :] - east_pred[..., 1 : cells_x + 1, :])
        - (east_pred[..., 4 : cells_x + 4, :] - east_pred[..., 0:cells_x, :])
    ) / 12.0
    flux_north = (
        8.0 * (north_pred[..., 3 : cells_y + 3] - north_pred[..., 1 : cells_y + 1])
        - (north_pred[..., 4 : cells_y + 4] - north_pred[..., 0:cells_y])
    ) / 12.0
    height_new = height[..., 3 : cells_x + 3, 3 : cells_y + 3] - speed * (flux_east + flux_north)
    east_inner = east_pred[..., 2 : cells_x + 2, :]
    north_inner = north_pred[..., 2 : cells_y + 2]
    turning = coriolis_part[..., None, :, :]
    return jnp.stack(
        [height_new, east_inner + turning * north_inner, north_inner - turning * east_inner],
        axis=-4,
    )


def one_substep(state, coriolis, wave_speed, edges, count_x, count_y, index_x, index_y):
    faces = state.shape[0]
    cells_x = state.shape[3]
    cells_y = state.shape[4]
    padded = padded_2(state, (("tx", 3), ("ty", 4)), 3)
    west_rim = state[:, :, :, 0:3, :]
    east_rim = jnp.flip(state[:, :, :, cells_x - 3 :, :], 3)
    south_rim = jnp.swapaxes(state[:, :, :, :, 0:3], 3, 4)
    north_rim = jnp.swapaxes(jnp.flip(state[:, :, :, :, cells_y - 3 :], 4), 3, 4)
    west_part = spread(west_rim, "tx", 0)
    east_part = spread(east_rim, "tx", count_x - 1)
    west_full, east_full = (
        lax.all_gather(west_part, "ty", axis=4, tiled=True),
        lax.all_gather(east_part, "ty", axis=4, tiled=True),
    )
    south_row, north_row = (
        lax.all_gather(south_rim, "tx", axis=4, tiled=True),
        lax.all_gather(north_rim, "tx", axis=4, tiled=True),
    )
    south_all, north_all = (
        lax.all_gather(south_row, "ty", axis=0, tiled=True),
        lax.all_gather(north_row, "ty", axis=0, tiled=True),
    )
    south_full = south_all[0:faces]
    north_full = north_all[(count_y - 1) * faces : count_y * faces]
    edge_store = jnp.stack([west_full, east_full, south_full, north_full])
    halos = []
    for side_index in range(4):
        if side_index < 2:
            slabs = jnp.stack(
                [
                    side_halo(edge_store, edges, face_index, side_index, index_y * cells_y, cells_y)
                    for face_index in range(faces)
                ]
            )
        else:
            slabs = jnp.stack(
                [
                    side_halo(edge_store, edges, face_index, side_index, index_x * cells_x, cells_x)
                    for face_index in range(faces)
                ]
            )
        halos.append(slabs)
    west_region = padded[:, :, :, 0:3, 3 : cells_y + 3]
    padded = padded.at[:, :, :, 0:3, 3 : cells_y + 3].set(
        jnp.where(index_x == 0, jnp.flip(halos[0], 3), west_region)
    )
    east_region = padded[:, :, :, cells_x + 3 : cells_x + 6, 3 : cells_y + 3]
    padded = padded.at[:, :, :, cells_x + 3 : cells_x + 6, 3 : cells_y + 3].set(
        jnp.where(index_x == count_x - 1, halos[1], east_region)
    )
    south_region = padded[:, :, :, 3 : cells_x + 3, 0:3]
    padded = padded.at[:, :, :, 3 : cells_x + 3, 0:3].set(
        jnp.where(index_y == 0, jnp.swapaxes(jnp.flip(halos[2], 3), 3, 4), south_region)
    )
    north_region = padded[:, :, :, 3 : cells_x + 3, cells_y + 3 : cells_y + 6]
    padded = padded.at[:, :, :, 3 : cells_x + 3, cells_y + 3 : cells_y + 6].set(
        jnp.where(index_y == count_y - 1, jnp.swapaxes(halos[3], 3, 4), north_region)
    )
    return advance(padded, wave_speed, coriolis, cells_x, cells_y)


def on_device(state, coriolis, wave_speed, edges):
    count_x = lax.axis_size("tx")
    count_y = lax.axis_size("ty")
    index_x = lax.axis_index("tx")
    index_y = lax.axis_index("ty")
    for substep_index in range(SUBSTEPS):
        state = one_substep(state, coriolis, wave_speed, edges, count_x, count_y, index_x, index_y)
    return state


def fits(state):
    count_x = lax.axis_size("tx")
    faces, fields, levels, cells_x, cells_y = state.shape
    return (
        lax.axis_size("ty") == 2
        and faces % 2 == 0
        and levels == 4
        and cells_x == 6
        and cells_y == 24
        and count_x == 8
        and cells_x * count_x == 2 * cells_y
        and 2 * cells_y + 2 * MARGIN <= WINDOW
    )


def either(state, coriolis, wave_speed, edges):
    if fits(state):
        return fast_on_device(state, coriolis, wave_speed, edges)
    return on_device(state, coriolis, wave_speed, edges)


def solution(mesh):
    in_specs = (P("member", None, None, "tx", "ty"), P(None, "tx", "ty"), P(), P())
    out_specs = P("member", None, None, "tx", "ty")
    return jax.shard_map(
        either, mesh=mesh, in_specs=in_specs, out_specs=out_specs, check_vma=False
    )
```

```python
import functools

import jax
import jax.numpy as jnp
from jax import lax
from jax.experimental import pallas as pl
from jax.experimental.pallas import tpu as pltpu
from jax.sharding import PartitionSpec as P

SUBSTEPS = 2
LANES = 128
WINDOW = 64
MARGIN = 8
VMEM_LIMIT = 32 * 1024 * 1024
SMALL_VMEM_LIMIT = 8 * 1024 * 1024


def wrap(index, count):
    index = jnp.where(index < 0, index + count, index)
    return jnp.where(index >= count, index - count, index)


def lane_shift(amount):
    return amount & (LANES - 1)


def windows(source, target, count_x, index_y, cx, cy):
    spare = cy - 2 * cx
    near = jnp.minimum(target, count_x - 1 - target)
    rim = (source == 0) | (source == count_x - 1)
    starts = []
    for inward in (cx // 2, cx):
        start = jnp.maximum(jnp.minimum(cx * near - inward, spare), 0)
        start = jnp.where(rim, start, 0)
        starts.append(jnp.where(index_y == 0, start, spare - start))
    close, far = starts
    upside = source == count_x - 1
    return jnp.where(upside, far, close), jnp.where(upside, close, far)


def unit_place(field, x, cx, group, width):
    per_row = 60 // width
    index = field * cx + x
    return (index // per_row) * group, (index % per_row) * width


def chunk_targets(count_x, full_rows, small_rows):
    sense = 1 - 2 * lax.axis_index("ty")
    return [
        (full_rows + place * small_rows, -sense * distance)
        for place, distance in enumerate((2, 3))
    ]


def put_chunk(cx, cy, count_x, block_ref, line_ref, out_ref, top, offset):
    pairs = 3
    group = 4 * pairs
    fields = 3
    half = cx // 2
    width = 2 * cx
    index_x = lax.axis_index("tx")
    target = wrap(index_x + offset, count_x)
    starts = windows(index_x, target, count_x, lax.axis_index("ty"), cx, cy)
    position = lax.broadcasted_iota(jnp.int32, (group, LANES), 1) % WINDOW
    from_lane = {lane: position >= lane for lane in range(0, 60, width)}
    blocks = {}

    def put(row, lane, lines):
        blocks[row] = lines if row not in blocks else jnp.where(from_lane[lane], lines, blocks[row])

    if block_ref is not None:
        for field in range(fields):
            for x in range(cx):
                row = field * half * group + (x // 2) * group
                at, lane = unit_place(field, x, cx, group, width)
                shift = lane_shift(lane - MARGIN - (x % 2) * cy - starts[x // half])
                put(at, lane, pltpu.roll(block_ref[row : row + group], shift, 1))
    else:
        at = unit_place(fields, 0, cx, group, width)[0]
        blocks[at] = out_ref[top + at : top + at + group]
    if line_ref is not None:
        for part in range(2):
            at, lane = unit_place(fields, part, cx, group, width)
            shift = lane_shift(lane - MARGIN - starts[part])
            put(at, lane, pltpu.roll(line_ref[16 * part : 16 * part + group], shift, 1))
    for row, lines in blocks.items():
        out_ref[top + row : top + row + group] = lines


def pack_kernel(cx, cy, count_x, full_rows, small_rows, state_ref, swap_ref):
    faces, fields = state_ref.shape[:2]
    levels = state_ref.shape[3]
    group = (faces // 2) * levels
    half = cx // 2
    swap_ref[:full_rows] = jnp.zeros((full_rows, LANES), jnp.float32)
    for face in range(faces):
        for parity in range(2):
            lane = (face % 2) * WINDOW + MARGIN + parity * cy
            for xp in range(half):
                for field in range(fields):
                    row = field * half * group + xp * group + (face // 2) * levels
                    swap_ref[row : row + levels, lane : lane + cy] = state_ref[
                        face, field, 2 * xp + parity
                    ]
    for top, offset in chunk_targets(count_x, full_rows, small_rows):
        put_chunk(cx, cy, count_x, swap_ref, None, swap_ref, top, offset)


def pack_coriolis_kernel(
    cx, cy, count_x, full_rows, small_rows, coriolis_ref, swap_in, swap_ref, line_ref
):
    faces = coriolis_ref.shape[0]
    pairs = faces // 2
    half = cx // 2
    base = 3 * half * 4 * pairs
    line_ref[...] = jnp.zeros(line_ref.shape, jnp.float32)
    for face in range(faces):
        lane = (face % 2) * WINDOW + MARGIN
        for x in range(cx):
            line = coriolis_ref[face, x : x + 1]
            row = base + (x // 2) * pairs + face // 2
            at = lane + (x % 2) * cy
            swap_ref[row : row + 1, at : at + cy] = line
            row = (x // half) * 16 + (x % half) * pairs + face // 2
            line_ref[row : row + 1, lane : lane + cy] = line
    for top, offset in chunk_targets(count_x, full_rows, small_rows):
        put_chunk(cx, cy, count_x, None, line_ref, swap_ref, top, offset)


def keep_kernel(cx, cy, count_x, small_rows, swap_ref, line_ref, keep_ref, middle_ref):
    sense = 1 - 2 * lax.axis_index("ty")
    put_chunk(cx, cy, count_x, swap_ref, line_ref, middle_ref, 0, count_x // 2)
    for place, distance in enumerate((2, 3)):
        top = place * small_rows
        put_chunk(cx, cy, count_x, swap_ref, line_ref, keep_ref, top, sense * distance)


def mix_kernel(full_rows, small_rows, swap_ref, other_ref, keep_ref, near_ref, second_ref, third_ref):
    near_ref[:full_rows] = swap_ref[:full_rows]
    near_ref[full_rows:] = other_ref[:full_rows]
    for place, far_ref in enumerate((second_ref, third_ref)):
        at = place * small_rows
        far_ref[:small_rows] = keep_ref[at : at + small_rows]
        at += full_rows
        far_ref[small_rows:] = other_ref[at : at + small_rows]


def placer(cx, cy, count_x, full_rows, small_rows, z_ref, cor_ref):
    fields = z_ref.shape[0]
    levels = 4
    group = z_ref.shape[1] // (cx * count_x + 8)
    pairs = group // levels
    half = cx // 2
    chunk = cx * group
    index_x = lax.axis_index("tx")
    index_y = lax.axis_index("ty")
    south_half = lax.broadcasted_iota(jnp.int32, (group, LANES), 1) % WINDOW < MARGIN + cy
    south_is_own = index_y == 0
    own_half = south_half == south_is_own

    def row_of(x):
        return (x + 4) * group

    def from_owner(offset):
        source = wrap(index_x - offset, count_x)
        return source, pl.multiple_of(source * chunk, 8)

    def put_coriolis(start, x, values, at):
        for pair in range(pairs):
            line = values[at + pair : at + pair + 1]
            rows = pl.ds(start + x * group + pair * levels, levels)
            cor_ref[rows] = jnp.broadcast_to(line, (levels, LANES))

    def put_block(start, lines_of):
        base = fields * half * group
        for field in range(fields):
            for xp in range(half):
                even, odd = lines_of(field * half * group + xp * group, group)
                z_ref[field, pl.ds(start + row_of(2 * xp), group)] = even
                z_ref[field, pl.ds(start + row_of(2 * xp + 1), group)] = odd
        for parity, values in enumerate(lines_of(base, half * pairs)):
            for xp in range(half):
                put_coriolis(start, 2 * xp + parity, values, xp * pairs)

    def put_distant(source, start, lines_of):
        starts_south = windows(source, index_x, count_x, 0, cx, cy)
        starts_north = [cy - 2 * cx - start for start in starts_south]
        is_rim = (source == 0) | (source == count_x - 1)
        starts_north = [jnp.where(is_rim, start, cy - 2 * cx) for start in starts_north]
        shifts = {
            (part, lane): (
                lane_shift(MARGIN + starts_south[part] - lane),
                lane_shift(MARGIN + cy + starts_north[part] - lane),
            )
            for part in range(2)
            for lane in range(0, 60, 2 * cx)
        }

        def lines_at(field, x, part):
            at, lane = unit_place(field, x, cx, group, 2 * cx)
            return lines_of(at, *shifts[part, lane])

        for field in range(fields):
            for x in range(cx):
                z_ref[field, pl.ds(start + row_of(x), group)] = lines_at(field, x, x // half)
        for part in range(2):
            values = lines_at(fields, part, part)
            for x in range(half):
                put_coriolis(start, part * half + x, values, x * pairs)

    def place_own(own_ref, other_ref):
        def own_lines(row, rows):
            mine = own_ref[row : row + rows]
            theirs = other_ref[row : row + rows]
            up, down = index_y * cy, (1 - index_y) * cy
            keep = own_half[:rows]
            even = jnp.where(keep, pltpu.roll(mine, up, 1), pltpu.roll(theirs, down, 1))
            mine = pltpu.roll(mine, lane_shift(-down), 1)
            theirs = pltpu.roll(theirs, lane_shift(-up), 1)
            return even, jnp.where(keep, mine, theirs)

        put_block(from_owner(0)[1], own_lines)

    def place_got(block_ref, toward, south_first):
        south_top = pl.multiple_of(south_first * full_rows, 8)
        north_top = pl.multiple_of((1 - south_first) * full_rows, 8)

        def near_lines(row, rows):
            south = block_ref[pl.ds(south_top + row, rows)]
            north = block_ref[pl.ds(north_top + row, rows)]
            low = south_half[:rows]
            even = jnp.where(low, south, pltpu.roll(north, cy, 1))
            return even, jnp.where(low, pltpu.roll(south, LANES - cy, 1), north)

        put_block(from_owner(toward)[1], near_lines)
        for place, distance in enumerate((2, 3)):
            top = 2 * full_rows + 2 * place * small_rows
            south_at = pl.multiple_of(top + south_first * small_rows, 8)
            north_at = pl.multiple_of(top + (1 - south_first) * small_rows, 8)

            def far_lines(at, south_shift, north_shift, south_at=south_at, north_at=north_at):
                south = pltpu.roll(block_ref[pl.ds(south_at + at, group)], south_shift, 1)
                north = pltpu.roll(block_ref[pl.ds(north_at + at, group)], north_shift, 1)
                return jnp.where(south_half, south, north)

            put_distant(*from_owner(toward * distance), far_lines)

    def place_middle(got_ref, got_other_ref):
        def middle_lines(at, south_shift, north_shift):
            row = 2 * full_rows + 4 * small_rows + at
            mine_shift = jnp.where(south_is_own, south_shift, north_shift)
            other_shift = jnp.where(south_is_own, north_shift, south_shift)
            mine = pltpu.roll(got_ref[row : row + group], mine_shift, 1)
            theirs = pltpu.roll(got_other_ref[row : row + group], other_shift, 1)
            return jnp.where(own_half, mine, theirs)

        put_distant(*from_owner(count_x // 2), middle_lines)

    return place_own, place_got, place_middle


def own_kernel(sizes, own_ref, other_ref, z_ref, cor_ref):
    placer(*sizes, z_ref, cor_ref)[0](own_ref, other_ref)


def got_kernel(sizes, got_ref, z_in, cor_in, z_ref, cor_ref):
    index_y = lax.axis_index("ty")
    placer(*sizes, z_ref, cor_ref)[1](got_ref, 1 - 2 * index_y, index_y)


def step_kernel(
    sizes, got_ref, got_other_ref, table_in, z_in, cor_in, out_hbm, z_ref, cor_ref,
    pred_ref, store_ref, tile_ref, flip_ref, speed_ref, table_ref, out_ref, sems,
):
    table_copy = pltpu.make_async_copy(table_in, table_ref, sems.at[0])
    table_copy.start()
    cx, cy, count_x = sizes[:3]
    levels = 4
    slots = 16
    cells = cx * count_x
    faces = store_ref.shape[0] // 4
    pairs = faces // 2
    group = pairs * levels
    chunk = cx * group
    index_x = lax.axis_index("tx")
    index_y = lax.axis_index("ty")

    def row_of(x):
        return (x + 4) * group

    def lanes_of(rows):
        return lax.broadcasted_iota(jnp.int32, (rows, LANES), 1)

    _, place_got, place_middle = placer(*sizes, z_ref, cor_ref)
    place_got(got_other_ref, 2 * index_y - 1, 1 - index_y)
    place_middle(got_ref, got_other_ref)

    table_copy.wait()
    level_of = lax.broadcasted_iota(jnp.int32, speed_ref.shape, 0) % levels
    speeds = jnp.full(speed_ref.shape, table_ref[0], jnp.float32)
    for index in range(1, levels):
        speeds = jnp.where(level_of == index, table_ref[index], speeds)
    speed_ref[...] = speeds

    lane_8 = lanes_of(8)
    place_8 = lane_8 % WINDOW
    gap = WINDOW - cells + 3
    wide = gap + 3 * levels
    row_tiles = range(0, cells, 8)
    rim_8 = ((place_8 >= MARGIN - 3) & (place_8 < MARGIN)) | (
        (place_8 >= MARGIN + cells) & (place_8 < MARGIN + cells + 3)
    )

    def collect():
        for pair in range(pairs):
            merged = [jnp.zeros((8, LANES), jnp.float32)] * len(row_tiles)
            for slot, field in ((0, 0), (1, 2)):
                for level in range(levels):
                    offset = slot * wide + 3 * level
                    here = place_8 - offset
                    wanted = ((here >= 0) & (here < 3)) | ((here >= gap) & (here < gap + 3))
                    shift = (offset - (MARGIN + cells - 3)) % LANES
                    lines = z_ref[field, pl.ds(row_of(0) + pair * levels + level, cells, group)]
                    lines = pltpu.roll(lines, shift, 1)
                    merged = [
                        jnp.where(wanted, lines[row : row + 8], old)
                        for row, old in zip(row_tiles, merged)
                    ]
            flip_ref[pair, :, :cells] = jnp.concatenate(merged, axis=0).T
            for slot in range(2):
                for side in (2, 3):
                    for odd in range(2):
                        for depth in range(3):
                            base = slot * wide
                            if side == 3:
                                base += odd * WINDOW + 2 - depth
                            else:
                                base += ((odd + 1) % 2) * WINDOW + gap + depth
                            at = slot * slots + depth * levels
                            store_ref[(2 * pair + odd) * 4 + side, at : at + levels] = flip_ref[
                                pair, pl.ds(base, levels, 3)
                            ]
            for slot in range(2):
                for side in (0, 1):
                    for depth in range(3):
                        x = depth if side == 0 else cells - 1 - depth
                        row = row_of(x) + pair * levels
                        lines = z_ref[slot, row : row + levels]
                        at = slot * slots + depth * levels
                        for odd in range(2):
                            store_ref[(2 * pair + odd) * 4 + side, at : at + levels] = lines

    def fetch(face, side, positions):
        at = levels + (face * 4 + side) * 3
        neighbour = table_ref[at].astype(jnp.int32)
        far_side = table_ref[at + 1].astype(jnp.int32)
        flipped = table_ref[at + 2].astype(jnp.int32)
        first = jnp.where(far_side < 2, MARGIN + WINDOW * (neighbour & 1), 0)
        start = first + jnp.where(flipped == 1, cells - 1, 0)
        step = 1 - 2 * flipped
        sign = ((1 - 2 * (side % 2)) * (2 * (far_side & 1) - 1)).astype(jnp.float32)
        index = neighbour * 4 + far_side
        parts = []
        for slot, position in enumerate(positions):
            order = (start + step * position) & (LANES - 1)
            for half_at in (0, 8):
                at = slot * slots + half_at
                lines = jnp.take_along_axis(store_ref[index, at : at + 8], order, axis=1)
                parts.append(lines if slot == 0 else sign * lines)
        return parts[:2], parts[2:]

    def depth_rows(parts, depth):
        at = (depth % 2) * levels
        return parts[depth // 2][at : at + levels]

    def rim_rows(side):
        left = lane_8 < WINDOW
        for pair in range(pairs):
            first = fetch(2 * pair, side, [lane_8 - MARGIN] * 2)
            second = fetch(2 * pair + 1, side, [lane_8 - (MARGIN + WINDOW)] * 2)
            for slot in range(2):
                both = [jnp.where(left, a, b) for a, b in zip(first[slot], second[slot])]
                for depth in range(3):
                    x = -1 - depth if side == 0 else cells + depth
                    row = row_of(x) + pair * levels
                    z_ref[slot, row : row + levels] = depth_rows(both, depth)

    tile_wide = WINDOW - cells - 3 + 3 * levels

    def put_tile(tile, parts, odd, side, base=0):
        for depth in range(3):
            if side == 3:
                at = base + odd * WINDOW + depth
            else:
                at = base + ((odd + 1) % 2) * WINDOW + tile_wide - 3 * levels + 2 - depth
            tile_ref[tile, pl.ds(at, levels, 3)] = depth_rows(parts, depth)

    def rim_columns_all():
        for pair in range(pairs):
            for odd in range(2):
                for side in (2, 3):
                    for slot, parts in enumerate(fetch(2 * pair + odd, side, [lane_8] * 2)):
                        put_tile(pair, parts, odd, side, slot * tile_wide)
            turned = tile_ref[pair].T[:cells]
            for slot, field in ((0, 0), (1, 2)):
                for level in range(levels):
                    shift = (MARGIN + cells - slot * tile_wide - 3 * level) % LANES
                    rolled = pltpu.roll(turned, shift, 1)
                    at = pl.ds(row_of(0) + pair * levels + level, cells, group)
                    lines = z_ref[field, at]
                    lines = [
                        jnp.where(rim_8, rolled[row : row + 8], lines[row : row + 8])
                        for row in row_tiles
                    ]
                    z_ref[field, at] = jnp.concatenate(lines, axis=0)

    def rim_columns_own():
        for odd in range(2):
            for side in (2, 3):
                total = [jnp.zeros((8, LANES), jnp.float32)] * 2
                for pair in range(pairs):
                    places = [8 * pair, 8 * (pairs + pair)]
                    positions = [lane_8 + (index_x * cx - place) for place in places]
                    fetched = fetch(2 * pair + odd, side, positions)
                    for place, parts in zip(places, fetched):
                        here = (lane_8 >= place) & (lane_8 < place + 8)
                        total = [jnp.where(here, a, b) for a, b in zip(parts, total)]
                put_tile(0, total, odd, side)
        turned = tile_ref[0].T
        for slot, field in ((0, 0), (1, 2)):
            for pair in range(pairs):
                row = 8 * (slot * pairs + pair)
                for level in range(levels):
                    shift = (MARGIN + cells - 3 * level) % LANES
                    rolled = pltpu.roll(turned[row : row + 8], shift, 1)[:cx]
                    start = row_of(0) + index_x * chunk + pair * levels + level
                    at = pl.ds(start, cx, group)
                    z_ref[field, at] = jnp.where(rim_8[:cx], rolled, z_ref[field, at])

    def predict(at, rows):
        speed = speed_ref[:rows]
        ahead = z_ref[0, pl.ds(at + group, rows)]
        behind = z_ref[0, pl.ds(at - group, rows)]
        pred_ref[pl.ds(at, rows)] = z_ref[1, pl.ds(at, rows)] - speed * (0.5 * (ahead - behind))

    def update(at, rows):
        speed = speed_ref[:rows]
        height = z_ref[0, pl.ds(at, rows)]
        north_pred = z_ref[2, pl.ds(at, rows)] - speed * (
            0.5 * (pltpu.roll(height, LANES - 1, 1) - pltpu.roll(height, 1, 1))
        )
        east_pred = pred_ref[pl.ds(at, rows)]
        flux_east = 8.0 * (
            pred_ref[pl.ds(at + group, rows)] - pred_ref[pl.ds(at - group, rows)]
        ) - (pred_ref[pl.ds(at + 2 * group, rows)] - pred_ref[pl.ds(at - 2 * group, rows)])
        flux_north = 8.0 * (
            pltpu.roll(north_pred, LANES - 1, 1) - pltpu.roll(north_pred, 1, 1)
        ) - (pltpu.roll(north_pred, LANES - 2, 1) - pltpu.roll(north_pred, 2, 1))
        height = height - speed * ((flux_east + flux_north) * (1.0 / 12.0))
        turning = cor_ref[pl.ds(at - row_of(0), rows)]
        return height, east_pred + turning * north_pred, north_pred - turning * east_pred

    collect()
    rim_rows(0)
    rim_rows(1)
    rim_columns_all()
    for first in range(-2, cells + 2, 4):
        predict(row_of(first), 4 * group)
    for index in range(count_x):
        at = row_of(0) + index * chunk
        for field, values in enumerate(update(at, chunk)):
            z_ref[field, at : at + chunk] = values

    collect()

    @pl.when(index_x == 0)
    def _():
        rim_rows(0)

    @pl.when(index_x == count_x - 1)
    def _():
        rim_rows(1)

    rim_columns_own()
    at = pl.multiple_of(row_of(0) + index_x * chunk, 8)
    predict(at - 2 * group, chunk + 4 * group)
    copies = []
    for field, values in enumerate(update(at, chunk)):
        for odd in range(2):
            shift = LANES - (MARGIN + odd * WINDOW) - index_y * cy
            rolled = pltpu.roll(values, shift, 1)
            for x in range(cx):
                for pair in range(pairs):
                    row = x * group + pair * levels
                    out_ref[field, 2 * pair + odd, x] = rolled[row : row + levels, :cy]
        copy = pltpu.make_async_copy(out_ref.at[field], out_hbm.at[:, field], sems.at[1 + field])
        copy.start()
        copies.append(copy)
    for copy in copies:
        copy.wait()


def fast_on_device(state, coriolis, wave_speed, edges):
    count_x = lax.axis_size("tx")
    faces, fields, levels, cx, cy = state.shape
    pairs = faces // 2
    group = pairs * levels
    cells = cx * count_x
    full_rows = fields * (cx // 2) * group + (cx // 2) * pairs
    full_rows = -(-full_rows // 8) * 8
    small_rows = unit_place(fields, 1, cx, group, 2 * cx)[0] + group
    in_vmem = pl.BlockSpec(memory_space=pltpu.VMEM)
    params = pltpu.CompilerParams(vmem_limit_bytes=SMALL_VMEM_LIMIT)
    swap_shape = jax.ShapeDtypeStruct((full_rows + 2 * small_rows, LANES), jnp.float32)
    swap = pl.pallas_call(
        functools.partial(pack_kernel, cx, cy, count_x, full_rows, small_rows),
        out_shape=swap_shape,
        in_specs=[in_vmem],
        out_specs=in_vmem,
        compiler_params=params,
        name="pack",
    )(jnp.swapaxes(state, 2, 3))
    swap, lines = pl.pallas_call(
        functools.partial(pack_coriolis_kernel, cx, cy, count_x, full_rows, small_rows),
        out_shape=[swap_shape, jax.ShapeDtypeStruct((32, LANES), jnp.float32)],
        in_specs=[in_vmem] * 2,
        out_specs=[in_vmem] * 2,
        input_output_aliases={1: 0},
        compiler_params=params,
        name="pack_coriolis",
    )(coriolis, swap)
    keep, middle = pl.pallas_call(
        functools.partial(keep_kernel, cx, cy, count_x, small_rows),
        out_shape=[
            jax.ShapeDtypeStruct((2 * small_rows, LANES), jnp.float32),
            jax.ShapeDtypeStruct((small_rows, LANES), jnp.float32),
        ],
        in_specs=[pl.BlockSpec(memory_space=pltpu.VMEM)] * 2,
        out_specs=[pl.BlockSpec(memory_space=pltpu.VMEM)] * 2,
        compiler_params=pltpu.CompilerParams(vmem_limit_bytes=SMALL_VMEM_LIMIT),
        name="keep",
    )(swap, lines)

    def moved(block, distance):
        pairs_of = []
        for index in range(count_x):
            for core in range(2):
                target = (index + distance * (1 - 2 * core)) % count_x
                pairs_of.append((2 * index + core, 2 * target + core))
        return lax.ppermute(block, ("tx", "ty"), pairs_of)

    def across(block):
        return lax.ppermute(block, "ty", [(0, 1), (1, 0)])

    other = across(swap)
    messages = pl.pallas_call(
        functools.partial(mix_kernel, full_rows, small_rows),
        out_shape=[
            jax.ShapeDtypeStruct((2 * rows, LANES), jnp.float32)
            for rows in (full_rows, small_rows, small_rows)
        ],
        in_specs=[pl.BlockSpec(memory_space=pltpu.VMEM)] * 3,
        out_specs=[pl.BlockSpec(memory_space=pltpu.VMEM)] * 3,
        compiler_params=pltpu.CompilerParams(vmem_limit_bytes=SMALL_VMEM_LIMIT),
        name="messages",
    )(swap, other, keep)
    got = [moved(block, place + 1) for place, block in enumerate(messages)]
    got = jnp.concatenate([*got, moved(middle, count_x // 2)])
    table = jnp.concatenate([wave_speed, edges.reshape(-1).astype(jnp.float32)])
    got, table = lax.optimization_barrier((got, table))
    passed = across(got)

    sizes = (cx, cy, count_x, full_rows, small_rows)
    state_rows = [
        jax.ShapeDtypeStruct((fields, (cells + 8) * group, LANES), jnp.float32),
        jax.ShapeDtypeStruct((cells * group, LANES), jnp.float32),
    ]
    rows = pl.pallas_call(
        functools.partial(own_kernel, sizes),
        out_shape=state_rows,
        in_specs=[in_vmem] * 2,
        out_specs=[in_vmem] * 2,
        compiler_params=params,
        name="place_own",
    )(swap, other)
    rows = pl.pallas_call(
        functools.partial(got_kernel, sizes),
        out_shape=state_rows,
        in_specs=[in_vmem] * 3,
        out_specs=[in_vmem] * 2,
        input_output_aliases={1: 0, 2: 1},
        compiler_params=params,
        name="place_got",
    )(got, *rows)
    out, _, _ = pl.pallas_call(
        functools.partial(step_kernel, sizes),
        out_shape=[jax.ShapeDtypeStruct((faces, fields, cx, levels, cy), jnp.float32)]
        + state_rows,
        in_specs=[in_vmem] * 5,
        out_specs=[pl.BlockSpec(memory_space=pltpu.HBM)] + [in_vmem] * 2,
        input_output_aliases={3: 1, 4: 2},
        scratch_shapes=[
            pltpu.VMEM(((cells + 8) * group, LANES), jnp.float32),
            pltpu.VMEM((faces * 4, 32, LANES), jnp.float32),
            pltpu.VMEM((pairs, LANES, LANES), jnp.float32),
            pltpu.VMEM((pairs, LANES, LANES), jnp.float32),
            pltpu.VMEM(((cx + 4) * group, LANES), jnp.float32),
            pltpu.SMEM(table.shape, jnp.float32),
            pltpu.VMEM((fields, faces, cx, levels, cy), jnp.float32),
            pltpu.SemaphoreType.DMA((1 + fields,)),
        ],
        compiler_params=pltpu.CompilerParams(vmem_limit_bytes=VMEM_LIMIT),
        name="substeps",
    )(got, passed, table, *rows)
    return jnp.swapaxes(out, 2, 3)


def padded_2(block, sides, width):
    for axis, dim in sides:
        count = lax.axis_size(axis)
        forward = [(i, i + 1) for i in range(count - 1)]
        backward = [(target, source) for source, target in forward]
        low = lax.ppermute(
            lax.slice_in_dim(block, block.shape[dim] - width, None, axis=dim), axis, forward
        )
        high = lax.ppermute(lax.slice_in_dim(block, 0, width, axis=dim), axis, backward)
        block = jnp.concatenate([low, block, high], axis=dim)
    return block


def spread(block, axis, owner):
    block = jnp.where(lax.axis_index(axis) == owner, block, jnp.zeros_like(block))
    return lax.psum(block, axis)


def rotate_strip(strip_data, side_index, far_side, flipped):
    normal_part = jnp.where(far_side < 2, strip_data[1], strip_data[2])
    along_part = jnp.where(far_side < 2, strip_data[2], strip_data[1])
    sign_here = 2.0 * (side_index % 2) - 1.0
    sign_there = (2 * (far_side % 2) - 1).astype(jnp.float32)
    normal_part = -sign_here * sign_there * normal_part
    along_part = (1 - 2 * flipped).astype(jnp.float32) * along_part
    if side_index < 2:
        return jnp.stack([strip_data[0], normal_part, along_part])
    return jnp.stack([strip_data[0], along_part, normal_part])


def window_strip(store, side_pick, neighbour, flipped, start, width):
    full_length = store.shape[5]
    begin = jnp.where(flipped == 1, full_length - start - width, start)
    zero = jnp.zeros((), jnp.int32)
    sizes_here = (1, 1, store.shape[2], store.shape[3], store.shape[4], width)
    piece = lax.dynamic_slice(store, (side_pick, neighbour, zero, zero, zero, begin), sizes_here)[
        0, 0
    ]
    return jnp.where(flipped == 1, jnp.flip(piece, 3), piece)


def side_halo(edge_store, edges, face_index, side_index, start, width):
    neighbour = edges[face_index, side_index, 0]
    far_side = edges[face_index, side_index, 1]
    flipped = edges[face_index, side_index, 2]
    strip_data = window_strip(edge_store, far_side, neighbour, flipped, start, width)
    return rotate_strip(strip_data, side_index, far_side, flipped)


def advance(padded, wave_speed, coriolis_part, cells_x, cells_y):
    height = padded[..., 0, :, :, :]
    wind_east = padded[..., 1, :, :, :]
    wind_north = padded[..., 2, :, :, :]
    speed = wave_speed[:, None, None]
    east_pred = wind_east[..., 1 : cells_x + 5, 3 : cells_y + 3] - speed * (
        0.5
        * (
            height[..., 2 : cells_x + 6, 3 : cells_y + 3]
            - height[..., 0 : cells_x + 4, 3 : cells_y + 3]
        )
    )
    north_pred = wind_north[..., 3 : cells_x + 3, 1 : cells_y + 5] - speed * (
        0.5
        * (
            height[..., 3 : cells_x + 3, 2 : cells_y + 6]
            - height[..., 3 : cells_x + 3, 0 : cells_y + 4]
        )
    )
    flux_east = (
        8.0 * (east_pred[..., 3 : cells_x + 3, :] - east_pred[..., 1 : cells_x + 1, :])
        - (east_pred[..., 4 : cells_x + 4, :] - east_pred[..., 0:cells_x, :])
    ) / 12.0
    flux_north = (
        8.0 * (north_pred[..., 3 : cells_y + 3] - north_pred[..., 1 : cells_y + 1])
        - (north_pred[..., 4 : cells_y + 4] - north_pred[..., 0:cells_y])
    ) / 12.0
    height_new = height[..., 3 : cells_x + 3, 3 : cells_y + 3] - speed * (flux_east + flux_north)
    east_inner = east_pred[..., 2 : cells_x + 2, :]
    north_inner = north_pred[..., 2 : cells_y + 2]
    turning = coriolis_part[..., None, :, :]
    return jnp.stack(
        [height_new, east_inner + turning * north_inner, north_inner - turning * east_inner],
        axis=-4,
    )


def one_substep(state, coriolis, wave_speed, edges, count_x, count_y, index_x, index_y):
    faces = state.shape[0]
    cells_x = state.shape[3]
    cells_y = state.shape[4]
    padded = padded_2(state, (("tx", 3), ("ty", 4)), 3)
    west_rim = state[:, :, :, 0:3, :]
    east_rim = jnp.flip(state[:, :, :, cells_x - 3 :, :], 3)
    south_rim = jnp.swapaxes(state[:, :, :, :, 0:3], 3, 4)
    north_rim = jnp.swapaxes(jnp.flip(state[:, :, :, :, cells_y - 3 :], 4), 3, 4)
    west_part = spread(west_rim, "tx", 0)
    east_part = spread(east_rim, "tx", count_x - 1)
    west_full, east_full = (
        lax.all_gather(west_part, "ty", axis=4, tiled=True),
        lax.all_gather(east_part, "ty", axis=4, tiled=True),
    )
    south_row, north_row = (
        lax.all_gather(south_rim, "tx", axis=4, tiled=True),
        lax.all_gather(north_rim, "tx", axis=4, tiled=True),
    )
    south_all, north_all = (
        lax.all_gather(south_row, "ty", axis=0, tiled=True),
        lax.all_gather(north_row, "ty", axis=0, tiled=True),
    )
    south_full = south_all[0:faces]
    north_full = north_all[(count_y - 1) * faces : count_y * faces]
    edge_store = jnp.stack([west_full, east_full, south_full, north_full])
    halos = []
    for side_index in range(4):
        if side_index < 2:
            slabs = jnp.stack(
                [
                    side_halo(edge_store, edges, face_index, side_index, index_y * cells_y, cells_y)
                    for face_index in range(faces)
                ]
            )
        else:
            slabs = jnp.stack(
                [
                    side_halo(edge_store, edges, face_index, side_index, index_x * cells_x, cells_x)
                    for face_index in range(faces)
                ]
            )
        halos.append(slabs)
    west_region = padded[:, :, :, 0:3, 3 : cells_y + 3]
    padded = padded.at[:, :, :, 0:3, 3 : cells_y + 3].set(
        jnp.where(index_x == 0, jnp.flip(halos[0], 3), west_region)
    )
    east_region = padded[:, :, :, cells_x + 3 : cells_x + 6, 3 : cells_y + 3]
    padded = padded.at[:, :, :, cells_x + 3 : cells_x + 6, 3 : cells_y + 3].set(
        jnp.where(index_x == count_x - 1, halos[1], east_region)
    )
    south_region = padded[:, :, :, 3 : cells_x + 3, 0:3]
    padded = padded.at[:, :, :, 3 : cells_x + 3, 0:3].set(
        jnp.where(index_y == 0, jnp.swapaxes(jnp.flip(halos[2], 3), 3, 4), south_region)
    )
    north_region = padded[:, :, :, 3 : cells_x + 3, cells_y + 3 : cells_y + 6]
    padded = padded.at[:, :, :, 3 : cells_x + 3, cells_y + 3 : cells_y + 6].set(
        jnp.where(index_y == count_y - 1, jnp.swapaxes(halos[3], 3, 4), north_region)
    )
    return advance(padded, wave_speed, coriolis, cells_x, cells_y)


def on_device(state, coriolis, wave_speed, edges):
    count_x = lax.axis_size("tx")
    count_y = lax.axis_size("ty")
    index_x = lax.axis_index("tx")
    index_y = lax.axis_index("ty")
    for substep_index in range(SUBSTEPS):
        state = one_substep(state, coriolis, wave_speed, edges, count_x, count_y, index_x, index_y)
    return state


def fits(state):
    count_x = lax.axis_size("tx")
    faces, fields, levels, cells_x, cells_y = state.shape
    return (
        lax.axis_size("ty") == 2
        and faces % 2 == 0
        and levels == 4
        and cells_x == 6
        and cells_y == 24
        and count_x == 8
        and cells_x * count_x == 2 * cells_y
        and 2 * cells_y + 2 * MARGIN <= WINDOW
    )


def either(state, coriolis, wave_speed, edges):
    if fits(state):
        return fast_on_device(state, coriolis, wave_speed, edges)
    return on_device(state, coriolis, wave_speed, edges)


def solution(mesh):
    in_specs = (P("member", None, None, "tx", "ty"), P(None, "tx", "ty"), P(), P())
    out_specs = P("member", None, None, "tx", "ty")
    return jax.shard_map(
        either, mesh=mesh, in_specs=in_specs, out_specs=out_specs, check_vma=False
    )
```

```python
import functools

import jax
import jax.numpy as jnp
from jax import lax
from jax.experimental import pallas as pl
from jax.experimental.pallas import tpu as pltpu
from jax.sharding import PartitionSpec as P

SUBSTEPS = 2
LANES = 128
WINDOW = 64
MARGIN = 8
VMEM_LIMIT = 32 * 1024 * 1024
SMALL_VMEM_LIMIT = 8 * 1024 * 1024


def wrap(index, count):
    index = jnp.where(index < 0, index + count, index)
    return jnp.where(index >= count, index - count, index)


def lane_shift(amount):
    return amount & (LANES - 1)


def windows(source, target, count_x, index_y, cx, cy):
    spare = cy - 2 * cx
    near = jnp.minimum(target, count_x - 1 - target)
    rim = (source == 0) | (source == count_x - 1)
    starts = []
    for inward in (cx // 2, cx):
        start = jnp.maximum(jnp.minimum(cx * near - inward, spare), 0)
        start = jnp.where(rim, start, 0)
        starts.append(jnp.where(index_y == 0, start, spare - start))
    close, far = starts
    upside = source == count_x - 1
    return jnp.where(upside, far, close), jnp.where(upside, close, far)


def unit_place(field, x, cx, group, width):
    per_row = 60 // width
    index = field * cx + x
    return (index // per_row) * group, (index % per_row) * width


def chunk_targets(count_x, full_rows, small_rows):
    sense = 1 - 2 * lax.axis_index("ty")
    return [
        (full_rows + place * small_rows, -sense * distance)
        for place, distance in enumerate((2, 3))
    ]


def put_chunk(cx, cy, count_x, block_ref, line_ref, out_ref, top, offset):
    pairs = 3
    group = 4 * pairs
    fields = 3
    half = cx // 2
    width = 2 * cx
    index_x = lax.axis_index("tx")
    target = wrap(index_x + offset, count_x)
    starts = windows(index_x, target, count_x, lax.axis_index("ty"), cx, cy)
    position = lax.broadcasted_iota(jnp.int32, (group, LANES), 1) % WINDOW
    from_lane = {lane: position >= lane for lane in range(0, 60, width)}
    blocks = {}

    def put(row, lane, lines):
        blocks[row] = lines if row not in blocks else jnp.where(from_lane[lane], lines, blocks[row])

    if block_ref is not None:
        for field in range(fields):
            for x in range(cx):
                row = field * half * group + (x // 2) * group
                at, lane = unit_place(field, x, cx, group, width)
                shift = lane_shift(lane - MARGIN - (x % 2) * cy - starts[x // half])
                put(at, lane, pltpu.roll(block_ref[row : row + group], shift, 1))
    else:
        at = unit_place(fields, 0, cx, group, width)[0]
        blocks[at] = out_ref[top + at : top + at + group]
    if line_ref is not None:
        for part in range(2):
            at, lane = unit_place(fields, part, cx, group, width)
            shift = lane_shift(lane - MARGIN - starts[part])
            put(at, lane, pltpu.roll(line_ref[16 * part : 16 * part + group], shift, 1))
    for row, lines in blocks.items():
        out_ref[top + row : top + row + group] = lines


def pack_kernel(cx, cy, count_x, full_rows, small_rows, state_ref, swap_ref):
    faces, fields = state_ref.shape[:2]
    levels = state_ref.shape[3]
    group = (faces // 2) * levels
    half = cx // 2
    swap_ref[:full_rows] = jnp.zeros((full_rows, LANES), jnp.float32)
    for face in range(faces):
        for parity in range(2):
            lane = (face % 2) * WINDOW + MARGIN + parity * cy
            for xp in range(half):
                for field in range(fields):
                    row = field * half * group + xp * group + (face // 2) * levels
                    swap_ref[row : row + levels, lane : lane + cy] = state_ref[
                        face, field, 2 * xp + parity
                    ]
    for top, offset in chunk_targets(count_x, full_rows, small_rows):
        put_chunk(cx, cy, count_x, swap_ref, None, swap_ref, top, offset)


def pack_coriolis_kernel(
    cx, cy, count_x, full_rows, small_rows, coriolis_ref, swap_in, swap_ref, line_ref
):
    faces = coriolis_ref.shape[0]
    pairs = faces // 2
    half = cx // 2
    base = 3 * half * 4 * pairs
    line_ref[...] = jnp.zeros(line_ref.shape, jnp.float32)
    for face in range(faces):
        lane = (face % 2) * WINDOW + MARGIN
        for x in range(cx):
            line = coriolis_ref[face, x : x + 1]
            row = base + (x // 2) * pairs + face // 2
            at = lane + (x % 2) * cy
            swap_ref[row : row + 1, at : at + cy] = line
            row = (x // half) * 16 + (x % half) * pairs + face // 2
            line_ref[row : row + 1, lane : lane + cy] = line
    for top, offset in chunk_targets(count_x, full_rows, small_rows):
        put_chunk(cx, cy, count_x, None, line_ref, swap_ref, top, offset)


def keep_kernel(cx, cy, count_x, small_rows, swap_ref, line_ref, keep_ref, middle_ref):
    sense = 1 - 2 * lax.axis_index("ty")
    put_chunk(cx, cy, count_x, swap_ref, line_ref, middle_ref, 0, count_x // 2)
    for place, distance in enumerate((2, 3)):
        top = place * small_rows
        put_chunk(cx, cy, count_x, swap_ref, line_ref, keep_ref, top, sense * distance)


def mix_kernel(full_rows, small_rows, swap_ref, other_ref, keep_ref, near_ref, second_ref, third_ref):
    near_ref[:full_rows] = swap_ref[:full_rows]
    near_ref[full_rows:] = other_ref[:full_rows]
    for place, far_ref in enumerate((second_ref, third_ref)):
        at = place * small_rows
        far_ref[:small_rows] = keep_ref[at : at + small_rows]
        at += full_rows
        far_ref[small_rows:] = other_ref[at : at + small_rows]


def placer(cx, cy, count_x, full_rows, small_rows, z_ref, cor_ref):
    fields = z_ref.shape[0]
    levels = 4
    group = z_ref.shape[1] // (cx * count_x + 8)
    pairs = group // levels
    half = cx // 2
    chunk = cx * group
    index_x = lax.axis_index("tx")
    index_y = lax.axis_index("ty")
    south_half = lax.broadcasted_iota(jnp.int32, (group, LANES), 1) % WINDOW < MARGIN + cy
    south_is_own = index_y == 0
    own_half = south_half == south_is_own

    def row_of(x):
        return (x + 4) * group

    def from_owner(offset):
        source = wrap(index_x - offset, count_x)
        return source, pl.multiple_of(source * chunk, 8)

    def put_coriolis(start, x, values, at):
        for pair in range(pairs):
            line = values[at + pair : at + pair + 1]
            rows = pl.ds(start + x * group + pair * levels, levels)
            cor_ref[rows] = jnp.broadcast_to(line, (levels, LANES))

    def put_block(start, lines_of):
        base = fields * half * group
        for field in range(fields):
            for xp in range(half):
                even, odd = lines_of(field * half * group + xp * group, group)
                z_ref[field, pl.ds(start + row_of(2 * xp), group)] = even
                z_ref[field, pl.ds(start + row_of(2 * xp + 1), group)] = odd
        for parity, values in enumerate(lines_of(base, half * pairs)):
            for xp in range(half):
                put_coriolis(start, 2 * xp + parity, values, xp * pairs)

    def put_distant(source, start, lines_of):
        starts_south = windows(source, index_x, count_x, 0, cx, cy)
        starts_north = [cy - 2 * cx - start for start in starts_south]
        is_rim = (source == 0) | (source == count_x - 1)
        starts_north = [jnp.where(is_rim, start, cy - 2 * cx) for start in starts_north]
        shifts = {
            (part, lane): (
                lane_shift(MARGIN + starts_south[part] - lane),
                lane_shift(MARGIN + cy + starts_north[part] - lane),
            )
            for part in range(2)
            for lane in range(0, 60, 2 * cx)
        }

        def lines_at(field, x, part):
            at, lane = unit_place(field, x, cx, group, 2 * cx)
            return lines_of(at, *shifts[part, lane])

        for field in range(fields):
            for x in range(cx):
                z_ref[field, pl.ds(start + row_of(x), group)] = lines_at(field, x, x // half)
        for part in range(2):
            values = lines_at(fields, part, part)
            for x in range(half):
                put_coriolis(start, part * half + x, values, x * pairs)

    def place_own(own_ref, other_ref):
        def own_lines(row, rows):
            mine = own_ref[row : row + rows]
            theirs = other_ref[row : row + rows]
            up, down = index_y * cy, (1 - index_y) * cy
            keep = own_half[:rows]
            even = jnp.where(keep, pltpu.roll(mine, up, 1), pltpu.roll(theirs, down, 1))
            mine = pltpu.roll(mine, lane_shift(-down), 1)
            theirs = pltpu.roll(theirs, lane_shift(-up), 1)
            return even, jnp.where(keep, mine, theirs)

        put_block(from_owner(0)[1], own_lines)

    def place_got(block_ref, toward, south_first):
        south_top = pl.multiple_of(south_first * full_rows, 8)
        north_top = pl.multiple_of((1 - south_first) * full_rows, 8)

        def near_lines(row, rows):
            south = block_ref[pl.ds(south_top + row, rows)]
            north = block_ref[pl.ds(north_top + row, rows)]
            low = south_half[:rows]
            even = jnp.where(low, south, pltpu.roll(north, cy, 1))
            return even, jnp.where(low, pltpu.roll(south, LANES - cy, 1), north)

        put_block(from_owner(toward)[1], near_lines)
        for place, distance in enumerate((2, 3)):
            top = 2 * full_rows + 2 * place * small_rows
            south_at = pl.multiple_of(top + south_first * small_rows, 8)
            north_at = pl.multiple_of(top + (1 - south_first) * small_rows, 8)

            def far_lines(at, south_shift, north_shift, south_at=south_at, north_at=north_at):
                south = pltpu.roll(block_ref[pl.ds(south_at + at, group)], south_shift, 1)
                north = pltpu.roll(block_ref[pl.ds(north_at + at, group)], north_shift, 1)
                return jnp.where(south_half, south, north)

            put_distant(*from_owner(toward * distance), far_lines)

    def place_middle(got_ref, got_other_ref):
        def middle_lines(at, south_shift, north_shift):
            row = 2 * full_rows + 4 * small_rows + at
            mine_shift = jnp.where(south_is_own, south_shift, north_shift)
            other_shift = jnp.where(south_is_own, north_shift, south_shift)
            mine = pltpu.roll(got_ref[row : row + group], mine_shift, 1)
            theirs = pltpu.roll(got_other_ref[row : row + group], other_shift, 1)
            return jnp.where(own_half, mine, theirs)

        put_distant(*from_owner(count_x // 2), middle_lines)

    return place_own, place_got, place_middle


def own_kernel(sizes, own_ref, other_ref, z_ref, cor_ref):
    placer(*sizes, z_ref, cor_ref)[0](own_ref, other_ref)


def got_kernel(sizes, got_ref, z_in, cor_in, z_ref, cor_ref):
    index_y = lax.axis_index("ty")
    placer(*sizes, z_ref, cor_ref)[1](got_ref, 1 - 2 * index_y, index_y)


def step_kernel(
    sizes, got_ref, got_other_ref, table_in, z_in, cor_in, out_hbm, z_ref, cor_ref,
    pred_ref, store_ref, tile_ref, flip_ref, speed_ref, table_ref, out_ref, sems,
):
    table_copy = pltpu.make_async_copy(table_in, table_ref, sems.at[0])
    table_copy.start()
    cx, cy, count_x = sizes[:3]
    levels = 4
    slots = 16
    cells = cx * count_x
    faces = store_ref.shape[0] // 4
    pairs = faces // 2
    group = pairs * levels
    chunk = cx * group
    index_x = lax.axis_index("tx")
    index_y = lax.axis_index("ty")

    def row_of(x):
        return (x + 4) * group

    def lanes_of(rows):
        return lax.broadcasted_iota(jnp.int32, (rows, LANES), 1)

    _, place_got, place_middle = placer(*sizes, z_ref, cor_ref)
    place_got(got_other_ref, 2 * index_y - 1, 1 - index_y)
    place_middle(got_ref, got_other_ref)

    table_copy.wait()
    level_of = lax.broadcasted_iota(jnp.int32, speed_ref.shape, 0) % levels
    speeds = jnp.full(speed_ref.shape, table_ref[0], jnp.float32)
    for index in range(1, levels):
        speeds = jnp.where(level_of == index, table_ref[index], speeds)
    speed_ref[...] = speeds

    lane_8 = lanes_of(8)
    place_8 = lane_8 % WINDOW
    gap = WINDOW - cells + 3
    wide = gap + 3 * levels
    row_tiles = range(0, cells, 8)
    rim_8 = ((place_8 >= MARGIN - 3) & (place_8 < MARGIN)) | (
        (place_8 >= MARGIN + cells) & (place_8 < MARGIN + cells + 3)
    )

    def collect():
        for pair in range(pairs):
            merged = [jnp.zeros((8, LANES), jnp.float32)] * len(row_tiles)
            for slot, field in ((0, 0), (1, 2)):
                for level in range(levels):
                    offset = slot * wide + 3 * level
                    here = place_8 - offset
                    wanted = ((here >= 0) & (here < 3)) | ((here >= gap) & (here < gap + 3))
                    shift = (offset - (MARGIN + cells - 3)) % LANES
                    lines = z_ref[field, pl.ds(row_of(0) + pair * levels + level, cells, group)]
                    lines = pltpu.roll(lines, shift, 1)
                    merged = [
                        jnp.where(wanted, lines[row : row + 8], old)
                        for row, old in zip(row_tiles, merged)
                    ]
            flip_ref[pair, :, :cells] = jnp.concatenate(merged, axis=0).T
            for slot in range(2):
                for side in (2, 3):
                    for odd in range(2):
                        for depth in range(3):
                            base = slot * wide
                            if side == 3:
                                base += odd * WINDOW + 2 - depth
                            else:
                                base += ((odd + 1) % 2) * WINDOW + gap + depth
                            at = slot * slots + depth * levels
                            store_ref[(2 * pair + odd) * 4 + side, at : at + levels] = flip_ref[
                                pair, pl.ds(base, levels, 3)
                            ]
            for slot in range(2):
                for side in (0, 1):
                    for depth in range(3):
                        x = depth if side == 0 else cells - 1 - depth
                        row = row_of(x) + pair * levels
                        lines = z_ref[slot, row : row + levels]
                        at = slot * slots + depth * levels
                        for odd in range(2):
                            store_ref[(2 * pair + odd) * 4 + side, at : at + levels] = lines

    def fetch(face, side, positions):
        at = levels + (face * 4 + side) * 3
        neighbour = table_ref[at].astype(jnp.int32)
        far_side = table_ref[at + 1].astype(jnp.int32)
        flipped = table_ref[at + 2].astype(jnp.int32)
        first = jnp.where(far_side < 2, MARGIN + WINDOW * (neighbour & 1), 0)
        start = first + jnp.where(flipped == 1, cells - 1, 0)
        step = 1 - 2 * flipped
        sign = ((1 - 2 * (side % 2)) * (2 * (far_side & 1) - 1)).astype(jnp.float32)
        index = neighbour * 4 + far_side
        parts = []
        for slot, position in enumerate(positions):
            order = (start + step * position) & (LANES - 1)
            for half_at in (0, 8):
                at = slot * slots + half_at
                lines = jnp.take_along_axis(store_ref[index, at : at + 8], order, axis=1)
                parts.append(lines if slot == 0 else sign * lines)
        return parts[:2], parts[2:]

    def depth_rows(parts, depth):
        at = (depth % 2) * levels
        return parts[depth // 2][at : at + levels]

    def rim_rows(side):
        left = lane_8 < WINDOW
        for pair in range(pairs):
            first = fetch(2 * pair, side, [lane_8 - MARGIN] * 2)
            second = fetch(2 * pair + 1, side, [lane_8 - (MARGIN + WINDOW)] * 2)
            for slot in range(2):
                both = [jnp.where(left, a, b) for a, b in zip(first[slot], second[slot])]
                for depth in range(3):
                    x = -1 - depth if side == 0 else cells + depth
                    row = row_of(x) + pair * levels
                    z_ref[slot, row : row + levels] = depth_rows(both, depth)

    tile_wide = WINDOW - cells - 3 + 3 * levels

    def put_tile(tile, parts, odd, side, base=0):
        for depth in range(3):
            if side == 3:
                at = base + odd * WINDOW + depth
            else:
                at = base + ((odd + 1) % 2) * WINDOW + tile_wide - 3 * levels + 2 - depth
            tile_ref[tile, pl.ds(at, levels, 3)] = depth_rows(parts, depth)

    def rim_columns_all():
        for pair in range(pairs):
            for odd in range(2):
                for side in (2, 3):
                    for slot, parts in enumerate(fetch(2 * pair + odd, side, [lane_8] * 2)):
                        put_tile(pair, parts, odd, side, slot * tile_wide)
            turned = tile_ref[pair].T[:cells]
            for slot, field in ((0, 0), (1, 2)):
                for level in range(levels):
                    shift = (MARGIN + cells - slot * tile_wide - 3 * level) % LANES
                    rolled = pltpu.roll(turned, shift, 1)
                    at = pl.ds(row_of(0) + pair * levels + level, cells, group)
                    lines = z_ref[field, at]
                    lines = [
                        jnp.where(rim_8, rolled[row : row + 8], lines[row : row + 8])
                        for row in row_tiles
                    ]
                    z_ref[field, at] = jnp.concatenate(lines, axis=0)

    def rim_columns_own():
        for odd in range(2):
            for side in (2, 3):
                total = [jnp.zeros((8, LANES), jnp.float32)] * 2
                for pair in range(pairs):
                    places = [8 * pair, 8 * (pairs + pair)]
                    positions = [lane_8 + (index_x * cx - place) for place in places]
                    fetched = fetch(2 * pair + odd, side, positions)
                    for place, parts in zip(places, fetched):
                        here = (lane_8 >= place) & (lane_8 < place + 8)
                        total = [jnp.where(here, a, b) for a, b in zip(parts, total)]
                put_tile(0, total, odd, side)
        turned = tile_ref[0].T
        for slot, field in ((0, 0), (1, 2)):
            for pair in range(pairs):
                row = 8 * (slot * pairs + pair)
                for level in range(levels):
                    shift = (MARGIN + cells - 3 * level) % LANES
                    rolled = pltpu.roll(turned[row : row + 8], shift, 1)[:cx]
                    start = row_of(0) + index_x * chunk + pair * levels + level
                    at = pl.ds(start, cx, group)
                    z_ref[field, at] = jnp.where(rim_8[:cx], rolled, z_ref[field, at])

    def predict(at, rows):
        speed = speed_ref[:rows]
        ahead = z_ref[0, pl.ds(at + group, rows)]
        behind = z_ref[0, pl.ds(at - group, rows)]
        pred_ref[pl.ds(at, rows)] = z_ref[1, pl.ds(at, rows)] - speed * (0.5 * (ahead - behind))

    def update(at, rows):
        speed = speed_ref[:rows]
        height = z_ref[0, pl.ds(at, rows)]
        north_pred = z_ref[2, pl.ds(at, rows)] - speed * (
            0.5 * (pltpu.roll(height, LANES - 1, 1) - pltpu.roll(height, 1, 1))
        )
        east_pred = pred_ref[pl.ds(at, rows)]
        flux_east = 8.0 * (
            pred_ref[pl.ds(at + group, rows)] - pred_ref[pl.ds(at - group, rows)]
        ) - (pred_ref[pl.ds(at + 2 * group, rows)] - pred_ref[pl.ds(at - 2 * group, rows)])
        flux_north = 8.0 * (
            pltpu.roll(north_pred, LANES - 1, 1) - pltpu.roll(north_pred, 1, 1)
        ) - (pltpu.roll(north_pred, LANES - 2, 1) - pltpu.roll(north_pred, 2, 1))
        height = height - speed * ((flux_east + flux_north) * (1.0 / 12.0))
        turning = cor_ref[pl.ds(at - row_of(0), rows)]
        return height, east_pred + turning * north_pred, north_pred - turning * east_pred

    def all_faces():
        rim_rows(0)
        rim_rows(1)
        rim_columns_all()
        for first in range(-2, cells + 2, 4):
            predict(row_of(first), 4 * group)
        def update_part(index, carry):
            at = pl.multiple_of(row_of(0) + index * (2 * chunk), 8)
            for field, values in enumerate(update(at, 2 * chunk)):
                z_ref[field, pl.ds(at, 2 * chunk)] = values
            return carry

        lax.fori_loop(0, count_x // 2, update_part, 0)

    def own_rows():

        @pl.when(index_x == 0)
        def _():
            rim_rows(0)

        @pl.when(index_x == count_x - 1)
        def _():
            rim_rows(1)

        rim_columns_own()
        at = pl.multiple_of(row_of(0) + index_x * chunk, 8)
        predict(at - 2 * group, chunk + 4 * group)
        copies = []
        for field, values in enumerate(update(at, chunk)):
            for odd in range(2):
                shift = LANES - (MARGIN + odd * WINDOW) - index_y * cy
                rolled = pltpu.roll(values, shift, 1)
                for x in range(cx):
                    for pair in range(pairs):
                        row = x * group + pair * levels
                        out_ref[field, 2 * pair + odd, x] = rolled[row : row + levels, :cy]
            copy = pltpu.make_async_copy(out_ref.at[field], out_hbm.at[:, field], sems.at[1 + field])
            copy.start()
            copies.append(copy)
        for copy in copies:
            copy.wait()

    def substep(index, carry):
        collect()
        pl.when(index == 0)(all_faces)
        pl.when(index == SUBSTEPS - 1)(own_rows)
        return carry

    lax.fori_loop(0, SUBSTEPS, substep, 0)


def fast_on_device(state, coriolis, wave_speed, edges):
    count_x = lax.axis_size("tx")
    faces, fields, levels, cx, cy = state.shape
    pairs = faces // 2
    group = pairs * levels
    cells = cx * count_x
    full_rows = fields * (cx // 2) * group + (cx // 2) * pairs
    full_rows = -(-full_rows // 8) * 8
    small_rows = unit_place(fields, 1, cx, group, 2 * cx)[0] + group
    in_vmem = pl.BlockSpec(memory_space=pltpu.VMEM)
    params = pltpu.CompilerParams(vmem_limit_bytes=SMALL_VMEM_LIMIT)
    swap_shape = jax.ShapeDtypeStruct((full_rows + 2 * small_rows, LANES), jnp.float32)
    swap = pl.pallas_call(
        functools.partial(pack_kernel, cx, cy, count_x, full_rows, small_rows),
        out_shape=swap_shape,
        in_specs=[in_vmem],
        out_specs=in_vmem,
        compiler_params=params,
        name="pack",
    )(jnp.swapaxes(state, 2, 3))
    swap, lines = pl.pallas_call(
        functools.partial(pack_coriolis_kernel, cx, cy, count_x, full_rows, small_rows),
        out_shape=[swap_shape, jax.ShapeDtypeStruct((32, LANES), jnp.float32)],
        in_specs=[in_vmem] * 2,
        out_specs=[in_vmem] * 2,
        input_output_aliases={1: 0},
        compiler_params=params,
        name="pack_coriolis",
    )(coriolis, swap)
    keep, middle = pl.pallas_call(
        functools.partial(keep_kernel, cx, cy, count_x, small_rows),
        out_shape=[
            jax.ShapeDtypeStruct((2 * small_rows, LANES), jnp.float32),
            jax.ShapeDtypeStruct((small_rows, LANES), jnp.float32),
        ],
        in_specs=[pl.BlockSpec(memory_space=pltpu.VMEM)] * 2,
        out_specs=[pl.BlockSpec(memory_space=pltpu.VMEM)] * 2,
        compiler_params=pltpu.CompilerParams(vmem_limit_bytes=SMALL_VMEM_LIMIT),
        name="keep",
    )(swap, lines)

    def moved(block, distance):
        pairs_of = []
        for index in range(count_x):
            for core in range(2):
                target = (index + distance * (1 - 2 * core)) % count_x
                pairs_of.append((2 * index + core, 2 * target + core))
        return lax.ppermute(block, ("tx", "ty"), pairs_of)

    def across(block):
        return lax.ppermute(block, "ty", [(0, 1), (1, 0)])

    other = across(swap)
    messages = pl.pallas_call(
        functools.partial(mix_kernel, full_rows, small_rows),
        out_shape=[
            jax.ShapeDtypeStruct((2 * rows, LANES), jnp.float32)
            for rows in (full_rows, small_rows, small_rows)
        ],
        in_specs=[pl.BlockSpec(memory_space=pltpu.VMEM)] * 3,
        out_specs=[pl.BlockSpec(memory_space=pltpu.VMEM)] * 3,
        compiler_params=pltpu.CompilerParams(vmem_limit_bytes=SMALL_VMEM_LIMIT),
        name="messages",
    )(swap, other, keep)
    got = [moved(block, place + 1) for place, block in enumerate(messages)]
    got = jnp.concatenate([*got, moved(middle, count_x // 2)])
    table = jnp.concatenate([wave_speed, edges.reshape(-1).astype(jnp.float32)])
    got, table = lax.optimization_barrier((got, table))
    passed = across(got)

    sizes = (cx, cy, count_x, full_rows, small_rows)
    state_rows = [
        jax.ShapeDtypeStruct((fields, (cells + 8) * group, LANES), jnp.float32),
        jax.ShapeDtypeStruct((cells * group, LANES), jnp.float32),
    ]
    rows = pl.pallas_call(
        functools.partial(own_kernel, sizes),
        out_shape=state_rows,
        in_specs=[in_vmem] * 2,
        out_specs=[in_vmem] * 2,
        compiler_params=params,
        name="place_own",
    )(swap, other)
    rows = pl.pallas_call(
        functools.partial(got_kernel, sizes),
        out_shape=state_rows,
        in_specs=[in_vmem] * 3,
        out_specs=[in_vmem] * 2,
        input_output_aliases={1: 0, 2: 1},
        compiler_params=params,
        name="place_got",
    )(got, *rows)
    out, _, _ = pl.pallas_call(
        functools.partial(step_kernel, sizes),
        out_shape=[jax.ShapeDtypeStruct((faces, fields, cx, levels, cy), jnp.float32)]
        + state_rows,
        in_specs=[in_vmem] * 5,
        out_specs=[pl.BlockSpec(memory_space=pltpu.HBM)] + [in_vmem] * 2,
        input_output_aliases={3: 1, 4: 2},
        scratch_shapes=[
            pltpu.VMEM(((cells + 8) * group, LANES), jnp.float32),
            pltpu.VMEM((faces * 4, 32, LANES), jnp.float32),
            pltpu.VMEM((pairs, LANES, LANES), jnp.float32),
            pltpu.VMEM((pairs, LANES, LANES), jnp.float32),
            pltpu.VMEM((2 * cx * group, LANES), jnp.float32),
            pltpu.SMEM(table.shape, jnp.float32),
            pltpu.VMEM((fields, faces, cx, levels, cy), jnp.float32),
            pltpu.SemaphoreType.DMA((1 + fields,)),
        ],
        compiler_params=pltpu.CompilerParams(vmem_limit_bytes=VMEM_LIMIT),
        name="substeps",
    )(got, passed, table, *rows)
    return jnp.swapaxes(out, 2, 3)


def padded_2(block, sides, width):
    for axis, dim in sides:
        count = lax.axis_size(axis)
        forward = [(i, i + 1) for i in range(count - 1)]
        backward = [(target, source) for source, target in forward]
        low = lax.ppermute(
            lax.slice_in_dim(block, block.shape[dim] - width, None, axis=dim), axis, forward
        )
        high = lax.ppermute(lax.slice_in_dim(block, 0, width, axis=dim), axis, backward)
        block = jnp.concatenate([low, block, high], axis=dim)
    return block


def spread(block, axis, owner):
    block = jnp.where(lax.axis_index(axis) == owner, block, jnp.zeros_like(block))
    return lax.psum(block, axis)


def rotate_strip(strip_data, side_index, far_side, flipped):
    normal_part = jnp.where(far_side < 2, strip_data[1], strip_data[2])
    along_part = jnp.where(far_side < 2, strip_data[2], strip_data[1])
    sign_here = 2.0 * (side_index % 2) - 1.0
    sign_there = (2 * (far_side % 2) - 1).astype(jnp.float32)
    normal_part = -sign_here * sign_there * normal_part
    along_part = (1 - 2 * flipped).astype(jnp.float32) * along_part
    if side_index < 2:
        return jnp.stack([strip_data[0], normal_part, along_part])
    return jnp.stack([strip_data[0], along_part, normal_part])


def window_strip(store, side_pick, neighbour, flipped, start, width):
    full_length = store.shape[5]
    begin = jnp.where(flipped == 1, full_length - start - width, start)
    zero = jnp.zeros((), jnp.int32)
    sizes_here = (1, 1, store.shape[2], store.shape[3], store.shape[4], width)
    piece = lax.dynamic_slice(store, (side_pick, neighbour, zero, zero, zero, begin), sizes_here)[
        0, 0
    ]
    return jnp.where(flipped == 1, jnp.flip(piece, 3), piece)


def side_halo(edge_store, edges, face_index, side_index, start, width):
    neighbour = edges[face_index, side_index, 0]
    far_side = edges[face_index, side_index, 1]
    flipped = edges[face_index, side_index, 2]
    strip_data = window_strip(edge_store, far_side, neighbour, flipped, start, width)
    return rotate_strip(strip_data, side_index, far_side, flipped)


def advance(padded, wave_speed, coriolis_part, cells_x, cells_y):
    height = padded[..., 0, :, :, :]
    wind_east = padded[..., 1, :, :, :]
    wind_north = padded[..., 2, :, :, :]
    speed = wave_speed[:, None, None]
    east_pred = wind_east[..., 1 : cells_x + 5, 3 : cells_y + 3] - speed * (
        0.5
        * (
            height[..., 2 : cells_x + 6, 3 : cells_y + 3]
            - height[..., 0 : cells_x + 4, 3 : cells_y + 3]
        )
    )
    north_pred = wind_north[..., 3 : cells_x + 3, 1 : cells_y + 5] - speed * (
        0.5
        * (
            height[..., 3 : cells_x + 3, 2 : cells_y + 6]
            - height[..., 3 : cells_x + 3, 0 : cells_y + 4]
        )
    )
    flux_east = (
        8.0 * (east_pred[..., 3 : cells_x + 3, :] - east_pred[..., 1 : cells_x + 1, :])
        - (east_pred[..., 4 : cells_x + 4, :] - east_pred[..., 0:cells_x, :])
    ) / 12.0
    flux_north = (
        8.0 * (north_pred[..., 3 : cells_y + 3] - north_pred[..., 1 : cells_y + 1])
        - (north_pred[..., 4 : cells_y + 4] - north_pred[..., 0:cells_y])
    ) / 12.0
    height_new = height[..., 3 : cells_x + 3, 3 : cells_y + 3] - speed * (flux_east + flux_north)
    east_inner = east_pred[..., 2 : cells_x + 2, :]
    north_inner = north_pred[..., 2 : cells_y + 2]
    turning = coriolis_part[..., None, :, :]
    return jnp.stack(
        [height_new, east_inner + turning * north_inner, north_inner - turning * east_inner],
        axis=-4,
    )


def one_substep(state, coriolis, wave_speed, edges, count_x, count_y, index_x, index_y):
    faces = state.shape[0]
    cells_x = state.shape[3]
    cells_y = state.shape[4]
    padded = padded_2(state, (("tx", 3), ("ty", 4)), 3)
    west_rim = state[:, :, :, 0:3, :]
    east_rim = jnp.flip(state[:, :, :, cells_x - 3 :, :], 3)
    south_rim = jnp.swapaxes(state[:, :, :, :, 0:3], 3, 4)
    north_rim = jnp.swapaxes(jnp.flip(state[:, :, :, :, cells_y - 3 :], 4), 3, 4)
    west_part = spread(west_rim, "tx", 0)
    east_part = spread(east_rim, "tx", count_x - 1)
    west_full, east_full = (
        lax.all_gather(west_part, "ty", axis=4, tiled=True),
        lax.all_gather(east_part, "ty", axis=4, tiled=True),
    )
    south_row, north_row = (
        lax.all_gather(south_rim, "tx", axis=4, tiled=True),
        lax.all_gather(north_rim, "tx", axis=4, tiled=True),
    )
    south_all, north_all = (
        lax.all_gather(south_row, "ty", axis=0, tiled=True),
        lax.all_gather(north_row, "ty", axis=0, tiled=True),
    )
    south_full = south_all[0:faces]
    north_full = north_all[(count_y - 1) * faces : count_y * faces]
    edge_store = jnp.stack([west_full, east_full, south_full, north_full])
    halos = []
    for side_index in range(4):
        if side_index < 2:
            slabs = jnp.stack(
                [
                    side_halo(edge_store, edges, face_index, side_index, index_y * cells_y, cells_y)
                    for face_index in range(faces)
                ]
            )
        else:
            slabs = jnp.stack(
                [
                    side_halo(edge_store, edges, face_index, side_index, index_x * cells_x, cells_x)
                    for face_index in range(faces)
                ]
            )
        halos.append(slabs)
    west_region = padded[:, :, :, 0:3, 3 : cells_y + 3]
    padded = padded.at[:, :, :, 0:3, 3 : cells_y + 3].set(
        jnp.where(index_x == 0, jnp.flip(halos[0], 3), west_region)
    )
    east_region = padded[:, :, :, cells_x + 3 : cells_x + 6, 3 : cells_y + 3]
    padded = padded.at[:, :, :, cells_x + 3 : cells_x + 6, 3 : cells_y + 3].set(
        jnp.where(index_x == count_x - 1, halos[1], east_region)
    )
    south_region = padded[:, :, :, 3 : cells_x + 3, 0:3]
    padded = padded.at[:, :, :, 3 : cells_x + 3, 0:3].set(
        jnp.where(index_y == 0, jnp.swapaxes(jnp.flip(halos[2], 3), 3, 4), south_region)
    )
    north_region = padded[:, :, :, 3 : cells_x + 3, cells_y + 3 : cells_y + 6]
    padded = padded.at[:, :, :, 3 : cells_x + 3, cells_y + 3 : cells_y + 6].set(
        jnp.where(index_y == count_y - 1, jnp.swapaxes(halos[3], 3, 4), north_region)
    )
    return advance(padded, wave_speed, coriolis, cells_x, cells_y)


def on_device(state, coriolis, wave_speed, edges):
    count_x = lax.axis_size("tx")
    count_y = lax.axis_size("ty")
    index_x = lax.axis_index("tx")
    index_y = lax.axis_index("ty")
    for substep_index in range(SUBSTEPS):
        state = one_substep(state, coriolis, wave_speed, edges, count_x, count_y, index_x, index_y)
    return state


def fits(state):
    count_x = lax.axis_size("tx")
    faces, fields, levels, cells_x, cells_y = state.shape
    return (
        lax.axis_size("ty") == 2
        and faces % 2 == 0
        and levels == 4
        and cells_x == 6
        and cells_y == 24
        and count_x == 8
        and cells_x * count_x == 2 * cells_y
        and 2 * cells_y + 2 * MARGIN <= WINDOW
    )


def either(state, coriolis, wave_speed, edges):
    if fits(state):
        return fast_on_device(state, coriolis, wave_speed, edges)
    return on_device(state, coriolis, wave_speed, edges)


def solution(mesh):
    in_specs = (P("member", None, None, "tx", "ty"), P(None, "tx", "ty"), P(), P())
    out_specs = P("member", None, None, "tx", "ty")
    return jax.shard_map(
        either, mesh=mesh, in_specs=in_specs, out_specs=out_specs, check_vma=False
    )
```

```python
import functools

import jax
import jax.numpy as jnp
from jax import lax
from jax.experimental import pallas as pl
from jax.experimental.pallas import tpu as pltpu
from jax.sharding import PartitionSpec as P

SUBSTEPS = 2
LANES = 128
WINDOW = 64
MARGIN = 8
VMEM_LIMIT = 32 * 1024 * 1024
SMALL_VMEM_LIMIT = 8 * 1024 * 1024


def wrap(index, count):
    index = jnp.where(index < 0, index + count, index)
    return jnp.where(index >= count, index - count, index)


def lane_shift(amount):
    return amount & (LANES - 1)


def windows(source, target, count_x, index_y, cx, cy):
    spare = cy - 2 * cx
    near = jnp.minimum(target, count_x - 1 - target)
    rim = (source == 0) | (source == count_x - 1)
    starts = []
    for inward in (cx // 2, cx):
        start = jnp.maximum(jnp.minimum(cx * near - inward, spare), 0)
        start = jnp.where(rim, start, 0)
        starts.append(jnp.where(index_y == 0, start, spare - start))
    close, far = starts
    upside = source == count_x - 1
    return jnp.where(upside, far, close), jnp.where(upside, close, far)


def unit_place(field, x, cx, group, width):
    per_row = 60 // width
    index = field * cx + x
    return (index // per_row) * group, (index % per_row) * width


def chunk_targets(count_x, full_rows, small_rows):
    sense = 1 - 2 * lax.axis_index("ty")
    return [
        (full_rows + place * small_rows, -sense * distance)
        for place, distance in enumerate((2, 3))
    ]


def put_chunk(cx, cy, count_x, block_ref, line_ref, out_ref, top, offset):
    pairs = 3
    group = 4 * pairs
    fields = 3
    half = cx // 2
    width = 2 * cx
    index_x = lax.axis_index("tx")
    target = wrap(index_x + offset, count_x)
    starts = windows(index_x, target, count_x, lax.axis_index("ty"), cx, cy)
    position = lax.broadcasted_iota(jnp.int32, (group, LANES), 1) % WINDOW
    from_lane = {lane: position >= lane for lane in range(0, 60, width)}
    blocks = {}

    def put(row, lane, lines):
        blocks[row] = lines if row not in blocks else jnp.where(from_lane[lane], lines, blocks[row])

    if block_ref is not None:
        for field in range(fields):
            for x in range(cx):
                row = field * half * group + (x // 2) * group
                at, lane = unit_place(field, x, cx, group, width)
                shift = lane_shift(lane - MARGIN - (x % 2) * cy - starts[x // half])
                put(at, lane, pltpu.roll(block_ref[row : row + group], shift, 1))
    else:
        at = unit_place(fields, 0, cx, group, width)[0]
        blocks[at] = out_ref[top + at : top + at + group]
    if line_ref is not None:
        for part in range(2):
            at, lane = unit_place(fields, part, cx, group, width)
            shift = lane_shift(lane - MARGIN - starts[part])
            put(at, lane, pltpu.roll(line_ref[16 * part : 16 * part + group], shift, 1))
    for row, lines in blocks.items():
        out_ref[top + row : top + row + group] = lines


def pack_kernel(cx, cy, count_x, full_rows, small_rows, state_ref, swap_ref):
    faces, fields = state_ref.shape[:2]
    levels = state_ref.shape[3]
    group = (faces // 2) * levels
    half = cx // 2
    swap_ref[:full_rows] = jnp.zeros((full_rows, LANES), jnp.float32)
    for face in range(faces):
        for parity in range(2):
            lane = (face % 2) * WINDOW + MARGIN + parity * cy
            for xp in range(half):
                for field in range(fields):
                    row = field * half * group + xp * group + (face // 2) * levels
                    swap_ref[row : row + levels, lane : lane + cy] = state_ref[
                        face, field, 2 * xp + parity
                    ]
    for top, offset in chunk_targets(count_x, full_rows, small_rows):
        put_chunk(cx, cy, count_x, swap_ref, None, swap_ref, top, offset)


def pack_coriolis_kernel(
    cx, cy, count_x, full_rows, small_rows, coriolis_ref, swap_in, swap_ref, line_ref
):
    faces = coriolis_ref.shape[0]
    pairs = faces // 2
    half = cx // 2
    base = 3 * half * 4 * pairs
    line_ref[...] = jnp.zeros(line_ref.shape, jnp.float32)
    for face in range(faces):
        lane = (face % 2) * WINDOW + MARGIN
        for x in range(cx):
            line = coriolis_ref[face, x : x + 1]
            row = base + (x // 2) * pairs + face // 2
            at = lane + (x % 2) * cy
            swap_ref[row : row + 1, at : at + cy] = line
            row = (x // half) * 16 + (x % half) * pairs + face // 2
            line_ref[row : row + 1, lane : lane + cy] = line
    for top, offset in chunk_targets(count_x, full_rows, small_rows):
        put_chunk(cx, cy, count_x, None, line_ref, swap_ref, top, offset)


def keep_kernel(cx, cy, count_x, small_rows, swap_ref, line_ref, keep_ref, middle_ref):
    sense = 1 - 2 * lax.axis_index("ty")
    put_chunk(cx, cy, count_x, swap_ref, line_ref, middle_ref, 0, count_x // 2)
    for place, distance in enumerate((2, 3)):
        top = place * small_rows
        put_chunk(cx, cy, count_x, swap_ref, line_ref, keep_ref, top, sense * distance)


def mix_kernel(
    full_rows, small_rows, swap_ref, other_ref, keep_ref, middle_ref,
    near_ref, third_ref, second_ref, fourth_ref,
):
    near_ref[:full_rows] = swap_ref[:full_rows]
    near_ref[full_rows:] = other_ref[:full_rows]
    for place, far_ref in enumerate((second_ref, third_ref)):
        at = place * small_rows
        far_ref[:small_rows] = keep_ref[at : at + small_rows]
        at += full_rows
        far_ref[small_rows:] = other_ref[at : at + small_rows]
    fourth_ref[...] = middle_ref[...]


def placer(cx, cy, count_x, full_rows, small_rows, z_ref, cor_ref):
    fields = z_ref.shape[0]
    levels = 4
    group = z_ref.shape[1] // (cx * count_x + 8)
    pairs = group // levels
    half = cx // 2
    chunk = cx * group
    index_x = lax.axis_index("tx")
    index_y = lax.axis_index("ty")
    south_half = lax.broadcasted_iota(jnp.int32, (group, LANES), 1) % WINDOW < MARGIN + cy
    south_is_own = index_y == 0
    own_half = south_half == south_is_own

    def row_of(x):
        return (x + 4) * group

    def from_owner(offset):
        source = wrap(index_x - offset, count_x)
        return source, pl.multiple_of(source * chunk, 8)

    def put_coriolis(start, x, values, at):
        for pair in range(pairs):
            line = values[at + pair : at + pair + 1]
            rows = pl.ds(start + x * group + pair * levels, levels)
            cor_ref[rows] = jnp.broadcast_to(line, (levels, LANES))

    def put_block(start, lines_of):
        base = fields * half * group
        for field in range(fields):
            for xp in range(half):
                even, odd = lines_of(field * half * group + xp * group, group)
                z_ref[field, pl.ds(start + row_of(2 * xp), group)] = even
                z_ref[field, pl.ds(start + row_of(2 * xp + 1), group)] = odd
        for parity, values in enumerate(lines_of(base, half * pairs)):
            for xp in range(half):
                put_coriolis(start, 2 * xp + parity, values, xp * pairs)

    def put_distant(source, start, lines_of):
        starts_south = windows(source, index_x, count_x, 0, cx, cy)
        starts_north = [cy - 2 * cx - start for start in starts_south]
        is_rim = (source == 0) | (source == count_x - 1)
        starts_north = [jnp.where(is_rim, start, cy - 2 * cx) for start in starts_north]
        shifts = {
            (part, lane): (
                lane_shift(MARGIN + starts_south[part] - lane),
                lane_shift(MARGIN + cy + starts_north[part] - lane),
            )
            for part in range(2)
            for lane in range(0, 60, 2 * cx)
        }

        def lines_at(field, x, part):
            at, lane = unit_place(field, x, cx, group, 2 * cx)
            return lines_of(at, *shifts[part, lane])

        for field in range(fields):
            for x in range(cx):
                z_ref[field, pl.ds(start + row_of(x), group)] = lines_at(field, x, x // half)
        for part in range(2):
            values = lines_at(fields, part, part)
            for x in range(half):
                put_coriolis(start, part * half + x, values, x * pairs)

    def place_own(own_ref, other_ref):
        def own_lines(row, rows):
            mine = own_ref[row : row + rows]
            theirs = other_ref[row : row + rows]
            up, down = index_y * cy, (1 - index_y) * cy
            keep = own_half[:rows]
            even = jnp.where(keep, pltpu.roll(mine, up, 1), pltpu.roll(theirs, down, 1))
            mine = pltpu.roll(mine, lane_shift(-down), 1)
            theirs = pltpu.roll(theirs, lane_shift(-up), 1)
            return even, jnp.where(keep, mine, theirs)

        put_block(from_owner(0)[1], own_lines)

    def place_got(block_ref, toward, south_first):
        south_top = pl.multiple_of(south_first * full_rows, 8)
        north_top = pl.multiple_of((1 - south_first) * full_rows, 8)

        def near_lines(row, rows):
            south = block_ref[pl.ds(south_top + row, rows)]
            north = block_ref[pl.ds(north_top + row, rows)]
            low = south_half[:rows]
            even = jnp.where(low, south, pltpu.roll(north, cy, 1))
            return even, jnp.where(low, pltpu.roll(south, LANES - cy, 1), north)

        put_block(from_owner(toward)[1], near_lines)
        for place, distance in enumerate((3, 2)):
            top = 2 * full_rows + 2 * place * small_rows
            south_at = pl.multiple_of(top + south_first * small_rows, 8)
            north_at = pl.multiple_of(top + (1 - south_first) * small_rows, 8)

            def far_lines(at, south_shift, north_shift, south_at=south_at, north_at=north_at):
                south = pltpu.roll(block_ref[pl.ds(south_at + at, group)], south_shift, 1)
                north = pltpu.roll(block_ref[pl.ds(north_at + at, group)], north_shift, 1)
                return jnp.where(south_half, south, north)

            put_distant(*from_owner(toward * distance), far_lines)

    def place_middle(got_ref, got_other_ref):
        def middle_lines(at, south_shift, north_shift):
            row = 2 * full_rows + 4 * small_rows + at
            mine_shift = jnp.where(south_is_own, south_shift, north_shift)
            other_shift = jnp.where(south_is_own, north_shift, south_shift)
            mine = pltpu.roll(got_ref[row : row + group], mine_shift, 1)
            theirs = pltpu.roll(got_other_ref[row : row + group], other_shift, 1)
            return jnp.where(own_half, mine, theirs)

        put_distant(*from_owner(count_x // 2), middle_lines)

    return place_own, place_got, place_middle


def own_kernel(sizes, own_ref, other_ref, z_ref, cor_ref):
    placer(*sizes, z_ref, cor_ref)[0](own_ref, other_ref)


def got_kernel(sizes, got_ref, z_in, cor_in, z_ref, cor_ref):
    index_y = lax.axis_index("ty")
    placer(*sizes, z_ref, cor_ref)[1](got_ref, 1 - 2 * index_y, index_y)


def step_kernel(
    sizes, got_ref, got_other_ref, table_in, z_in, cor_in, out_hbm, z_ref, cor_ref,
    pred_ref, store_ref, tile_ref, flip_ref, speed_ref, table_ref, out_ref, sems,
):
    table_copy = pltpu.make_async_copy(table_in, table_ref, sems.at[0])
    table_copy.start()
    cx, cy, count_x = sizes[:3]
    levels = 4
    slots = 16
    cells = cx * count_x
    faces = store_ref.shape[0] // 4
    pairs = faces // 2
    group = pairs * levels
    chunk = cx * group
    index_x = lax.axis_index("tx")
    index_y = lax.axis_index("ty")

    def row_of(x):
        return (x + 4) * group

    def lanes_of(rows):
        return lax.broadcasted_iota(jnp.int32, (rows, LANES), 1)

    _, place_got, place_middle = placer(*sizes, z_ref, cor_ref)
    place_got(got_other_ref, 2 * index_y - 1, 1 - index_y)
    place_middle(got_ref, got_other_ref)

    table_copy.wait()
    level_of = lax.broadcasted_iota(jnp.int32, speed_ref.shape, 0) % levels
    speeds = jnp.full(speed_ref.shape, table_ref[0], jnp.float32)
    for index in range(1, levels):
        speeds = jnp.where(level_of == index, table_ref[index], speeds)
    speed_ref[...] = speeds

    lane_8 = lanes_of(8)
    place_8 = lane_8 % WINDOW
    gap = WINDOW - cells + 3
    wide = gap + 3 * levels
    row_tiles = range(0, cells, 8)
    rim_8 = ((place_8 >= MARGIN - 3) & (place_8 < MARGIN)) | (
        (place_8 >= MARGIN + cells) & (place_8 < MARGIN + cells + 3)
    )

    def collect():
        for pair in range(pairs):
            merged = [jnp.zeros((8, LANES), jnp.float32)] * len(row_tiles)
            for slot, field in ((0, 0), (1, 2)):
                for level in range(levels):
                    offset = slot * wide + 3 * level
                    here = place_8 - offset
                    wanted = ((here >= 0) & (here < 3)) | ((here >= gap) & (here < gap + 3))
                    shift = (offset - (MARGIN + cells - 3)) % LANES
                    lines = z_ref[field, pl.ds(row_of(0) + pair * levels + level, cells, group)]
                    lines = pltpu.roll(lines, shift, 1)
                    merged = [
                        jnp.where(wanted, lines[row : row + 8], old)
                        for row, old in zip(row_tiles, merged)
                    ]
            flip_ref[pair, :, :cells] = jnp.concatenate(merged, axis=0).T
            for slot in range(2):
                for side in (2, 3):
                    for odd in range(2):
                        for depth in range(3):
                            base = slot * wide
                            if side == 3:
                                base += odd * WINDOW + 2 - depth
                            else:
                                base += ((odd + 1) % 2) * WINDOW + gap + depth
                            at = slot * slots + depth * levels
                            store_ref[(2 * pair + odd) * 4 + side, at : at + levels] = flip_ref[
                                pair, pl.ds(base, levels, 3)
                            ]
            for slot in range(2):
                for side in (0, 1):
                    for depth in range(3):
                        x = depth if side == 0 else cells - 1 - depth
                        row = row_of(x) + pair * levels
                        lines = z_ref[slot, row : row + levels]
                        at = slot * slots + depth * levels
                        for odd in range(2):
                            store_ref[(2 * pair + odd) * 4 + side, at : at + levels] = lines

    def fetch(face, side, positions):
        at = levels + (face * 4 + side) * 3
        neighbour = table_ref[at].astype(jnp.int32)
        far_side = table_ref[at + 1].astype(jnp.int32)
        flipped = table_ref[at + 2].astype(jnp.int32)
        first = jnp.where(far_side < 2, MARGIN + WINDOW * (neighbour & 1), 0)
        start = first + jnp.where(flipped == 1, cells - 1, 0)
        step = 1 - 2 * flipped
        sign = ((1 - 2 * (side % 2)) * (2 * (far_side & 1) - 1)).astype(jnp.float32)
        index = neighbour * 4 + far_side
        parts = []
        for slot, position in enumerate(positions):
            order = (start + step * position) & (LANES - 1)
            for half_at in (0, 8):
                at = slot * slots + half_at
                lines = jnp.take_along_axis(store_ref[index, at : at + 8], order, axis=1)
                parts.append(lines if slot == 0 else sign * lines)
        return parts[:2], parts[2:]

    def depth_rows(parts, depth):
        at = (depth % 2) * levels
        return parts[depth // 2][at : at + levels]

    def rim_rows(side):
        left = lane_8 < WINDOW
        for pair in range(pairs):
            first = fetch(2 * pair, side, [lane_8 - MARGIN] * 2)
            second = fetch(2 * pair + 1, side, [lane_8 - (MARGIN + WINDOW)] * 2)
            for slot in range(2):
                both = [jnp.where(left, a, b) for a, b in zip(first[slot], second[slot])]
                for depth in range(3):
                    x = -1 - depth if side == 0 else cells + depth
                    row = row_of(x) + pair * levels
                    z_ref[slot, row : row + levels] = depth_rows(both, depth)

    tile_wide = WINDOW - cells - 3 + 3 * levels

    def put_tile(tile, parts, odd, side, base=0):
        for depth in range(3):
            if side == 3:
                at = base + odd * WINDOW + depth
            else:
                at = base + ((odd + 1) % 2) * WINDOW + tile_wide - 3 * levels + 2 - depth
            tile_ref[tile, pl.ds(at, levels, 3)] = depth_rows(parts, depth)

    def rim_columns_all():
        for pair in range(pairs):
            for odd in range(2):
                for side in (2, 3):
                    for slot, parts in enumerate(fetch(2 * pair + odd, side, [lane_8] * 2)):
                        put_tile(pair, parts, odd, side, slot * tile_wide)
            turned = tile_ref[pair].T[:cells]
            for slot, field in ((0, 0), (1, 2)):
                for level in range(levels):
                    shift = (MARGIN + cells - slot * tile_wide - 3 * level) % LANES
                    rolled = pltpu.roll(turned, shift, 1)
                    at = pl.ds(row_of(0) + pair * levels + level, cells, group)
                    lines = z_ref[field, at]
                    lines = [
                        jnp.where(rim_8, rolled[row : row + 8], lines[row : row + 8])
                        for row in row_tiles
                    ]
                    z_ref[field, at] = jnp.concatenate(lines, axis=0)

    def rim_columns_own():
        for odd in range(2):
            for side in (2, 3):
                total = [jnp.zeros((8, LANES), jnp.float32)] * 2
                for pair in range(pairs):
                    places = [8 * pair, 8 * (pairs + pair)]
                    positions = [lane_8 + (index_x * cx - place) for place in places]
                    fetched = fetch(2 * pair + odd, side, positions)
                    for place, parts in zip(places, fetched):
                        here = (lane_8 >= place) & (lane_8 < place + 8)
                        total = [jnp.where(here, a, b) for a, b in zip(parts, total)]
                put_tile(0, total, odd, side)
        turned = tile_ref[0].T
        for slot, field in ((0, 0), (1, 2)):
            for pair in range(pairs):
                row = 8 * (slot * pairs + pair)
                for level in range(levels):
                    shift = (MARGIN + cells - 3 * level) % LANES
                    rolled = pltpu.roll(turned[row : row + 8], shift, 1)[:cx]
                    start = row_of(0) + index_x * chunk + pair * levels + level
                    at = pl.ds(start, cx, group)
                    z_ref[field, at] = jnp.where(rim_8[:cx], rolled, z_ref[field, at])

    def predict(at, rows):
        speed = speed_ref[:rows]
        ahead = z_ref[0, pl.ds(at + group, rows)]
        behind = z_ref[0, pl.ds(at - group, rows)]
        pred_ref[pl.ds(at, rows)] = z_ref[1, pl.ds(at, rows)] - speed * (0.5 * (ahead - behind))

    def update(at, rows):
        speed = speed_ref[:rows]
        height = z_ref[0, pl.ds(at, rows)]
        north_pred = z_ref[2, pl.ds(at, rows)] - speed * (
            0.5 * (pltpu.roll(height, LANES - 1, 1) - pltpu.roll(height, 1, 1))
        )
        east_pred = pred_ref[pl.ds(at, rows)]
        flux_east = 8.0 * (
            pred_ref[pl.ds(at + group, rows)] - pred_ref[pl.ds(at - group, rows)]
        ) - (pred_ref[pl.ds(at + 2 * group, rows)] - pred_ref[pl.ds(at - 2 * group, rows)])
        flux_north = 8.0 * (
            pltpu.roll(north_pred, LANES - 1, 1) - pltpu.roll(north_pred, 1, 1)
        ) - (pltpu.roll(north_pred, LANES - 2, 1) - pltpu.roll(north_pred, 2, 1))
        height = height - speed * ((flux_east + flux_north) * (1.0 / 12.0))
        turning = cor_ref[pl.ds(at - row_of(0), rows)]
        return height, east_pred + turning * north_pred, north_pred - turning * east_pred

    def all_faces():
        rim_rows(0)
        rim_rows(1)
        rim_columns_all()
        for first in range(-2, cells + 2, 4):
            predict(row_of(first), 4 * group)
        def update_part(index, carry):
            at = pl.multiple_of(row_of(0) + index * (2 * chunk), 8)
            for field, values in enumerate(update(at, 2 * chunk)):
                z_ref[field, pl.ds(at, 2 * chunk)] = values
            return carry

        lax.fori_loop(0, count_x // 2, update_part, 0)

    def own_rows():

        @pl.when(index_x == 0)
        def _():
            rim_rows(0)

        @pl.when(index_x == count_x - 1)
        def _():
            rim_rows(1)

        rim_columns_own()
        at = pl.multiple_of(row_of(0) + index_x * chunk, 8)
        predict(at - 2 * group, chunk + 4 * group)
        copies = []
        for field, values in enumerate(update(at, chunk)):
            for odd in range(2):
                shift = LANES - (MARGIN + odd * WINDOW) - index_y * cy
                rolled = pltpu.roll(values, shift, 1)
                for x in range(cx):
                    for pair in range(pairs):
                        row = x * group + pair * levels
                        out_ref[field, 2 * pair + odd, x] = rolled[row : row + levels, :cy]
            copy = pltpu.make_async_copy(out_ref.at[field], out_hbm.at[:, field], sems.at[1 + field])
            copy.start()
            copies.append(copy)
        for copy in copies:
            copy.wait()

    def substep(index, carry):
        collect()
        pl.when(index == 0)(all_faces)
        pl.when(index == SUBSTEPS - 1)(own_rows)
        return carry

    lax.fori_loop(0, SUBSTEPS, substep, 0)


def fast_on_device(state, coriolis, wave_speed, edges):
    count_x = lax.axis_size("tx")
    faces, fields, levels, cx, cy = state.shape
    pairs = faces // 2
    group = pairs * levels
    cells = cx * count_x
    full_rows = fields * (cx // 2) * group + (cx // 2) * pairs
    full_rows = -(-full_rows // 8) * 8
    small_rows = unit_place(fields, 1, cx, group, 2 * cx)[0] + group
    in_vmem = pl.BlockSpec(memory_space=pltpu.VMEM)
    params = pltpu.CompilerParams(vmem_limit_bytes=SMALL_VMEM_LIMIT)
    swap_shape = jax.ShapeDtypeStruct((full_rows + 2 * small_rows, LANES), jnp.float32)
    swap = pl.pallas_call(
        functools.partial(pack_kernel, cx, cy, count_x, full_rows, small_rows),
        out_shape=swap_shape,
        in_specs=[in_vmem],
        out_specs=in_vmem,
        compiler_params=params,
        name="pack",
    )(jnp.swapaxes(state, 2, 3))
    swap, lines = pl.pallas_call(
        functools.partial(pack_coriolis_kernel, cx, cy, count_x, full_rows, small_rows),
        out_shape=[swap_shape, jax.ShapeDtypeStruct((32, LANES), jnp.float32)],
        in_specs=[in_vmem] * 2,
        out_specs=[in_vmem] * 2,
        input_output_aliases={1: 0},
        compiler_params=params,
        name="pack_coriolis",
    )(coriolis, swap)
    keep, middle = pl.pallas_call(
        functools.partial(keep_kernel, cx, cy, count_x, small_rows),
        out_shape=[
            jax.ShapeDtypeStruct((2 * small_rows, LANES), jnp.float32),
            jax.ShapeDtypeStruct((small_rows, LANES), jnp.float32),
        ],
        in_specs=[pl.BlockSpec(memory_space=pltpu.VMEM)] * 2,
        out_specs=[pl.BlockSpec(memory_space=pltpu.VMEM)] * 2,
        compiler_params=pltpu.CompilerParams(vmem_limit_bytes=SMALL_VMEM_LIMIT),
        name="keep",
    )(swap, lines)

    def moved(block, distance):
        pairs_of = []
        for index in range(count_x):
            for core in range(2):
                target = (index + distance * (1 - 2 * core)) % count_x
                pairs_of.append((2 * index + core, 2 * target + core))
        return lax.ppermute(block, ("tx", "ty"), pairs_of)

    def across(block):
        return lax.ppermute(block, "ty", [(0, 1), (1, 0)])

    other = across(swap)
    messages = pl.pallas_call(
        functools.partial(mix_kernel, full_rows, small_rows),
        out_shape=[
            jax.ShapeDtypeStruct((rows, LANES), jnp.float32)
            for rows in (2 * full_rows, 2 * small_rows, 2 * small_rows, small_rows)
        ],
        in_specs=[in_vmem] * 4,
        out_specs=[in_vmem] * 4,
        compiler_params=params,
        name="messages",
    )(swap, other, keep, middle)
    got = [moved(block, distance) for block, distance in zip(messages, (1, 3, 2, count_x // 2))]
    got = jnp.concatenate(got)
    table = jnp.concatenate([wave_speed, edges.reshape(-1).astype(jnp.float32)])
    got, table = lax.optimization_barrier((got, table))
    passed = across(got)

    sizes = (cx, cy, count_x, full_rows, small_rows)
    state_rows = [
        jax.ShapeDtypeStruct((fields, (cells + 8) * group, LANES), jnp.float32),
        jax.ShapeDtypeStruct((cells * group, LANES), jnp.float32),
    ]
    rows = pl.pallas_call(
        functools.partial(own_kernel, sizes),
        out_shape=state_rows,
        in_specs=[in_vmem] * 2,
        out_specs=[in_vmem] * 2,
        compiler_params=params,
        name="place_own",
    )(swap, other)
    rows = pl.pallas_call(
        functools.partial(got_kernel, sizes),
        out_shape=state_rows,
        in_specs=[in_vmem] * 3,
        out_specs=[in_vmem] * 2,
        input_output_aliases={1: 0, 2: 1},
        compiler_params=params,
        name="place_got",
    )(got, *rows)
    out, _, _ = pl.pallas_call(
        functools.partial(step_kernel, sizes),
        out_shape=[jax.ShapeDtypeStruct((faces, fields, cx, levels, cy), jnp.float32)]
        + state_rows,
        in_specs=[in_vmem] * 5,
        out_specs=[pl.BlockSpec(memory_space=pltpu.HBM)] + [in_vmem] * 2,
        input_output_aliases={3: 1, 4: 2},
        scratch_shapes=[
            pltpu.VMEM(((cells + 8) * group, LANES), jnp.float32),
            pltpu.VMEM((faces * 4, 32, LANES), jnp.float32),
            pltpu.VMEM((pairs, LANES, LANES), jnp.float32),
            pltpu.VMEM((pairs, LANES, LANES), jnp.float32),
            pltpu.VMEM((2 * cx * group, LANES), jnp.float32),
            pltpu.SMEM(table.shape, jnp.float32),
            pltpu.VMEM((fields, faces, cx, levels, cy), jnp.float32),
            pltpu.SemaphoreType.DMA((1 + fields,)),
        ],
        compiler_params=pltpu.CompilerParams(vmem_limit_bytes=VMEM_LIMIT),
        name="substeps",
    )(got, passed, table, *rows)
    return jnp.swapaxes(out, 2, 3)


def padded_2(block, sides, width):
    for axis, dim in sides:
        count = lax.axis_size(axis)
        forward = [(i, i + 1) for i in range(count - 1)]
        backward = [(target, source) for source, target in forward]
        low = lax.ppermute(
            lax.slice_in_dim(block, block.shape[dim] - width, None, axis=dim), axis, forward
        )
        high = lax.ppermute(lax.slice_in_dim(block, 0, width, axis=dim), axis, backward)
        block = jnp.concatenate([low, block, high], axis=dim)
    return block


def spread(block, axis, owner):
    block = jnp.where(lax.axis_index(axis) == owner, block, jnp.zeros_like(block))
    return lax.psum(block, axis)


def rotate_strip(strip_data, side_index, far_side, flipped):
    normal_part = jnp.where(far_side < 2, strip_data[1], strip_data[2])
    along_part = jnp.where(far_side < 2, strip_data[2], strip_data[1])
    sign_here = 2.0 * (side_index % 2) - 1.0
    sign_there = (2 * (far_side % 2) - 1).astype(jnp.float32)
    normal_part = -sign_here * sign_there * normal_part
    along_part = (1 - 2 * flipped).astype(jnp.float32) * along_part
    if side_index < 2:
        return jnp.stack([strip_data[0], normal_part, along_part])
    return jnp.stack([strip_data[0], along_part, normal_part])


def window_strip(store, side_pick, neighbour, flipped, start, width):
    full_length = store.shape[5]
    begin = jnp.where(flipped == 1, full_length - start - width, start)
    zero = jnp.zeros((), jnp.int32)
    sizes_here = (1, 1, store.shape[2], store.shape[3], store.shape[4], width)
    piece = lax.dynamic_slice(store, (side_pick, neighbour, zero, zero, zero, begin), sizes_here)[
        0, 0
    ]
    return jnp.where(flipped == 1, jnp.flip(piece, 3), piece)


def side_halo(edge_store, edges, face_index, side_index, start, width):
    neighbour = edges[face_index, side_index, 0]
    far_side = edges[face_index, side_index, 1]
    flipped = edges[face_index, side_index, 2]
    strip_data = window_strip(edge_store, far_side, neighbour, flipped, start, width)
    return rotate_strip(strip_data, side_index, far_side, flipped)


def advance(padded, wave_speed, coriolis_part, cells_x, cells_y):
    height = padded[..., 0, :, :, :]
    wind_east = padded[..., 1, :, :, :]
    wind_north = padded[..., 2, :, :, :]
    speed = wave_speed[:, None, None]
    east_pred = wind_east[..., 1 : cells_x + 5, 3 : cells_y + 3] - speed * (
        0.5
        * (
            height[..., 2 : cells_x + 6, 3 : cells_y + 3]
            - height[..., 0 : cells_x + 4, 3 : cells_y + 3]
        )
    )
    north_pred = wind_north[..., 3 : cells_x + 3, 1 : cells_y + 5] - speed * (
        0.5
        * (
            height[..., 3 : cells_x + 3, 2 : cells_y + 6]
            - height[..., 3 : cells_x + 3, 0 : cells_y + 4]
        )
    )
    flux_east = (
        8.0 * (east_pred[..., 3 : cells_x + 3, :] - east_pred[..., 1 : cells_x + 1, :])
        - (east_pred[..., 4 : cells_x + 4, :] - east_pred[..., 0:cells_x, :])
    ) / 12.0
    flux_north = (
        8.0 * (north_pred[..., 3 : cells_y + 3] - north_pred[..., 1 : cells_y + 1])
        - (north_pred[..., 4 : cells_y + 4] - north_pred[..., 0:cells_y])
    ) / 12.0
    height_new = height[..., 3 : cells_x + 3, 3 : cells_y + 3] - speed * (flux_east + flux_north)
    east_inner = east_pred[..., 2 : cells_x + 2, :]
    north_inner = north_pred[..., 2 : cells_y + 2]
    turning = coriolis_part[..., None, :, :]
    return jnp.stack(
        [height_new, east_inner + turning * north_inner, north_inner - turning * east_inner],
        axis=-4,
    )


def one_substep(state, coriolis, wave_speed, edges, count_x, count_y, index_x, index_y):
    faces = state.shape[0]
    cells_x = state.shape[3]
    cells_y = state.shape[4]
    padded = padded_2(state, (("tx", 3), ("ty", 4)), 3)
    west_rim = state[:, :, :, 0:3, :]
    east_rim = jnp.flip(state[:, :, :, cells_x - 3 :, :], 3)
    south_rim = jnp.swapaxes(state[:, :, :, :, 0:3], 3, 4)
    north_rim = jnp.swapaxes(jnp.flip(state[:, :, :, :, cells_y - 3 :], 4), 3, 4)
    west_part = spread(west_rim, "tx", 0)
    east_part = spread(east_rim, "tx", count_x - 1)
    west_full, east_full = (
        lax.all_gather(west_part, "ty", axis=4, tiled=True),
        lax.all_gather(east_part, "ty", axis=4, tiled=True),
    )
    south_row, north_row = (
        lax.all_gather(south_rim, "tx", axis=4, tiled=True),
        lax.all_gather(north_rim, "tx", axis=4, tiled=True),
    )
    south_all, north_all = (
        lax.all_gather(south_row, "ty", axis=0, tiled=True),
        lax.all_gather(north_row, "ty", axis=0, tiled=True),
    )
    south_full = south_all[0:faces]
    north_full = north_all[(count_y - 1) * faces : count_y * faces]
    edge_store = jnp.stack([west_full, east_full, south_full, north_full])
    halos = []
    for side_index in range(4):
        if side_index < 2:
            slabs = jnp.stack(
                [
                    side_halo(edge_store, edges, face_index, side_index, index_y * cells_y, cells_y)
                    for face_index in range(faces)
                ]
            )
        else:
            slabs = jnp.stack(
                [
                    side_halo(edge_store, edges, face_index, side_index, index_x * cells_x, cells_x)
                    for face_index in range(faces)
                ]
            )
        halos.append(slabs)
    west_region = padded[:, :, :, 0:3, 3 : cells_y + 3]
    padded = padded.at[:, :, :, 0:3, 3 : cells_y + 3].set(
        jnp.where(index_x == 0, jnp.flip(halos[0], 3), west_region)
    )
    east_region = padded[:, :, :, cells_x + 3 : cells_x + 6, 3 : cells_y + 3]
    padded = padded.at[:, :, :, cells_x + 3 : cells_x + 6, 3 : cells_y + 3].set(
        jnp.where(index_x == count_x - 1, halos[1], east_region)
    )
    south_region = padded[:, :, :, 3 : cells_x + 3, 0:3]
    padded = padded.at[:, :, :, 3 : cells_x + 3, 0:3].set(
        jnp.where(index_y == 0, jnp.swapaxes(jnp.flip(halos[2], 3), 3, 4), south_region)
    )
    north_region = padded[:, :, :, 3 : cells_x + 3, cells_y + 3 : cells_y + 6]
    padded = padded.at[:, :, :, 3 : cells_x + 3, cells_y + 3 : cells_y + 6].set(
        jnp.where(index_y == count_y - 1, jnp.swapaxes(halos[3], 3, 4), north_region)
    )
    return advance(padded, wave_speed, coriolis, cells_x, cells_y)


def on_device(state, coriolis, wave_speed, edges):
    count_x = lax.axis_size("tx")
    count_y = lax.axis_size("ty")
    index_x = lax.axis_index("tx")
    index_y = lax.axis_index("ty")
    for substep_index in range(SUBSTEPS):
        state = one_substep(state, coriolis, wave_speed, edges, count_x, count_y, index_x, index_y)
    return state


def fits(state):
    count_x = lax.axis_size("tx")
    faces, fields, levels, cells_x, cells_y = state.shape
    return (
        lax.axis_size("ty") == 2
        and faces % 2 == 0
        and levels == 4
        and cells_x == 6
        and cells_y == 24
        and count_x == 8
        and cells_x * count_x == 2 * cells_y
        and 2 * cells_y + 2 * MARGIN <= WINDOW
    )


def either(state, coriolis, wave_speed, edges):
    if fits(state):
        return fast_on_device(state, coriolis, wave_speed, edges)
    return on_device(state, coriolis, wave_speed, edges)


def solution(mesh):
    in_specs = (P("member", None, None, "tx", "ty"), P(None, "tx", "ty"), P(), P())
    out_specs = P("member", None, None, "tx", "ty")
    return jax.shard_map(
        either, mesh=mesh, in_specs=in_specs, out_specs=out_specs, check_vma=False
    )
```

```python
import functools

import jax
import jax.numpy as jnp
from jax import lax
from jax.experimental import pallas as pl
from jax.experimental.pallas import tpu as pltpu
from jax.sharding import PartitionSpec as P

SUBSTEPS = 2
LANES = 128
WINDOW = 64
MARGIN = 8
VMEM_LIMIT = 32 * 1024 * 1024
SMALL_VMEM_LIMIT = 8 * 1024 * 1024


def wrap(index, count):
    index = jnp.where(index < 0, index + count, index)
    return jnp.where(index >= count, index - count, index)


def lane_shift(amount):
    return amount & (LANES - 1)


def windows(source, target, count_x, index_y, cx, cy):
    spare = cy - 2 * cx
    near = jnp.minimum(target, count_x - 1 - target)
    rim = (source == 0) | (source == count_x - 1)
    starts = []
    for inward in (cx // 2, cx):
        start = jnp.maximum(jnp.minimum(cx * near - inward, spare), 0)
        start = jnp.where(rim, start, 0)
        starts.append(jnp.where(index_y == 0, start, spare - start))
    close, far = starts
    upside = source == count_x - 1
    return jnp.where(upside, far, close), jnp.where(upside, close, far)


def unit_place(field, x, cx, group, width):
    per_row = 60 // width
    index = field * cx + x
    return (index // per_row) * group, (index % per_row) * width


def chunk_targets(count_x, full_rows, small_rows):
    sense = 1 - 2 * lax.axis_index("ty")
    return [
        (full_rows + place * small_rows, -sense * distance)
        for place, distance in enumerate((2, 3))
    ]


def put_chunk(cx, cy, count_x, block_ref, line_ref, out_ref, top, offset):
    pairs = 3
    group = 4 * pairs
    fields = 3
    half = cx // 2
    width = 2 * cx
    index_x = lax.axis_index("tx")
    target = wrap(index_x + offset, count_x)
    starts = windows(index_x, target, count_x, lax.axis_index("ty"), cx, cy)
    position = lax.broadcasted_iota(jnp.int32, (group, LANES), 1) % WINDOW
    from_lane = {lane: position >= lane for lane in range(0, 60, width)}
    blocks = {}

    def put(row, lane, lines):
        blocks[row] = lines if row not in blocks else jnp.where(from_lane[lane], lines, blocks[row])

    if block_ref is not None:
        for field in range(fields):
            for x in range(cx):
                row = field * half * group + (x // 2) * group
                at, lane = unit_place(field, x, cx, group, width)
                shift = lane_shift(lane - MARGIN - (x % 2) * cy - starts[x // half])
                put(at, lane, pltpu.roll(block_ref[row : row + group], shift, 1))
    else:
        at = unit_place(fields, 0, cx, group, width)[0]
        blocks[at] = out_ref[top + at : top + at + group]
    if line_ref is not None:
        for part in range(2):
            at, lane = unit_place(fields, part, cx, group, width)
            shift = lane_shift(lane - MARGIN - starts[part])
            put(at, lane, pltpu.roll(line_ref[16 * part : 16 * part + group], shift, 1))
    for row, lines in blocks.items():
        out_ref[top + row : top + row + group] = lines


def pack_kernel(cx, cy, count_x, full_rows, small_rows, state_ref, swap_ref):
    faces, fields = state_ref.shape[:2]
    levels = state_ref.shape[3]
    group = (faces // 2) * levels
    half = cx // 2
    swap_ref[:full_rows] = jnp.zeros((full_rows, LANES), jnp.float32)
    for face in range(faces):
        for parity in range(2):
            lane = (face % 2) * WINDOW + MARGIN + parity * cy
            for xp in range(half):
                for field in range(fields):
                    row = field * half * group + xp * group + (face // 2) * levels
                    swap_ref[row : row + levels, lane : lane + cy] = state_ref[
                        face, field, 2 * xp + parity
                    ]
    for top, offset in chunk_targets(count_x, full_rows, small_rows):
        put_chunk(cx, cy, count_x, swap_ref, None, swap_ref, top, offset)


def pack_coriolis_kernel(
    cx, cy, count_x, full_rows, small_rows, coriolis_ref, swap_in, swap_ref, line_ref
):
    faces = coriolis_ref.shape[0]
    pairs = faces // 2
    half = cx // 2
    base = 3 * half * 4 * pairs
    line_ref[...] = jnp.zeros(line_ref.shape, jnp.float32)
    for face in range(faces):
        lane = (face % 2) * WINDOW + MARGIN
        for x in range(cx):
            line = coriolis_ref[face, x : x + 1]
            row = base + (x // 2) * pairs + face // 2
            at = lane + (x % 2) * cy
            swap_ref[row : row + 1, at : at + cy] = line
            row = (x // half) * 16 + (x % half) * pairs + face // 2
            line_ref[row : row + 1, lane : lane + cy] = line
    for top, offset in chunk_targets(count_x, full_rows, small_rows):
        put_chunk(cx, cy, count_x, None, line_ref, swap_ref, top, offset)


def keep_kernel(cx, cy, count_x, small_rows, swap_ref, line_ref, keep_ref, middle_ref):
    sense = 1 - 2 * lax.axis_index("ty")
    put_chunk(cx, cy, count_x, swap_ref, line_ref, middle_ref, 0, count_x // 2)
    for place, distance in enumerate((2, 3)):
        top = place * small_rows
        put_chunk(cx, cy, count_x, swap_ref, line_ref, keep_ref, top, sense * distance)


def mix_kernel(
    full_rows, small_rows, swap_ref, other_ref, keep_ref, middle_ref,
    near_ref, third_ref, second_ref, fourth_ref,
):
    near_ref[:full_rows] = swap_ref[:full_rows]
    near_ref[full_rows:] = other_ref[:full_rows]
    for place, far_ref in enumerate((second_ref, third_ref)):
        at = place * small_rows
        far_ref[:small_rows] = keep_ref[at : at + small_rows]
        at += full_rows
        far_ref[small_rows:] = other_ref[at : at + small_rows]
    fourth_ref[...] = middle_ref[...]


def placer(cx, cy, count_x, full_rows, small_rows, z_ref, cor_ref):
    fields = z_ref.shape[0]
    levels = 4
    group = z_ref.shape[1] // (cx * count_x + 8)
    pairs = group // levels
    half = cx // 2
    chunk = cx * group
    index_x = lax.axis_index("tx")
    index_y = lax.axis_index("ty")
    south_half = lax.broadcasted_iota(jnp.int32, (group, LANES), 1) % WINDOW < MARGIN + cy
    south_is_own = index_y == 0
    own_half = south_half == south_is_own

    def row_of(x):
        return (x + 4) * group

    def from_owner(offset):
        source = wrap(index_x - offset, count_x)
        return source, pl.multiple_of(source * chunk, 8)

    def put_coriolis(start, x, values, at):
        for pair in range(pairs):
            line = values[at + pair : at + pair + 1]
            rows = pl.ds(start + x * group + pair * levels, levels)
            cor_ref[rows] = jnp.broadcast_to(line, (levels, LANES))

    def put_block(start, lines_of):
        base = fields * half * group
        for field in range(fields):
            for xp in range(half):
                even, odd = lines_of(field * half * group + xp * group, group)
                z_ref[field, pl.ds(start + row_of(2 * xp), group)] = even
                z_ref[field, pl.ds(start + row_of(2 * xp + 1), group)] = odd
        for parity, values in enumerate(lines_of(base, half * pairs)):
            for xp in range(half):
                put_coriolis(start, 2 * xp + parity, values, xp * pairs)

    def put_distant(source, start, lines_of):
        starts_south = windows(source, index_x, count_x, 0, cx, cy)
        starts_north = [cy - 2 * cx - start for start in starts_south]
        is_rim = (source == 0) | (source == count_x - 1)
        starts_north = [jnp.where(is_rim, start, cy - 2 * cx) for start in starts_north]
        shifts = {
            (part, lane): (
                lane_shift(MARGIN + starts_south[part] - lane),
                lane_shift(MARGIN + cy + starts_north[part] - lane),
            )
            for part in range(2)
            for lane in range(0, 60, 2 * cx)
        }

        def lines_at(field, x, part):
            at, lane = unit_place(field, x, cx, group, 2 * cx)
            return lines_of(at, *shifts[part, lane])

        for field in range(fields):
            for x in range(cx):
                z_ref[field, pl.ds(start + row_of(x), group)] = lines_at(field, x, x // half)
        for part in range(2):
            values = lines_at(fields, part, part)
            for x in range(half):
                put_coriolis(start, part * half + x, values, x * pairs)

    def place_own(own_ref, other_ref):
        def own_lines(row, rows):
            mine = own_ref[row : row + rows]
            theirs = other_ref[row : row + rows]
            up, down = index_y * cy, (1 - index_y) * cy
            keep = own_half[:rows]
            even = jnp.where(keep, pltpu.roll(mine, up, 1), pltpu.roll(theirs, down, 1))
            mine = pltpu.roll(mine, lane_shift(-down), 1)
            theirs = pltpu.roll(theirs, lane_shift(-up), 1)
            return even, jnp.where(keep, mine, theirs)

        put_block(from_owner(0)[1], own_lines)

    def place_near(block_ref, toward, south_first):
        south_top = pl.multiple_of(south_first * full_rows, 8)
        north_top = pl.multiple_of((1 - south_first) * full_rows, 8)

        def near_lines(row, rows):
            south = block_ref[pl.ds(south_top + row, rows)]
            north = block_ref[pl.ds(north_top + row, rows)]
            low = south_half[:rows]
            even = jnp.where(low, south, pltpu.roll(north, cy, 1))
            return even, jnp.where(low, pltpu.roll(south, LANES - cy, 1), north)

        put_block(from_owner(toward)[1], near_lines)

    def place_far(block_ref, toward, south_first):
        for place, distance in enumerate((3, 2)):
            top = 2 * place * small_rows
            south_at = pl.multiple_of(top + south_first * small_rows, 8)
            north_at = pl.multiple_of(top + (1 - south_first) * small_rows, 8)

            def far_lines(at, south_shift, north_shift, south_at=south_at, north_at=north_at):
                south = pltpu.roll(block_ref[pl.ds(south_at + at, group)], south_shift, 1)
                north = pltpu.roll(block_ref[pl.ds(north_at + at, group)], north_shift, 1)
                return jnp.where(south_half, south, north)

            put_distant(*from_owner(toward * distance), far_lines)

    def place_middle(got_ref, passed_ref):
        def middle_lines(at, south_shift, north_shift):
            row = 4 * small_rows + at
            mine_shift = jnp.where(south_is_own, south_shift, north_shift)
            other_shift = jnp.where(south_is_own, north_shift, south_shift)
            mine = pltpu.roll(got_ref[row : row + group], mine_shift, 1)
            theirs = pltpu.roll(passed_ref[row : row + group], other_shift, 1)
            return jnp.where(own_half, mine, theirs)

        put_distant(*from_owner(count_x // 2), middle_lines)

    return place_own, place_near, place_far, place_middle


def own_kernel(sizes, own_ref, other_ref, far_ref, z_ref, cor_ref):
    place_own, _, place_far, _ = placer(*sizes, z_ref, cor_ref)
    index_y = lax.axis_index("ty")
    place_own(own_ref, other_ref)
    place_far(far_ref, 1 - 2 * index_y, index_y)


def got_kernel(sizes, near_ref, far_ref, passed_ref, z_in, cor_in, z_ref, cor_ref):
    _, place_near, place_far, place_middle = placer(*sizes, z_ref, cor_ref)
    index_y = lax.axis_index("ty")
    place_near(near_ref, 1 - 2 * index_y, index_y)
    place_far(passed_ref, 2 * index_y - 1, 1 - index_y)
    place_middle(far_ref, passed_ref)


def step_kernel(
    sizes, passed_ref, table_in, z_in, cor_in, out_hbm, z_ref, cor_ref,
    pred_ref, store_ref, tile_ref, flip_ref, speed_ref, table_ref, out_ref, sems,
):
    table_copy = pltpu.make_async_copy(table_in, table_ref, sems.at[0])
    table_copy.start()
    cx, cy, count_x = sizes[:3]
    levels = 4
    slots = 16
    cells = cx * count_x
    faces = store_ref.shape[0] // 4
    pairs = faces // 2
    group = pairs * levels
    chunk = cx * group
    index_x = lax.axis_index("tx")
    index_y = lax.axis_index("ty")

    def row_of(x):
        return (x + 4) * group

    def lanes_of(rows):
        return lax.broadcasted_iota(jnp.int32, (rows, LANES), 1)

    place_near = placer(*sizes, z_ref, cor_ref)[1]
    place_near(passed_ref, 2 * index_y - 1, 1 - index_y)

    table_copy.wait()
    level_of = lax.broadcasted_iota(jnp.int32, speed_ref.shape, 0) % levels
    speeds = jnp.full(speed_ref.shape, table_ref[0], jnp.float32)
    for index in range(1, levels):
        speeds = jnp.where(level_of == index, table_ref[index], speeds)
    speed_ref[...] = speeds

    lane_8 = lanes_of(8)
    place_8 = lane_8 % WINDOW
    gap = WINDOW - cells + 3
    wide = gap + 3 * levels
    row_tiles = range(0, cells, 8)
    rim_8 = ((place_8 >= MARGIN - 3) & (place_8 < MARGIN)) | (
        (place_8 >= MARGIN + cells) & (place_8 < MARGIN + cells + 3)
    )

    def collect():
        for pair in range(pairs):
            merged = [jnp.zeros((8, LANES), jnp.float32)] * len(row_tiles)
            for slot, field in ((0, 0), (1, 2)):
                for level in range(levels):
                    offset = slot * wide + 3 * level
                    here = place_8 - offset
                    wanted = ((here >= 0) & (here < 3)) | ((here >= gap) & (here < gap + 3))
                    shift = (offset - (MARGIN + cells - 3)) % LANES
                    lines = z_ref[field, pl.ds(row_of(0) + pair * levels + level, cells, group)]
                    lines = pltpu.roll(lines, shift, 1)
                    merged = [
                        jnp.where(wanted, lines[row : row + 8], old)
                        for row, old in zip(row_tiles, merged)
                    ]
            flip_ref[pair, :, :cells] = jnp.concatenate(merged, axis=0).T
            for slot in range(2):
                for side in (2, 3):
                    for odd in range(2):
                        for depth in range(3):
                            base = slot * wide
                            if side == 3:
                                base += odd * WINDOW + 2 - depth
                            else:
                                base += ((odd + 1) % 2) * WINDOW + gap + depth
                            at = slot * slots + depth * levels
                            store_ref[(2 * pair + odd) * 4 + side, at : at + levels] = flip_ref[
                                pair, pl.ds(base, levels, 3)
                            ]
            for slot in range(2):
                for side in (0, 1):
                    for depth in range(3):
                        x = depth if side == 0 else cells - 1 - depth
                        row = row_of(x) + pair * levels
                        lines = z_ref[slot, row : row + levels]
                        at = slot * slots + depth * levels
                        for odd in range(2):
                            store_ref[(2 * pair + odd) * 4 + side, at : at + levels] = lines

    def fetch(face, side, positions):
        at = levels + (face * 4 + side) * 3
        neighbour = table_ref[at].astype(jnp.int32)
        far_side = table_ref[at + 1].astype(jnp.int32)
        flipped = table_ref[at + 2].astype(jnp.int32)
        first = jnp.where(far_side < 2, MARGIN + WINDOW * (neighbour & 1), 0)
        start = first + jnp.where(flipped == 1, cells - 1, 0)
        step = 1 - 2 * flipped
        sign = ((1 - 2 * (side % 2)) * (2 * (far_side & 1) - 1)).astype(jnp.float32)
        index = neighbour * 4 + far_side
        parts = []
        for slot, position in enumerate(positions):
            order = (start + step * position) & (LANES - 1)
            for half_at in (0, 8):
                at = slot * slots + half_at
                lines = jnp.take_along_axis(store_ref[index, at : at + 8], order, axis=1)
                parts.append(lines if slot == 0 else sign * lines)
        return parts[:2], parts[2:]

    def depth_rows(parts, depth):
        at = (depth % 2) * levels
        return parts[depth // 2][at : at + levels]

    def rim_rows(side):
        left = lane_8 < WINDOW
        for pair in range(pairs):
            first = fetch(2 * pair, side, [lane_8 - MARGIN] * 2)
            second = fetch(2 * pair + 1, side, [lane_8 - (MARGIN + WINDOW)] * 2)
            for slot in range(2):
                both = [jnp.where(left, a, b) for a, b in zip(first[slot], second[slot])]
                for depth in range(3):
                    x = -1 - depth if side == 0 else cells + depth
                    row = row_of(x) + pair * levels
                    z_ref[slot, row : row + levels] = depth_rows(both, depth)

    tile_wide = WINDOW - cells - 3 + 3 * levels

    def put_tile(tile, parts, odd, side, base=0):
        for depth in range(3):
            if side == 3:
                at = base + odd * WINDOW + depth
            else:
                at = base + ((odd + 1) % 2) * WINDOW + tile_wide - 3 * levels + 2 - depth
            tile_ref[tile, pl.ds(at, levels, 3)] = depth_rows(parts, depth)

    def rim_columns_all():
        for pair in range(pairs):
            for odd in range(2):
                for side in (2, 3):
                    for slot, parts in enumerate(fetch(2 * pair + odd, side, [lane_8] * 2)):
                        put_tile(pair, parts, odd, side, slot * tile_wide)
            turned = tile_ref[pair].T[:cells]
            for slot, field in ((0, 0), (1, 2)):
                for level in range(levels):
                    shift = (MARGIN + cells - slot * tile_wide - 3 * level) % LANES
                    rolled = pltpu.roll(turned, shift, 1)
                    at = pl.ds(row_of(0) + pair * levels + level, cells, group)
                    lines = z_ref[field, at]
                    lines = [
                        jnp.where(rim_8, rolled[row : row + 8], lines[row : row + 8])
                        for row in row_tiles
                    ]
                    z_ref[field, at] = jnp.concatenate(lines, axis=0)

    def rim_columns_own():
        for odd in range(2):
            for side in (2, 3):
                total = [jnp.zeros((8, LANES), jnp.float32)] * 2
                for pair in range(pairs):
                    places = [8 * pair, 8 * (pairs + pair)]
                    positions = [lane_8 + (index_x * cx - place) for place in places]
                    fetched = fetch(2 * pair + odd, side, positions)
                    for place, parts in zip(places, fetched):
                        here = (lane_8 >= place) & (lane_8 < place + 8)
                        total = [jnp.where(here, a, b) for a, b in zip(parts, total)]
                put_tile(0, total, odd, side)
        turned = tile_ref[0].T
        for slot, field in ((0, 0), (1, 2)):
            for pair in range(pairs):
                row = 8 * (slot * pairs + pair)
                for level in range(levels):
                    shift = (MARGIN + cells - 3 * level) % LANES
                    rolled = pltpu.roll(turned[row : row + 8], shift, 1)[:cx]
                    start = row_of(0) + index_x * chunk + pair * levels + level
                    at = pl.ds(start, cx, group)
                    z_ref[field, at] = jnp.where(rim_8[:cx], rolled, z_ref[field, at])

    def predict(at, rows):
        speed = speed_ref[:rows]
        ahead = z_ref[0, pl.ds(at + group, rows)]
        behind = z_ref[0, pl.ds(at - group, rows)]
        pred_ref[pl.ds(at, rows)] = z_ref[1, pl.ds(at, rows)] - speed * (0.5 * (ahead - behind))

    def update(at, rows):
        speed = speed_ref[:rows]
        height = z_ref[0, pl.ds(at, rows)]
        north_pred = z_ref[2, pl.ds(at, rows)] - speed * (
            0.5 * (pltpu.roll(height, LANES - 1, 1) - pltpu.roll(height, 1, 1))
        )
        east_pred = pred_ref[pl.ds(at, rows)]
        flux_east = 8.0 * (
            pred_ref[pl.ds(at + group, rows)] - pred_ref[pl.ds(at - group, rows)]
        ) - (pred_ref[pl.ds(at + 2 * group, rows)] - pred_ref[pl.ds(at - 2 * group, rows)])
        flux_north = 8.0 * (
            pltpu.roll(north_pred, LANES - 1, 1) - pltpu.roll(north_pred, 1, 1)
        ) - (pltpu.roll(north_pred, LANES - 2, 1) - pltpu.roll(north_pred, 2, 1))
        height = height - speed * ((flux_east + flux_north) * (1.0 / 12.0))
        turning = cor_ref[pl.ds(at - row_of(0), rows)]
        return height, east_pred + turning * north_pred, north_pred - turning * east_pred

    def all_faces():
        rim_rows(0)
        rim_rows(1)
        rim_columns_all()
        for first in range(-2, cells + 2, 4):
            predict(row_of(first), 4 * group)
        def update_part(index, carry):
            at = pl.multiple_of(row_of(0) + index * (2 * chunk), 8)
            for field, values in enumerate(update(at, 2 * chunk)):
                z_ref[field, pl.ds(at, 2 * chunk)] = values
            return carry

        lax.fori_loop(0, count_x // 2, update_part, 0)

    def own_rows():

        @pl.when(index_x == 0)
        def _():
            rim_rows(0)

        @pl.when(index_x == count_x - 1)
        def _():
            rim_rows(1)

        rim_columns_own()
        at = pl.multiple_of(row_of(0) + index_x * chunk, 8)
        predict(at - 2 * group, chunk + 4 * group)
        copies = []
        for field, values in enumerate(update(at, chunk)):
            for odd in range(2):
                shift = LANES - (MARGIN + odd * WINDOW) - index_y * cy
                rolled = pltpu.roll(values, shift, 1)
                for x in range(cx):
                    for pair in range(pairs):
                        row = x * group + pair * levels
                        out_ref[field, 2 * pair + odd, x] = rolled[row : row + levels, :cy]
            copy = pltpu.make_async_copy(out_ref.at[field], out_hbm.at[:, field], sems.at[1 + field])
            copy.start()
            copies.append(copy)
        for copy in copies:
            copy.wait()

    def substep(index, carry):
        collect()
        pl.when(index == 0)(all_faces)
        pl.when(index == SUBSTEPS - 1)(own_rows)
        return carry

    lax.fori_loop(0, SUBSTEPS, substep, 0)


def fast_on_device(state, coriolis, wave_speed, edges):
    count_x = lax.axis_size("tx")
    faces, fields, levels, cx, cy = state.shape
    pairs = faces // 2
    group = pairs * levels
    cells = cx * count_x
    full_rows = fields * (cx // 2) * group + (cx // 2) * pairs
    full_rows = -(-full_rows // 8) * 8
    small_rows = unit_place(fields, 1, cx, group, 2 * cx)[0] + group
    in_vmem = pl.BlockSpec(memory_space=pltpu.VMEM)
    params = pltpu.CompilerParams(vmem_limit_bytes=SMALL_VMEM_LIMIT)
    swap_shape = jax.ShapeDtypeStruct((full_rows + 2 * small_rows, LANES), jnp.float32)
    swap = pl.pallas_call(
        functools.partial(pack_kernel, cx, cy, count_x, full_rows, small_rows),
        out_shape=swap_shape,
        in_specs=[in_vmem],
        out_specs=in_vmem,
        compiler_params=params,
        name="pack",
    )(jnp.swapaxes(state, 2, 3))
    swap, lines = pl.pallas_call(
        functools.partial(pack_coriolis_kernel, cx, cy, count_x, full_rows, small_rows),
        out_shape=[swap_shape, jax.ShapeDtypeStruct((32, LANES), jnp.float32)],
        in_specs=[in_vmem] * 2,
        out_specs=[in_vmem] * 2,
        input_output_aliases={1: 0},
        compiler_params=params,
        name="pack_coriolis",
    )(coriolis, swap)
    keep, middle = pl.pallas_call(
        functools.partial(keep_kernel, cx, cy, count_x, small_rows),
        out_shape=[
            jax.ShapeDtypeStruct((2 * small_rows, LANES), jnp.float32),
            jax.ShapeDtypeStruct((small_rows, LANES), jnp.float32),
        ],
        in_specs=[pl.BlockSpec(memory_space=pltpu.VMEM)] * 2,
        out_specs=[pl.BlockSpec(memory_space=pltpu.VMEM)] * 2,
        compiler_params=pltpu.CompilerParams(vmem_limit_bytes=SMALL_VMEM_LIMIT),
        name="keep",
    )(swap, lines)

    def moved(block, distance):
        pairs_of = []
        for index in range(count_x):
            for core in range(2):
                target = (index + distance * (1 - 2 * core)) % count_x
                pairs_of.append((2 * index + core, 2 * target + core))
        return lax.ppermute(block, ("tx", "ty"), pairs_of)

    def across(block):
        return lax.ppermute(block, "ty", [(0, 1), (1, 0)])

    other = across(swap)
    messages = pl.pallas_call(
        functools.partial(mix_kernel, full_rows, small_rows),
        out_shape=[
            jax.ShapeDtypeStruct((rows, LANES), jnp.float32)
            for rows in (2 * full_rows, 2 * small_rows, 2 * small_rows, small_rows)
        ],
        in_specs=[in_vmem] * 4,
        out_specs=[in_vmem] * 4,
        compiler_params=params,
        name="messages",
    )(swap, other, keep, middle)
    near, *far = [
        moved(block, distance) for block, distance in zip(messages, (1, 3, 2, count_x // 2))
    ]
    far = jnp.concatenate(far)
    table = jnp.concatenate([wave_speed, edges.reshape(-1).astype(jnp.float32)])
    near, table = lax.optimization_barrier((near, table))
    far_passed = across(far)
    near_passed = across(near)

    sizes = (cx, cy, count_x, full_rows, small_rows)
    state_rows = [
        jax.ShapeDtypeStruct((fields, (cells + 8) * group, LANES), jnp.float32),
        jax.ShapeDtypeStruct((cells * group, LANES), jnp.float32),
    ]
    rows = pl.pallas_call(
        functools.partial(own_kernel, sizes),
        out_shape=state_rows,
        in_specs=[in_vmem] * 3,
        out_specs=[in_vmem] * 2,
        compiler_params=params,
        name="place_own",
    )(swap, other, far)
    rows = pl.pallas_call(
        functools.partial(got_kernel, sizes),
        out_shape=state_rows,
        in_specs=[in_vmem] * 5,
        out_specs=[in_vmem] * 2,
        input_output_aliases={3: 0, 4: 1},
        compiler_params=params,
        name="place_got",
    )(near, far, far_passed, *rows)
    out, _, _ = pl.pallas_call(
        functools.partial(step_kernel, sizes),
        out_shape=[jax.ShapeDtypeStruct((faces, fields, cx, levels, cy), jnp.float32)]
        + state_rows,
        in_specs=[in_vmem] * 4,
        out_specs=[pl.BlockSpec(memory_space=pltpu.HBM)] + [in_vmem] * 2,
        input_output_aliases={2: 1, 3: 2},
        scratch_shapes=[
            pltpu.VMEM(((cells + 8) * group, LANES), jnp.float32),
            pltpu.VMEM((faces * 4, 32, LANES), jnp.float32),
            pltpu.VMEM((pairs, LANES, LANES), jnp.float32),
            pltpu.VMEM((pairs, LANES, LANES), jnp.float32),
            pltpu.VMEM((2 * cx * group, LANES), jnp.float32),
            pltpu.SMEM(table.shape, jnp.float32),
            pltpu.VMEM((fields, faces, cx, levels, cy), jnp.float32),
            pltpu.SemaphoreType.DMA((1 + fields,)),
        ],
        compiler_params=pltpu.CompilerParams(vmem_limit_bytes=VMEM_LIMIT),
        name="substeps",
    )(near_passed, table, *rows)
    return jnp.swapaxes(out, 2, 3)


def padded_2(block, sides, width):
    for axis, dim in sides:
        count = lax.axis_size(axis)
        forward = [(i, i + 1) for i in range(count - 1)]
        backward = [(target, source) for source, target in forward]
        low = lax.ppermute(
            lax.slice_in_dim(block, block.shape[dim] - width, None, axis=dim), axis, forward
        )
        high = lax.ppermute(lax.slice_in_dim(block, 0, width, axis=dim), axis, backward)
        block = jnp.concatenate([low, block, high], axis=dim)
    return block


def spread(block, axis, owner):
    block = jnp.where(lax.axis_index(axis) == owner, block, jnp.zeros_like(block))
    return lax.psum(block, axis)


def rotate_strip(strip_data, side_index, far_side, flipped):
    normal_part = jnp.where(far_side < 2, strip_data[1], strip_data[2])
    along_part = jnp.where(far_side < 2, strip_data[2], strip_data[1])
    sign_here = 2.0 * (side_index % 2) - 1.0
    sign_there = (2 * (far_side % 2) - 1).astype(jnp.float32)
    normal_part = -sign_here * sign_there * normal_part
    along_part = (1 - 2 * flipped).astype(jnp.float32) * along_part
    if side_index < 2:
        return jnp.stack([strip_data[0], normal_part, along_part])
    return jnp.stack([strip_data[0], along_part, normal_part])


def window_strip(store, side_pick, neighbour, flipped, start, width):
    full_length = store.shape[5]
    begin = jnp.where(flipped == 1, full_length - start - width, start)
    zero = jnp.zeros((), jnp.int32)
    sizes_here = (1, 1, store.shape[2], store.shape[3], store.shape[4], width)
    piece = lax.dynamic_slice(store, (side_pick, neighbour, zero, zero, zero, begin), sizes_here)[
        0, 0
    ]
    return jnp.where(flipped == 1, jnp.flip(piece, 3), piece)


def side_halo(edge_store, edges, face_index, side_index, start, width):
    neighbour = edges[face_index, side_index, 0]
    far_side = edges[face_index, side_index, 1]
    flipped = edges[face_index, side_index, 2]
    strip_data = window_strip(edge_store, far_side, neighbour, flipped, start, width)
    return rotate_strip(strip_data, side_index, far_side, flipped)


def advance(padded, wave_speed, coriolis_part, cells_x, cells_y):
    height = padded[..., 0, :, :, :]
    wind_east = padded[..., 1, :, :, :]
    wind_north = padded[..., 2, :, :, :]
    speed = wave_speed[:, None, None]
    east_pred = wind_east[..., 1 : cells_x + 5, 3 : cells_y + 3] - speed * (
        0.5
        * (
            height[..., 2 : cells_x + 6, 3 : cells_y + 3]
            - height[..., 0 : cells_x + 4, 3 : cells_y + 3]
        )
    )
    north_pred = wind_north[..., 3 : cells_x + 3, 1 : cells_y + 5] - speed * (
        0.5
        * (
            height[..., 3 : cells_x + 3, 2 : cells_y + 6]
            - height[..., 3 : cells_x + 3, 0 : cells_y + 4]
        )
    )
    flux_east = (
        8.0 * (east_pred[..., 3 : cells_x + 3, :] - east_pred[..., 1 : cells_x + 1, :])
        - (east_pred[..., 4 : cells_x + 4, :] - east_pred[..., 0:cells_x, :])
    ) / 12.0
    flux_north = (
        8.0 * (north_pred[..., 3 : cells_y + 3] - north_pred[..., 1 : cells_y + 1])
        - (north_pred[..., 4 : cells_y + 4] - north_pred[..., 0:cells_y])
    ) / 12.0
    height_new = height[..., 3 : cells_x + 3, 3 : cells_y + 3] - speed * (flux_east + flux_north)
    east_inner = east_pred[..., 2 : cells_x + 2, :]
    north_inner = north_pred[..., 2 : cells_y + 2]
    turning = coriolis_part[..., None, :, :]
    return jnp.stack(
        [height_new, east_inner + turning * north_inner, north_inner - turning * east_inner],
        axis=-4,
    )


def one_substep(state, coriolis, wave_speed, edges, count_x, count_y, index_x, index_y):
    faces = state.shape[0]
    cells_x = state.shape[3]
    cells_y = state.shape[4]
    padded = padded_2(state, (("tx", 3), ("ty", 4)), 3)
    west_rim = state[:, :, :, 0:3, :]
    east_rim = jnp.flip(state[:, :, :, cells_x - 3 :, :], 3)
    south_rim = jnp.swapaxes(state[:, :, :, :, 0:3], 3, 4)
    north_rim = jnp.swapaxes(jnp.flip(state[:, :, :, :, cells_y - 3 :], 4), 3, 4)
    west_part = spread(west_rim, "tx", 0)
    east_part = spread(east_rim, "tx", count_x - 1)
    west_full, east_full = (
        lax.all_gather(west_part, "ty", axis=4, tiled=True),
        lax.all_gather(east_part, "ty", axis=4, tiled=True),
    )
    south_row, north_row = (
        lax.all_gather(south_rim, "tx", axis=4, tiled=True),
        lax.all_gather(north_rim, "tx", axis=4, tiled=True),
    )
    south_all, north_all = (
        lax.all_gather(south_row, "ty", axis=0, tiled=True),
        lax.all_gather(north_row, "ty", axis=0, tiled=True),
    )
    south_full = south_all[0:faces]
    north_full = north_all[(count_y - 1) * faces : count_y * faces]
    edge_store = jnp.stack([west_full, east_full, south_full, north_full])
    halos = []
    for side_index in range(4):
        if side_index < 2:
            slabs = jnp.stack(
                [
                    side_halo(edge_store, edges, face_index, side_index, index_y * cells_y, cells_y)
                    for face_index in range(faces)
                ]
            )
        else:
            slabs = jnp.stack(
                [
                    side_halo(edge_store, edges, face_index, side_index, index_x * cells_x, cells_x)
                    for face_index in range(faces)
                ]
            )
        halos.append(slabs)
    west_region = padded[:, :, :, 0:3, 3 : cells_y + 3]
    padded = padded.at[:, :, :, 0:3, 3 : cells_y + 3].set(
        jnp.where(index_x == 0, jnp.flip(halos[0], 3), west_region)
    )
    east_region = padded[:, :, :, cells_x + 3 : cells_x + 6, 3 : cells_y + 3]
    padded = padded.at[:, :, :, cells_x + 3 : cells_x + 6, 3 : cells_y + 3].set(
        jnp.where(index_x == count_x - 1, halos[1], east_region)
    )
    south_region = padded[:, :, :, 3 : cells_x + 3, 0:3]
    padded = padded.at[:, :, :, 3 : cells_x + 3, 0:3].set(
        jnp.where(index_y == 0, jnp.swapaxes(jnp.flip(halos[2], 3), 3, 4), south_region)
    )
    north_region = padded[:, :, :, 3 : cells_x + 3, cells_y + 3 : cells_y + 6]
    padded = padded.at[:, :, :, 3 : cells_x + 3, cells_y + 3 : cells_y + 6].set(
        jnp.where(index_y == count_y - 1, jnp.swapaxes(halos[3], 3, 4), north_region)
    )
    return advance(padded, wave_speed, coriolis, cells_x, cells_y)


def on_device(state, coriolis, wave_speed, edges):
    count_x = lax.axis_size("tx")
    count_y = lax.axis_size("ty")
    index_x = lax.axis_index("tx")
    index_y = lax.axis_index("ty")
    for substep_index in range(SUBSTEPS):
        state = one_substep(state, coriolis, wave_speed, edges, count_x, count_y, index_x, index_y)
    return state


def fits(state):
    count_x = lax.axis_size("tx")
    faces, fields, levels, cells_x, cells_y = state.shape
    return (
        lax.axis_size("ty") == 2
        and faces % 2 == 0
        and levels == 4
        and cells_x == 6
        and cells_y == 24
        and count_x == 8
        and cells_x * count_x == 2 * cells_y
        and 2 * cells_y + 2 * MARGIN <= WINDOW
    )


def either(state, coriolis, wave_speed, edges):
    if fits(state):
        return fast_on_device(state, coriolis, wave_speed, edges)
    return on_device(state, coriolis, wave_speed, edges)


def solution(mesh):
    in_specs = (P("member", None, None, "tx", "ty"), P(None, "tx", "ty"), P(), P())
    out_specs = P("member", None, None, "tx", "ty")
    return jax.shard_map(
        either, mesh=mesh, in_specs=in_specs, out_specs=out_specs, check_vma=False
    )
```

```python
import functools

import jax
import jax.numpy as jnp
from jax import lax
from jax.experimental import pallas as pl
from jax.experimental.pallas import tpu as pltpu
from jax.sharding import PartitionSpec as P

SUBSTEPS = 2
LANES = 128
WINDOW = 64
MARGIN = 8
VMEM_LIMIT = 32 * 1024 * 1024
SMALL_VMEM_LIMIT = 8 * 1024 * 1024


def wrap(index, count):
    index = jnp.where(index < 0, index + count, index)
    return jnp.where(index >= count, index - count, index)


def lane_shift(amount):
    return amount & (LANES - 1)


def windows(source, target, count_x, index_y, cx, cy):
    spare = cy - 2 * cx
    near = jnp.minimum(target, count_x - 1 - target)
    rim = (source == 0) | (source == count_x - 1)
    starts = []
    for inward in (cx // 2, cx):
        start = jnp.maximum(jnp.minimum(cx * near - inward, spare), 0)
        start = jnp.where(rim, start, 0)
        starts.append(jnp.where(index_y == 0, start, spare - start))
    close, far = starts
    upside = source == count_x - 1
    return jnp.where(upside, far, close), jnp.where(upside, close, far)


def unit_place(field, x, cx, group, width):
    per_row = 60 // width
    index = field * cx + x
    return (index // per_row) * group, (index % per_row) * width


def chunk_targets(count_x, full_rows, small_rows):
    sense = 1 - 2 * lax.axis_index("ty")
    return [
        (full_rows + place * small_rows, -sense * distance)
        for place, distance in enumerate((2, 3))
    ]


def put_chunk(cx, cy, count_x, block_ref, line_ref, out_ref, top, offset):
    pairs = 3
    group = 4 * pairs
    fields = 3
    half = cx // 2
    width = 2 * cx
    index_x = lax.axis_index("tx")
    target = wrap(index_x + offset, count_x)
    starts = windows(index_x, target, count_x, lax.axis_index("ty"), cx, cy)
    position = lax.broadcasted_iota(jnp.int32, (group, LANES), 1) % WINDOW
    from_lane = {lane: position >= lane for lane in range(0, 60, width)}
    blocks = {}

    def put(row, lane, lines):
        blocks[row] = lines if row not in blocks else jnp.where(from_lane[lane], lines, blocks[row])

    if block_ref is not None:
        for field in range(fields):
            for x in range(cx):
                row = field * half * group + (x // 2) * group
                at, lane = unit_place(field, x, cx, group, width)
                shift = lane_shift(lane - MARGIN - (x % 2) * cy - starts[x // half])
                put(at, lane, pltpu.roll(block_ref[row : row + group], shift, 1))
    else:
        at = unit_place(fields, 0, cx, group, width)[0]
        blocks[at] = out_ref[top + at : top + at + group]
    if line_ref is not None:
        for part in range(2):
            at, lane = unit_place(fields, part, cx, group, width)
            shift = lane_shift(lane - MARGIN - starts[part])
            put(at, lane, pltpu.roll(line_ref[16 * part : 16 * part + group], shift, 1))
    for row, lines in blocks.items():
        out_ref[top + row : top + row + group] = lines


def pack_kernel(cx, cy, count_x, full_rows, small_rows, state_ref, swap_ref):
    faces, fields = state_ref.shape[:2]
    levels = state_ref.shape[3]
    group = (faces // 2) * levels
    half = cx // 2
    swap_ref[:full_rows] = jnp.zeros((full_rows, LANES), jnp.float32)
    for face in range(faces):
        for parity in range(2):
            lane = (face % 2) * WINDOW + MARGIN + parity * cy
            for xp in range(half):
                for field in range(fields):
                    row = field * half * group + xp * group + (face // 2) * levels
                    swap_ref[row : row + levels, lane : lane + cy] = state_ref[
                        face, field, 2 * xp + parity
                    ]
    for top, offset in chunk_targets(count_x, full_rows, small_rows):
        put_chunk(cx, cy, count_x, swap_ref, None, swap_ref, top, offset)


def pack_coriolis_kernel(
    cx, cy, count_x, full_rows, small_rows, coriolis_ref, swap_in, swap_ref, line_ref
):
    faces = coriolis_ref.shape[0]
    pairs = faces // 2
    half = cx // 2
    base = 3 * half * 4 * pairs
    line_ref[...] = jnp.zeros(line_ref.shape, jnp.float32)
    for face in range(faces):
        lane = (face % 2) * WINDOW + MARGIN
        for x in range(cx):
            line = coriolis_ref[face, x : x + 1]
            row = base + (x // 2) * pairs + face // 2
            at = lane + (x % 2) * cy
            swap_ref[row : row + 1, at : at + cy] = line
            row = (x // half) * 16 + (x % half) * pairs + face // 2
            line_ref[row : row + 1, lane : lane + cy] = line
    for top, offset in chunk_targets(count_x, full_rows, small_rows):
        put_chunk(cx, cy, count_x, None, line_ref, swap_ref, top, offset)


def keep_kernel(cx, cy, count_x, small_rows, swap_ref, line_ref, keep_ref, middle_ref):
    sense = 1 - 2 * lax.axis_index("ty")
    put_chunk(cx, cy, count_x, swap_ref, line_ref, middle_ref, 0, count_x // 2)
    for place, distance in enumerate((2, 3)):
        top = place * small_rows
        put_chunk(cx, cy, count_x, swap_ref, line_ref, keep_ref, top, sense * distance)


def mix_kernel(
    full_rows, small_rows, swap_ref, other_ref, keep_ref, middle_ref,
    near_ref, third_ref, second_ref, fourth_ref,
):
    near_ref[:full_rows] = swap_ref[:full_rows]
    near_ref[full_rows:] = other_ref[:full_rows]
    for place, far_ref in enumerate((second_ref, third_ref)):
        at = place * small_rows
        far_ref[:small_rows] = keep_ref[at : at + small_rows]
        at += full_rows
        far_ref[small_rows:] = other_ref[at : at + small_rows]
    fourth_ref[...] = middle_ref[...]


def placer(cx, cy, count_x, full_rows, small_rows, z_ref, cor_ref):
    fields = z_ref.shape[0]
    levels = 4
    group = z_ref.shape[1] // (cx * count_x + 8)
    pairs = group // levels
    half = cx // 2
    chunk = cx * group
    index_x = lax.axis_index("tx")
    index_y = lax.axis_index("ty")
    south_half = lax.broadcasted_iota(jnp.int32, (group, LANES), 1) % WINDOW < MARGIN + cy
    south_is_own = index_y == 0
    own_half = south_half == south_is_own

    def row_of(x):
        return (x + 4) * group

    def from_owner(offset):
        source = wrap(index_x - offset, count_x)
        return source, pl.multiple_of(source * chunk, 8)

    def put_coriolis(start, x, values, at):
        for pair in range(pairs):
            line = values[at + pair : at + pair + 1]
            rows = pl.ds(start + x * group + pair * levels, levels)
            cor_ref[rows] = jnp.broadcast_to(line, (levels, LANES))

    def put_block(start, lines_of):
        base = fields * half * group
        for field in range(fields):
            for xp in range(half):
                even, odd = lines_of(field * half * group + xp * group, group)
                z_ref[field, pl.ds(start + row_of(2 * xp), group)] = even
                z_ref[field, pl.ds(start + row_of(2 * xp + 1), group)] = odd
        for parity, values in enumerate(lines_of(base, half * pairs)):
            for xp in range(half):
                put_coriolis(start, 2 * xp + parity, values, xp * pairs)

    def put_distant(source, start, lines_of):
        starts_south = windows(source, index_x, count_x, 0, cx, cy)
        starts_north = [cy - 2 * cx - start for start in starts_south]
        is_rim = (source == 0) | (source == count_x - 1)
        starts_north = [jnp.where(is_rim, start, cy - 2 * cx) for start in starts_north]
        shifts = {
            (part, lane): (
                lane_shift(MARGIN + starts_south[part] - lane),
                lane_shift(MARGIN + cy + starts_north[part] - lane),
            )
            for part in range(2)
            for lane in range(0, 60, 2 * cx)
        }

        def lines_at(field, x, part):
            at, lane = unit_place(field, x, cx, group, 2 * cx)
            return lines_of(at, *shifts[part, lane])

        for field in range(fields):
            for x in range(cx):
                z_ref[field, pl.ds(start + row_of(x), group)] = lines_at(field, x, x // half)
        for part in range(2):
            values = lines_at(fields, part, part)
            for x in range(half):
                put_coriolis(start, part * half + x, values, x * pairs)

    def place_own(own_ref, other_ref):
        def own_lines(row, rows):
            mine = own_ref[row : row + rows]
            theirs = other_ref[row : row + rows]
            up, down = index_y * cy, (1 - index_y) * cy
            keep = own_half[:rows]
            even = jnp.where(keep, pltpu.roll(mine, up, 1), pltpu.roll(theirs, down, 1))
            mine = pltpu.roll(mine, lane_shift(-down), 1)
            theirs = pltpu.roll(theirs, lane_shift(-up), 1)
            return even, jnp.where(keep, mine, theirs)

        put_block(from_owner(0)[1], own_lines)

    def place_near(block_ref, toward, south_first):
        south_top = pl.multiple_of(south_first * full_rows, 8)
        north_top = pl.multiple_of((1 - south_first) * full_rows, 8)

        def near_lines(row, rows):
            south = block_ref[pl.ds(south_top + row, rows)]
            north = block_ref[pl.ds(north_top + row, rows)]
            low = south_half[:rows]
            even = jnp.where(low, south, pltpu.roll(north, cy, 1))
            return even, jnp.where(low, pltpu.roll(south, LANES - cy, 1), north)

        put_block(from_owner(toward)[1], near_lines)

    def place_far(block_ref, toward, south_first):
        for place, distance in enumerate((3, 2)):
            top = 2 * place * small_rows
            south_at = pl.multiple_of(top + south_first * small_rows, 8)
            north_at = pl.multiple_of(top + (1 - south_first) * small_rows, 8)

            def far_lines(at, south_shift, north_shift, south_at=south_at, north_at=north_at):
                south = pltpu.roll(block_ref[pl.ds(south_at + at, group)], south_shift, 1)
                north = pltpu.roll(block_ref[pl.ds(north_at + at, group)], north_shift, 1)
                return jnp.where(south_half, south, north)

            put_distant(*from_owner(toward * distance), far_lines)

    def place_middle(got_ref, passed_ref):
        def middle_lines(at, south_shift, north_shift):
            row = 4 * small_rows + at
            mine_shift = jnp.where(south_is_own, south_shift, north_shift)
            other_shift = jnp.where(south_is_own, north_shift, south_shift)
            mine = pltpu.roll(got_ref[row : row + group], mine_shift, 1)
            theirs = pltpu.roll(passed_ref[row : row + group], other_shift, 1)
            return jnp.where(own_half, mine, theirs)

        put_distant(*from_owner(count_x // 2), middle_lines)

    return place_own, place_near, place_far, place_middle


def own_kernel(sizes, own_ref, other_ref, near_ref, z_ref, cor_ref):
    place_own, place_near = placer(*sizes, z_ref, cor_ref)[:2]
    index_y = lax.axis_index("ty")
    place_own(own_ref, other_ref)
    place_near(near_ref, 1 - 2 * index_y, index_y)


def got_kernel(sizes, far_ref, passed_ref, z_in, cor_in, z_ref, cor_ref):
    _, place_near, place_far, _ = placer(*sizes, z_ref, cor_ref)
    index_y = lax.axis_index("ty")
    place_far(far_ref, 1 - 2 * index_y, index_y)
    place_near(passed_ref, 2 * index_y - 1, 1 - index_y)


def step_kernel(
    sizes, far_ref, passed_ref, table_in, z_in, cor_in, out_hbm, z_ref, cor_ref,
    pred_ref, store_ref, tile_ref, flip_ref, speed_ref, table_ref, out_ref, sems,
):
    table_copy = pltpu.make_async_copy(table_in, table_ref, sems.at[0])
    table_copy.start()
    cx, cy, count_x = sizes[:3]
    levels = 4
    slots = 16
    cells = cx * count_x
    faces = store_ref.shape[0] // 4
    pairs = faces // 2
    group = pairs * levels
    chunk = cx * group
    index_x = lax.axis_index("tx")
    index_y = lax.axis_index("ty")

    def row_of(x):
        return (x + 4) * group

    def lanes_of(rows):
        return lax.broadcasted_iota(jnp.int32, (rows, LANES), 1)

    place_far, place_middle = placer(*sizes, z_ref, cor_ref)[2:]
    place_far(passed_ref, 2 * index_y - 1, 1 - index_y)
    place_middle(far_ref, passed_ref)

    table_copy.wait()
    level_of = lax.broadcasted_iota(jnp.int32, speed_ref.shape, 0) % levels
    speeds = jnp.full(speed_ref.shape, table_ref[0], jnp.float32)
    for index in range(1, levels):
        speeds = jnp.where(level_of == index, table_ref[index], speeds)
    speed_ref[...] = speeds

    lane_8 = lanes_of(8)
    place_8 = lane_8 % WINDOW
    gap = WINDOW - cells + 3
    wide = gap + 3 * levels
    row_tiles = range(0, cells, 8)
    rim_8 = ((place_8 >= MARGIN - 3) & (place_8 < MARGIN)) | (
        (place_8 >= MARGIN + cells) & (place_8 < MARGIN + cells + 3)
    )

    def collect():
        for pair in range(pairs):
            merged = [jnp.zeros((8, LANES), jnp.float32)] * len(row_tiles)
            for slot, field in ((0, 0), (1, 2)):
                for level in range(levels):
                    offset = slot * wide + 3 * level
                    here = place_8 - offset
                    wanted = ((here >= 0) & (here < 3)) | ((here >= gap) & (here < gap + 3))
                    shift = (offset - (MARGIN + cells - 3)) % LANES
                    lines = z_ref[field, pl.ds(row_of(0) + pair * levels + level, cells, group)]
                    lines = pltpu.roll(lines, shift, 1)
                    merged = [
                        jnp.where(wanted, lines[row : row + 8], old)
                        for row, old in zip(row_tiles, merged)
                    ]
            flip_ref[pair, :, :cells] = jnp.concatenate(merged, axis=0).T
            for slot in range(2):
                for side in (2, 3):
                    for odd in range(2):
                        for depth in range(3):
                            base = slot * wide
                            if side == 3:
                                base += odd * WINDOW + 2 - depth
                            else:
                                base += ((odd + 1) % 2) * WINDOW + gap + depth
                            at = slot * slots + depth * levels
                            store_ref[(2 * pair + odd) * 4 + side, at : at + levels] = flip_ref[
                                pair, pl.ds(base, levels, 3)
                            ]
            for slot in range(2):
                for side in (0, 1):
                    for depth in range(3):
                        x = depth if side == 0 else cells - 1 - depth
                        row = row_of(x) + pair * levels
                        lines = z_ref[slot, row : row + levels]
                        at = slot * slots + depth * levels
                        for odd in range(2):
                            store_ref[(2 * pair + odd) * 4 + side, at : at + levels] = lines

    def fetch(face, side, positions):
        at = levels + (face * 4 + side) * 3
        neighbour = table_ref[at].astype(jnp.int32)
        far_side = table_ref[at + 1].astype(jnp.int32)
        flipped = table_ref[at + 2].astype(jnp.int32)
        first = jnp.where(far_side < 2, MARGIN + WINDOW * (neighbour & 1), 0)
        start = first + jnp.where(flipped == 1, cells - 1, 0)
        step = 1 - 2 * flipped
        sign = ((1 - 2 * (side % 2)) * (2 * (far_side & 1) - 1)).astype(jnp.float32)
        index = neighbour * 4 + far_side
        parts = []
        for slot, position in enumerate(positions):
            order = (start + step * position) & (LANES - 1)
            for half_at in (0, 8):
                at = slot * slots + half_at
                lines = jnp.take_along_axis(store_ref[index, at : at + 8], order, axis=1)
                parts.append(lines if slot == 0 else sign * lines)
        return parts[:2], parts[2:]

    def depth_rows(parts, depth):
        at = (depth % 2) * levels
        return parts[depth // 2][at : at + levels]

    def rim_rows(side):
        left = lane_8 < WINDOW
        for pair in range(pairs):
            first = fetch(2 * pair, side, [lane_8 - MARGIN] * 2)
            second = fetch(2 * pair + 1, side, [lane_8 - (MARGIN + WINDOW)] * 2)
            for slot in range(2):
                both = [jnp.where(left, a, b) for a, b in zip(first[slot], second[slot])]
                for depth in range(3):
                    x = -1 - depth if side == 0 else cells + depth
                    row = row_of(x) + pair * levels
                    z_ref[slot, row : row + levels] = depth_rows(both, depth)

    tile_wide = WINDOW - cells - 3 + 3 * levels

    def put_tile(tile, parts, odd, side, base=0):
        for depth in range(3):
            if side == 3:
                at = base + odd * WINDOW + depth
            else:
                at = base + ((odd + 1) % 2) * WINDOW + tile_wide - 3 * levels + 2 - depth
            tile_ref[tile, pl.ds(at, levels, 3)] = depth_rows(parts, depth)

    def rim_columns_all():
        for pair in range(pairs):
            for odd in range(2):
                for side in (2, 3):
                    for slot, parts in enumerate(fetch(2 * pair + odd, side, [lane_8] * 2)):
                        put_tile(pair, parts, odd, side, slot * tile_wide)
            turned = tile_ref[pair].T[:cells]
            for slot, field in ((0, 0), (1, 2)):
                for level in range(levels):
                    shift = (MARGIN + cells - slot * tile_wide - 3 * level) % LANES
                    rolled = pltpu.roll(turned, shift, 1)
                    at = pl.ds(row_of(0) + pair * levels + level, cells, group)
                    lines = z_ref[field, at]
                    lines = [
                        jnp.where(rim_8, rolled[row : row + 8], lines[row : row + 8])
                        for row in row_tiles
                    ]
                    z_ref[field, at] = jnp.concatenate(lines, axis=0)

    def rim_columns_own():
        for odd in range(2):
            for side in (2, 3):
                total = [jnp.zeros((8, LANES), jnp.float32)] * 2
                for pair in range(pairs):
                    places = [8 * pair, 8 * (pairs + pair)]
                    positions = [lane_8 + (index_x * cx - place) for place in places]
                    fetched = fetch(2 * pair + odd, side, positions)
                    for place, parts in zip(places, fetched):
                        here = (lane_8 >= place) & (lane_8 < place + 8)
                        total = [jnp.where(here, a, b) for a, b in zip(parts, total)]
                put_tile(0, total, odd, side)
        turned = tile_ref[0].T
        for slot, field in ((0, 0), (1, 2)):
            for pair in range(pairs):
                row = 8 * (slot * pairs + pair)
                for level in range(levels):
                    shift = (MARGIN + cells - 3 * level) % LANES
                    rolled = pltpu.roll(turned[row : row + 8], shift, 1)[:cx]
                    start = row_of(0) + index_x * chunk + pair * levels + level
                    at = pl.ds(start, cx, group)
                    z_ref[field, at] = jnp.where(rim_8[:cx], rolled, z_ref[field, at])

    def predict(at, rows):
        speed = speed_ref[:rows]
        ahead = z_ref[0, pl.ds(at + group, rows)]
        behind = z_ref[0, pl.ds(at - group, rows)]
        pred_ref[pl.ds(at, rows)] = z_ref[1, pl.ds(at, rows)] - speed * (0.5 * (ahead - behind))

    def update(at, rows):
        speed = speed_ref[:rows]
        height = z_ref[0, pl.ds(at, rows)]
        north_pred = z_ref[2, pl.ds(at, rows)] - speed * (
            0.5 * (pltpu.roll(height, LANES - 1, 1) - pltpu.roll(height, 1, 1))
        )
        east_pred = pred_ref[pl.ds(at, rows)]
        flux_east = 8.0 * (
            pred_ref[pl.ds(at + group, rows)] - pred_ref[pl.ds(at - group, rows)]
        ) - (pred_ref[pl.ds(at + 2 * group, rows)] - pred_ref[pl.ds(at - 2 * group, rows)])
        flux_north = 8.0 * (
            pltpu.roll(north_pred, LANES - 1, 1) - pltpu.roll(north_pred, 1, 1)
        ) - (pltpu.roll(north_pred, LANES - 2, 1) - pltpu.roll(north_pred, 2, 1))
        height = height - speed * ((flux_east + flux_north) * (1.0 / 12.0))
        turning = cor_ref[pl.ds(at - row_of(0), rows)]
        return height, east_pred + turning * north_pred, north_pred - turning * east_pred

    def all_faces():
        rim_rows(0)
        rim_rows(1)
        rim_columns_all()
        for first in range(-2, cells + 2, 4):
            predict(row_of(first), 4 * group)
        def update_part(index, carry):
            at = pl.multiple_of(row_of(0) + index * (2 * chunk), 8)
            for field, values in enumerate(update(at, 2 * chunk)):
                z_ref[field, pl.ds(at, 2 * chunk)] = values
            return carry

        lax.fori_loop(0, count_x // 2, update_part, 0)

    def own_rows():

        @pl.when(index_x == 0)
        def _():
            rim_rows(0)

        @pl.when(index_x == count_x - 1)
        def _():
            rim_rows(1)

        rim_columns_own()
        at = pl.multiple_of(row_of(0) + index_x * chunk, 8)
        predict(at - 2 * group, chunk + 4 * group)
        copies = []
        for field, values in enumerate(update(at, chunk)):
            for odd in range(2):
                shift = LANES - (MARGIN + odd * WINDOW) - index_y * cy
                rolled = pltpu.roll(values, shift, 1)
                for x in range(cx):
                    for pair in range(pairs):
                        row = x * group + pair * levels
                        out_ref[field, 2 * pair + odd, x] = rolled[row : row + levels, :cy]
            copy = pltpu.make_async_copy(out_ref.at[field], out_hbm.at[:, field], sems.at[1 + field])
            copy.start()
            copies.append(copy)
        for copy in copies:
            copy.wait()

    def substep(index, carry):
        collect()
        pl.when(index == 0)(all_faces)
        pl.when(index == SUBSTEPS - 1)(own_rows)
        return carry

    lax.fori_loop(0, SUBSTEPS, substep, 0)


def fast_on_device(state, coriolis, wave_speed, edges):
    count_x = lax.axis_size("tx")
    faces, fields, levels, cx, cy = state.shape
    pairs = faces // 2
    group = pairs * levels
    cells = cx * count_x
    full_rows = fields * (cx // 2) * group + (cx // 2) * pairs
    full_rows = -(-full_rows // 8) * 8
    small_rows = unit_place(fields, 1, cx, group, 2 * cx)[0] + group
    in_vmem = pl.BlockSpec(memory_space=pltpu.VMEM)
    params = pltpu.CompilerParams(vmem_limit_bytes=SMALL_VMEM_LIMIT)
    swap_shape = jax.ShapeDtypeStruct((full_rows + 2 * small_rows, LANES), jnp.float32)
    swap = pl.pallas_call(
        functools.partial(pack_kernel, cx, cy, count_x, full_rows, small_rows),
        out_shape=swap_shape,
        in_specs=[in_vmem],
        out_specs=in_vmem,
        compiler_params=params,
        name="pack",
    )(jnp.swapaxes(state, 2, 3))
    swap, lines = pl.pallas_call(
        functools.partial(pack_coriolis_kernel, cx, cy, count_x, full_rows, small_rows),
        out_shape=[swap_shape, jax.ShapeDtypeStruct((32, LANES), jnp.float32)],
        in_specs=[in_vmem] * 2,
        out_specs=[in_vmem] * 2,
        input_output_aliases={1: 0},
        compiler_params=params,
        name="pack_coriolis",
    )(coriolis, swap)
    keep, middle = pl.pallas_call(
        functools.partial(keep_kernel, cx, cy, count_x, small_rows),
        out_shape=[
            jax.ShapeDtypeStruct((2 * small_rows, LANES), jnp.float32),
            jax.ShapeDtypeStruct((small_rows, LANES), jnp.float32),
        ],
        in_specs=[pl.BlockSpec(memory_space=pltpu.VMEM)] * 2,
        out_specs=[pl.BlockSpec(memory_space=pltpu.VMEM)] * 2,
        compiler_params=pltpu.CompilerParams(vmem_limit_bytes=SMALL_VMEM_LIMIT),
        name="keep",
    )(swap, lines)

    def moved(block, distance):
        pairs_of = []
        for index in range(count_x):
            for core in range(2):
                target = (index + distance * (1 - 2 * core)) % count_x
                pairs_of.append((2 * index + core, 2 * target + core))
        return lax.ppermute(block, ("tx", "ty"), pairs_of)

    def across(block):
        return lax.ppermute(block, "ty", [(0, 1), (1, 0)])

    other = across(swap)
    messages = pl.pallas_call(
        functools.partial(mix_kernel, full_rows, small_rows),
        out_shape=[
            jax.ShapeDtypeStruct((rows, LANES), jnp.float32)
            for rows in (2 * full_rows, 2 * small_rows, 2 * small_rows, small_rows)
        ],
        in_specs=[in_vmem] * 4,
        out_specs=[in_vmem] * 4,
        compiler_params=params,
        name="messages",
    )(swap, other, keep, middle)
    near, third, second, fourth = [
        moved(block, distance) for block, distance in zip(messages, (1, 3, 2, count_x // 2))
    ]
    near, fourth = lax.optimization_barrier((near, fourth))
    far = jnp.concatenate([third, second, fourth])
    table = jnp.concatenate([wave_speed, edges.reshape(-1).astype(jnp.float32)])
    far, table = lax.optimization_barrier((far, table))
    near_passed = across(near)
    far_passed = across(far)

    sizes = (cx, cy, count_x, full_rows, small_rows)
    state_rows = [
        jax.ShapeDtypeStruct((fields, (cells + 8) * group, LANES), jnp.float32),
        jax.ShapeDtypeStruct((cells * group, LANES), jnp.float32),
    ]
    rows = pl.pallas_call(
        functools.partial(own_kernel, sizes),
        out_shape=state_rows,
        in_specs=[in_vmem] * 3,
        out_specs=[in_vmem] * 2,
        compiler_params=params,
        name="place_own",
    )(swap, other, near)
    rows = pl.pallas_call(
        functools.partial(got_kernel, sizes),
        out_shape=state_rows,
        in_specs=[in_vmem] * 4,
        out_specs=[in_vmem] * 2,
        input_output_aliases={2: 0, 3: 1},
        compiler_params=params,
        name="place_got",
    )(far, near_passed, *rows)
    out, _, _ = pl.pallas_call(
        functools.partial(step_kernel, sizes),
        out_shape=[jax.ShapeDtypeStruct((faces, fields, cx, levels, cy), jnp.float32)]
        + state_rows,
        in_specs=[in_vmem] * 5,
        out_specs=[pl.BlockSpec(memory_space=pltpu.HBM)] + [in_vmem] * 2,
        input_output_aliases={3: 1, 4: 2},
        scratch_shapes=[
            pltpu.VMEM(((cells + 8) * group, LANES), jnp.float32),
            pltpu.VMEM((faces * 4, 32, LANES), jnp.float32),
            pltpu.VMEM((pairs, LANES, LANES), jnp.float32),
            pltpu.VMEM((pairs, LANES, LANES), jnp.float32),
            pltpu.VMEM((2 * cx * group, LANES), jnp.float32),
            pltpu.SMEM(table.shape, jnp.float32),
            pltpu.VMEM((fields, faces, cx, levels, cy), jnp.float32),
            pltpu.SemaphoreType.DMA((1 + fields,)),
        ],
        compiler_params=pltpu.CompilerParams(vmem_limit_bytes=VMEM_LIMIT),
        name="substeps",
    )(far, far_passed, table, *rows)
    return jnp.swapaxes(out, 2, 3)


def padded_2(block, sides, width):
    for axis, dim in sides:
        count = lax.axis_size(axis)
        forward = [(i, i + 1) for i in range(count - 1)]
        backward = [(target, source) for source, target in forward]
        low = lax.ppermute(
            lax.slice_in_dim(block, block.shape[dim] - width, None, axis=dim), axis, forward
        )
        high = lax.ppermute(lax.slice_in_dim(block, 0, width, axis=dim), axis, backward)
        block = jnp.concatenate([low, block, high], axis=dim)
    return block


def spread(block, axis, owner):
    block = jnp.where(lax.axis_index(axis) == owner, block, jnp.zeros_like(block))
    return lax.psum(block, axis)


def rotate_strip(strip_data, side_index, far_side, flipped):
    normal_part = jnp.where(far_side < 2, strip_data[1], strip_data[2])
    along_part = jnp.where(far_side < 2, strip_data[2], strip_data[1])
    sign_here = 2.0 * (side_index % 2) - 1.0
    sign_there = (2 * (far_side % 2) - 1).astype(jnp.float32)
    normal_part = -sign_here * sign_there * normal_part
    along_part = (1 - 2 * flipped).astype(jnp.float32) * along_part
    if side_index < 2:
        return jnp.stack([strip_data[0], normal_part, along_part])
    return jnp.stack([strip_data[0], along_part, normal_part])


def window_strip(store, side_pick, neighbour, flipped, start, width):
    full_length = store.shape[5]
    begin = jnp.where(flipped == 1, full_length - start - width, start)
    zero = jnp.zeros((), jnp.int32)
    sizes_here = (1, 1, store.shape[2], store.shape[3], store.shape[4], width)
    piece = lax.dynamic_slice(store, (side_pick, neighbour, zero, zero, zero, begin), sizes_here)[
        0, 0
    ]
    return jnp.where(flipped == 1, jnp.flip(piece, 3), piece)


def side_halo(edge_store, edges, face_index, side_index, start, width):
    neighbour = edges[face_index, side_index, 0]
    far_side = edges[face_index, side_index, 1]
    flipped = edges[face_index, side_index, 2]
    strip_data = window_strip(edge_store, far_side, neighbour, flipped, start, width)
    return rotate_strip(strip_data, side_index, far_side, flipped)


def advance(padded, wave_speed, coriolis_part, cells_x, cells_y):
    height = padded[..., 0, :, :, :]
    wind_east = padded[..., 1, :, :, :]
    wind_north = padded[..., 2, :, :, :]
    speed = wave_speed[:, None, None]
    east_pred = wind_east[..., 1 : cells_x + 5, 3 : cells_y + 3] - speed * (
        0.5
        * (
            height[..., 2 : cells_x + 6, 3 : cells_y + 3]
            - height[..., 0 : cells_x + 4, 3 : cells_y + 3]
        )
    )
    north_pred = wind_north[..., 3 : cells_x + 3, 1 : cells_y + 5] - speed * (
        0.5
        * (
            height[..., 3 : cells_x + 3, 2 : cells_y + 6]
            - height[..., 3 : cells_x + 3, 0 : cells_y + 4]
        )
    )
    flux_east = (
        8.0 * (east_pred[..., 3 : cells_x + 3, :] - east_pred[..., 1 : cells_x + 1, :])
        - (east_pred[..., 4 : cells_x + 4, :] - east_pred[..., 0:cells_x, :])
    ) / 12.0
    flux_north = (
        8.0 * (north_pred[..., 3 : cells_y + 3] - north_pred[..., 1 : cells_y + 1])
        - (north_pred[..., 4 : cells_y + 4] - north_pred[..., 0:cells_y])
    ) / 12.0
    height_new = height[..., 3 : cells_x + 3, 3 : cells_y + 3] - speed * (flux_east + flux_north)
    east_inner = east_pred[..., 2 : cells_x + 2, :]
    north_inner = north_pred[..., 2 : cells_y + 2]
    turning = coriolis_part[..., None, :, :]
    return jnp.stack(
        [height_new, east_inner + turning * north_inner, north_inner - turning * east_inner],
        axis=-4,
    )


def one_substep(state, coriolis, wave_speed, edges, count_x, count_y, index_x, index_y):
    faces = state.shape[0]
    cells_x = state.shape[3]
    cells_y = state.shape[4]
    padded = padded_2(state, (("tx", 3), ("ty", 4)), 3)
    west_rim = state[:, :, :, 0:3, :]
    east_rim = jnp.flip(state[:, :, :, cells_x - 3 :, :], 3)
    south_rim = jnp.swapaxes(state[:, :, :, :, 0:3], 3, 4)
    north_rim = jnp.swapaxes(jnp.flip(state[:, :, :, :, cells_y - 3 :], 4), 3, 4)
    west_part = spread(west_rim, "tx", 0)
    east_part = spread(east_rim, "tx", count_x - 1)
    west_full, east_full = (
        lax.all_gather(west_part, "ty", axis=4, tiled=True),
        lax.all_gather(east_part, "ty", axis=4, tiled=True),
    )
    south_row, north_row = (
        lax.all_gather(south_rim, "tx", axis=4, tiled=True),
        lax.all_gather(north_rim, "tx", axis=4, tiled=True),
    )
    south_all, north_all = (
        lax.all_gather(south_row, "ty", axis=0, tiled=True),
        lax.all_gather(north_row, "ty", axis=0, tiled=True),
    )
    south_full = south_all[0:faces]
    north_full = north_all[(count_y - 1) * faces : count_y * faces]
    edge_store = jnp.stack([west_full, east_full, south_full, north_full])
    halos = []
    for side_index in range(4):
        if side_index < 2:
            slabs = jnp.stack(
                [
                    side_halo(edge_store, edges, face_index, side_index, index_y * cells_y, cells_y)
                    for face_index in range(faces)
                ]
            )
        else:
            slabs = jnp.stack(
                [
                    side_halo(edge_store, edges, face_index, side_index, index_x * cells_x, cells_x)
                    for face_index in range(faces)
                ]
            )
        halos.append(slabs)
    west_region = padded[:, :, :, 0:3, 3 : cells_y + 3]
    padded = padded.at[:, :, :, 0:3, 3 : cells_y + 3].set(
        jnp.where(index_x == 0, jnp.flip(halos[0], 3), west_region)
    )
    east_region = padded[:, :, :, cells_x + 3 : cells_x + 6, 3 : cells_y + 3]
    padded = padded.at[:, :, :, cells_x + 3 : cells_x + 6, 3 : cells_y + 3].set(
        jnp.where(index_x == count_x - 1, halos[1], east_region)
    )
    south_region = padded[:, :, :, 3 : cells_x + 3, 0:3]
    padded = padded.at[:, :, :, 3 : cells_x + 3, 0:3].set(
        jnp.where(index_y == 0, jnp.swapaxes(jnp.flip(halos[2], 3), 3, 4), south_region)
    )
    north_region = padded[:, :, :, 3 : cells_x + 3, cells_y + 3 : cells_y + 6]
    padded = padded.at[:, :, :, 3 : cells_x + 3, cells_y + 3 : cells_y + 6].set(
        jnp.where(index_y == count_y - 1, jnp.swapaxes(halos[3], 3, 4), north_region)
    )
    return advance(padded, wave_speed, coriolis, cells_x, cells_y)


def on_device(state, coriolis, wave_speed, edges):
    count_x = lax.axis_size("tx")
    count_y = lax.axis_size("ty")
    index_x = lax.axis_index("tx")
    index_y = lax.axis_index("ty")
    for substep_index in range(SUBSTEPS):
        state = one_substep(state, coriolis, wave_speed, edges, count_x, count_y, index_x, index_y)
    return state


def fits(state):
    count_x = lax.axis_size("tx")
    faces, fields, levels, cells_x, cells_y = state.shape
    return (
        lax.axis_size("ty") == 2
        and faces % 2 == 0
        and levels == 4
        and cells_x == 6
        and cells_y == 24
        and count_x == 8
        and cells_x * count_x == 2 * cells_y
        and 2 * cells_y + 2 * MARGIN <= WINDOW
    )


def either(state, coriolis, wave_speed, edges):
    if fits(state):
        return fast_on_device(state, coriolis, wave_speed, edges)
    return on_device(state, coriolis, wave_speed, edges)


def solution(mesh):
    in_specs = (P("member", None, None, "tx", "ty"), P(None, "tx", "ty"), P(), P())
    out_specs = P("member", None, None, "tx", "ty")
    return jax.shard_map(
        either, mesh=mesh, in_specs=in_specs, out_specs=out_specs, check_vma=False
    )
```

```python
import functools

import jax
import jax.numpy as jnp
from jax import lax
from jax.experimental import pallas as pl
from jax.experimental.pallas import tpu as pltpu
from jax.sharding import PartitionSpec as P

SUBSTEPS = 2
LANES = 128
WINDOW = 64
MARGIN = 8
VMEM_LIMIT = 32 * 1024 * 1024
SMALL_VMEM_LIMIT = 8 * 1024 * 1024


def wrap(index, count):
    index = jnp.where(index < 0, index + count, index)
    return jnp.where(index >= count, index - count, index)


def lane_shift(amount):
    return amount & (LANES - 1)


def windows(source, target, count_x, index_y, cx, cy):
    spare = cy - 2 * cx
    near = jnp.minimum(target, count_x - 1 - target)
    rim = (source == 0) | (source == count_x - 1)
    starts = []
    for inward in (cx // 2, cx):
        start = jnp.maximum(jnp.minimum(cx * near - inward, spare), 0)
        start = jnp.where(rim, start, 0)
        starts.append(jnp.where(index_y == 0, start, spare - start))
    close, far = starts
    upside = source == count_x - 1
    return jnp.where(upside, far, close), jnp.where(upside, close, far)


def unit_place(field, x, cx, group, width):
    per_row = 60 // width
    index = field * cx + x
    return (index // per_row) * group, (index % per_row) * width


def chunk_targets(count_x, full_rows, small_rows):
    sense = 1 - 2 * lax.axis_index("ty")
    return [
        (full_rows + place * small_rows, -sense * distance)
        for place, distance in enumerate((2, 3))
    ]


def put_chunk(cx, cy, count_x, block_ref, line_ref, out_ref, top, offset):
    pairs = 3
    group = 4 * pairs
    fields = 3
    half = cx // 2
    width = 2 * cx
    index_x = lax.axis_index("tx")
    target = wrap(index_x + offset, count_x)
    starts = windows(index_x, target, count_x, lax.axis_index("ty"), cx, cy)
    position = lax.broadcasted_iota(jnp.int32, (group, LANES), 1) % WINDOW
    from_lane = {lane: position >= lane for lane in range(0, 60, width)}
    blocks = {}

    def put(row, lane, lines):
        blocks[row] = lines if row not in blocks else jnp.where(from_lane[lane], lines, blocks[row])

    if block_ref is not None:
        for field in range(fields):
            for x in range(cx):
                row = field * half * group + (x // 2) * group
                at, lane = unit_place(field, x, cx, group, width)
                shift = lane_shift(lane - MARGIN - (x % 2) * cy - starts[x // half])
                put(at, lane, pltpu.roll(block_ref[row : row + group], shift, 1))
    else:
        at = unit_place(fields, 0, cx, group, width)[0]
        blocks[at] = out_ref[top + at : top + at + group]
    if line_ref is not None:
        for part in range(2):
            at, lane = unit_place(fields, part, cx, group, width)
            shift = lane_shift(lane - MARGIN - starts[part])
            put(at, lane, pltpu.roll(line_ref[16 * part : 16 * part + group], shift, 1))
    for row, lines in blocks.items():
        out_ref[top + row : top + row + group] = lines


def pack_kernel(cx, cy, count_x, full_rows, small_rows, state_ref, swap_ref):
    faces, fields = state_ref.shape[:2]
    levels = state_ref.shape[3]
    group = (faces // 2) * levels
    half = cx // 2
    swap_ref[:full_rows] = jnp.zeros((full_rows, LANES), jnp.float32)
    for face in range(faces):
        for parity in range(2):
            lane = (face % 2) * WINDOW + MARGIN + parity * cy
            for xp in range(half):
                for field in range(fields):
                    row = field * half * group + xp * group + (face // 2) * levels
                    swap_ref[row : row + levels, lane : lane + cy] = state_ref[
                        face, field, 2 * xp + parity
                    ]
    for top, offset in chunk_targets(count_x, full_rows, small_rows):
        put_chunk(cx, cy, count_x, swap_ref, None, swap_ref, top, offset)


def pack_coriolis_kernel(
    cx, cy, count_x, full_rows, small_rows, coriolis_ref, swap_in, swap_ref, line_ref
):
    faces = coriolis_ref.shape[0]
    pairs = faces // 2
    half = cx // 2
    base = 3 * half * 4 * pairs
    line_ref[...] = jnp.zeros(line_ref.shape, jnp.float32)
    for face in range(faces):
        lane = (face % 2) * WINDOW + MARGIN
        for x in range(cx):
            line = coriolis_ref[face, x : x + 1]
            row = base + (x // 2) * pairs + face // 2
            at = lane + (x % 2) * cy
            swap_ref[row : row + 1, at : at + cy] = line
            row = (x // half) * 16 + (x % half) * pairs + face // 2
            line_ref[row : row + 1, lane : lane + cy] = line
    for top, offset in chunk_targets(count_x, full_rows, small_rows):
        put_chunk(cx, cy, count_x, None, line_ref, swap_ref, top, offset)


def keep_kernel(cx, cy, count_x, small_rows, swap_ref, line_ref, keep_ref, middle_ref):
    sense = 1 - 2 * lax.axis_index("ty")
    put_chunk(cx, cy, count_x, swap_ref, line_ref, middle_ref, 0, count_x // 2)
    for place, distance in enumerate((2, 3)):
        top = place * small_rows
        put_chunk(cx, cy, count_x, swap_ref, line_ref, keep_ref, top, sense * distance)


def mix_kernel(
    full_rows, small_rows, swap_ref, other_ref, keep_ref, middle_ref,
    near_ref, third_ref, second_ref, fourth_ref,
):
    near_ref[:full_rows] = swap_ref[:full_rows]
    near_ref[full_rows:] = other_ref[:full_rows]
    for place, far_ref in enumerate((second_ref, third_ref)):
        at = place * small_rows
        far_ref[:small_rows] = keep_ref[at : at + small_rows]
        at += full_rows
        far_ref[small_rows:] = other_ref[at : at + small_rows]
    fourth_ref[...] = middle_ref[...]


def placer(cx, cy, count_x, full_rows, small_rows, z_ref, cor_ref):
    fields = z_ref.shape[0]
    levels = 4
    group = z_ref.shape[1] // (cx * count_x + 8)
    pairs = group // levels
    half = cx // 2
    chunk = cx * group
    index_x = lax.axis_index("tx")
    index_y = lax.axis_index("ty")
    south_half = lax.broadcasted_iota(jnp.int32, (group, LANES), 1) % WINDOW < MARGIN + cy
    south_is_own = index_y == 0
    own_half = south_half == south_is_own

    def row_of(x):
        return (x + 4) * group

    def from_owner(offset):
        source = wrap(index_x - offset, count_x)
        return source, pl.multiple_of(source * chunk, 8)

    def put_coriolis(start, x, values, at):
        for pair in range(pairs):
            line = values[at + pair : at + pair + 1]
            rows = pl.ds(start + x * group + pair * levels, levels)
            cor_ref[rows] = jnp.broadcast_to(line, (levels, LANES))

    def put_block(start, lines_of):
        base = fields * half * group
        for field in range(fields):
            for xp in range(half):
                even, odd = lines_of(field * half * group + xp * group, group)
                z_ref[field, pl.ds(start + row_of(2 * xp), group)] = even
                z_ref[field, pl.ds(start + row_of(2 * xp + 1), group)] = odd
        for parity, values in enumerate(lines_of(base, half * pairs)):
            for xp in range(half):
                put_coriolis(start, 2 * xp + parity, values, xp * pairs)

    def put_distant(source, start, lines_of):
        starts_south = windows(source, index_x, count_x, 0, cx, cy)
        starts_north = [cy - 2 * cx - start for start in starts_south]
        is_rim = (source == 0) | (source == count_x - 1)
        starts_north = [jnp.where(is_rim, start, cy - 2 * cx) for start in starts_north]
        shifts = {
            (part, lane): (
                lane_shift(MARGIN + starts_south[part] - lane),
                lane_shift(MARGIN + cy + starts_north[part] - lane),
            )
            for part in range(2)
            for lane in range(0, 60, 2 * cx)
        }

        def lines_at(field, x, part):
            at, lane = unit_place(field, x, cx, group, 2 * cx)
            return lines_of(at, *shifts[part, lane])

        for field in range(fields):
            for x in range(cx):
                z_ref[field, pl.ds(start + row_of(x), group)] = lines_at(field, x, x // half)
        for part in range(2):
            values = lines_at(fields, part, part)
            for x in range(half):
                put_coriolis(start, part * half + x, values, x * pairs)

    def place_own(own_ref, other_ref):
        def own_lines(row, rows):
            mine = own_ref[row : row + rows]
            theirs = other_ref[row : row + rows]
            up, down = index_y * cy, (1 - index_y) * cy
            keep = own_half[:rows]
            even = jnp.where(keep, pltpu.roll(mine, up, 1), pltpu.roll(theirs, down, 1))
            mine = pltpu.roll(mine, lane_shift(-down), 1)
            theirs = pltpu.roll(theirs, lane_shift(-up), 1)
            return even, jnp.where(keep, mine, theirs)

        put_block(from_owner(0)[1], own_lines)

    def place_near(block_ref, toward, south_first):
        south_top = pl.multiple_of(south_first * full_rows, 8)
        north_top = pl.multiple_of((1 - south_first) * full_rows, 8)

        def near_lines(row, rows):
            south = block_ref[pl.ds(south_top + row, rows)]
            north = block_ref[pl.ds(north_top + row, rows)]
            low = south_half[:rows]
            even = jnp.where(low, south, pltpu.roll(north, cy, 1))
            return even, jnp.where(low, pltpu.roll(south, LANES - cy, 1), north)

        put_block(from_owner(toward)[1], near_lines)

    def place_far(block_ref, toward, south_first):
        for place, distance in enumerate((3, 2)):
            top = 2 * place * small_rows
            south_at = pl.multiple_of(top + south_first * small_rows, 8)
            north_at = pl.multiple_of(top + (1 - south_first) * small_rows, 8)

            def far_lines(at, south_shift, north_shift, south_at=south_at, north_at=north_at):
                south = pltpu.roll(block_ref[pl.ds(south_at + at, group)], south_shift, 1)
                north = pltpu.roll(block_ref[pl.ds(north_at + at, group)], north_shift, 1)
                return jnp.where(south_half, south, north)

            put_distant(*from_owner(toward * distance), far_lines)

    def place_middle(got_ref, passed_ref):
        def middle_lines(at, south_shift, north_shift):
            row = 2 * full_rows + at
            mine_shift = jnp.where(south_is_own, south_shift, north_shift)
            other_shift = jnp.where(south_is_own, north_shift, south_shift)
            mine = pltpu.roll(got_ref[row : row + group], mine_shift, 1)
            theirs = pltpu.roll(passed_ref[row : row + group], other_shift, 1)
            return jnp.where(own_half, mine, theirs)

        put_distant(*from_owner(count_x // 2), middle_lines)

    return place_own, place_near, place_far, place_middle


def own_kernel(sizes, own_ref, other_ref, near_ref, z_ref, cor_ref):
    place_own, place_near = placer(*sizes, z_ref, cor_ref)[:2]
    index_y = lax.axis_index("ty")
    place_own(own_ref, other_ref)
    place_near(near_ref, 1 - 2 * index_y, index_y)


def got_kernel(sizes, near_ref, far_ref, passed_ref, z_in, cor_in, z_ref, cor_ref):
    _, place_near, place_far, place_middle = placer(*sizes, z_ref, cor_ref)
    index_y = lax.axis_index("ty")
    place_far(far_ref, 1 - 2 * index_y, index_y)
    place_near(passed_ref, 2 * index_y - 1, 1 - index_y)
    place_middle(near_ref, passed_ref)


def step_kernel(
    sizes, passed_ref, table_in, z_in, cor_in, out_hbm, z_ref, cor_ref,
    pred_ref, store_ref, tile_ref, flip_ref, speed_ref, table_ref, out_ref, sems,
):
    table_copy = pltpu.make_async_copy(table_in, table_ref, sems.at[0])
    table_copy.start()
    cx, cy, count_x = sizes[:3]
    levels = 4
    slots = 16
    cells = cx * count_x
    faces = store_ref.shape[0] // 4
    pairs = faces // 2
    group = pairs * levels
    chunk = cx * group
    index_x = lax.axis_index("tx")
    index_y = lax.axis_index("ty")

    def row_of(x):
        return (x + 4) * group

    def lanes_of(rows):
        return lax.broadcasted_iota(jnp.int32, (rows, LANES), 1)

    place_far = placer(*sizes, z_ref, cor_ref)[2]
    place_far(passed_ref, 2 * index_y - 1, 1 - index_y)

    table_copy.wait()
    level_of = lax.broadcasted_iota(jnp.int32, speed_ref.shape, 0) % levels
    speeds = jnp.full(speed_ref.shape, table_ref[0], jnp.float32)
    for index in range(1, levels):
        speeds = jnp.where(level_of == index, table_ref[index], speeds)
    speed_ref[...] = speeds

    lane_8 = lanes_of(8)
    place_8 = lane_8 % WINDOW
    gap = WINDOW - cells + 3
    wide = gap + 3 * levels
    row_tiles = range(0, cells, 8)
    rim_8 = ((place_8 >= MARGIN - 3) & (place_8 < MARGIN)) | (
        (place_8 >= MARGIN + cells) & (place_8 < MARGIN + cells + 3)
    )

    def collect():
        for pair in range(pairs):
            merged = [jnp.zeros((8, LANES), jnp.float32)] * len(row_tiles)
            for slot, field in ((0, 0), (1, 2)):
                for level in range(levels):
                    offset = slot * wide + 3 * level
                    here = place_8 - offset
                    wanted = ((here >= 0) & (here < 3)) | ((here >= gap) & (here < gap + 3))
                    shift = (offset - (MARGIN + cells - 3)) % LANES
                    lines = z_ref[field, pl.ds(row_of(0) + pair * levels + level, cells, group)]
                    lines = pltpu.roll(lines, shift, 1)
                    merged = [
                        jnp.where(wanted, lines[row : row + 8], old)
                        for row, old in zip(row_tiles, merged)
                    ]
            flip_ref[pair, :, :cells] = jnp.concatenate(merged, axis=0).T
            for slot in range(2):
                for side in (2, 3):
                    for odd in range(2):
                        for depth in range(3):
                            base = slot * wide
                            if side == 3:
                                base += odd * WINDOW + 2 - depth
                            else:
                                base += ((odd + 1) % 2) * WINDOW + gap + depth
                            at = slot * slots + depth * levels
                            store_ref[(2 * pair + odd) * 4 + side, at : at + levels] = flip_ref[
                                pair, pl.ds(base, levels, 3)
                            ]
            for slot in range(2):
                for side in (0, 1):
                    for depth in range(3):
                        x = depth if side == 0 else cells - 1 - depth
                        row = row_of(x) + pair * levels
                        lines = z_ref[slot, row : row + levels]
                        at = slot * slots + depth * levels
                        for odd in range(2):
                            store_ref[(2 * pair + odd) * 4 + side, at : at + levels] = lines

    def fetch(face, side, positions):
        at = levels + (face * 4 + side) * 3
        neighbour = table_ref[at].astype(jnp.int32)
        far_side = table_ref[at + 1].astype(jnp.int32)
        flipped = table_ref[at + 2].astype(jnp.int32)
        first = jnp.where(far_side < 2, MARGIN + WINDOW * (neighbour & 1), 0)
        start = first + jnp.where(flipped == 1, cells - 1, 0)
        step = 1 - 2 * flipped
        sign = ((1 - 2 * (side % 2)) * (2 * (far_side & 1) - 1)).astype(jnp.float32)
        index = neighbour * 4 + far_side
        parts = []
        for slot, position in enumerate(positions):
            order = (start + step * position) & (LANES - 1)
            for half_at in (0, 8):
                at = slot * slots + half_at
                lines = jnp.take_along_axis(store_ref[index, at : at + 8], order, axis=1)
                parts.append(lines if slot == 0 else sign * lines)
        return parts[:2], parts[2:]

    def depth_rows(parts, depth):
        at = (depth % 2) * levels
        return parts[depth // 2][at : at + levels]

    def rim_rows(side):
        left = lane_8 < WINDOW
        for pair in range(pairs):
            first = fetch(2 * pair, side, [lane_8 - MARGIN] * 2)
            second = fetch(2 * pair + 1, side, [lane_8 - (MARGIN + WINDOW)] * 2)
            for slot in range(2):
                both = [jnp.where(left, a, b) for a, b in zip(first[slot], second[slot])]
                for depth in range(3):
                    x = -1 - depth if side == 0 else cells + depth
                    row = row_of(x) + pair * levels
                    z_ref[slot, row : row + levels] = depth_rows(both, depth)

    tile_wide = WINDOW - cells - 3 + 3 * levels

    def put_tile(tile, parts, odd, side, base=0):
        for depth in range(3):
            if side == 3:
                at = base + odd * WINDOW + depth
            else:
                at = base + ((odd + 1) % 2) * WINDOW + tile_wide - 3 * levels + 2 - depth
            tile_ref[tile, pl.ds(at, levels, 3)] = depth_rows(parts, depth)

    def rim_columns_all():
        for pair in range(pairs):
            for odd in range(2):
                for side in (2, 3):
                    for slot, parts in enumerate(fetch(2 * pair + odd, side, [lane_8] * 2)):
                        put_tile(pair, parts, odd, side, slot * tile_wide)
            turned = tile_ref[pair].T[:cells]
            for slot, field in ((0, 0), (1, 2)):
                for level in range(levels):
                    shift = (MARGIN + cells - slot * tile_wide - 3 * level) % LANES
                    rolled = pltpu.roll(turned, shift, 1)
                    at = pl.ds(row_of(0) + pair * levels + level, cells, group)
                    lines = z_ref[field, at]
                    lines = [
                        jnp.where(rim_8, rolled[row : row + 8], lines[row : row + 8])
                        for row in row_tiles
                    ]
                    z_ref[field, at] = jnp.concatenate(lines, axis=0)

    def rim_columns_own():
        for odd in range(2):
            for side in (2, 3):
                total = [jnp.zeros((8, LANES), jnp.float32)] * 2
                for pair in range(pairs):
                    places = [8 * pair, 8 * (pairs + pair)]
                    positions = [lane_8 + (index_x * cx - place) for place in places]
                    fetched = fetch(2 * pair + odd, side, positions)
                    for place, parts in zip(places, fetched):
                        here = (lane_8 >= place) & (lane_8 < place + 8)
                        total = [jnp.where(here, a, b) for a, b in zip(parts, total)]
                put_tile(0, total, odd, side)
        turned = tile_ref[0].T
        for slot, field in ((0, 0), (1, 2)):
            for pair in range(pairs):
                row = 8 * (slot * pairs + pair)
                for level in range(levels):
                    shift = (MARGIN + cells - 3 * level) % LANES
                    rolled = pltpu.roll(turned[row : row + 8], shift, 1)[:cx]
                    start = row_of(0) + index_x * chunk + pair * levels + level
                    at = pl.ds(start, cx, group)
                    z_ref[field, at] = jnp.where(rim_8[:cx], rolled, z_ref[field, at])

    def predict(at, rows):
        speed = speed_ref[:rows]
        ahead = z_ref[0, pl.ds(at + group, rows)]
        behind = z_ref[0, pl.ds(at - group, rows)]
        pred_ref[pl.ds(at, rows)] = z_ref[1, pl.ds(at, rows)] - speed * (0.5 * (ahead - behind))

    def update(at, rows):
        speed = speed_ref[:rows]
        height = z_ref[0, pl.ds(at, rows)]
        north_pred = z_ref[2, pl.ds(at, rows)] - speed * (
            0.5 * (pltpu.roll(height, LANES - 1, 1) - pltpu.roll(height, 1, 1))
        )
        east_pred = pred_ref[pl.ds(at, rows)]
        flux_east = 8.0 * (
            pred_ref[pl.ds(at + group, rows)] - pred_ref[pl.ds(at - group, rows)]
        ) - (pred_ref[pl.ds(at + 2 * group, rows)] - pred_ref[pl.ds(at - 2 * group, rows)])
        flux_north = 8.0 * (
            pltpu.roll(north_pred, LANES - 1, 1) - pltpu.roll(north_pred, 1, 1)
        ) - (pltpu.roll(north_pred, LANES - 2, 1) - pltpu.roll(north_pred, 2, 1))
        height = height - speed * ((flux_east + flux_north) * (1.0 / 12.0))
        turning = cor_ref[pl.ds(at - row_of(0), rows)]
        return height, east_pred + turning * north_pred, north_pred - turning * east_pred

    def all_faces():
        rim_rows(0)
        rim_rows(1)
        rim_columns_all()
        for first in range(-2, cells + 2, 4):
            predict(row_of(first), 4 * group)
        def update_part(index, carry):
            at = pl.multiple_of(row_of(0) + index * (2 * chunk), 8)
            for field, values in enumerate(update(at, 2 * chunk)):
                z_ref[field, pl.ds(at, 2 * chunk)] = values
            return carry

        lax.fori_loop(0, count_x // 2, update_part, 0)

    def own_rows():

        @pl.when(index_x == 0)
        def _():
            rim_rows(0)

        @pl.when(index_x == count_x - 1)
        def _():
            rim_rows(1)

        rim_columns_own()
        at = pl.multiple_of(row_of(0) + index_x * chunk, 8)
        predict(at - 2 * group, chunk + 4 * group)
        copies = []
        for field, values in enumerate(update(at, chunk)):
            for odd in range(2):
                shift = LANES - (MARGIN + odd * WINDOW) - index_y * cy
                rolled = pltpu.roll(values, shift, 1)
                for x in range(cx):
                    for pair in range(pairs):
                        row = x * group + pair * levels
                        out_ref[field, 2 * pair + odd, x] = rolled[row : row + levels, :cy]
            copy = pltpu.make_async_copy(out_ref.at[field], out_hbm.at[:, field], sems.at[1 + field])
            copy.start()
            copies.append(copy)
        for copy in copies:
            copy.wait()

    def substep(index, carry):
        collect()
        pl.when(index == 0)(all_faces)
        pl.when(index == SUBSTEPS - 1)(own_rows)
        return carry

    lax.fori_loop(0, SUBSTEPS, substep, 0)


def fast_on_device(state, coriolis, wave_speed, edges):
    count_x = lax.axis_size("tx")
    faces, fields, levels, cx, cy = state.shape
    pairs = faces // 2
    group = pairs * levels
    cells = cx * count_x
    full_rows = fields * (cx // 2) * group + (cx // 2) * pairs
    full_rows = -(-full_rows // 8) * 8
    small_rows = unit_place(fields, 1, cx, group, 2 * cx)[0] + group
    in_vmem = pl.BlockSpec(memory_space=pltpu.VMEM)
    params = pltpu.CompilerParams(vmem_limit_bytes=SMALL_VMEM_LIMIT)
    swap_shape = jax.ShapeDtypeStruct((full_rows + 2 * small_rows, LANES), jnp.float32)
    swap = pl.pallas_call(
        functools.partial(pack_kernel, cx, cy, count_x, full_rows, small_rows),
        out_shape=swap_shape,
        in_specs=[in_vmem],
        out_specs=in_vmem,
        compiler_params=params,
        name="pack",
    )(jnp.swapaxes(state, 2, 3))
    swap, lines = pl.pallas_call(
        functools.partial(pack_coriolis_kernel, cx, cy, count_x, full_rows, small_rows),
        out_shape=[swap_shape, jax.ShapeDtypeStruct((32, LANES), jnp.float32)],
        in_specs=[in_vmem] * 2,
        out_specs=[in_vmem] * 2,
        input_output_aliases={1: 0},
        compiler_params=params,
        name="pack_coriolis",
    )(coriolis, swap)
    keep, middle = pl.pallas_call(
        functools.partial(keep_kernel, cx, cy, count_x, small_rows),
        out_shape=[
            jax.ShapeDtypeStruct((2 * small_rows, LANES), jnp.float32),
            jax.ShapeDtypeStruct((small_rows, LANES), jnp.float32),
        ],
        in_specs=[pl.BlockSpec(memory_space=pltpu.VMEM)] * 2,
        out_specs=[pl.BlockSpec(memory_space=pltpu.VMEM)] * 2,
        compiler_params=pltpu.CompilerParams(vmem_limit_bytes=SMALL_VMEM_LIMIT),
        name="keep",
    )(swap, lines)

    def moved(block, distance):
        pairs_of = []
        for index in range(count_x):
            for core in range(2):
                target = (index + distance * (1 - 2 * core)) % count_x
                pairs_of.append((2 * index + core, 2 * target + core))
        return lax.ppermute(block, ("tx", "ty"), pairs_of)

    def across(block):
        return lax.ppermute(block, "ty", [(0, 1), (1, 0)])

    other = across(swap)
    messages = pl.pallas_call(
        functools.partial(mix_kernel, full_rows, small_rows),
        out_shape=[
            jax.ShapeDtypeStruct((rows, LANES), jnp.float32)
            for rows in (2 * full_rows, 2 * small_rows, 2 * small_rows, small_rows)
        ],
        in_specs=[in_vmem] * 4,
        out_specs=[in_vmem] * 4,
        compiler_params=params,
        name="messages",
    )(swap, other, keep, middle)
    near, third, second, fourth = [
        moved(block, distance) for block, distance in zip(messages, (1, 3, 2, count_x // 2))
    ]
    near = jnp.concatenate([near, fourth])
    far = jnp.concatenate([third, second])
    table = jnp.concatenate([wave_speed, edges.reshape(-1).astype(jnp.float32)])
    far, table = lax.optimization_barrier((far, table))
    near_passed = across(near)
    far_passed = across(far)

    sizes = (cx, cy, count_x, full_rows, small_rows)
    state_rows = [
        jax.ShapeDtypeStruct((fields, (cells + 8) * group, LANES), jnp.float32),
        jax.ShapeDtypeStruct((cells * group, LANES), jnp.float32),
    ]
    rows = pl.pallas_call(
        functools.partial(own_kernel, sizes),
        out_shape=state_rows,
        in_specs=[in_vmem] * 3,
        out_specs=[in_vmem] * 2,
        compiler_params=params,
        name="place_own",
    )(swap, other, near)
    rows = pl.pallas_call(
        functools.partial(got_kernel, sizes),
        out_shape=state_rows,
        in_specs=[in_vmem] * 5,
        out_specs=[in_vmem] * 2,
        input_output_aliases={3: 0, 4: 1},
        compiler_params=params,
        name="place_got",
    )(near, far, near_passed, *rows)
    out, _, _ = pl.pallas_call(
        functools.partial(step_kernel, sizes),
        out_shape=[jax.ShapeDtypeStruct((faces, fields, cx, levels, cy), jnp.float32)]
        + state_rows,
        in_specs=[in_vmem] * 4,
        out_specs=[pl.BlockSpec(memory_space=pltpu.HBM)] + [in_vmem] * 2,
        input_output_aliases={2: 1, 3: 2},
        scratch_shapes=[
            pltpu.VMEM(((cells + 8) * group, LANES), jnp.float32),
            pltpu.VMEM((faces * 4, 32, LANES), jnp.float32),
            pltpu.VMEM((pairs, LANES, LANES), jnp.float32),
            pltpu.VMEM((pairs, LANES, LANES), jnp.float32),
            pltpu.VMEM((2 * cx * group, LANES), jnp.float32),
            pltpu.SMEM(table.shape, jnp.float32),
            pltpu.VMEM((fields, faces, cx, levels, cy), jnp.float32),
            pltpu.SemaphoreType.DMA((1 + fields,)),
        ],
        compiler_params=pltpu.CompilerParams(vmem_limit_bytes=VMEM_LIMIT),
        name="substeps",
    )(far_passed, table, *rows)
    return jnp.swapaxes(out, 2, 3)


def padded_2(block, sides, width):
    for axis, dim in sides:
        count = lax.axis_size(axis)
        forward = [(i, i + 1) for i in range(count - 1)]
        backward = [(target, source) for source, target in forward]
        low = lax.ppermute(
            lax.slice_in_dim(block, block.shape[dim] - width, None, axis=dim), axis, forward
        )
        high = lax.ppermute(lax.slice_in_dim(block, 0, width, axis=dim), axis, backward)
        block = jnp.concatenate([low, block, high], axis=dim)
    return block


def spread(block, axis, owner):
    block = jnp.where(lax.axis_index(axis) == owner, block, jnp.zeros_like(block))
    return lax.psum(block, axis)


def rotate_strip(strip_data, side_index, far_side, flipped):
    normal_part = jnp.where(far_side < 2, strip_data[1], strip_data[2])
    along_part = jnp.where(far_side < 2, strip_data[2], strip_data[1])
    sign_here = 2.0 * (side_index % 2) - 1.0
    sign_there = (2 * (far_side % 2) - 1).astype(jnp.float32)
    normal_part = -sign_here * sign_there * normal_part
    along_part = (1 - 2 * flipped).astype(jnp.float32) * along_part
    if side_index < 2:
        return jnp.stack([strip_data[0], normal_part, along_part])
    return jnp.stack([strip_data[0], along_part, normal_part])


def window_strip(store, side_pick, neighbour, flipped, start, width):
    full_length = store.shape[5]
    begin = jnp.where(flipped == 1, full_length - start - width, start)
    zero = jnp.zeros((), jnp.int32)
    sizes_here = (1, 1, store.shape[2], store.shape[3], store.shape[4], width)
    piece = lax.dynamic_slice(store, (side_pick, neighbour, zero, zero, zero, begin), sizes_here)[
        0, 0
    ]
    return jnp.where(flipped == 1, jnp.flip(piece, 3), piece)


def side_halo(edge_store, edges, face_index, side_index, start, width):
    neighbour = edges[face_index, side_index, 0]
    far_side = edges[face_index, side_index, 1]
    flipped = edges[face_index, side_index, 2]
    strip_data = window_strip(edge_store, far_side, neighbour, flipped, start, width)
    return rotate_strip(strip_data, side_index, far_side, flipped)


def advance(padded, wave_speed, coriolis_part, cells_x, cells_y):
    height = padded[..., 0, :, :, :]
    wind_east = padded[..., 1, :, :, :]
    wind_north = padded[..., 2, :, :, :]
    speed = wave_speed[:, None, None]
    east_pred = wind_east[..., 1 : cells_x + 5, 3 : cells_y + 3] - speed * (
        0.5
        * (
            height[..., 2 : cells_x + 6, 3 : cells_y + 3]
            - height[..., 0 : cells_x + 4, 3 : cells_y + 3]
        )
    )
    north_pred = wind_north[..., 3 : cells_x + 3, 1 : cells_y + 5] - speed * (
        0.5
        * (
            height[..., 3 : cells_x + 3, 2 : cells_y + 6]
            - height[..., 3 : cells_x + 3, 0 : cells_y + 4]
        )
    )
    flux_east = (
        8.0 * (east_pred[..., 3 : cells_x + 3, :] - east_pred[..., 1 : cells_x + 1, :])
        - (east_pred[..., 4 : cells_x + 4, :] - east_pred[..., 0:cells_x, :])
    ) / 12.0
    flux_north = (
        8.0 * (north_pred[..., 3 : cells_y + 3] - north_pred[..., 1 : cells_y + 1])
        - (north_pred[..., 4 : cells_y + 4] - north_pred[..., 0:cells_y])
    ) / 12.0
    height_new = height[..., 3 : cells_x + 3, 3 : cells_y + 3] - speed * (flux_east + flux_north)
    east_inner = east_pred[..., 2 : cells_x + 2, :]
    north_inner = north_pred[..., 2 : cells_y + 2]
    turning = coriolis_part[..., None, :, :]
    return jnp.stack(
        [height_new, east_inner + turning * north_inner, north_inner - turning * east_inner],
        axis=-4,
    )


def one_substep(state, coriolis, wave_speed, edges, count_x, count_y, index_x, index_y):
    faces = state.shape[0]
    cells_x = state.shape[3]
    cells_y = state.shape[4]
    padded = padded_2(state, (("tx", 3), ("ty", 4)), 3)
    west_rim = state[:, :, :, 0:3, :]
    east_rim = jnp.flip(state[:, :, :, cells_x - 3 :, :], 3)
    south_rim = jnp.swapaxes(state[:, :, :, :, 0:3], 3, 4)
    north_rim = jnp.swapaxes(jnp.flip(state[:, :, :, :, cells_y - 3 :], 4), 3, 4)
    west_part = spread(west_rim, "tx", 0)
    east_part = spread(east_rim, "tx", count_x - 1)
    west_full, east_full = (
        lax.all_gather(west_part, "ty", axis=4, tiled=True),
        lax.all_gather(east_part, "ty", axis=4, tiled=True),
    )
    south_row, north_row = (
        lax.all_gather(south_rim, "tx", axis=4, tiled=True),
        lax.all_gather(north_rim, "tx", axis=4, tiled=True),
    )
    south_all, north_all = (
        lax.all_gather(south_row, "ty", axis=0, tiled=True),
        lax.all_gather(north_row, "ty", axis=0, tiled=True),
    )
    south_full = south_all[0:faces]
    north_full = north_all[(count_y - 1) * faces : count_y * faces]
    edge_store = jnp.stack([west_full, east_full, south_full, north_full])
    halos = []
    for side_index in range(4):
        if side_index < 2:
            slabs = jnp.stack(
                [
                    side_halo(edge_store, edges, face_index, side_index, index_y * cells_y, cells_y)
                    for face_index in range(faces)
                ]
            )
        else:
            slabs = jnp.stack(
                [
                    side_halo(edge_store, edges, face_index, side_index, index_x * cells_x, cells_x)
                    for face_index in range(faces)
                ]
            )
        halos.append(slabs)
    west_region = padded[:, :, :, 0:3, 3 : cells_y + 3]
    padded = padded.at[:, :, :, 0:3, 3 : cells_y + 3].set(
        jnp.where(index_x == 0, jnp.flip(halos[0], 3), west_region)
    )
    east_region = padded[:, :, :, cells_x + 3 : cells_x + 6, 3 : cells_y + 3]
    padded = padded.at[:, :, :, cells_x + 3 : cells_x + 6, 3 : cells_y + 3].set(
        jnp.where(index_x == count_x - 1, halos[1], east_region)
    )
    south_region = padded[:, :, :, 3 : cells_x + 3, 0:3]
    padded = padded.at[:, :, :, 3 : cells_x + 3, 0:3].set(
        jnp.where(index_y == 0, jnp.swapaxes(jnp.flip(halos[2], 3), 3, 4), south_region)
    )
    north_region = padded[:, :, :, 3 : cells_x + 3, cells_y + 3 : cells_y + 6]
    padded = padded.at[:, :, :, 3 : cells_x + 3, cells_y + 3 : cells_y + 6].set(
        jnp.where(index_y == count_y - 1, jnp.swapaxes(halos[3], 3, 4), north_region)
    )
    return advance(padded, wave_speed, coriolis, cells_x, cells_y)


def on_device(state, coriolis, wave_speed, edges):
    count_x = lax.axis_size("tx")
    count_y = lax.axis_size("ty")
    index_x = lax.axis_index("tx")
    index_y = lax.axis_index("ty")
    for substep_index in range(SUBSTEPS):
        state = one_substep(state, coriolis, wave_speed, edges, count_x, count_y, index_x, index_y)
    return state


def fits(state):
    count_x = lax.axis_size("tx")
    faces, fields, levels, cells_x, cells_y = state.shape
    return (
        lax.axis_size("ty") == 2
        and faces % 2 == 0
        and levels == 4
        and cells_x == 6
        and cells_y == 24
        and count_x == 8
        and cells_x * count_x == 2 * cells_y
        and 2 * cells_y + 2 * MARGIN <= WINDOW
    )


def either(state, coriolis, wave_speed, edges):
    if fits(state):
        return fast_on_device(state, coriolis, wave_speed, edges)
    return on_device(state, coriolis, wave_speed, edges)


def solution(mesh):
    in_specs = (P("member", None, None, "tx", "ty"), P(None, "tx", "ty"), P(), P())
    out_specs = P("member", None, None, "tx", "ty")
    return jax.shard_map(
        either, mesh=mesh, in_specs=in_specs, out_specs=out_specs, check_vma=False
    )
```

```python
import functools

import jax
import jax.numpy as jnp
from jax import lax
from jax.experimental import pallas as pl
from jax.experimental.pallas import tpu as pltpu
from jax.sharding import PartitionSpec as P

SUBSTEPS = 2
LANES = 128
WINDOW = 64
MARGIN = 8
VMEM_LIMIT = 32 * 1024 * 1024
SMALL_VMEM_LIMIT = 8 * 1024 * 1024


def wrap(index, count):
    index = jnp.where(index < 0, index + count, index)
    return jnp.where(index >= count, index - count, index)


def lane_shift(amount):
    return amount & (LANES - 1)


def windows(source, target, count_x, index_y, cx, cy):
    spare = cy - 2 * cx
    near = jnp.minimum(target, count_x - 1 - target)
    rim = (source == 0) | (source == count_x - 1)
    starts = []
    for inward in (cx // 2, cx):
        start = jnp.maximum(jnp.minimum(cx * near - inward, spare), 0)
        start = jnp.where(rim, start, 0)
        starts.append(jnp.where(index_y == 0, start, spare - start))
    close, far = starts
    upside = source == count_x - 1
    return jnp.where(upside, far, close), jnp.where(upside, close, far)


def unit_place(field, x, cx, group, width):
    per_row = 60 // width
    index = field * cx + x
    return (index // per_row) * group, (index % per_row) * width


def chunk_targets(count_x, full_rows, small_rows):
    sense = 1 - 2 * lax.axis_index("ty")
    return [
        (full_rows + place * small_rows, -sense * distance)
        for place, distance in enumerate((2, 3))
    ]


def put_chunk(cx, cy, count_x, block_ref, line_ref, out_ref, top, offset):
    pairs = 3
    group = 4 * pairs
    fields = 3
    half = cx // 2
    width = 2 * cx
    index_x = lax.axis_index("tx")
    target = wrap(index_x + offset, count_x)
    starts = windows(index_x, target, count_x, lax.axis_index("ty"), cx, cy)
    position = lax.broadcasted_iota(jnp.int32, (group, LANES), 1) % WINDOW
    from_lane = {lane: position >= lane for lane in range(0, 60, width)}
    blocks = {}

    def put(row, lane, lines):
        blocks[row] = lines if row not in blocks else jnp.where(from_lane[lane], lines, blocks[row])

    if block_ref is not None:
        for field in range(fields):
            for x in range(cx):
                row = field * half * group + (x // 2) * group
                at, lane = unit_place(field, x, cx, group, width)
                shift = lane_shift(lane - MARGIN - (x % 2) * cy - starts[x // half])
                put(at, lane, pltpu.roll(block_ref[row : row + group], shift, 1))
    else:
        at = unit_place(fields, 0, cx, group, width)[0]
        blocks[at] = out_ref[top + at : top + at + group]
    if line_ref is not None:
        for part in range(2):
            at, lane = unit_place(fields, part, cx, group, width)
            shift = lane_shift(lane - MARGIN - starts[part])
            put(at, lane, pltpu.roll(line_ref[16 * part : 16 * part + group], shift, 1))
    for row, lines in blocks.items():
        out_ref[top + row : top + row + group] = lines


def pack_kernel(cx, cy, count_x, full_rows, small_rows, state_ref, swap_ref):
    faces, fields = state_ref.shape[:2]
    levels = state_ref.shape[3]
    group = (faces // 2) * levels
    half = cx // 2
    swap_ref[:full_rows] = jnp.zeros((full_rows, LANES), jnp.float32)
    for face in range(faces):
        for parity in range(2):
            lane = (face % 2) * WINDOW + MARGIN + parity * cy
            for xp in range(half):
                for field in range(fields):
                    row = field * half * group + xp * group + (face // 2) * levels
                    swap_ref[row : row + levels, lane : lane + cy] = state_ref[
                        face, field, 2 * xp + parity
                    ]
    for top, offset in chunk_targets(count_x, full_rows, small_rows):
        put_chunk(cx, cy, count_x, swap_ref, None, swap_ref, top, offset)


def pack_coriolis_kernel(
    cx, cy, count_x, full_rows, small_rows, coriolis_ref, swap_in, swap_ref, line_ref
):
    faces = coriolis_ref.shape[0]
    pairs = faces // 2
    half = cx // 2
    base = 3 * half * 4 * pairs
    line_ref[...] = jnp.zeros(line_ref.shape, jnp.float32)
    for face in range(faces):
        lane = (face % 2) * WINDOW + MARGIN
        for x in range(cx):
            line = coriolis_ref[face, x : x + 1]
            row = base + (x // 2) * pairs + face // 2
            at = lane + (x % 2) * cy
            swap_ref[row : row + 1, at : at + cy] = line
            row = (x // half) * 16 + (x % half) * pairs + face // 2
            line_ref[row : row + 1, lane : lane + cy] = line
    for top, offset in chunk_targets(count_x, full_rows, small_rows):
        put_chunk(cx, cy, count_x, None, line_ref, swap_ref, top, offset)


def keep_kernel(cx, cy, count_x, small_rows, swap_ref, line_ref, keep_ref, middle_ref):
    sense = 1 - 2 * lax.axis_index("ty")
    put_chunk(cx, cy, count_x, swap_ref, line_ref, middle_ref, 0, count_x // 2)
    for place, distance in enumerate((2, 3)):
        top = place * small_rows
        put_chunk(cx, cy, count_x, swap_ref, line_ref, keep_ref, top, sense * distance)


def mix_kernel(
    full_rows, small_rows, swap_ref, other_ref, keep_ref, middle_ref,
    near_ref, third_ref, second_ref, fourth_ref,
):
    near_ref[:full_rows] = swap_ref[:full_rows]
    near_ref[full_rows:] = other_ref[:full_rows]
    for place, far_ref in enumerate((second_ref, third_ref)):
        at = place * small_rows
        far_ref[:small_rows] = keep_ref[at : at + small_rows]
        at += full_rows
        far_ref[small_rows:] = other_ref[at : at + small_rows]
    fourth_ref[...] = middle_ref[...]


def placer(cx, cy, count_x, full_rows, small_rows, z_ref, cor_ref):
    fields = z_ref.shape[0]
    levels = 4
    group = z_ref.shape[1] // (cx * count_x + 8)
    pairs = group // levels
    half = cx // 2
    chunk = cx * group
    index_x = lax.axis_index("tx")
    index_y = lax.axis_index("ty")
    south_half = lax.broadcasted_iota(jnp.int32, (group, LANES), 1) % WINDOW < MARGIN + cy
    south_is_own = index_y == 0
    own_half = south_half == south_is_own

    def row_of(x):
        return (x + 4) * group

    def from_owner(offset):
        source = wrap(index_x - offset, count_x)
        return source, pl.multiple_of(source * chunk, 8)

    def put_coriolis(start, x, values, at):
        for pair in range(pairs):
            line = values[at + pair : at + pair + 1]
            rows = pl.ds(start + x * group + pair * levels, levels)
            cor_ref[rows] = jnp.broadcast_to(line, (levels, LANES))

    def put_block(start, lines_of):
        base = fields * half * group
        for field in range(fields):
            for xp in range(half):
                even, odd = lines_of(field * half * group + xp * group, group)
                z_ref[field, pl.ds(start + row_of(2 * xp), group)] = even
                z_ref[field, pl.ds(start + row_of(2 * xp + 1), group)] = odd
        for parity, values in enumerate(lines_of(base, half * pairs)):
            for xp in range(half):
                put_coriolis(start, 2 * xp + parity, values, xp * pairs)

    def put_distant(source, start, lines_of):
        starts_south = windows(source, index_x, count_x, 0, cx, cy)
        starts_north = [cy - 2 * cx - start for start in starts_south]
        is_rim = (source == 0) | (source == count_x - 1)
        starts_north = [jnp.where(is_rim, start, cy - 2 * cx) for start in starts_north]
        shifts = {
            (part, lane): (
                lane_shift(MARGIN + starts_south[part] - lane),
                lane_shift(MARGIN + cy + starts_north[part] - lane),
            )
            for part in range(2)
            for lane in range(0, 60, 2 * cx)
        }

        def lines_at(field, x, part):
            at, lane = unit_place(field, x, cx, group, 2 * cx)
            return lines_of(at, *shifts[part, lane])

        for field in range(fields):
            for x in range(cx):
                z_ref[field, pl.ds(start + row_of(x), group)] = lines_at(field, x, x // half)
        for part in range(2):
            values = lines_at(fields, part, part)
            for x in range(half):
                put_coriolis(start, part * half + x, values, x * pairs)

    def place_own(own_ref, other_ref):
        def own_lines(row, rows):
            mine = own_ref[row : row + rows]
            theirs = other_ref[row : row + rows]
            up, down = index_y * cy, (1 - index_y) * cy
            keep = own_half[:rows]
            even = jnp.where(keep, pltpu.roll(mine, up, 1), pltpu.roll(theirs, down, 1))
            mine = pltpu.roll(mine, lane_shift(-down), 1)
            theirs = pltpu.roll(theirs, lane_shift(-up), 1)
            return even, jnp.where(keep, mine, theirs)

        put_block(from_owner(0)[1], own_lines)

    def place_near(block_ref, toward, south_first):
        south_top = pl.multiple_of(south_first * full_rows, 8)
        north_top = pl.multiple_of((1 - south_first) * full_rows, 8)

        def near_lines(row, rows):
            south = block_ref[pl.ds(south_top + row, rows)]
            north = block_ref[pl.ds(north_top + row, rows)]
            low = south_half[:rows]
            even = jnp.where(low, south, pltpu.roll(north, cy, 1))
            return even, jnp.where(low, pltpu.roll(south, LANES - cy, 1), north)

        put_block(from_owner(toward)[1], near_lines)

    def place_far(block_ref, toward, south_first):
        for place, distance in enumerate((3, 2)):
            top = 2 * place * small_rows
            south_at = pl.multiple_of(top + south_first * small_rows, 8)
            north_at = pl.multiple_of(top + (1 - south_first) * small_rows, 8)

            def far_lines(at, south_shift, north_shift, south_at=south_at, north_at=north_at):
                south = pltpu.roll(block_ref[pl.ds(south_at + at, group)], south_shift, 1)
                north = pltpu.roll(block_ref[pl.ds(north_at + at, group)], north_shift, 1)
                return jnp.where(south_half, south, north)

            put_distant(*from_owner(toward * distance), far_lines)

    def place_middle(got_ref, passed_ref):
        def middle_lines(at, south_shift, north_shift):
            row = 4 * small_rows + at
            mine_shift = jnp.where(south_is_own, south_shift, north_shift)
            other_shift = jnp.where(south_is_own, north_shift, south_shift)
            mine = pltpu.roll(got_ref[row : row + group], mine_shift, 1)
            theirs = pltpu.roll(passed_ref[row : row + group], other_shift, 1)
            return jnp.where(own_half, mine, theirs)

        put_distant(*from_owner(count_x // 2), middle_lines)

    return place_own, place_near, place_far, place_middle


def own_kernel(sizes, own_ref, other_ref, near_ref, z_ref, cor_ref):
    z_ref[...] = jnp.zeros(z_ref.shape, jnp.float32)
    cor_ref[...] = jnp.zeros(cor_ref.shape, jnp.float32)
    place_own, place_near = placer(*sizes, z_ref, cor_ref)[:2]
    index_y = lax.axis_index("ty")
    place_own(own_ref, other_ref)
    place_near(near_ref, 1 - 2 * index_y, index_y)


def got_kernel(sizes, far_ref, passed_ref, z_in, cor_in, z_ref, cor_ref):
    _, place_near, place_far, _ = placer(*sizes, z_ref, cor_ref)
    index_y = lax.axis_index("ty")
    place_far(far_ref, 1 - 2 * index_y, index_y)
    place_near(passed_ref, 2 * index_y - 1, 1 - index_y)


def step_kernel(
    sizes, far_ref, passed_ref, table_in, z_in, cor_in, out_hbm, z_ref, cor_ref,
    pred_ref, store_ref, tile_ref, flip_ref, speed_ref, table_ref, out_ref, sems,
):
    table_copy = pltpu.make_async_copy(table_in, table_ref, sems.at[0])
    table_copy.start()
    cx, cy, count_x = sizes[:3]
    levels = 4
    slots = 16
    cells = cx * count_x
    faces = store_ref.shape[0] // 4
    pairs = faces // 2
    group = pairs * levels
    chunk = cx * group
    index_x = lax.axis_index("tx")
    index_y = lax.axis_index("ty")

    def row_of(x):
        return (x + 4) * group

    def lanes_of(rows):
        return lax.broadcasted_iota(jnp.int32, (rows, LANES), 1)

    place_far, place_middle = placer(*sizes, z_ref, cor_ref)[2:]
    place_far(passed_ref, 2 * index_y - 1, 1 - index_y)
    place_middle(far_ref, passed_ref)

    table_copy.wait()
    level_of = lax.broadcasted_iota(jnp.int32, speed_ref.shape, 0) % levels
    speeds = jnp.full(speed_ref.shape, table_ref[0], jnp.float32)
    for index in range(1, levels):
        speeds = jnp.where(level_of == index, table_ref[index], speeds)
    speed_ref[...] = speeds

    lane_8 = lanes_of(8)
    place_8 = lane_8 % WINDOW
    gap = WINDOW - cells + 3
    wide = gap + 3 * levels
    row_tiles = range(0, cells, 8)
    rim_8 = ((place_8 >= MARGIN - 3) & (place_8 < MARGIN)) | (
        (place_8 >= MARGIN + cells) & (place_8 < MARGIN + cells + 3)
    )

    def collect():
        for pair in range(pairs):
            merged = [jnp.zeros((8, LANES), jnp.float32)] * len(row_tiles)
            for slot, field in ((0, 0), (1, 2)):
                for level in range(levels):
                    offset = slot * wide + 3 * level
                    here = place_8 - offset
                    wanted = ((here >= 0) & (here < 3)) | ((here >= gap) & (here < gap + 3))
                    shift = (offset - (MARGIN + cells - 3)) % LANES
                    lines = z_ref[field, pl.ds(row_of(0) + pair * levels + level, cells, group)]
                    lines = pltpu.roll(lines, shift, 1)
                    merged = [
                        jnp.where(wanted, lines[row : row + 8], old)
                        for row, old in zip(row_tiles, merged)
                    ]
            flip_ref[pair, :, :cells] = jnp.concatenate(merged, axis=0).T
            for slot in range(2):
                for side in (2, 3):
                    for odd in range(2):
                        for depth in range(3):
                            base = slot * wide
                            if side == 3:
                                base += odd * WINDOW + 2 - depth
                            else:
                                base += ((odd + 1) % 2) * WINDOW + gap + depth
                            at = slot * slots + depth * levels
                            store_ref[(2 * pair + odd) * 4 + side, at : at + levels] = flip_ref[
                                pair, pl.ds(base, levels, 3)
                            ]
            for slot in range(2):
                for side in (0, 1):
                    for depth in range(3):
                        x = depth if side == 0 else cells - 1 - depth
                        row = row_of(x) + pair * levels
                        lines = z_ref[slot, row : row + levels]
                        at = slot * slots + depth * levels
                        for odd in range(2):
                            store_ref[(2 * pair + odd) * 4 + side, at : at + levels] = lines

    def fetch(face, side, positions):
        at = levels + (face * 4 + side) * 3
        neighbour = table_ref[at].astype(jnp.int32)
        far_side = table_ref[at + 1].astype(jnp.int32)
        flipped = table_ref[at + 2].astype(jnp.int32)
        first = jnp.where(far_side < 2, MARGIN + WINDOW * (neighbour & 1), 0)
        start = first + jnp.where(flipped == 1, cells - 1, 0)
        step = 1 - 2 * flipped
        sign = ((1 - 2 * (side % 2)) * (2 * (far_side & 1) - 1)).astype(jnp.float32)
        index = neighbour * 4 + far_side
        parts = []
        for slot, position in enumerate(positions):
            order = (start + step * position) & (LANES - 1)
            for half_at in (0, 8):
                at = slot * slots + half_at
                lines = jnp.take_along_axis(store_ref[index, at : at + 8], order, axis=1)
                parts.append(lines if slot == 0 else sign * lines)
        return parts[:2], parts[2:]

    def depth_rows(parts, depth):
        at = (depth % 2) * levels
        return parts[depth // 2][at : at + levels]

    def rim_rows(side):
        left = lane_8 < WINDOW
        cells_8 = (place_8 >= MARGIN) & (place_8 < MARGIN + cells)
        for pair in range(pairs):
            first = fetch(2 * pair, side, [lane_8 - MARGIN] * 2)
            second = fetch(2 * pair + 1, side, [lane_8 - (MARGIN + WINDOW)] * 2)
            for slot in range(2):
                both = [jnp.where(left, a, b) for a, b in zip(first[slot], second[slot])]
                both = [jnp.where(cells_8, lines, 0.0) for lines in both]
                for depth in range(3):
                    x = -1 - depth if side == 0 else cells + depth
                    row = row_of(x) + pair * levels
                    z_ref[slot, row : row + levels] = depth_rows(both, depth)

    tile_wide = WINDOW - cells - 3 + 3 * levels

    def put_tile(tile, parts, odd, side, base=0):
        for depth in range(3):
            if side == 3:
                at = base + odd * WINDOW + depth
            else:
                at = base + ((odd + 1) % 2) * WINDOW + tile_wide - 3 * levels + 2 - depth
            tile_ref[tile, pl.ds(at, levels, 3)] = depth_rows(parts, depth)

    def rim_columns_all():
        for pair in range(pairs):
            for odd in range(2):
                for side in (2, 3):
                    for slot, parts in enumerate(fetch(2 * pair + odd, side, [lane_8] * 2)):
                        put_tile(pair, parts, odd, side, slot * tile_wide)
            turned = tile_ref[pair].T[:cells]
            for slot, field in ((0, 0), (1, 2)):
                for level in range(levels):
                    shift = (MARGIN + cells - slot * tile_wide - 3 * level) % LANES
                    rolled = pltpu.roll(turned, shift, 1)
                    at = pl.ds(row_of(0) + pair * levels + level, cells, group)
                    lines = z_ref[field, at]
                    lines = [
                        jnp.where(rim_8, rolled[row : row + 8], lines[row : row + 8])
                        for row in row_tiles
                    ]
                    z_ref[field, at] = jnp.concatenate(lines, axis=0)

    def rim_columns_own():
        for odd in range(2):
            for side in (2, 3):
                total = [jnp.zeros((8, LANES), jnp.float32)] * 2
                for pair in range(pairs):
                    places = [8 * pair, 8 * (pairs + pair)]
                    positions = [lane_8 + (index_x * cx - place) for place in places]
                    fetched = fetch(2 * pair + odd, side, positions)
                    for place, parts in zip(places, fetched):
                        here = (lane_8 >= place) & (lane_8 < place + 8)
                        total = [jnp.where(here, a, b) for a, b in zip(parts, total)]
                put_tile(0, total, odd, side)
        turned = tile_ref[0].T
        for slot, field in ((0, 0), (1, 2)):
            for pair in range(pairs):
                row = 8 * (slot * pairs + pair)
                for level in range(levels):
                    shift = (MARGIN + cells - 3 * level) % LANES
                    rolled = pltpu.roll(turned[row : row + 8], shift, 1)[:cx]
                    start = row_of(0) + index_x * chunk + pair * levels + level
                    at = pl.ds(start, cx, group)
                    z_ref[field, at] = jnp.where(rim_8[:cx], rolled, z_ref[field, at])

    def predict(at, rows):
        speed = speed_ref[:rows]
        ahead = z_ref[0, pl.ds(at + group, rows)]
        behind = z_ref[0, pl.ds(at - group, rows)]
        pred_ref[pl.ds(at, rows)] = z_ref[1, pl.ds(at, rows)] - speed * (0.5 * (ahead - behind))

    ahead_by = lax.broadcasted_iota(jnp.int32, (LANES, LANES), 0) - lanes_of(LANES)

    def band(entries):
        matrix = jnp.zeros((LANES, LANES), jnp.float32)
        for offset, value in entries:
            matrix = jnp.where(ahead_by == offset, value, matrix)
        return matrix

    slope = band(((1, 0.5), (-1, -0.5)))
    flux = band(((1, 8.0), (-1, -8.0), (2, -1.0), (-2, 1.0)))

    def times(values, matrix):
        return jnp.dot(
            values, matrix, precision=lax.Precision.HIGHEST, preferred_element_type=jnp.float32
        )

    def update(at, rows):
        speed = speed_ref[:rows]
        height = z_ref[0, pl.ds(at, rows)]
        north_pred = z_ref[2, pl.ds(at, rows)] - speed * times(height, slope)
        east_pred = pred_ref[pl.ds(at, rows)]
        flux_east = 8.0 * (
            pred_ref[pl.ds(at + group, rows)] - pred_ref[pl.ds(at - group, rows)]
        ) - (pred_ref[pl.ds(at + 2 * group, rows)] - pred_ref[pl.ds(at - 2 * group, rows)])
        flux_north = times(north_pred, flux)
        height = height - speed * ((flux_east + flux_north) * (1.0 / 12.0))
        turning = cor_ref[pl.ds(at - row_of(0), rows)]
        return height, east_pred + turning * north_pred, north_pred - turning * east_pred

    def all_faces():
        rim_rows(0)
        rim_rows(1)
        rim_columns_all()
        for first in range(-2, cells + 2, 4):
            predict(row_of(first), 4 * group)
        def update_part(index, carry):
            at = pl.multiple_of(row_of(0) + index * (2 * chunk), 8)
            for field, values in enumerate(update(at, 2 * chunk)):
                z_ref[field, pl.ds(at, 2 * chunk)] = values
            return carry

        lax.fori_loop(0, count_x // 2, update_part, 0)

    def own_rows():

        @pl.when(index_x == 0)
        def _():
            rim_rows(0)

        @pl.when(index_x == count_x - 1)
        def _():
            rim_rows(1)

        rim_columns_own()
        at = pl.multiple_of(row_of(0) + index_x * chunk, 8)
        predict(at - 2 * group, chunk + 4 * group)
        copies = []
        for field, values in enumerate(update(at, chunk)):
            for odd in range(2):
                shift = LANES - (MARGIN + odd * WINDOW) - index_y * cy
                rolled = pltpu.roll(values, shift, 1)
                for x in range(cx):
                    for pair in range(pairs):
                        row = x * group + pair * levels
                        out_ref[field, 2 * pair + odd, x] = rolled[row : row + levels, :cy]
            copy = pltpu.make_async_copy(out_ref.at[field], out_hbm.at[:, field], sems.at[1 + field])
            copy.start()
            copies.append(copy)
        for copy in copies:
            copy.wait()

    def substep(index, carry):
        collect()
        pl.when(index == 0)(all_faces)
        pl.when(index == SUBSTEPS - 1)(own_rows)
        return carry

    lax.fori_loop(0, SUBSTEPS, substep, 0)


def fast_on_device(state, coriolis, wave_speed, edges):
    count_x = lax.axis_size("tx")
    faces, fields, levels, cx, cy = state.shape
    pairs = faces // 2
    group = pairs * levels
    cells = cx * count_x
    full_rows = fields * (cx // 2) * group + (cx // 2) * pairs
    full_rows = -(-full_rows // 8) * 8
    small_rows = unit_place(fields, 1, cx, group, 2 * cx)[0] + group
    in_vmem = pl.BlockSpec(memory_space=pltpu.VMEM)
    params = pltpu.CompilerParams(vmem_limit_bytes=SMALL_VMEM_LIMIT)
    swap_shape = jax.ShapeDtypeStruct((full_rows + 2 * small_rows, LANES), jnp.float32)
    swap = pl.pallas_call(
        functools.partial(pack_kernel, cx, cy, count_x, full_rows, small_rows),
        out_shape=swap_shape,
        in_specs=[in_vmem],
        out_specs=in_vmem,
        compiler_params=params,
        name="pack",
    )(jnp.swapaxes(state, 2, 3))
    swap, lines = pl.pallas_call(
        functools.partial(pack_coriolis_kernel, cx, cy, count_x, full_rows, small_rows),
        out_shape=[swap_shape, jax.ShapeDtypeStruct((32, LANES), jnp.float32)],
        in_specs=[in_vmem] * 2,
        out_specs=[in_vmem] * 2,
        input_output_aliases={1: 0},
        compiler_params=params,
        name="pack_coriolis",
    )(coriolis, swap)
    keep, middle = pl.pallas_call(
        functools.partial(keep_kernel, cx, cy, count_x, small_rows),
        out_shape=[
            jax.ShapeDtypeStruct((2 * small_rows, LANES), jnp.float32),
            jax.ShapeDtypeStruct((small_rows, LANES), jnp.float32),
        ],
        in_specs=[pl.BlockSpec(memory_space=pltpu.VMEM)] * 2,
        out_specs=[pl.BlockSpec(memory_space=pltpu.VMEM)] * 2,
        compiler_params=pltpu.CompilerParams(vmem_limit_bytes=SMALL_VMEM_LIMIT),
        name="keep",
    )(swap, lines)

    def moved(block, distance):
        pairs_of = []
        for index in range(count_x):
            for core in range(2):
                target = (index + distance * (1 - 2 * core)) % count_x
                pairs_of.append((2 * index + core, 2 * target + core))
        return lax.ppermute(block, ("tx", "ty"), pairs_of)

    def across(block):
        return lax.ppermute(block, "ty", [(0, 1), (1, 0)])

    other = across(swap)
    messages = pl.pallas_call(
        functools.partial(mix_kernel, full_rows, small_rows),
        out_shape=[
            jax.ShapeDtypeStruct((rows, LANES), jnp.float32)
            for rows in (2 * full_rows, 2 * small_rows, 2 * small_rows, small_rows)
        ],
        in_specs=[in_vmem] * 4,
        out_specs=[in_vmem] * 4,
        compiler_params=params,
        name="messages",
    )(swap, other, keep, middle)
    near, third, second, fourth = [
        moved(block, distance) for block, distance in zip(messages, (1, 3, 2, count_x // 2))
    ]
    near, fourth = lax.optimization_barrier((near, fourth))
    far = jnp.concatenate([third, second, fourth])
    table = jnp.concatenate([wave_speed, edges.reshape(-1).astype(jnp.float32)])
    far, table = lax.optimization_barrier((far, table))
    near_passed = across(near)
    far_passed = across(far)

    sizes = (cx, cy, count_x, full_rows, small_rows)
    state_rows = [
        jax.ShapeDtypeStruct((fields, (cells + 8) * group, LANES), jnp.float32),
        jax.ShapeDtypeStruct((cells * group, LANES), jnp.float32),
    ]
    rows = pl.pallas_call(
        functools.partial(own_kernel, sizes),
        out_shape=state_rows,
        in_specs=[in_vmem] * 3,
        out_specs=[in_vmem] * 2,
        compiler_params=params,
        name="place_own",
    )(swap, other, near)
    rows = pl.pallas_call(
        functools.partial(got_kernel, sizes),
        out_shape=state_rows,
        in_specs=[in_vmem] * 4,
        out_specs=[in_vmem] * 2,
        input_output_aliases={2: 0, 3: 1},
        compiler_params=params,
        name="place_got",
    )(far, near_passed, *rows)
    out, _, _ = pl.pallas_call(
        functools.partial(step_kernel, sizes),
        out_shape=[jax.ShapeDtypeStruct((faces, fields, cx, levels, cy), jnp.float32)]
        + state_rows,
        in_specs=[in_vmem] * 5,
        out_specs=[pl.BlockSpec(memory_space=pltpu.HBM)] + [in_vmem] * 2,
        input_output_aliases={3: 1, 4: 2},
        scratch_shapes=[
            pltpu.VMEM(((cells + 8) * group, LANES), jnp.float32),
            pltpu.VMEM((faces * 4, 32, LANES), jnp.float32),
            pltpu.VMEM((pairs, LANES, LANES), jnp.float32),
            pltpu.VMEM((pairs, LANES, LANES), jnp.float32),
            pltpu.VMEM((2 * cx * group, LANES), jnp.float32),
            pltpu.SMEM(table.shape, jnp.float32),
            pltpu.VMEM((fields, faces, cx, levels, cy), jnp.float32),
            pltpu.SemaphoreType.DMA((1 + fields,)),
        ],
        compiler_params=pltpu.CompilerParams(vmem_limit_bytes=VMEM_LIMIT),
        name="substeps",
    )(far, far_passed, table, *rows)
    return jnp.swapaxes(out, 2, 3)


def padded_2(block, sides, width):
    for axis, dim in sides:
        count = lax.axis_size(axis)
        forward = [(i, i + 1) for i in range(count - 1)]
        backward = [(target, source) for source, target in forward]
        low = lax.ppermute(
            lax.slice_in_dim(block, block.shape[dim] - width, None, axis=dim), axis, forward
        )
        high = lax.ppermute(lax.slice_in_dim(block, 0, width, axis=dim), axis, backward)
        block = jnp.concatenate([low, block, high], axis=dim)
    return block


def spread(block, axis, owner):
    block = jnp.where(lax.axis_index(axis) == owner, block, jnp.zeros_like(block))
    return lax.psum(block, axis)


def rotate_strip(strip_data, side_index, far_side, flipped):
    normal_part = jnp.where(far_side < 2, strip_data[1], strip_data[2])
    along_part = jnp.where(far_side < 2, strip_data[2], strip_data[1])
    sign_here = 2.0 * (side_index % 2) - 1.0
    sign_there = (2 * (far_side % 2) - 1).astype(jnp.float32)
    normal_part = -sign_here * sign_there * normal_part
    along_part = (1 - 2 * flipped).astype(jnp.float32) * along_part
    if side_index < 2:
        return jnp.stack([strip_data[0], normal_part, along_part])
    return jnp.stack([strip_data[0], along_part, normal_part])


def window_strip(store, side_pick, neighbour, flipped, start, width):
    full_length = store.shape[5]
    begin = jnp.where(flipped == 1, full_length - start - width, start)
    zero = jnp.zeros((), jnp.int32)
    sizes_here = (1, 1, store.shape[2], store.shape[3], store.shape[4], width)
    piece = lax.dynamic_slice(store, (side_pick, neighbour, zero, zero, zero, begin), sizes_here)[
        0, 0
    ]
    return jnp.where(flipped == 1, jnp.flip(piece, 3), piece)


def side_halo(edge_store, edges, face_index, side_index, start, width):
    neighbour = edges[face_index, side_index, 0]
    far_side = edges[face_index, side_index, 1]
    flipped = edges[face_index, side_index, 2]
    strip_data = window_strip(edge_store, far_side, neighbour, flipped, start, width)
    return rotate_strip(strip_data, side_index, far_side, flipped)


def advance(padded, wave_speed, coriolis_part, cells_x, cells_y):
    height = padded[..., 0, :, :, :]
    wind_east = padded[..., 1, :, :, :]
    wind_north = padded[..., 2, :, :, :]
    speed = wave_speed[:, None, None]
    east_pred = wind_east[..., 1 : cells_x + 5, 3 : cells_y + 3] - speed * (
        0.5
        * (
            height[..., 2 : cells_x + 6, 3 : cells_y + 3]
            - height[..., 0 : cells_x + 4, 3 : cells_y + 3]
        )
    )
    north_pred = wind_north[..., 3 : cells_x + 3, 1 : cells_y + 5] - speed * (
        0.5
        * (
            height[..., 3 : cells_x + 3, 2 : cells_y + 6]
            - height[..., 3 : cells_x + 3, 0 : cells_y + 4]
        )
    )
    flux_east = (
        8.0 * (east_pred[..., 3 : cells_x + 3, :] - east_pred[..., 1 : cells_x + 1, :])
        - (east_pred[..., 4 : cells_x + 4, :] - east_pred[..., 0:cells_x, :])
    ) / 12.0
    flux_north = (
        8.0 * (north_pred[..., 3 : cells_y + 3] - north_pred[..., 1 : cells_y + 1])
        - (north_pred[..., 4 : cells_y + 4] - north_pred[..., 0:cells_y])
    ) / 12.0
    height_new = height[..., 3 : cells_x + 3, 3 : cells_y + 3] - speed * (flux_east + flux_north)
    east_inner = east_pred[..., 2 : cells_x + 2, :]
    north_inner = north_pred[..., 2 : cells_y + 2]
    turning = coriolis_part[..., None, :, :]
    return jnp.stack(
        [height_new, east_inner + turning * north_inner, north_inner - turning * east_inner],
        axis=-4,
    )


def one_substep(state, coriolis, wave_speed, edges, count_x, count_y, index_x, index_y):
    faces = state.shape[0]
    cells_x = state.shape[3]
    cells_y = state.shape[4]
    padded = padded_2(state, (("tx", 3), ("ty", 4)), 3)
    west_rim = state[:, :, :, 0:3, :]
    east_rim = jnp.flip(state[:, :, :, cells_x - 3 :, :], 3)
    south_rim = jnp.swapaxes(state[:, :, :, :, 0:3], 3, 4)
    north_rim = jnp.swapaxes(jnp.flip(state[:, :, :, :, cells_y - 3 :], 4), 3, 4)
    west_part = spread(west_rim, "tx", 0)
    east_part = spread(east_rim, "tx", count_x - 1)
    west_full, east_full = (
        lax.all_gather(west_part, "ty", axis=4, tiled=True),
        lax.all_gather(east_part, "ty", axis=4, tiled=True),
    )
    south_row, north_row = (
        lax.all_gather(south_rim, "tx", axis=4, tiled=True),
        lax.all_gather(north_rim, "tx", axis=4, tiled=True),
    )
    south_all, north_all = (
        lax.all_gather(south_row, "ty", axis=0, tiled=True),
        lax.all_gather(north_row, "ty", axis=0, tiled=True),
    )
    south_full = south_all[0:faces]
    north_full = north_all[(count_y - 1) * faces : count_y * faces]
    edge_store = jnp.stack([west_full, east_full, south_full, north_full])
    halos = []
    for side_index in range(4):
        if side_index < 2:
            slabs = jnp.stack(
                [
                    side_halo(edge_store, edges, face_index, side_index, index_y * cells_y, cells_y)
                    for face_index in range(faces)
                ]
            )
        else:
            slabs = jnp.stack(
                [
                    side_halo(edge_store, edges, face_index, side_index, index_x * cells_x, cells_x)
                    for face_index in range(faces)
                ]
            )
        halos.append(slabs)
    west_region = padded[:, :, :, 0:3, 3 : cells_y + 3]
    padded = padded.at[:, :, :, 0:3, 3 : cells_y + 3].set(
        jnp.where(index_x == 0, jnp.flip(halos[0], 3), west_region)
    )
    east_region = padded[:, :, :, cells_x + 3 : cells_x + 6, 3 : cells_y + 3]
    padded = padded.at[:, :, :, cells_x + 3 : cells_x + 6, 3 : cells_y + 3].set(
        jnp.where(index_x == count_x - 1, halos[1], east_region)
    )
    south_region = padded[:, :, :, 3 : cells_x + 3, 0:3]
    padded = padded.at[:, :, :, 3 : cells_x + 3, 0:3].set(
        jnp.where(index_y == 0, jnp.swapaxes(jnp.flip(halos[2], 3), 3, 4), south_region)
    )
    north_region = padded[:, :, :, 3 : cells_x + 3, cells_y + 3 : cells_y + 6]
    padded = padded.at[:, :, :, 3 : cells_x + 3, cells_y + 3 : cells_y + 6].set(
        jnp.where(index_y == count_y - 1, jnp.swapaxes(halos[3], 3, 4), north_region)
    )
    return advance(padded, wave_speed, coriolis, cells_x, cells_y)


def on_device(state, coriolis, wave_speed, edges):
    count_x = lax.axis_size("tx")
    count_y = lax.axis_size("ty")
    index_x = lax.axis_index("tx")
    index_y = lax.axis_index("ty")
    for substep_index in range(SUBSTEPS):
        state = one_substep(state, coriolis, wave_speed, edges, count_x, count_y, index_x, index_y)
    return state


def fits(state):
    count_x = lax.axis_size("tx")
    faces, fields, levels, cells_x, cells_y = state.shape
    return (
        lax.axis_size("ty") == 2
        and faces % 2 == 0
        and levels == 4
        and cells_x == 6
        and cells_y == 24
        and count_x == 8
        and cells_x * count_x == 2 * cells_y
        and 2 * cells_y + 2 * MARGIN <= WINDOW
    )


def either(state, coriolis, wave_speed, edges):
    if fits(state):
        return fast_on_device(state, coriolis, wave_speed, edges)
    return on_device(state, coriolis, wave_speed, edges)


def solution(mesh):
    in_specs = (P("member", None, None, "tx", "ty"), P(None, "tx", "ty"), P(), P())
    out_specs = P("member", None, None, "tx", "ty")
    return jax.shard_map(
        either, mesh=mesh, in_specs=in_specs, out_specs=out_specs, check_vma=False
    )
```

```python
import functools

import jax
import jax.numpy as jnp
from jax import lax
from jax.experimental import pallas as pl
from jax.experimental.pallas import tpu as pltpu
from jax.sharding import PartitionSpec as P

SUBSTEPS = 2
LANES = 128
WINDOW = 64
MARGIN = 8
VMEM_LIMIT = 32 * 1024 * 1024
SMALL_VMEM_LIMIT = 8 * 1024 * 1024


def wrap(index, count):
    index = jnp.where(index < 0, index + count, index)
    return jnp.where(index >= count, index - count, index)


def lane_shift(amount):
    return amount & (LANES - 1)


def windows(source, target, count_x, index_y, cx, cy):
    spare = cy - 2 * cx
    near = jnp.minimum(target, count_x - 1 - target)
    rim = (source == 0) | (source == count_x - 1)
    starts = []
    for inward in (cx // 2, cx):
        start = jnp.maximum(jnp.minimum(cx * near - inward, spare), 0)
        start = jnp.where(rim, start, 0)
        starts.append(jnp.where(index_y == 0, start, spare - start))
    close, far = starts
    upside = source == count_x - 1
    return jnp.where(upside, far, close), jnp.where(upside, close, far)


def unit_place(field, x, cx, group, width):
    per_row = 60 // width
    index = field * cx + x
    return (index // per_row) * group, (index % per_row) * width


def chunk_targets(count_x, full_rows, small_rows):
    sense = 1 - 2 * lax.axis_index("ty")
    return [
        (full_rows + place * small_rows, -sense * distance)
        for place, distance in enumerate((2, 3))
    ]


def put_chunk(cx, cy, count_x, block_ref, line_ref, out_ref, top, offset):
    pairs = 3
    group = 4 * pairs
    fields = 3
    half = cx // 2
    width = 2 * cx
    index_x = lax.axis_index("tx")
    target = wrap(index_x + offset, count_x)
    starts = windows(index_x, target, count_x, lax.axis_index("ty"), cx, cy)
    position = lax.broadcasted_iota(jnp.int32, (group, LANES), 1) % WINDOW
    from_lane = {lane: position >= lane for lane in range(0, 60, width)}
    blocks = {}

    def put(row, lane, lines):
        blocks[row] = lines if row not in blocks else jnp.where(from_lane[lane], lines, blocks[row])

    if block_ref is not None:
        for field in range(fields):
            for x in range(cx):
                row = field * half * group + (x // 2) * group
                at, lane = unit_place(field, x, cx, group, width)
                shift = lane_shift(lane - MARGIN - (x % 2) * cy - starts[x // half])
                put(at, lane, pltpu.roll(block_ref[row : row + group], shift, 1))
    else:
        at = unit_place(fields, 0, cx, group, width)[0]
        blocks[at] = out_ref[top + at : top + at + group]
    if line_ref is not None:
        for part in range(2):
            at, lane = unit_place(fields, part, cx, group, width)
            shift = lane_shift(lane - MARGIN - starts[part])
            put(at, lane, pltpu.roll(line_ref[16 * part : 16 * part + group], shift, 1))
    for row, lines in blocks.items():
        out_ref[top + row : top + row + group] = lines


def pack_kernel(cx, cy, count_x, full_rows, small_rows, state_ref, swap_ref):
    faces, fields = state_ref.shape[:2]
    levels = state_ref.shape[3]
    group = (faces // 2) * levels
    half = cx // 2
    swap_ref[:full_rows] = jnp.zeros((full_rows, LANES), jnp.float32)
    for face in range(faces):
        for parity in range(2):
            lane = (face % 2) * WINDOW + MARGIN + parity * cy
            for xp in range(half):
                for field in range(fields):
                    row = field * half * group + xp * group + (face // 2) * levels
                    swap_ref[row : row + levels, lane : lane + cy] = state_ref[
                        face, field, 2 * xp + parity
                    ]
    for top, offset in chunk_targets(count_x, full_rows, small_rows):
        put_chunk(cx, cy, count_x, swap_ref, None, swap_ref, top, offset)


def pack_coriolis_kernel(
    cx, cy, count_x, full_rows, small_rows, coriolis_ref, swap_in, swap_ref, line_ref
):
    faces = coriolis_ref.shape[0]
    pairs = faces // 2
    half = cx // 2
    base = 3 * half * 4 * pairs
    line_ref[...] = jnp.zeros(line_ref.shape, jnp.float32)
    for face in range(faces):
        lane = (face % 2) * WINDOW + MARGIN
        for x in range(cx):
            line = coriolis_ref[face, x : x + 1]
            row = base + (x // 2) * pairs + face // 2
            at = lane + (x % 2) * cy
            swap_ref[row : row + 1, at : at + cy] = line
            row = (x // half) * 16 + (x % half) * pairs + face // 2
            line_ref[row : row + 1, lane : lane + cy] = line
    for top, offset in chunk_targets(count_x, full_rows, small_rows):
        put_chunk(cx, cy, count_x, None, line_ref, swap_ref, top, offset)


def keep_kernel(cx, cy, count_x, small_rows, swap_ref, line_ref, keep_ref, middle_ref):
    sense = 1 - 2 * lax.axis_index("ty")
    put_chunk(cx, cy, count_x, swap_ref, line_ref, middle_ref, 0, count_x // 2)
    for place, distance in enumerate((2, 3)):
        top = place * small_rows
        put_chunk(cx, cy, count_x, swap_ref, line_ref, keep_ref, top, sense * distance)


def mix_kernel(
    full_rows, small_rows, swap_ref, other_ref, keep_ref, middle_ref,
    near_ref, third_ref, second_ref, fourth_ref,
):
    near_ref[:full_rows] = swap_ref[:full_rows]
    near_ref[full_rows:] = other_ref[:full_rows]
    for place, far_ref in enumerate((second_ref, third_ref)):
        at = place * small_rows
        far_ref[:small_rows] = keep_ref[at : at + small_rows]
        at += full_rows
        far_ref[small_rows:] = other_ref[at : at + small_rows]
    fourth_ref[...] = middle_ref[...]


def placer(cx, cy, count_x, full_rows, small_rows, z_ref, cor_ref):
    fields = z_ref.shape[0]
    levels = 4
    group = z_ref.shape[1] // (cx * count_x + 8)
    pairs = group // levels
    half = cx // 2
    chunk = cx * group
    index_x = lax.axis_index("tx")
    index_y = lax.axis_index("ty")
    south_half = lax.broadcasted_iota(jnp.int32, (group, LANES), 1) % WINDOW < MARGIN + cy
    south_is_own = index_y == 0
    own_half = south_half == south_is_own

    def row_of(x):
        return (x + 4) * group

    def from_owner(offset):
        source = wrap(index_x - offset, count_x)
        return source, pl.multiple_of(source * chunk, 8)

    def put_coriolis(start, x, values, at):
        for pair in range(pairs):
            line = values[at + pair : at + pair + 1]
            rows = pl.ds(start + x * group + pair * levels, levels)
            cor_ref[rows] = jnp.broadcast_to(line, (levels, LANES))

    def put_block(start, lines_of):
        base = fields * half * group
        for field in range(fields):
            for xp in range(half):
                even, odd = lines_of(field * half * group + xp * group, group)
                z_ref[field, pl.ds(start + row_of(2 * xp), group)] = even
                z_ref[field, pl.ds(start + row_of(2 * xp + 1), group)] = odd
        for parity, values in enumerate(lines_of(base, half * pairs)):
            for xp in range(half):
                put_coriolis(start, 2 * xp + parity, values, xp * pairs)

    def put_distant(source, start, lines_of):
        starts_south = windows(source, index_x, count_x, 0, cx, cy)
        starts_north = [cy - 2 * cx - start for start in starts_south]
        is_rim = (source == 0) | (source == count_x - 1)
        starts_north = [jnp.where(is_rim, start, cy - 2 * cx) for start in starts_north]
        shifts = {
            (part, lane): (
                lane_shift(MARGIN + starts_south[part] - lane),
                lane_shift(MARGIN + cy + starts_north[part] - lane),
            )
            for part in range(2)
            for lane in range(0, 60, 2 * cx)
        }

        def lines_at(field, x, part):
            at, lane = unit_place(field, x, cx, group, 2 * cx)
            return lines_of(at, *shifts[part, lane])

        for field in range(fields):
            for x in range(cx):
                z_ref[field, pl.ds(start + row_of(x), group)] = lines_at(field, x, x // half)
        for part in range(2):
            values = lines_at(fields, part, part)
            for x in range(half):
                put_coriolis(start, part * half + x, values, x * pairs)

    def place_own(own_ref, other_ref):
        def own_lines(row, rows):
            mine = own_ref[row : row + rows]
            theirs = other_ref[row : row + rows]
            up, down = index_y * cy, (1 - index_y) * cy
            keep = own_half[:rows]
            even = jnp.where(keep, pltpu.roll(mine, up, 1), pltpu.roll(theirs, down, 1))
            mine = pltpu.roll(mine, lane_shift(-down), 1)
            theirs = pltpu.roll(theirs, lane_shift(-up), 1)
            return even, jnp.where(keep, mine, theirs)

        put_block(from_owner(0)[1], own_lines)

    def place_near(block_ref, toward, south_first):
        south_top = pl.multiple_of(south_first * full_rows, 8)
        north_top = pl.multiple_of((1 - south_first) * full_rows, 8)

        def near_lines(row, rows):
            south = block_ref[pl.ds(south_top + row, rows)]
            north = block_ref[pl.ds(north_top + row, rows)]
            low = south_half[:rows]
            even = jnp.where(low, south, pltpu.roll(north, cy, 1))
            return even, jnp.where(low, pltpu.roll(south, LANES - cy, 1), north)

        put_block(from_owner(toward)[1], near_lines)

    def place_far(block_ref, toward, south_first):
        for place, distance in enumerate((3, 2)):
            top = 2 * place * small_rows
            south_at = pl.multiple_of(top + south_first * small_rows, 8)
            north_at = pl.multiple_of(top + (1 - south_first) * small_rows, 8)

            def far_lines(at, south_shift, north_shift, south_at=south_at, north_at=north_at):
                south = pltpu.roll(block_ref[pl.ds(south_at + at, group)], south_shift, 1)
                north = pltpu.roll(block_ref[pl.ds(north_at + at, group)], north_shift, 1)
                return jnp.where(south_half, south, north)

            put_distant(*from_owner(toward * distance), far_lines)

    def place_middle(got_ref, passed_ref):
        def middle_lines(at, south_shift, north_shift):
            row = 2 * full_rows + at
            mine_shift = jnp.where(south_is_own, south_shift, north_shift)
            other_shift = jnp.where(south_is_own, north_shift, south_shift)
            mine = pltpu.roll(got_ref[row : row + group], mine_shift, 1)
            theirs = pltpu.roll(passed_ref[row : row + group], other_shift, 1)
            return jnp.where(own_half, mine, theirs)

        put_distant(*from_owner(count_x // 2), middle_lines)

    return place_own, place_near, place_far, place_middle


def own_kernel(sizes, own_ref, other_ref, near_ref, z_ref, cor_ref):
    place_own, place_near = placer(*sizes, z_ref, cor_ref)[:2]
    index_y = lax.axis_index("ty")
    place_own(own_ref, other_ref)
    place_near(near_ref, 1 - 2 * index_y, index_y)


def got_kernel(sizes, near_ref, far_ref, passed_ref, z_in, cor_in, z_ref, cor_ref):
    _, place_near, place_far, place_middle = placer(*sizes, z_ref, cor_ref)
    index_y = lax.axis_index("ty")
    place_far(far_ref, 1 - 2 * index_y, index_y)
    place_near(passed_ref, 2 * index_y - 1, 1 - index_y)
    place_middle(near_ref, passed_ref)


def step_kernel(
    sizes, passed_ref, table_in, z_in, cor_in, out_hbm, z_ref, cor_ref,
    pred_ref, store_ref, tile_ref, flip_ref, speed_ref, table_ref, out_ref, sems,
):
    table_copy = pltpu.make_async_copy(table_in, table_ref, sems.at[0])
    table_copy.start()
    cx, cy, count_x = sizes[:3]
    levels = 4
    slots = 16
    cells = cx * count_x
    faces = store_ref.shape[0] // 4
    pairs = faces // 2
    group = pairs * levels
    chunk = cx * group
    index_x = lax.axis_index("tx")
    index_y = lax.axis_index("ty")

    def row_of(x):
        return (x + 4) * group

    def lanes_of(rows):
        return lax.broadcasted_iota(jnp.int32, (rows, LANES), 1)

    place_far = placer(*sizes, z_ref, cor_ref)[2]
    place_far(passed_ref, 2 * index_y - 1, 1 - index_y)

    table_copy.wait()
    level_of = lax.broadcasted_iota(jnp.int32, speed_ref.shape, 0) % levels
    speeds = jnp.full(speed_ref.shape, table_ref[0], jnp.float32)
    for index in range(1, levels):
        speeds = jnp.where(level_of == index, table_ref[index], speeds)
    speed_ref[...] = speeds

    lane_8 = lanes_of(8)
    place_8 = lane_8 % WINDOW
    gap = WINDOW - cells + 3
    wide = gap + 3 * levels
    row_tiles = range(0, cells, 8)
    rim_8 = ((place_8 >= MARGIN - 3) & (place_8 < MARGIN)) | (
        (place_8 >= MARGIN + cells) & (place_8 < MARGIN + cells + 3)
    )

    def collect():
        for pair in range(pairs):
            merged = [jnp.zeros((8, LANES), jnp.float32)] * len(row_tiles)
            for slot, field in ((0, 0), (1, 2)):
                for level in range(levels):
                    offset = slot * wide + 3 * level
                    here = place_8 - offset
                    wanted = ((here >= 0) & (here < 3)) | ((here >= gap) & (here < gap + 3))
                    shift = (offset - (MARGIN + cells - 3)) % LANES
                    lines = z_ref[field, pl.ds(row_of(0) + pair * levels + level, cells, group)]
                    lines = pltpu.roll(lines, shift, 1)
                    merged = [
                        jnp.where(wanted, lines[row : row + 8], old)
                        for row, old in zip(row_tiles, merged)
                    ]
            flip_ref[pair, :, :cells] = jnp.concatenate(merged, axis=0).T
            for slot in range(2):
                for side in (2, 3):
                    for odd in range(2):
                        for depth in range(3):
                            base = slot * wide
                            if side == 3:
                                base += odd * WINDOW + 2 - depth
                            else:
                                base += ((odd + 1) % 2) * WINDOW + gap + depth
                            at = slot * slots + depth * levels
                            store_ref[(2 * pair + odd) * 4 + side, at : at + levels] = flip_ref[
                                pair, pl.ds(base, levels, 3)
                            ]
            for slot in range(2):
                for side in (0, 1):
                    for depth in range(3):
                        x = depth if side == 0 else cells - 1 - depth
                        row = row_of(x) + pair * levels
                        lines = z_ref[slot, row : row + levels]
                        at = slot * slots + depth * levels
                        for odd in range(2):
                            store_ref[(2 * pair + odd) * 4 + side, at : at + levels] = lines

    def fetch(face, side, positions):
        at = levels + (face * 4 + side) * 3
        neighbour = table_ref[at].astype(jnp.int32)
        far_side = table_ref[at + 1].astype(jnp.int32)
        flipped = table_ref[at + 2].astype(jnp.int32)
        first = jnp.where(far_side < 2, MARGIN + WINDOW * (neighbour & 1), 0)
        start = first + jnp.where(flipped == 1, cells - 1, 0)
        step = 1 - 2 * flipped
        sign = ((1 - 2 * (side % 2)) * (2 * (far_side & 1) - 1)).astype(jnp.float32)
        index = neighbour * 4 + far_side
        parts = []
        for slot, position in enumerate(positions):
            order = (start + step * position) & (LANES - 1)
            for half_at in (0, 8):
                at = slot * slots + half_at
                lines = jnp.take_along_axis(store_ref[index, at : at + 8], order, axis=1)
                parts.append(lines if slot == 0 else sign * lines)
        return parts[:2], parts[2:]

    def depth_rows(parts, depth):
        at = (depth % 2) * levels
        return parts[depth // 2][at : at + levels]

    def rim_rows(side):
        left = lane_8 < WINDOW
        for pair in range(pairs):
            first = fetch(2 * pair, side, [lane_8 - MARGIN] * 2)
            second = fetch(2 * pair + 1, side, [lane_8 - (MARGIN + WINDOW)] * 2)
            for slot in range(2):
                both = [jnp.where(left, a, b) for a, b in zip(first[slot], second[slot])]
                for depth in range(3):
                    x = -1 - depth if side == 0 else cells + depth
                    row = row_of(x) + pair * levels
                    z_ref[slot, row : row + levels] = depth_rows(both, depth)

    tile_wide = WINDOW - cells - 3 + 3 * levels

    def put_tile(tile, parts, odd, side, base=0):
        for depth in range(3):
            if side == 3:
                at = base + odd * WINDOW + depth
            else:
                at = base + ((odd + 1) % 2) * WINDOW + tile_wide - 3 * levels + 2 - depth
            tile_ref[tile, pl.ds(at, levels, 3)] = depth_rows(parts, depth)

    def rim_columns_all():
        for pair in range(pairs):
            for odd in range(2):
                for side in (2, 3):
                    for slot, parts in enumerate(fetch(2 * pair + odd, side, [lane_8] * 2)):
                        put_tile(pair, parts, odd, side, slot * tile_wide)
            turned = tile_ref[pair].T[:cells]
            for slot, field in ((0, 0), (1, 2)):
                for level in range(levels):
                    shift = (MARGIN + cells - slot * tile_wide - 3 * level) % LANES
                    rolled = pltpu.roll(turned, shift, 1)
                    at = pl.ds(row_of(0) + pair * levels + level, cells, group)
                    lines = z_ref[field, at]
                    lines = [
                        jnp.where(rim_8, rolled[row : row + 8], lines[row : row + 8])
                        for row in row_tiles
                    ]
                    z_ref[field, at] = jnp.concatenate(lines, axis=0)

    def rim_columns_own():
        for odd in range(2):
            for side in (2, 3):
                total = [jnp.zeros((8, LANES), jnp.float32)] * 2
                for pair in range(pairs):
                    places = [8 * pair, 8 * (pairs + pair)]
                    positions = [lane_8 + (index_x * cx - place) for place in places]
                    fetched = fetch(2 * pair + odd, side, positions)
                    for place, parts in zip(places, fetched):
                        here = (lane_8 >= place) & (lane_8 < place + 8)
                        total = [jnp.where(here, a, b) for a, b in zip(parts, total)]
                put_tile(0, total, odd, side)
        turned = tile_ref[0].T
        for slot, field in ((0, 0), (1, 2)):
            for pair in range(pairs):
                row = 8 * (slot * pairs + pair)
                for level in range(levels):
                    shift = (MARGIN + cells - 3 * level) % LANES
                    rolled = pltpu.roll(turned[row : row + 8], shift, 1)[:cx]
                    start = row_of(0) + index_x * chunk + pair * levels + level
                    at = pl.ds(start, cx, group)
                    z_ref[field, at] = jnp.where(rim_8[:cx], rolled, z_ref[field, at])

    def predict(at, rows):
        speed = speed_ref[:rows]
        ahead = z_ref[0, pl.ds(at + group, rows)]
        behind = z_ref[0, pl.ds(at - group, rows)]
        pred_ref[pl.ds(at, rows)] = z_ref[1, pl.ds(at, rows)] - speed * (0.5 * (ahead - behind))

    def update(at, rows):
        speed = speed_ref[:rows]
        height = z_ref[0, pl.ds(at, rows)]
        north_pred = z_ref[2, pl.ds(at, rows)] - speed * (
            0.5 * (pltpu.roll(height, LANES - 1, 1) - pltpu.roll(height, 1, 1))
        )
        east_pred = pred_ref[pl.ds(at, rows)]
        flux_east = 8.0 * (
            pred_ref[pl.ds(at + group, rows)] - pred_ref[pl.ds(at - group, rows)]
        ) - (pred_ref[pl.ds(at + 2 * group, rows)] - pred_ref[pl.ds(at - 2 * group, rows)])
        flux_north = 8.0 * (
            pltpu.roll(north_pred, LANES - 1, 1) - pltpu.roll(north_pred, 1, 1)
        ) - (pltpu.roll(north_pred, LANES - 2, 1) - pltpu.roll(north_pred, 2, 1))
        height = height - speed * ((flux_east + flux_north) * (1.0 / 12.0))
        turning = cor_ref[pl.ds(at - row_of(0), rows)]
        return height, east_pred + turning * north_pred, north_pred - turning * east_pred

    def all_faces():
        rim_rows(0)
        rim_rows(1)
        rim_columns_all()
        for first in range(-2, cells + 2, 4):
            predict(row_of(first), 4 * group)
        def update_part(index, carry):
            at = pl.multiple_of(row_of(0) + index * (2 * chunk), 8)
            for field, values in enumerate(update(at, 2 * chunk)):
                z_ref[field, pl.ds(at, 2 * chunk)] = values
            return carry

        lax.fori_loop(0, count_x // 2, update_part, 0)

    def own_rows():

        @pl.when(index_x == 0)
        def _():
            rim_rows(0)

        @pl.when(index_x == count_x - 1)
        def _():
            rim_rows(1)

        rim_columns_own()
        at = pl.multiple_of(row_of(0) + index_x * chunk, 8)
        predict(at - 2 * group, chunk + 4 * group)
        copies = []
        for field, values in enumerate(update(at, chunk)):
            for odd in range(2):
                shift = LANES - (MARGIN + odd * WINDOW) - index_y * cy
                rolled = pltpu.roll(values, shift, 1)
                for x in range(cx):
                    for pair in range(pairs):
                        row = x * group + pair * levels
                        out_ref[field, 2 * pair + odd, x] = rolled[row : row + levels, :cy]
            copy = pltpu.make_async_copy(out_ref.at[field], out_hbm.at[:, field], sems.at[1 + field])
            copy.start()
            copies.append(copy)
        for copy in copies:
            copy.wait()

    def substep(index, carry):
        collect()
        pl.when(index == 0)(all_faces)
        pl.when(index == SUBSTEPS - 1)(own_rows)
        return carry

    lax.fori_loop(0, SUBSTEPS, substep, 0)


def fast_on_device(state, coriolis, wave_speed, edges):
    count_x = lax.axis_size("tx")
    faces, fields, levels, cx, cy = state.shape
    pairs = faces // 2
    group = pairs * levels
    cells = cx * count_x
    full_rows = fields * (cx // 2) * group + (cx // 2) * pairs
    full_rows = -(-full_rows // 8) * 8
    small_rows = unit_place(fields, 1, cx, group, 2 * cx)[0] + group
    in_vmem = pl.BlockSpec(memory_space=pltpu.VMEM)
    params = pltpu.CompilerParams(vmem_limit_bytes=SMALL_VMEM_LIMIT)
    swap_shape = jax.ShapeDtypeStruct((full_rows + 2 * small_rows, LANES), jnp.float32)
    swap = pl.pallas_call(
        functools.partial(pack_kernel, cx, cy, count_x, full_rows, small_rows),
        out_shape=swap_shape,
        in_specs=[in_vmem],
        out_specs=in_vmem,
        compiler_params=params,
        name="pack",
    )(jnp.swapaxes(state, 2, 3))
    swap, lines = pl.pallas_call(
        functools.partial(pack_coriolis_kernel, cx, cy, count_x, full_rows, small_rows),
        out_shape=[swap_shape, jax.ShapeDtypeStruct((32, LANES), jnp.float32)],
        in_specs=[in_vmem] * 2,
        out_specs=[in_vmem] * 2,
        input_output_aliases={1: 0},
        compiler_params=params,
        name="pack_coriolis",
    )(coriolis, swap)
    keep, middle = pl.pallas_call(
        functools.partial(keep_kernel, cx, cy, count_x, small_rows),
        out_shape=[
            jax.ShapeDtypeStruct((2 * small_rows, LANES), jnp.float32),
            jax.ShapeDtypeStruct((small_rows, LANES), jnp.float32),
        ],
        in_specs=[pl.BlockSpec(memory_space=pltpu.VMEM)] * 2,
        out_specs=[pl.BlockSpec(memory_space=pltpu.VMEM)] * 2,
        compiler_params=pltpu.CompilerParams(vmem_limit_bytes=SMALL_VMEM_LIMIT),
        name="keep",
    )(swap, lines)

    def moved(block, distance):
        pairs_of = []
        for index in range(count_x):
            for core in range(2):
                target = (index + distance * (1 - 2 * core)) % count_x
                pairs_of.append((2 * index + core, 2 * target + core))
        return lax.ppermute(block, ("tx", "ty"), pairs_of)

    def across(block):
        return lax.ppermute(block, "ty", [(0, 1), (1, 0)])

    other = across(swap)
    messages = pl.pallas_call(
        functools.partial(mix_kernel, full_rows, small_rows),
        out_shape=[
            jax.ShapeDtypeStruct((rows, LANES), jnp.float32)
            for rows in (2 * full_rows, 2 * small_rows, 2 * small_rows, small_rows)
        ],
        in_specs=[in_vmem] * 4,
        out_specs=[in_vmem] * 4,
        compiler_params=params,
        name="messages",
    )(swap, other, keep, middle)
    near, third, second, fourth = [
        moved(block, distance) for block, distance in zip(messages, (1, 3, 2, count_x // 2))
    ]
    near = jnp.concatenate([near, fourth])
    far = jnp.concatenate([third, second])
    table = jnp.concatenate([wave_speed, edges.reshape(-1).astype(jnp.float32)])
    far, table = lax.optimization_barrier((far, table))
    near_passed = across(near)
    far_passed = jnp.concatenate([across(third), across(second)])

    sizes = (cx, cy, count_x, full_rows, small_rows)
    state_rows = [
        jax.ShapeDtypeStruct((fields, (cells + 8) * group, LANES), jnp.float32),
        jax.ShapeDtypeStruct((cells * group, LANES), jnp.float32),
    ]
    rows = pl.pallas_call(
        functools.partial(own_kernel, sizes),
        out_shape=state_rows,
        in_specs=[in_vmem] * 3,
        out_specs=[in_vmem] * 2,
        compiler_params=params,
        name="place_own",
    )(swap, other, near)
    rows = pl.pallas_call(
        functools.partial(got_kernel, sizes),
        out_shape=state_rows,
        in_specs=[in_vmem] * 5,
        out_specs=[in_vmem] * 2,
        input_output_aliases={3: 0, 4: 1},
        compiler_params=params,
        name="place_got",
    )(near, far, near_passed, *rows)
    out, _, _ = pl.pallas_call(
        functools.partial(step_kernel, sizes),
        out_shape=[jax.ShapeDtypeStruct((faces, fields, cx, levels, cy), jnp.float32)]
        + state_rows,
        in_specs=[in_vmem] * 4,
        out_specs=[pl.BlockSpec(memory_space=pltpu.HBM)] + [in_vmem] * 2,
        input_output_aliases={2: 1, 3: 2},
        scratch_shapes=[
            pltpu.VMEM(((cells + 8) * group, LANES), jnp.float32),
            pltpu.VMEM((faces * 4, 32, LANES), jnp.float32),
            pltpu.VMEM((pairs, LANES, LANES), jnp.float32),
            pltpu.VMEM((pairs, LANES, LANES), jnp.float32),
            pltpu.VMEM((2 * cx * group, LANES), jnp.float32),
            pltpu.SMEM(table.shape, jnp.float32),
            pltpu.VMEM((fields, faces, cx, levels, cy), jnp.float32),
            pltpu.SemaphoreType.DMA((1 + fields,)),
        ],
        compiler_params=pltpu.CompilerParams(vmem_limit_bytes=VMEM_LIMIT),
        name="substeps",
    )(far_passed, table, *rows)
    return jnp.swapaxes(out, 2, 3)


def padded_2(block, sides, width):
    for axis, dim in sides:
        count = lax.axis_size(axis)
        forward = [(i, i + 1) for i in range(count - 1)]
        backward = [(target, source) for source, target in forward]
        low = lax.ppermute(
            lax.slice_in_dim(block, block.shape[dim] - width, None, axis=dim), axis, forward
        )
        high = lax.ppermute(lax.slice_in_dim(block, 0, width, axis=dim), axis, backward)
        block = jnp.concatenate([low, block, high], axis=dim)
    return block


def spread(block, axis, owner):
    block = jnp.where(lax.axis_index(axis) == owner, block, jnp.zeros_like(block))
    return lax.psum(block, axis)


def rotate_strip(strip_data, side_index, far_side, flipped):
    normal_part = jnp.where(far_side < 2, strip_data[1], strip_data[2])
    along_part = jnp.where(far_side < 2, strip_data[2], strip_data[1])
    sign_here = 2.0 * (side_index % 2) - 1.0
    sign_there = (2 * (far_side % 2) - 1).astype(jnp.float32)
    normal_part = -sign_here * sign_there * normal_part
    along_part = (1 - 2 * flipped).astype(jnp.float32) * along_part
    if side_index < 2:
        return jnp.stack([strip_data[0], normal_part, along_part])
    return jnp.stack([strip_data[0], along_part, normal_part])


def window_strip(store, side_pick, neighbour, flipped, start, width):
    full_length = store.shape[5]
    begin = jnp.where(flipped == 1, full_length - start - width, start)
    zero = jnp.zeros((), jnp.int32)
    sizes_here = (1, 1, store.shape[2], store.shape[3], store.shape[4], width)
    piece = lax.dynamic_slice(store, (side_pick, neighbour, zero, zero, zero, begin), sizes_here)[
        0, 0
    ]
    return jnp.where(flipped == 1, jnp.flip(piece, 3), piece)


def side_halo(edge_store, edges, face_index, side_index, start, width):
    neighbour = edges[face_index, side_index, 0]
    far_side = edges[face_index, side_index, 1]
    flipped = edges[face_index, side_index, 2]
    strip_data = window_strip(edge_store, far_side, neighbour, flipped, start, width)
    return rotate_strip(strip_data, side_index, far_side, flipped)


def advance(padded, wave_speed, coriolis_part, cells_x, cells_y):
    height = padded[..., 0, :, :, :]
    wind_east = padded[..., 1, :, :, :]
    wind_north = padded[..., 2, :, :, :]
    speed = wave_speed[:, None, None]
    east_pred = wind_east[..., 1 : cells_x + 5, 3 : cells_y + 3] - speed * (
        0.5
        * (
            height[..., 2 : cells_x + 6, 3 : cells_y + 3]
            - height[..., 0 : cells_x + 4, 3 : cells_y + 3]
        )
    )
    north_pred = wind_north[..., 3 : cells_x + 3, 1 : cells_y + 5] - speed * (
        0.5
        * (
            height[..., 3 : cells_x + 3, 2 : cells_y + 6]
            - height[..., 3 : cells_x + 3, 0 : cells_y + 4]
        )
    )
    flux_east = (
        8.0 * (east_pred[..., 3 : cells_x + 3, :] - east_pred[..., 1 : cells_x + 1, :])
        - (east_pred[..., 4 : cells_x + 4, :] - east_pred[..., 0:cells_x, :])
    ) / 12.0
    flux_north = (
        8.0 * (north_pred[..., 3 : cells_y + 3] - north_pred[..., 1 : cells_y + 1])
        - (north_pred[..., 4 : cells_y + 4] - north_pred[..., 0:cells_y])
    ) / 12.0
    height_new = height[..., 3 : cells_x + 3, 3 : cells_y + 3] - speed * (flux_east + flux_north)
    east_inner = east_pred[..., 2 : cells_x + 2, :]
    north_inner = north_pred[..., 2 : cells_y + 2]
    turning = coriolis_part[..., None, :, :]
    return jnp.stack(
        [height_new, east_inner + turning * north_inner, north_inner - turning * east_inner],
        axis=-4,
    )


def one_substep(state, coriolis, wave_speed, edges, count_x, count_y, index_x, index_y):
    faces = state.shape[0]
    cells_x = state.shape[3]
    cells_y = state.shape[4]
    padded = padded_2(state, (("tx", 3), ("ty", 4)), 3)
    west_rim = state[:, :, :, 0:3, :]
    east_rim = jnp.flip(state[:, :, :, cells_x - 3 :, :], 3)
    south_rim = jnp.swapaxes(state[:, :, :, :, 0:3], 3, 4)
    north_rim = jnp.swapaxes(jnp.flip(state[:, :, :, :, cells_y - 3 :], 4), 3, 4)
    west_part = spread(west_rim, "tx", 0)
    east_part = spread(east_rim, "tx", count_x - 1)
    west_full, east_full = (
        lax.all_gather(west_part, "ty", axis=4, tiled=True),
        lax.all_gather(east_part, "ty", axis=4, tiled=True),
    )
    south_row, north_row = (
        lax.all_gather(south_rim, "tx", axis=4, tiled=True),
        lax.all_gather(north_rim, "tx", axis=4, tiled=True),
    )
    south_all, north_all = (
        lax.all_gather(south_row, "ty", axis=0, tiled=True),
        lax.all_gather(north_row, "ty", axis=0, tiled=True),
    )
    south_full = south_all[0:faces]
    north_full = north_all[(count_y - 1) * faces : count_y * faces]
    edge_store = jnp.stack([west_full, east_full, south_full, north_full])
    halos = []
    for side_index in range(4):
        if side_index < 2:
            slabs = jnp.stack(
                [
                    side_halo(edge_store, edges, face_index, side_index, index_y * cells_y, cells_y)
                    for face_index in range(faces)
                ]
            )
        else:
            slabs = jnp.stack(
                [
                    side_halo(edge_store, edges, face_index, side_index, index_x * cells_x, cells_x)
                    for face_index in range(faces)
                ]
            )
        halos.append(slabs)
    west_region = padded[:, :, :, 0:3, 3 : cells_y + 3]
    padded = padded.at[:, :, :, 0:3, 3 : cells_y + 3].set(
        jnp.where(index_x == 0, jnp.flip(halos[0], 3), west_region)
    )
    east_region = padded[:, :, :, cells_x + 3 : cells_x + 6, 3 : cells_y + 3]
    padded = padded.at[:, :, :, cells_x + 3 : cells_x + 6, 3 : cells_y + 3].set(
        jnp.where(index_x == count_x - 1, halos[1], east_region)
    )
    south_region = padded[:, :, :, 3 : cells_x + 3, 0:3]
    padded = padded.at[:, :, :, 3 : cells_x + 3, 0:3].set(
        jnp.where(index_y == 0, jnp.swapaxes(jnp.flip(halos[2], 3), 3, 4), south_region)
    )
    north_region = padded[:, :, :, 3 : cells_x + 3, cells_y + 3 : cells_y + 6]
    padded = padded.at[:, :, :, 3 : cells_x + 3, cells_y + 3 : cells_y + 6].set(
        jnp.where(index_y == count_y - 1, jnp.swapaxes(halos[3], 3, 4), north_region)
    )
    return advance(padded, wave_speed, coriolis, cells_x, cells_y)


def on_device(state, coriolis, wave_speed, edges):
    count_x = lax.axis_size("tx")
    count_y = lax.axis_size("ty")
    index_x = lax.axis_index("tx")
    index_y = lax.axis_index("ty")
    for substep_index in range(SUBSTEPS):
        state = one_substep(state, coriolis, wave_speed, edges, count_x, count_y, index_x, index_y)
    return state


def fits(state):
    count_x = lax.axis_size("tx")
    faces, fields, levels, cells_x, cells_y = state.shape
    return (
        lax.axis_size("ty") == 2
        and faces % 2 == 0
        and levels == 4
        and cells_x == 6
        and cells_y == 24
        and count_x == 8
        and cells_x * count_x == 2 * cells_y
        and 2 * cells_y + 2 * MARGIN <= WINDOW
    )


def either(state, coriolis, wave_speed, edges):
    if fits(state):
        return fast_on_device(state, coriolis, wave_speed, edges)
    return on_device(state, coriolis, wave_speed, edges)


def solution(mesh):
    in_specs = (P("member", None, None, "tx", "ty"), P(None, "tx", "ty"), P(), P())
    out_specs = P("member", None, None, "tx", "ty")
    return jax.shard_map(
        either, mesh=mesh, in_specs=in_specs, out_specs=out_specs, check_vma=False
    )
```
